32 devices in a mesh: energy: 8 (over z, x), slab: 4 (over y, core).
Axes of the slice: x: 2, y: 2, z: 4, core: 2. Of those that a mesh axis runs over, the one named last changes fastest.
Arguments:
- green_iso: float32 [16, 8, 384, 384], P('energy', 'slab')
- coupling: float32 [8, 384, 384], P('slab')
- lead_green: float32 [16, 384, 384], P('energy')
- energy_weight: float32 [16], P('energy'), may hold values from 0.01875 to 0.1875
- energy_group: int32 [16], P('energy'), may hold values from 0 to 3
- group_charge: float32 [4], replicated, may hold values from 0.02 to 0.2
- orbital_atom: int32 [384], replicated, may hold values from 0 to 47
- atom_cell: int32 [8, 48], P('slab'), may hold values from 0 to 65535
- doping: float32 [64, 64, 128], P('slab', 'energy'), may hold values from -6 to 6
Outputs:
- atom_density: float32 [4, 8, 48], P(None, 'slab')
- potential: float32 [64, 64, 128], P('slab', 'energy')
The draws below stay inside these ranges and needn't reach their ends.
All inputs are finite; a program needn't handle non-finite values.
Results may differ from the reference program's by a relative error of at most 0.0001.
Values sent between devices are 32-bit elements; how exact they have to be, the bound alone decides.
No kernel may reach another device: no remote copies, remote signals or barrier semaphores. Data moves between devices by JAX's collectives and lax.ppermute only.
A program may use at most 320 MiB of HBM per device.

```python
import math
import jax
import jax.numpy as jnp
from jax import lax

ORB = 384
ATOMS = 48
GROUPS = 4
GX_S = 8
GZ = 128
ITERS = 3
ENERGIES = 16
SLABS = 8
NX = 64
NY = 64


def rough_block(key, shape, low, high):
    first, second = jax.random.split(key)
    diag_values = jax.random.uniform(first, shape[:-1], jnp.float32, low, high)
    noise = jax.random.normal(second, shape, jnp.float32) * 0.15
    noise = noise / math.sqrt(ORB)
    return noise + diag_values[..., None] * jnp.eye(ORB, dtype=jnp.float32)


def draw_green_iso(key, part):
    return rough_block(jax.random.fold_in(key, 11), (ENERGIES, SLABS, ORB, ORB), 0.8, 1.2)


def draw_lead_green(key, part):
    return rough_block(jax.random.fold_in(key, 13), (ENERGIES, ORB, ORB), 0.5, 2.0)


def draw_coupling(key, part):
    first, second = jax.random.split(jax.random.fold_in(key, 17))
    logs = jax.random.uniform(first, (SLABS, ORB), jnp.float32, math.log(0.5), math.log(0.97))
    noise = jax.random.normal(second, (SLABS, ORB, ORB), jnp.float32) * 0.15
    noise = noise / math.sqrt(ORB)
    return noise + jnp.exp(logs)[..., None] * jnp.eye(ORB, dtype=jnp.float32)


def place_ends(drawn, own_key, low, largest):
    place = [jax.random.randint(jax.random.fold_in(own_key, axis), (), 0, length) for axis, length in enumerate(drawn.shape)]
    main_axis = drawn.shape.index(max(drawn.shape))
    next_to = place[:main_axis] + [(place[main_axis] + 1) % drawn.shape[main_axis]] + place[main_axis + 1:]
    return drawn.at[tuple(place)].set(low).at[tuple(next_to)].set(largest)


def block_scale(stream_key, shape, cuts, smallest, largest):
    def one(dim, shards_of):
        heights = jax.random.uniform(jax.random.fold_in(jax.random.fold_in(stream_key, 6), dim), (shards_of,), jnp.float32, smallest / len(cuts), largest / len(cuts))
        return jnp.repeat(jnp.exp(heights), shape[dim] // shards_of).reshape((-1,) + (1,) * (len(shape) - dim - 1))

    gain = one(*cuts[0])
    for cut in cuts[1:]:
        gain = gain * one(*cut)
    return gain


def normal_values(own_key, extent, scale, most, shards=(), kind=jnp.bfloat16):
    loudness = block_scale(own_key, extent, shards, -0.22, 0.18) if shards else 1.0
    drawn = jax.random.normal(own_key, extent, jnp.float32) * scale * loudness
    return jnp.minimum(jnp.maximum(drawn, -most), most).astype(kind)


def setup_inputs(seed: int = 0) -> dict:
    seeds = jax.random.split(jax.random.key(seed), 10)
    return {
        "green_iso": draw_green_iso(jax.random.fold_in(seeds[9], 71), 0),
        "coupling": draw_coupling(jax.random.fold_in(seeds[9], 71), 0),
        "lead_green": draw_lead_green(jax.random.fold_in(seeds[9], 71), 0),
        "energy_weight": jnp.clip(jnp.exp(math.log(0.1875) - 2.3025851 * jax.random.uniform(seeds[3], (ENERGIES,), jnp.float32) ** block_scale(seeds[3], (ENERGIES,), ((0, 8),), -0.2, 0.2)), 0.01875, 0.1875),
        "energy_group": place_ends(jax.random.randint(seeds[4], (ENERGIES,), 0, GROUPS), jax.random.fold_in(seeds[4], 1), 0, GROUPS - 1).astype(jnp.int32),
        "group_charge": jnp.clip(jnp.exp(jax.random.uniform(seeds[5], (GROUPS,), jnp.float32, math.log(0.02), math.log(0.2))), 0.02, 0.2),
        "orbital_atom": place_ends(jax.random.randint(seeds[6], (ORB,), 0, ATOMS), jax.random.fold_in(seeds[6], 1), 0, ATOMS - 1).astype(jnp.int32),
        "atom_cell": place_ends(jax.random.randint(seeds[7], (SLABS, ATOMS), 0, GX_S * NY * GZ), jax.random.fold_in(seeds[7], 1), 0, (GX_S * NY * GZ) - 1).astype(jnp.int32),
        "doping": normal_values(seeds[8], (NX, NY, GZ), 1.0, 6.0, ((0, 4), (1, 8)), jnp.float32),
    }


def matprod(left, right):
    return jnp.matmul(left, right, precision=lax.Precision.HIGHEST)


def operate(field):
    padded = jnp.pad(field, 1)
    beside = padded[2:, 1:-1, 1:-1] + padded[:-2, 1:-1, 1:-1]
    beside = beside + padded[1:-1, 2:, 1:-1] + padded[1:-1, :-2, 1:-1]
    beside = beside + padded[1:-1, 1:-1, 2:] + padded[1:-1, 1:-1, :-2]
    return 6.5 * field - beside


def reference(green_iso, coupling, lead_green, energy_weight, energy_group, group_charge, orbital_atom, atom_cell, doping):
    propagator = matprod(green_iso, coupling[None])

    def advance(state, slab_terms):
        prop_slab, green_slab = slab_terms
        state = matprod(matprod(prop_slab, state), jnp.swapaxes(prop_slab, -1, -2)) + green_slab
        return state, jnp.diagonal(state, axis1=1, axis2=2)

    final_state, diagonals = lax.scan(advance, lead_green, (jnp.swapaxes(propagator, 0, 1), jnp.swapaxes(green_iso, 0, 1)))
    weights = energy_weight[:, None] * (energy_group[:, None] == jnp.arange(GROUPS)[None, :]).astype(jnp.float32)
    orbital_density = jnp.einsum("eg,seo->gso", weights, diagonals, precision=lax.Precision.HIGHEST)
    membership = (orbital_atom[:, None] == jnp.arange(ATOMS)[None, :]).astype(jnp.float32)
    atom_density = jnp.einsum("gso,oa->gsa", orbital_density, membership, precision=lax.Precision.HIGHEST)
    charge = jnp.einsum("g,gsa->sa", group_charge, atom_density, precision=lax.Precision.HIGHEST)
    block_cells = GX_S * NY * GZ
    target = (jnp.arange(SLABS)[:, None] * block_cells + atom_cell).astype(jnp.int32)
    placed = jax.ops.segment_sum(charge.reshape(-1), target.reshape(-1), num_segments=NX * NY * GZ)
    source = doping + placed.reshape(doping.shape)
    potential = jnp.zeros_like(source)
    residual, direction = source, source
    norm_now = jnp.sum(residual * residual)
    for turn in range(ITERS):
        image = operate(direction)
        alpha = norm_now / jnp.sum(direction * image)
        potential = potential + alpha * direction
        residual = residual - alpha * image
        norm_next = jnp.sum(residual * residual)
        direction = residual + (norm_next / norm_now) * direction
        norm_now = norm_next
    return atom_density, potential
```

```python
import functools

import jax
import jax.numpy as jnp
from jax import lax
from jax.experimental import pallas as pl
from jax.experimental.pallas import tpu as pltpu
from jax.sharding import PartitionSpec as P

ITERS = 3
F32 = jnp.float32
BF16 = jnp.bfloat16
TILE = 128
BOTH = ("energy", "slab")


def split(a):
    high = a.astype(BF16)
    return high, (a - high.astype(F32)).astype(BF16)


def dot(a, b, transposed):
    dims = (((1,), (1 if transposed else 0,)), ((), ()))
    return lax.dot_general(a, b, dims, preferred_element_type=F32)


def product(left, right, transposed=False):
    n = right[0].shape[0 if transposed else 1]
    wide = dot(left[0], jnp.concatenate(right, 0 if transposed else 1), transposed)
    return wide[:, :n] + (wide[:, n:] + dot(left[1], right[0], transposed))


def diagonal_row(matrix):
    n = matrix.shape[0]
    rows = lax.broadcasted_iota(jnp.int32, (n, n), 0)
    columns = lax.broadcasted_iota(jnp.int32, (n, n), 1)
    return jnp.sum(jnp.where(rows == columns, matrix, 0.0), axis=0, keepdims=True)


def block_pairs(count):
    return [(i, j) for i in range(count) for j in range(i, count)]


def pack(matrix, out_ref):
    count = matrix.shape[0] // TILE
    for place, (i, j) in enumerate(block_pairs(count)):
        rows, columns = (slice(i * TILE, (i + 1) * TILE), slice(j * TILE, (j + 1) * TILE))
        out_ref[place] = 0.5 * (matrix[rows, columns] + matrix[columns, rows].T)


def unpack(in_ref, out_ref):
    count = out_ref.shape[0] // TILE
    for place, (i, j) in enumerate(block_pairs(count)):
        rows, columns = (slice(i * TILE, (i + 1) * TILE), slice(j * TILE, (j + 1) * TILE))
        out_ref[rows, columns] = in_ref[place]
        if i != j:
            out_ref[columns, rows] = in_ref[place].T


def copy_all(pairs, sems):
    copies = [pltpu.make_async_copy(src, dst, sems.at[i]) for i, (src, dst) in enumerate(pairs)]
    for copy in copies:
        copy.start()
    return copies


def first_kernel(energy, place_ref, iso, coupling, lead, *refs):
    if energy == 1:
        refs = refs[2:]
    own, sent, packed, diags, c_buf, g_buf, lead_buf, map_buf, sems, out_sem = refs
    place = place_ref[0]
    copies = copy_all(
        [
            (iso.at[energy, 0], g_buf.at[0]),
            (coupling.at[0], c_buf.at[0]),
            (iso.at[energy, 1], g_buf.at[1]),
            (coupling.at[1], c_buf.at[1]),
            (lead.at[energy], lead_buf),
        ],
        sems,
    )
    copies[0].wait()
    copies[1].wait()
    early = product(split(g_buf[0]), split(c_buf[0]))
    early_parts = split(early)
    copies[2].wait()
    copies[3].wait()
    late_parts = split(product(split(g_buf[1]), split(c_buf[1])))
    copies[4].wait()

    @pl.when(place == 0)
    def _():
        state = product(early_parts, split(lead_buf[...]))
        state = product(split(state), early_parts, True) + g_buf[0]
        diags[0:1, :] = diagonal_row(state)
        state = product(late_parts, split(state))
        state = product(split(state), late_parts, True) + g_buf[1]
        diags[1:2, :] = diagonal_row(state)
        pack(state, packed)

    @pl.when(place != 0)
    def _():
        map_buf[0] = early
        map_buf[1] = product(late_parts, early_parts)
        term = product(late_parts, split(g_buf[0]))
        term = product(split(term), late_parts, True) + g_buf[1]
        map_buf[2] = term
        diags[0:1, :] = diagonal_row(g_buf[0])
        diags[1:2, :] = diagonal_row(term)
        core = lax.rem(place, 2)

        @pl.when(core == energy)
        def _():
            copy = pltpu.make_async_copy(map_buf, own, out_sem)
            copy.start()
            copy.wait()

        @pl.when(core != energy)
        def _():
            copy = pltpu.make_async_copy(map_buf, sent, out_sem)
            copy.start()
            copy.wait()


def first_call(energy, place, iso, coupling, lead, maps):
    n = lead.shape[-1]
    blocks = len(block_pairs(n // TILE))
    vmem, hbm = (pl.BlockSpec(memory_space=pltpu.VMEM), pl.BlockSpec(memory_space=pl.ANY))
    smem = pl.BlockSpec(memory_space=pltpu.SMEM)
    map_shape = jax.ShapeDtypeStruct((3, n, n), F32)
    return pl.pallas_call(
        functools.partial(first_kernel, energy),
        out_shape=(
            map_shape,
            map_shape,
            jax.ShapeDtypeStruct((blocks, TILE, TILE), F32),
            jax.ShapeDtypeStruct((8, n), F32),
        ),
        in_specs=[smem, hbm, hbm, hbm] + [hbm] * len(maps),
        out_specs=(hbm, hbm, vmem, vmem),
        input_output_aliases={4: 0, 5: 1} if maps else {},
        scratch_shapes=[
            pltpu.VMEM((2, n, n), F32),
            pltpu.VMEM((2, n, n), F32),
            pltpu.VMEM((n, n), F32),
            pltpu.VMEM((3, n, n), F32),
            pltpu.SemaphoreType.DMA((5,)),
            pltpu.SemaphoreType.DMA,
        ],
        compiler_params=pltpu.CompilerParams(vmem_limit_bytes=24 * 2**20),
        cost_estimate=pl.CostEstimate(flops=36 * n**3, bytes_accessed=24 * n * n, transcendentals=0),
        name=f"slabs_{energy}",
    )(place, iso, coupling, lead, *maps)


def relay_kernel(place_ref, packed, maps, out, diags, state, map_buf, sems):
    @pl.when(place_ref[0] == 1)
    def _():
        copies = copy_all([(maps.at[1], map_buf.at[0]), (maps.at[2], map_buf.at[1])], sems)
        unpack(packed, state)
        copies[0].wait()
        composed = split(map_buf[0])
        term = product(composed, split(state[...]))
        copies[1].wait()
        term = product(split(term), composed, True) + map_buf[1]
        diags[0:1, :] = diagonal_row(term)
        pack(term, out)


def relay_call(place, packed, maps):
    n = maps.shape[-1]
    vmem, hbm = (pl.BlockSpec(memory_space=pltpu.VMEM), pl.BlockSpec(memory_space=pl.ANY))
    smem = pl.BlockSpec(memory_space=pltpu.SMEM)
    return pl.pallas_call(
        relay_kernel,
        out_shape=(
            jax.ShapeDtypeStruct(packed.shape, F32),
            jax.ShapeDtypeStruct((8, n), F32),
        ),
        in_specs=[smem, vmem, hbm],
        out_specs=(vmem, vmem),
        scratch_shapes=[
            pltpu.VMEM((n, n), F32),
            pltpu.VMEM((2, n, n), F32),
            pltpu.SemaphoreType.DMA((2,)),
        ],
        compiler_params=pltpu.CompilerParams(vmem_limit_bytes=16 * 2**20),
        cost_estimate=pl.CostEstimate(flops=12 * n**3, bytes_accessed=12 * n * n, transcendentals=0),
        name="relay",
    )(place, packed, maps)


def pass_kernel(turn, place_ref, packed, own, got, out, state, near_buf, far_buf, sems):
    place = place_ref[0]

    @pl.when((place == 2 * turn) | (place == 2 * turn + 1))
    def _():
        load_maps(lax.rem(place, 2), own, got, near_buf, far_buf, sems)
        unpack(packed, state)
        for buf in (near_buf, far_buf):
            composed = split(buf[1])
            term = product(composed, split(state[...]))
            state[...] = product(split(term), composed, True) + buf[2]
        pack(state[...], out)


def load_maps(core, own, got, near_buf, far_buf, sems):
    @pl.when(core == 0)
    def _():
        for copy in copy_all([(own, near_buf), (got, far_buf)], sems):
            copy.wait()

    @pl.when(core == 1)
    def _():
        for copy in copy_all([(got, near_buf), (own, far_buf)], sems):
            copy.wait()


def pass_call(turn, place, packed, own, got):
    n = own.shape[-1]
    vmem, hbm = (pl.BlockSpec(memory_space=pltpu.VMEM), pl.BlockSpec(memory_space=pl.ANY))
    smem = pl.BlockSpec(memory_space=pltpu.SMEM)
    return pl.pallas_call(
        functools.partial(pass_kernel, turn),
        out_shape=jax.ShapeDtypeStruct(packed.shape, F32),
        in_specs=[smem, vmem, hbm, hbm],
        out_specs=vmem,
        scratch_shapes=[
            pltpu.VMEM((n, n), F32),
            pltpu.VMEM((3, n, n), F32),
            pltpu.VMEM((3, n, n), F32),
            pltpu.SemaphoreType.DMA((2,)),
        ],
        compiler_params=pltpu.CompilerParams(vmem_limit_bytes=24 * 2**20),
        name="pass_on",
    )(place, packed, own, got)


def row_products(left, right):
    return jnp.sum(left * right, axis=1, keepdims=True)


def density_kernel(
    slab_total,
    place_ref,
    weight_ref,
    group_ref,
    orbital_atom,
    first_x,
    second_x,
    first_y,
    second_y,
    own,
    got,
    own_diags,
    got_diags,
    first_diags,
    second_diags,
    first_relayed,
    second_relayed,
    out,
    state,
    near_buf,
    far_buf,
    rows,
    sems,
):
    place = place_ref[0]
    core = lax.rem(place, 2)
    n = state.shape[0]
    rows[...] = jnp.zeros_like(rows)

    def quadratic(matrix, parts):
        return jnp.sum((matrix * product(split(matrix), parts)).T, axis=0, keepdims=True)

    @pl.when(place == 0)
    def _():
        rows[0:2, :] = first_diags[0:2, :]
        rows[2:4, :] = second_diags[0:2, :]

    @pl.when(place == 1)
    def _():
        for copy in copy_all([(got, near_buf), (own, far_buf)], sems):
            copy.wait()
        unpack(first_x, state)
        rows[0:1, :] = first_diags[0:1, :] + quadratic(near_buf[0], split(state[...]))
        rows[1:2, :] = first_relayed[0:1, :]
        unpack(second_x, state)
        rows[2:3, :] = second_diags[0:1, :] + quadratic(far_buf[0], split(state[...]))
        rows[3:4, :] = second_relayed[0:1, :]

    @pl.when(place >= 2)
    def _():
        load_maps(core, own, got, near_buf, far_buf, sems)

        @pl.when(core == 0)
        def _():
            unpack(first_y, state)
            rows[0:2, :] = own_diags[0:2, :]
            rows[2:4, :] = got_diags[0:2, :]

        @pl.when(core == 1)
        def _():
            unpack(second_y, state)
            rows[0:2, :] = got_diags[0:2, :]
            rows[2:4, :] = own_diags[0:2, :]

        parts = split(state[...])
        composed = split(near_buf[1])
        term = product(composed, parts)
        later = product(split(term), composed, True) + near_buf[2]
        rows[0:1, :] += quadratic(near_buf[0], parts)
        rows[1:2, :] += jnp.sum((near_buf[1] * term).T, axis=0, keepdims=True)
        parts = split(later)
        rows[2:3, :] += quadratic(far_buf[0], parts)
        rows[3:4, :] += quadratic(far_buf[1], parts)

    atoms = lax.broadcasted_iota(jnp.int32, (TILE, n), 0)
    member = (atoms == orbital_atom[...]).astype(BF16)
    rest = rows[...]
    folded = jnp.zeros((8, TILE), F32)
    for _ in range(3):
        piece = rest.astype(BF16)
        folded = folded + dot(piece, member, True)
        rest = rest - piece.astype(F32)
    slabs = lax.broadcasted_iota(jnp.int32, (slab_total, TILE), 0)
    for group in range(out.shape[0] // slab_total):
        block = jnp.zeros((slab_total, TILE), F32)
        for row in range(4):
            energy = jnp.where(place < 2, row // 2, core)
            slab = jnp.where(place < 2, 2 * place + row % 2, 2 * (place - core) + row)
            weight = jnp.where(group_ref[energy] == group, weight_ref[energy], 0.0)
            block = block + jnp.where(slabs == slab, weight, 0.0) * folded[row : row + 1, :]
        out[group * slab_total : (group + 1) * slab_total, :] = block


def density_call(place, weight, group, orbital_atom, groups, slab_total, vectors, maps):
    n = orbital_atom.shape[0]
    vmem, hbm = (pl.BlockSpec(memory_space=pltpu.VMEM), pl.BlockSpec(memory_space=pl.ANY))
    smem = pl.BlockSpec(memory_space=pltpu.SMEM)
    return pl.pallas_call(
        functools.partial(density_kernel, slab_total),
        out_shape=jax.ShapeDtypeStruct((groups * slab_total, TILE), F32),
        in_specs=[smem, smem, smem, vmem] + [vmem] * 4 + [hbm] * 2 + [vmem] * 6,
        out_specs=vmem,
        scratch_shapes=[
            pltpu.VMEM((n, n), F32),
            pltpu.VMEM((3, n, n), F32),
            pltpu.VMEM((3, n, n), F32),
            pltpu.VMEM((8, n), F32),
            pltpu.SemaphoreType.DMA((2,)),
        ],
        compiler_params=pltpu.CompilerParams(vmem_limit_bytes=24 * 2**20),
        cost_estimate=pl.CostEstimate(flops=30 * n**3, bytes_accessed=24 * n * n, transcendentals=0),
        name="density",
    )(place, weight, group, orbital_atom.reshape(1, n), *vectors[:4], *maps, *vectors[4:])


def over_slab(value, moves):
    count = lax.axis_size("slab")
    named = dict(moves)
    moves = [(i, named.get(i, i)) for i in range(count)]
    return lax.ppermute(value, "slab", moves)


def pairs_of(count):
    return [(i, i ^ 1) for i in range(count)]


def total_over(value, axis, strides):
    size = 1
    for name in axis if isinstance(axis, tuple) else (axis,):
        size *= lax.axis_size(name)
    got = [lax.ppermute(value, axis, [(i, i ^ k) for i in range(size)]) for k in strides]
    for other in got:
        value = value + other
    return value


def total_over_all(value):
    wires, slabs = (lax.axis_size("energy"), lax.axis_size("slab"))
    value = total_over(value, "slab", (1,))
    stride = 2
    while stride * 2 < slabs:
        value = total_over(value, "slab", (stride,))
        stride *= 2
    value = total_over(value, BOTH, (stride, slabs, stride + slabs))
    stride = 2
    while stride * 4 <= wires:
        value = total_over(value, "energy", (stride, 2 * stride, 3 * stride))
        stride *= 4
    if stride < wires:
        value = total_over(value, "energy", (stride,))
    return value


def with_halo(x, sides, width):
    for axis, dim in sides:
        size, length = (lax.axis_size(axis), x.shape[dim])
        up = [(i, (i + 1) % size) for i in range(size - 1)]
        down = [(j, i) for i, j in up]
        last = lax.slice_in_dim(x, length - width, length, axis=dim)
        initial = lax.slice_in_dim(x, 0, width, axis=dim)
        before = lax.ppermute(last, axis, up)
        after = lax.ppermute(initial, axis, down)
        x = jnp.concatenate([before, x, after], axis=dim)
    return x


def operate(field):
    padded = with_halo(field, (("energy", 1), ("slab", 0)), 1)
    beside = padded[2:, 1:-1] + padded[:-2, 1:-1] + padded[1:-1, 2:] + padded[1:-1, :-2]
    deeper = jnp.pad(field, ((0, 0), (0, 0), (1, 1)))
    beside = beside + deeper[:, :, 2:] + deeper[:, :, :-2]
    return 6.5 * field - beside


def two_products(residual, image):
    pair = jnp.stack([jnp.sum(residual * residual), jnp.sum(residual * image)])
    total = total_over_all(jnp.broadcast_to(pair[:, None], (2, TILE)))
    return total[0, 0], total[1, 0]


def sweep(green_iso, coupling, lead_green, energy_weight, energy_group, groups, orbital_atom):
    devices = lax.axis_size("slab")
    slab_total = devices * green_iso.shape[1]
    place = lax.axis_index("slab").astype(jnp.int32).reshape(1)
    own, sent, packed, first_diags = first_call(0, place, green_iso, coupling, lead_green, ())
    first_x = over_slab(packed, pairs_of(devices))
    own, sent, packed, second_diags = first_call(
        1, place, green_iso, coupling, lead_green, (own, sent)
    )
    second_x = over_slab(packed, pairs_of(devices))
    first_out, first_relayed = relay_call(place, first_x, sent)
    first_y = over_slab(first_out, [(1, 2), (2, 1)])
    got = over_slab(sent, pairs_of(devices)[2:])
    second_out, second_relayed = relay_call(place, second_x, own)
    second_y = over_slab(second_out, [(1, 3), (3, 1)])
    core = lax.rem(place[0], 2)
    own_diags = jnp.where(core == 0, first_diags, second_diags)
    got_diags = lax.ppermute(
        jnp.where(core == 0, second_diags, first_diags), "slab", pairs_of(devices)
    )
    first_in, second_in = (first_y, second_y)
    for turn in range(1, devices // 2 - 1):
        chosen = jnp.where(core == 0, first_in, second_in)
        passed = pass_call(turn, place, chosen, own, got)
        ahead = [(2 * turn + c, 2 * turn + 2 + c) for c in (0, 1)]
        arrived = over_slab(passed, ahead + [(j, i) for i, j in ahead])
        here = place[0] // 2 == turn + 1
        first_in = jnp.where(here, arrived, first_in)
        second_in = jnp.where(here, arrived, second_in)
    vectors = (
        first_x,
        second_x,
        first_in,
        second_in,
        own_diags,
        got_diags,
        first_diags,
        second_diags,
        first_relayed,
        second_relayed,
    )
    return density_call(
        place, energy_weight, energy_group, orbital_atom, groups, slab_total, vectors, (own, got)
    )


def on_device(
    green_iso,
    coupling,
    lead_green,
    energy_weight,
    energy_group,
    group_charge,
    orbital_atom,
    atom_cell,
    doping,
):
    slab_count, atom_count = atom_cell.shape
    groups = group_charge.shape[0]
    partial = sweep(
        green_iso, coupling, lead_green, energy_weight, energy_group, groups, orbital_atom
    )
    density = total_over_all(partial).reshape(groups, -1, TILE)
    atom_density = lax.dynamic_slice(
        density,
        (0, lax.axis_index("slab") * slab_count, 0),
        (groups, slab_count, atom_count),
    )
    charge = jnp.sum(group_charge[:, None, None] * atom_density, axis=0)
    depth = doping.shape[2]
    rows_y = doping.shape[1]
    width_x = doping.shape[0] // slab_count
    full_y = rows_y * lax.axis_size("energy")
    y_start = lax.axis_index("energy") * rows_y
    x_part = atom_cell // (full_y * depth)
    y_part = atom_cell // depth % full_y
    z_part = atom_cell % depth
    slab_place = jnp.arange(slab_count, dtype=jnp.int32)[:, None]
    inside = (y_part >= y_start) & (y_part < y_start + rows_y)
    volume = doping.size
    target = ((slab_place * width_x + x_part) * rows_y + (y_part - y_start)) * depth + z_part
    target = jnp.where(inside, target, volume)
    placed = jax.ops.segment_sum(charge.reshape(-1), target.reshape(-1), num_segments=volume + 1)[
        :volume
    ]
    source = doping + placed.reshape(doping.shape)
    potential = jnp.zeros_like(source)
    residual = source
    image = operate(residual)
    norm_now, product_now = two_products(residual, image)
    alpha = norm_now / product_now
    direction, along = (residual, image)
    for turn in range(ITERS):
        potential = potential + alpha * direction
        residual = residual - alpha * along
        if turn + 1 < ITERS:
            image = operate(residual)
            norm_next, product_now = two_products(residual, image)
            ratio = norm_next / norm_now
            alpha = norm_next / (product_now - ratio * norm_next / alpha)
            direction = residual + ratio * direction
            along = image + ratio * along
            norm_now = norm_next
    return (atom_density, potential)


def solution(mesh):
    in_specs = (
        P("energy", "slab", None, None),
        P("slab", None, None),
        P("energy", None, None),
        P("energy"),
        P("energy"),
        P(),
        P(),
        P("slab", None),
        P("slab", "energy", None),
    )
    out_specs = (P(None, "slab", None), P("slab", "energy", None))
    return jax.shard_map(
        on_device, mesh=mesh, in_specs=in_specs, out_specs=out_specs, check_vma=False
    )
```

```python
import functools

import jax
import jax.numpy as jnp
from jax import lax
from jax.experimental import pallas as pl
from jax.experimental.pallas import tpu as pltpu
from jax.sharding import PartitionSpec as P

ITERS = 3
F32 = jnp.float32
BF16 = jnp.bfloat16
TILE = 128
BOTH = ("energy", "slab")


def split(a):
    high = a.astype(BF16)
    return high, (a - high.astype(F32)).astype(BF16)


def dot(a, b, transposed):
    dims = (((1,), (1 if transposed else 0,)), ((), ()))
    return lax.dot_general(a, b, dims, preferred_element_type=F32)


def product(left, right, transposed=False):
    n = right[0].shape[0 if transposed else 1]
    wide = dot(left[0], jnp.concatenate(right, 0 if transposed else 1), transposed)
    return wide[:, :n] + (wide[:, n:] + dot(left[1], right[0], transposed))


def diagonal_row(matrix):
    n = matrix.shape[0]
    rows = lax.broadcasted_iota(jnp.int32, (n, n), 0)
    columns = lax.broadcasted_iota(jnp.int32, (n, n), 1)
    return jnp.sum(jnp.where(rows == columns, matrix, 0.0), axis=0, keepdims=True)


def block_pairs(count):
    return [(i, j) for i in range(count) for j in range(i, count)]


def pack(matrix, out_ref):
    count = matrix.shape[0] // TILE
    for place, (i, j) in enumerate(block_pairs(count)):
        rows, columns = (slice(i * TILE, (i + 1) * TILE), slice(j * TILE, (j + 1) * TILE))
        out_ref[place] = 0.5 * (matrix[rows, columns] + matrix[columns, rows].T)


def unpack(in_ref, out_ref):
    count = out_ref.shape[0] // TILE
    for place, (i, j) in enumerate(block_pairs(count)):
        rows, columns = (slice(i * TILE, (i + 1) * TILE), slice(j * TILE, (j + 1) * TILE))
        out_ref[rows, columns] = in_ref[place]
        if i != j:
            out_ref[columns, rows] = in_ref[place].T


def copy_all(pairs, sems):
    copies = [pltpu.make_async_copy(src, dst, sems.at[i]) for i, (src, dst) in enumerate(pairs)]
    for copy in copies:
        copy.start()
    return copies


def first_kernel(energy, place_ref, iso, coupling, lead, *refs):
    if energy == 1:
        refs = refs[2:]
    own, sent, packed, diags, c_buf, g_buf, lead_buf, map_buf, sems, out_sem = refs
    place = place_ref[0]
    copies = copy_all(
        [
            (iso.at[energy, 0], g_buf.at[0]),
            (coupling.at[0], c_buf.at[0]),
            (iso.at[energy, 1], g_buf.at[1]),
            (coupling.at[1], c_buf.at[1]),
            (lead.at[energy], lead_buf),
        ],
        sems,
    )
    copies[0].wait()
    copies[1].wait()
    early = product(split(g_buf[0]), split(c_buf[0]))
    early_parts = split(early)
    copies[2].wait()
    copies[3].wait()
    late_parts = split(product(split(g_buf[1]), split(c_buf[1])))
    copies[4].wait()

    @pl.when(place == 0)
    def _():
        state = product(early_parts, split(lead_buf[...]))
        state = product(split(state), early_parts, True) + g_buf[0]
        diags[0:1, :] = diagonal_row(state)
        state = product(late_parts, split(state))
        state = product(split(state), late_parts, True) + g_buf[1]
        diags[1:2, :] = diagonal_row(state)
        pack(state, packed)

    @pl.when(place != 0)
    def _():
        map_buf[0] = early
        map_buf[1] = product(late_parts, early_parts)
        term = product(late_parts, split(g_buf[0]))
        term = product(split(term), late_parts, True) + g_buf[1]
        map_buf[2] = term
        diags[0:1, :] = diagonal_row(g_buf[0])
        diags[1:2, :] = diagonal_row(term)
        core = lax.rem(place, 2)

        @pl.when(core == energy)
        def _():
            copy = pltpu.make_async_copy(map_buf, own, out_sem)
            copy.start()
            copy.wait()

        @pl.when(core != energy)
        def _():
            copy = pltpu.make_async_copy(map_buf, sent, out_sem)
            copy.start()
            copy.wait()


def first_call(energy, place, iso, coupling, lead, maps):
    n = lead.shape[-1]
    blocks = len(block_pairs(n // TILE))
    vmem, hbm = (pl.BlockSpec(memory_space=pltpu.VMEM), pl.BlockSpec(memory_space=pl.ANY))
    smem = pl.BlockSpec(memory_space=pltpu.SMEM)
    map_shape = jax.ShapeDtypeStruct((3, n, n), F32)
    return pl.pallas_call(
        functools.partial(first_kernel, energy),
        out_shape=(
            map_shape,
            map_shape,
            jax.ShapeDtypeStruct((blocks, TILE, TILE), F32),
            jax.ShapeDtypeStruct((8, n), F32),
        ),
        in_specs=[smem, hbm, hbm, hbm] + [hbm] * len(maps),
        out_specs=(hbm, hbm, vmem, vmem),
        input_output_aliases={4: 0, 5: 1} if maps else {},
        scratch_shapes=[
            pltpu.VMEM((2, n, n), F32),
            pltpu.VMEM((2, n, n), F32),
            pltpu.VMEM((n, n), F32),
            pltpu.VMEM((3, n, n), F32),
            pltpu.SemaphoreType.DMA((5,)),
            pltpu.SemaphoreType.DMA,
        ],
        compiler_params=pltpu.CompilerParams(vmem_limit_bytes=24 * 2**20),
        cost_estimate=pl.CostEstimate(flops=36 * n**3, bytes_accessed=24 * n * n, transcendentals=0),
        name=f"slabs_{energy}",
    )(place, iso, coupling, lead, *maps)


def relay_kernel(place_ref, packed, maps, out, diags, state, map_buf, sems):
    @pl.when(place_ref[0] == 1)
    def _():
        copies = copy_all([(maps.at[1], map_buf.at[0]), (maps.at[2], map_buf.at[1])], sems)
        unpack(packed, state)
        copies[0].wait()
        composed = split(map_buf[0])
        term = product(composed, split(state[...]))
        copies[1].wait()
        term = product(split(term), composed, True) + map_buf[1]
        diags[0:1, :] = diagonal_row(term)
        pack(term, out)


def relay_call(place, packed, maps):
    n = maps.shape[-1]
    vmem, hbm = (pl.BlockSpec(memory_space=pltpu.VMEM), pl.BlockSpec(memory_space=pl.ANY))
    smem = pl.BlockSpec(memory_space=pltpu.SMEM)
    return pl.pallas_call(
        relay_kernel,
        out_shape=(
            jax.ShapeDtypeStruct(packed.shape, F32),
            jax.ShapeDtypeStruct((8, n), F32),
        ),
        in_specs=[smem, vmem, hbm],
        out_specs=(vmem, vmem),
        scratch_shapes=[
            pltpu.VMEM((n, n), F32),
            pltpu.VMEM((2, n, n), F32),
            pltpu.SemaphoreType.DMA((2,)),
        ],
        compiler_params=pltpu.CompilerParams(vmem_limit_bytes=16 * 2**20),
        cost_estimate=pl.CostEstimate(flops=12 * n**3, bytes_accessed=12 * n * n, transcendentals=0),
        name="relay",
    )(place, packed, maps)


def pass_kernel(turn, place_ref, packed, own, got, out, state, near_buf, far_buf, sems):
    place = place_ref[0]

    @pl.when((place == 2 * turn) | (place == 2 * turn + 1))
    def _():
        load_maps(lax.rem(place, 2), own, got, near_buf, far_buf, sems)
        unpack(packed, state)
        for buf in (near_buf, far_buf):
            composed = split(buf[1])
            term = product(composed, split(state[...]))
            state[...] = product(split(term), composed, True) + buf[2]
        pack(state[...], out)


def load_maps(core, own, got, near_buf, far_buf, sems):
    @pl.when(core == 0)
    def _():
        for copy in copy_all([(own, near_buf), (got, far_buf)], sems):
            copy.wait()

    @pl.when(core == 1)
    def _():
        for copy in copy_all([(got, near_buf), (own, far_buf)], sems):
            copy.wait()


def pass_call(turn, place, packed, own, got):
    n = own.shape[-1]
    vmem, hbm = (pl.BlockSpec(memory_space=pltpu.VMEM), pl.BlockSpec(memory_space=pl.ANY))
    smem = pl.BlockSpec(memory_space=pltpu.SMEM)
    return pl.pallas_call(
        functools.partial(pass_kernel, turn),
        out_shape=jax.ShapeDtypeStruct(packed.shape, F32),
        in_specs=[smem, vmem, hbm, hbm],
        out_specs=vmem,
        scratch_shapes=[
            pltpu.VMEM((n, n), F32),
            pltpu.VMEM((3, n, n), F32),
            pltpu.VMEM((3, n, n), F32),
            pltpu.SemaphoreType.DMA((2,)),
        ],
        compiler_params=pltpu.CompilerParams(vmem_limit_bytes=24 * 2**20),
        name="pass_on",
    )(place, packed, own, got)


def row_products(left, right):
    return jnp.sum(left * right, axis=1, keepdims=True)


def density_kernel(
    pairs,
    place_ref,
    weight_ref,
    group_ref,
    orbital_atom,
    first_x,
    second_x,
    first_y,
    second_y,
    own,
    got,
    own_diags,
    got_diags,
    first_diags,
    second_diags,
    first_relayed,
    second_relayed,
    extra,
    out,
    state,
    near_buf,
    far_buf,
    rows,
    sems,
):
    place = place_ref[0]
    core = lax.rem(place, 2)
    n = state.shape[0]
    rows[...] = jnp.zeros_like(rows)

    def quadratic(matrix, parts):
        return jnp.sum((matrix * product(split(matrix), parts)).T, axis=0, keepdims=True)

    @pl.when(place == 0)
    def _():
        rows[0:2, :] = first_diags[0:2, :]
        rows[2:4, :] = second_diags[0:2, :]

    @pl.when(place == 1)
    def _():
        for copy in copy_all([(got, near_buf), (own, far_buf)], sems):
            copy.wait()
        unpack(first_x, state)
        rows[0:1, :] = first_diags[0:1, :] + quadratic(near_buf[0], split(state[...]))
        rows[1:2, :] = first_relayed[0:1, :]
        unpack(second_x, state)
        rows[2:3, :] = second_diags[0:1, :] + quadratic(far_buf[0], split(state[...]))
        rows[3:4, :] = second_relayed[0:1, :]

    @pl.when(place >= 2)
    def _():
        load_maps(core, own, got, near_buf, far_buf, sems)

        @pl.when(core == 0)
        def _():
            unpack(first_y, state)
            rows[0:2, :] = own_diags[0:2, :]
            rows[2:4, :] = got_diags[0:2, :]

        @pl.when(core == 1)
        def _():
            unpack(second_y, state)
            rows[0:2, :] = got_diags[0:2, :]
            rows[2:4, :] = own_diags[0:2, :]

        parts = split(state[...])
        composed = split(near_buf[1])
        term = product(composed, parts)
        later = product(split(term), composed, True) + near_buf[2]
        rows[0:1, :] += quadratic(near_buf[0], parts)
        rows[1:2, :] += jnp.sum((near_buf[1] * term).T, axis=0, keepdims=True)
        parts = split(later)
        rows[2:3, :] += quadratic(far_buf[0], parts)
        rows[3:4, :] += quadratic(far_buf[1], parts)

    atoms = lax.broadcasted_iota(jnp.int32, (TILE, n), 0)
    member = (atoms == orbital_atom[...]).astype(BF16)
    rest = rows[...]
    folded = jnp.zeros((8, TILE), F32)
    for _ in range(3):
        piece = rest.astype(BF16)
        folded = folded + dot(piece, member, True)
        rest = rest - piece.astype(F32)
    turned = pltpu.roll(folded, HALF, 1)
    pair_rows = lax.broadcasted_iota(jnp.int32, (pairs, TILE), 0)
    groups = (out.shape[0] - extra.shape[0]) // pairs
    for group in range(groups):
        block = jnp.zeros((pairs, TILE), F32)
        for row in range(4):
            energy = jnp.where(place < 2, row // 2, core)
            pair = jnp.where(place < 2, place, place - core + row // 2)
            weight = jnp.where(group_ref[energy] == group, weight_ref[energy], 0.0)
            value = (turned if row % 2 else folded)[row : row + 1, :]
            block = block + jnp.where(pair_rows == pair, weight, 0.0) * value
        out[group * pairs : (group + 1) * pairs, :] = block
    out[groups * pairs :, :] = extra[...]


def density_call(place, weight, group, orbital_atom, groups, pairs, vectors, maps):
    n = orbital_atom.shape[0]
    vmem, hbm = (pl.BlockSpec(memory_space=pltpu.VMEM), pl.BlockSpec(memory_space=pl.ANY))
    smem = pl.BlockSpec(memory_space=pltpu.SMEM)
    return pl.pallas_call(
        functools.partial(density_kernel, pairs),
        out_shape=jax.ShapeDtypeStruct((groups * pairs + vectors[-1].shape[0], TILE), F32),
        in_specs=[smem, smem, smem, vmem] + [vmem] * 4 + [hbm] * 2 + [vmem] * 7,
        out_specs=vmem,
        scratch_shapes=[
            pltpu.VMEM((n, n), F32),
            pltpu.VMEM((3, n, n), F32),
            pltpu.VMEM((3, n, n), F32),
            pltpu.VMEM((8, n), F32),
            pltpu.SemaphoreType.DMA((2,)),
        ],
        compiler_params=pltpu.CompilerParams(vmem_limit_bytes=24 * 2**20),
        cost_estimate=pl.CostEstimate(flops=30 * n**3, bytes_accessed=24 * n * n, transcendentals=0),
        name="density",
    )(place, weight, group, orbital_atom.reshape(1, n), *vectors[:4], *maps, *vectors[4:])


def over_slab(value, moves):
    count = lax.axis_size("slab")
    named = dict(moves)
    moves = [(i, named.get(i, i)) for i in range(count)]
    return lax.ppermute(value, "slab", moves)


def pairs_of(count):
    return [(i, i ^ 1) for i in range(count)]


def total_over(value, axis, strides):
    size = 1
    for name in axis if isinstance(axis, tuple) else (axis,):
        size *= lax.axis_size(name)
    got = [lax.ppermute(value, axis, [(i, i ^ k) for i in range(size)]) for k in strides]
    if len(got) == 1:
        return value + got[0]
    return (value + got[0]) + (got[1] + got[2])


def total_over_all(value):
    wires, slabs = (lax.axis_size("energy"), lax.axis_size("slab"))
    value = total_over(value, "slab", (1,))
    stride = 2
    while stride * 2 < slabs:
        value = total_over(value, "slab", (stride,))
        stride *= 2
    value = total_over(value, BOTH, (stride, slabs, stride + slabs))
    stride = 2
    while stride * 4 <= wires:
        value = total_over(value, "energy", (stride, 2 * stride, 3 * stride))
        stride *= 4
    if stride < wires:
        value = total_over(value, "energy", (stride,))
    return value


REACH = 5
HALF = 64


def edges_kernel(index_ref, cells, field, out, row):
    place = index_ref[0]
    atoms = cells.shape[1]
    length = field.shape[0]
    even = lax.rem(place, 2) == 0
    out[:REACH] = jnp.where(even, field[length - REACH :], field[:REACH])
    row[...] = jnp.zeros_like(row)
    row[0:1, 0:atoms] = cells[0:1, :].astype(F32)
    row[0:1, HALF : HALF + atoms] = cells[1:2, :].astype(F32)
    rows = lax.broadcasted_iota(jnp.int32, out.shape[1:], 0)
    out[REACH] = jnp.where(rows == place, row[0:1, :], 0.0)


def mix_kernel(index_ref, field, mine, other, out):
    length = field.shape[0]
    even = lax.rem(index_ref[0], 2) == 0
    out[:REACH] = jnp.where(even, field[:REACH], field[length - REACH :])
    out[REACH] = mine[REACH] + other[REACH]


def join_kernel(devices, index_ref, field, mixed, first, second, out, cells):
    place = index_ref[0]
    length = field.shape[0]
    even = lax.rem(place, 2) == 0
    one, two = (first[:REACH], second[:REACH])
    out[:REACH] = jnp.where(even, jnp.where(place == 0, 0.0, two), one)
    out[REACH : REACH + length] = field[...]
    out[REACH + length :] = jnp.where(even, one, jnp.where(place == devices - 1, 0.0, two))
    cells[...] = mixed[REACH] + second[REACH]


def shifted_pair(x, axis):
    size = x.shape[axis]
    before, after = (pltpu.roll(x, 1, axis), pltpu.roll(x, size - 1, axis))
    if axis == x.ndim - 1:
        lanes = lax.broadcasted_iota(jnp.int32, x.shape, axis)
        before = jnp.where(lanes == 0, 0.0, before)
        after = jnp.where(lanes == size - 1, 0.0, after)
    return before, after


def neighbours(x):
    centre = x[1:-1]
    up, down = shifted_pair(centre, 1)
    left, right = shifted_pair(centre, 2)
    return (x[2:] + x[:-2]) + (up + down) + (left + right)


def differences(x):
    centre = x[1:-1]
    up, down = shifted_pair(centre, 1)
    left, right = shifted_pair(centre, 2)
    along = (x[2:] - centre) + (x[:-2] - centre)
    across = (up - centre) + (down - centre)
    deep = (left - centre) + (right - centre)
    return along + (across + deep)


def grid_mask(shape, margin, length, rows, place, devices, wire, wires):
    planes = lax.broadcasted_iota(jnp.int32, shape, 0)
    row = lax.broadcasted_iota(jnp.int32, shape, 1)
    low_x = jnp.where(place == 0, margin, 0)
    high_x = jnp.where(place == devices - 1, margin + length, shape[0])
    low_y = jnp.where(wire == 0, rows, 0)
    high_y = jnp.where(wire == wires - 1, 2 * rows, shape[1])
    inside = (planes >= low_x) & (planes < high_x) & (row >= low_y) & (row < high_y)
    return inside.astype(F32)


def three_parts(x):
    parts = []
    for _ in range(3):
        parts.append(x.astype(BF16))
        x = x - parts[-1].astype(F32)
    return parts


def coordinates(cell, rows_y, depth):
    z_part = cell - depth * jnp.floor(cell * (1.0 / depth))
    plane = jnp.floor(cell * (1.0 / depth))
    x_part = jnp.floor(plane * (1.0 / rows_y))
    return x_part, plane - rows_y * x_part, z_part


WALKS = ((0, 1),), ((1, 1),), ((0, 2), (2, 1)), ((1, 3), (3, 1)), ((0, 6), (2, 4), (4, 1)), ((1, 10), (3, 5), (5, 1))
FACTORIAL = (1.0, 1.0, 2.0, 6.0, 24.0, 120.0)


def walk_counts(here, there, length):
    apart = jnp.abs(here - there)
    low = here + there + 2.0
    high = 2.0 * length - here - there
    at = []
    for steps in range(6):
        value = (apart == steps).astype(F32)
        if steps >= 2:
            value = value - (low == steps).astype(F32) - (high == steps).astype(F32)
        at.append(value)
    counts = []
    for steps, terms in enumerate(WALKS):
        total = None
        for distance, count in terms:
            term = at[distance] * (count / FACTORIAL[steps])
            total = term if total is None else total + term
        counts.append(total)
    return counts


def convolved(left, right):
    result = []
    for steps in range(6):
        total = left[0] * right[steps]
        for part in range(1, steps + 1):
            total = total + left[part] * right[steps - part]
        result.append(total)
    return result


def prepare_kernel(
    devices, wires, width_x, atoms, index_ref, cells, left, field, right, out, walks, row_hot, deep_hot
):
    place, wire = (index_ref[0], index_ref[1])
    planes, rows, depth = field.shape
    length = planes - 2 * REACH
    grid_y = rows * wires
    pairs = devices
    whole = (planes, 3 * rows, depth)
    mask = grid_mask(whole, REACH, length, rows, place, devices, wire, wires)
    source = jnp.concatenate([left[...], field[...], right[...]], axis=1) * mask

    def inner(x):
        extra = (x.shape[0] - length) // 2
        return x[extra : extra + length, rows : 2 * rows]

    chain = [source]
    for step in range(1, 6):
        chain.append(neighbours(chain[-1]) * mask[step : planes - step])
    blocks = [inner(x) for x in chain]
    near = source[2:-2]
    other = [near]
    for step in range(1, 4):
        other.append(differences(other[-1]) * mask[2 + step : planes - 2 - step])
    other = [inner(x) for x in other]
    lanes = lax.broadcasted_iota(jnp.int32, (8, depth), 1)
    sums = jnp.zeros((8, depth), F32)
    for base, fields in enumerate((blocks, other)):
        for steps in range(6):
            part = jnp.sum(fields[steps // 2] * fields[(steps + 1) // 2], axis=0)
            part = jnp.sum(jnp.sum(part, axis=1, keepdims=True), axis=0, keepdims=True)
            sums = jnp.where(lanes == 8 * base + steps, part, sums)
    out[...] = jnp.zeros_like(out)
    out[6 * pairs : 6 * pairs + 8, :] = sums
    mine = cells[pl.ds(place, 1), :]
    lane = lax.broadcasted_iota(jnp.int32, (1, depth), 1)
    odd = (lane >= HALF).astype(F32)
    used = lax.rem(lane, HALF) < atoms
    x_part, y_part, z_part = coordinates(mine, grid_y, depth)
    start = (wire * rows).astype(F32)
    ours = used & (y_part >= start) & (y_part < start + rows)
    at_row = jnp.where(ours, (x_part + width_x * odd) * rows + y_part - start, -1.0)
    cell_rows = length * rows
    row_iota = lax.broadcasted_iota(jnp.int32, (cell_rows, depth), 0).astype(F32)
    deep_iota = lax.broadcasted_iota(jnp.int32, (depth, depth), 0).astype(F32)
    at_rows = (row_iota == at_row).astype(F32)
    at_deep = (deep_iota == z_part).astype(BF16)
    for steps, block in enumerate(blocks):
        value = jnp.zeros((cell_rows, depth), F32)
        for part in three_parts(block.reshape(cell_rows, depth)):
            value = value + dot(part, at_deep, False)
        value = jnp.sum(value * at_rows, axis=0, keepdims=True)
        out[pl.ds(steps * pairs + place, 1), :] = value
    row_cells = cells[...]
    row_x, row_y, row_z = coordinates(row_cells, grid_y, depth)
    padded = jnp.concatenate([row_cells, jnp.zeros((depth - 8, depth), F32)], axis=0)
    column_x, column_y, column_z = coordinates(padded.T, grid_y, depth)
    row_lane = lax.broadcasted_iota(jnp.int32, (8, depth), 1)
    next_x, next_y, next_z = [jnp.concatenate([v[1:], v[:1]], axis=0) for v in (row_x, row_y, row_z)]

    def turned(now, later, step_now, step_later):
        value = jnp.where(row_lane >= HALF, now + step_now, later + step_later)
        return pltpu.roll(value, HALF, 1)

    even_x = row_x + width_x * (row_lane >= HALF).astype(F32)
    odd_x, odd_y, odd_z = (
        turned(row_x, next_x, 0.0, float(width_x)),
        turned(row_y, next_y, 0.0, 0.0),
        turned(row_z, next_z, 0.0, 0.0),
    )
    for slab in range(2 * pairs):
        pair, side = (slab // 2, slab % 2)
        base = float(slab * width_x)
        if side:
            there = (odd_x, odd_y, odd_z)
        else:
            there = (even_x, row_y, row_z)
        there = [v[pair : pair + 1, :] for v in there]
        here = [
            v[side * HALF : side * HALF + atoms, pair : pair + 1]
            for v in (column_x, column_y, column_z)
        ]
        shape = (atoms, depth)
        sizes = (2 * pairs * width_x, grid_y, depth)
        axes = []
        for axis in range(3):
            shift = base if axis == 0 else 0.0
            axes.append(
                walk_counts(
                    jnp.broadcast_to(here[axis] + shift, shape),
                    jnp.broadcast_to(there[axis] + shift, shape),
                    float(sizes[axis]),
                )
            )
        total = convolved(convolved(axes[0], axes[1]), axes[2])
        for steps in range(6):
            walks[steps, slab * atoms : (slab + 1) * atoms, :] = total[steps] * FACTORIAL[steps]
    wide = length + 4
    first_x = (place * length - 2).astype(F32)
    first_y = start - rows
    count = wide * 3 * rows
    rows_iota = lax.broadcasted_iota(jnp.int32, (count, depth), 0).astype(F32)
    used_row = lax.rem(row_lane, HALF) < atoms
    for pair in range(pairs):
        x_at = even_x[pair : pair + 1, :] + float(2 * pair * width_x) - first_x
        y_at = row_y[pair : pair + 1, :] - first_y
        good = (x_at >= 0) & (x_at < wide) & (y_at >= 0) & (y_at < 3 * rows) & used_row[0:1, :]
        target = jnp.where(good, x_at * (3 * rows) + y_at, -1.0)
        row_hot[:, pair * depth : (pair + 1) * depth] = (rows_iota == target).astype(BF16)
        z_at = column_z[:, pair : pair + 1]
        lanes_z = lax.broadcasted_iota(jnp.int32, (depth, depth), 1).astype(F32)
        deep_hot[pair * depth : (pair + 1) * depth, :] = (lanes_z == z_at).astype(F32)


def total_of(x):
    return jnp.sum(jnp.sum(x, axis=1, keepdims=True), axis=0, keepdims=True)


def quadratic_form(poly, moments, shift):
    total = None
    for i, one in enumerate(poly):
        for j, two in enumerate(poly):
            if j < i:
                continue
            term = one * two * moments[i + j + shift] * (1.0 if i == j else 2.0)
            total = term if total is None else total + term
    return total


def finish_kernel(
    devices,
    wires,
    atoms,
    index_ref,
    charge_ref,
    payload,
    walks,
    row_hot,
    deep_hot,
    left,
    field,
    right,
    density,
    potential,
):
    place, wire = (index_ref[0], index_ref[1])
    planes, rows, depth = field.shape
    length = planes - 2 * REACH
    pairs = devices
    groups = density.shape[0]
    charge = charge_ref[0] * payload[0:pairs, :]
    for group in range(1, groups):
        charge = charge + charge_ref[group] * payload[group * pairs : (group + 1) * pairs, :]
    for group in range(groups):
        value = payload[pl.ds(group * pairs + place, 1), :]
        density[group, 0:1, :] = value[:, :atoms]
        density[group, 1:2, :] = pltpu.roll(value, HALF, 1)[:, :atoms]
    square = jnp.concatenate([charge, jnp.zeros((depth - pairs, depth), F32)], axis=0)
    columns = square.T
    later = jnp.concatenate([charge[1:], jnp.zeros((1, depth), F32)], axis=0)
    lanes = lax.broadcasted_iota(jnp.int32, (pairs, depth), 1)
    even_row = jnp.where(lanes >= HALF, 2.0 * charge, charge)
    odd_row = pltpu.roll(jnp.where(lanes >= HALF, charge, 2.0 * later), HALF, 1)
    totals = [None] * 6
    for slab in range(2 * pairs):
        pair, side = (slab // 2, slab % 2)
        row = (odd_row if side else even_row)[pair : pair + 1, :]
        column = columns[side * HALF : side * HALF + atoms, pair : pair + 1]
        outer = column * row
        for steps in range(6):
            term = walks[steps, slab * atoms : (slab + 1) * atoms, :] * outer
            totals[steps] = term if totals[steps] is None else totals[steps] + term
    base = groups * pairs
    crossed = []
    for steps in range(6):
        cross = 2.0 * charge * payload[base + steps * pairs : base + (steps + 1) * pairs, :]
        crossed.append(total_of(totals[steps]) + total_of(cross))
    sums = payload[base + 6 * pairs : base + 6 * pairs + 1, :]
    plain = [sums[:, steps : steps + 1] + crossed[steps] for steps in range(6)]
    moved = []
    for steps in range(6):
        value = sums[:, 8 + steps : 9 + steps]
        binomial = 1
        for part in range(steps, -1, -1):
            value = value + (binomial * (-6.0) ** (steps - part)) * crossed[part]
            binomial = binomial * part // (steps - part + 1)
        moved.append(value)
    smooth = plain[1] > 3.5 * plain[0]
    level = jnp.where(smooth, 0.5, 6.5)
    moments = [jnp.where(smooth, two, one) for one, two in zip(plain, moved)]
    residual, direction = ([jnp.ones_like(level)], [jnp.ones_like(level)])
    norm = moments[0]
    alphas, betas = ([], [])
    for turn in range(ITERS):
        energy = level * quadratic_form(direction, moments, 0) - quadratic_form(direction, moments, 1)
        alpha = norm / energy
        alphas.append(alpha)
        if turn + 1 == ITERS:
            break
        longer = residual + [jnp.zeros_like(level)]
        for i, value in enumerate(direction):
            longer[i] = longer[i] - alpha * level * value
            longer[i + 1] = longer[i + 1] + alpha * value
        residual = longer
        following = quadratic_form(residual, moments, 0)
        beta = following / norm
        betas.append(beta)
        norm = following
        direction = [
            value + beta * direction[i] if i < len(direction) else value
            for i, value in enumerate(residual)
        ]
    pieces = [[], [], []]
    for pair in range(pairs):
        hot = deep_hot[pair * depth : (pair + 1) * depth, :]
        for place_in, piece in enumerate(three_parts(columns[:, pair : pair + 1] * hot)):
            pieces[place_in].append(piece)
    spread = jnp.concatenate([jnp.concatenate(piece, axis=0) for piece in pieces], axis=1)
    placed = dot(row_hot[...], spread, False)
    placed = placed[:, :depth] + (placed[:, depth : 2 * depth] + placed[:, 2 * depth :])
    margin = ITERS - 1
    wide = (length + 2 * margin, 3 * rows, depth)
    mask = grid_mask(wide, margin, length, rows, place, devices, wire, wires)
    cut = slice(REACH - margin, REACH + length + margin)
    source = jnp.concatenate([left[cut], field[cut], right[cut]], axis=1) * mask
    source = source + placed.reshape(wide)
    residual, direction = (source, source)
    total = alphas[0] * source[margin:-margin, rows : 2 * rows]
    for turn in range(ITERS - 1):
        image = 6.5 * direction[1:-1] - neighbours(direction)
        inner_mask = mask[turn + 1 : wide[0] - turn - 1]
        residual = (residual[1:-1] - alphas[turn] * image) * inner_mask
        direction = residual + betas[turn] * direction[1:-1]
        extra = margin - turn - 1
        block = direction[extra : extra + length, rows : 2 * rows]
        total = total + alphas[turn + 1] * block
    potential[...] = total


def local_call(kernel, shapes, scratch, specs, name, limit, *operands):
    vmem, smem = (pl.BlockSpec(memory_space=pltpu.VMEM), pl.BlockSpec(memory_space=pltpu.SMEM))
    single = not isinstance(shapes, tuple)
    return pl.pallas_call(
        kernel,
        out_shape=shapes,
        in_specs=[smem if spec == "s" else vmem for spec in specs],
        out_specs=vmem if single else (vmem,) * len(shapes),
        scratch_shapes=scratch,
        compiler_params=pltpu.CompilerParams(vmem_limit_bytes=limit * 2**20),
        name=name,
    )(*operands)


def gather_field(index, atom_cell, doping):
    devices, wires = (lax.axis_size("slab"), lax.axis_size("energy"))
    length, rows, depth = doping.shape
    edge = jax.ShapeDtypeStruct((REACH + 1, rows, depth), F32)
    scratch = [pltpu.VMEM((8, depth), F32)]
    mine = local_call(edges_kernel, edge, scratch, "svv", "edges", 8, index, atom_cell, doping)
    first = lax.ppermute(mine, "slab", pairs_of(devices))
    mixed = local_call(mix_kernel, edge, [], "svvv", "mix", 8, index, doping, mine, first)
    turn = [(i, (i + 1) % devices if i % 2 else (i - 1) % devices) for i in range(devices)]
    second = lax.ppermute(mixed, "slab", turn)
    shapes = (
        jax.ShapeDtypeStruct((length + 2 * REACH, rows, depth), F32),
        jax.ShapeDtypeStruct((rows, depth), F32),
    )
    field, cells = local_call(
        functools.partial(join_kernel, devices),
        shapes,
        [],
        "svvvv",
        "join",
        8,
        index,
        doping,
        mixed,
        first,
        second,
    )
    if devices > 4:
        cells = lax.psum(mine[REACH], "slab")
    right = lax.ppermute(field, "energy", [((i + 1) % wires, i) for i in range(wires)])
    left = lax.ppermute(field, "energy", [(i, (i + 1) % wires) for i in range(wires)])
    return cells, left, field, right


def prepare(index, cells, left, field, right, atom_cell):
    devices, wires = (lax.axis_size("slab"), lax.axis_size("energy"))
    planes, rows, depth = field.shape
    length = planes - 2 * REACH
    atoms = atom_cell.shape[1]
    shapes = (
        jax.ShapeDtypeStruct((6 * devices + 8, depth), F32),
        jax.ShapeDtypeStruct((6, 2 * devices * atoms, depth), F32),
        jax.ShapeDtypeStruct(((length + 4) * 3 * rows, devices * depth), BF16),
        jax.ShapeDtypeStruct((devices * depth, depth), F32),
    )
    kernel = functools.partial(prepare_kernel, devices, wires, length // 2, atoms)
    return local_call(kernel, shapes, [], "svvvv", "prepare", 32, index, cells, left, field, right)


def finish(index, group_charge, payload, prepared, left, field, right, atom_cell):
    devices, wires = (lax.axis_size("slab"), lax.axis_size("energy"))
    planes, rows, depth = field.shape
    slabs, atoms = atom_cell.shape
    shapes = (
        jax.ShapeDtypeStruct((group_charge.shape[0], slabs, atoms), F32),
        jax.ShapeDtypeStruct((planes - 2 * REACH, rows, depth), F32),
    )
    kernel = functools.partial(finish_kernel, devices, wires, atoms)
    return local_call(
        kernel,
        shapes,
        [],
        "ssvvvvvvv",
        "finish",
        32,
        index,
        group_charge,
        payload,
        *prepared,
        left,
        field,
        right,
    )


def sweep(
    place,
    green_iso,
    coupling,
    lead_green,
    energy_weight,
    energy_group,
    groups,
    orbital_atom,
    extra,
):
    devices = lax.axis_size("slab")
    own, sent, packed, first_diags = first_call(0, place, green_iso, coupling, lead_green, ())
    first_x = over_slab(packed, pairs_of(devices))
    own, sent, packed, second_diags = first_call(
        1, place, green_iso, coupling, lead_green, (own, sent)
    )
    second_x = over_slab(packed, pairs_of(devices))
    first_out, first_relayed = relay_call(place, first_x, sent)
    first_y = over_slab(first_out, [(1, 2), (2, 1)])
    got = over_slab(sent, pairs_of(devices)[2:])
    second_out, second_relayed = relay_call(place, second_x, own)
    second_y = over_slab(second_out, [(1, 3), (3, 1)])
    core = lax.rem(place[0], 2)
    own_diags = jnp.where(core == 0, first_diags, second_diags)
    got_diags = lax.ppermute(
        jnp.where(core == 0, second_diags, first_diags), "slab", pairs_of(devices)
    )
    first_in, second_in = (first_y, second_y)
    for turn in range(1, devices // 2 - 1):
        chosen = jnp.where(core == 0, first_in, second_in)
        passed = pass_call(turn, place, chosen, own, got)
        ahead = [(2 * turn + c, 2 * turn + 2 + c) for c in (0, 1)]
        arrived = over_slab(passed, ahead + [(j, i) for i, j in ahead])
        here = place[0] // 2 == turn + 1
        first_in = jnp.where(here, arrived, first_in)
        second_in = jnp.where(here, arrived, second_in)
    vectors = (
        first_x,
        second_x,
        first_in,
        second_in,
        own_diags,
        got_diags,
        first_diags,
        second_diags,
        first_relayed,
        second_relayed,
        extra,
    )
    return density_call(
        place, energy_weight, energy_group, orbital_atom, groups, devices, vectors, (own, got)
    )


def on_device(
    green_iso,
    coupling,
    lead_green,
    energy_weight,
    energy_group,
    group_charge,
    orbital_atom,
    atom_cell,
    doping,
):
    groups = group_charge.shape[0]
    index = jnp.stack([lax.axis_index("slab"), lax.axis_index("energy")]).astype(jnp.int32)
    cells, *fields = gather_field(index, atom_cell, doping)
    extra, *prepared = prepare(index, cells, *fields, atom_cell)
    payload = sweep(
        index,
        green_iso,
        coupling,
        lead_green,
        energy_weight,
        energy_group,
        groups,
        orbital_atom,
        extra,
    )
    payload = total_over_all(payload)
    return finish(index, group_charge, payload, prepared, *fields, atom_cell)


def solution(mesh):
    in_specs = (
        P("energy", "slab", None, None),
        P("slab", None, None),
        P("energy", None, None),
        P("energy"),
        P("energy"),
        P(),
        P(),
        P("slab", None),
        P("slab", "energy", None),
    )
    out_specs = (P(None, "slab", None), P("slab", "energy", None))
    return jax.shard_map(
        on_device, mesh=mesh, in_specs=in_specs, out_specs=out_specs, check_vma=False
    )
```

```python
import functools

import jax
import jax.numpy as jnp
from jax import lax
from jax.experimental import pallas as pl
from jax.experimental.pallas import tpu as pltpu
from jax.sharding import PartitionSpec as P

ITERS = 3
F32 = jnp.float32
BF16 = jnp.bfloat16
TILE = 128
BOTH = ("energy", "slab")
REACH = 5
HALF = 64


def split(a):
    high = a.astype(BF16)
    return high, (a - high.astype(F32)).astype(BF16)


def dot(a, b, transposed):
    dims = (((1,), (1 if transposed else 0,)), ((), ()))
    return lax.dot_general(a, b, dims, preferred_element_type=F32)


def product(left, right, transposed=False):
    n = right[0].shape[0 if transposed else 1]
    wide = dot(left[0], jnp.concatenate(right, 0 if transposed else 1), transposed)
    return wide[:, :n] + (wide[:, n:] + dot(left[1], right[0], transposed))


def diagonal_row(matrix):
    rows = lax.broadcasted_iota(jnp.int32, (TILE, TILE), 0)
    columns = lax.broadcasted_iota(jnp.int32, (TILE, TILE), 1)
    parts = []
    for start in range(0, matrix.shape[0], TILE):
        block = matrix[start : start + TILE, start : start + TILE]
        parts.append(jnp.sum(jnp.where(rows == columns, block, 0.0), axis=0, keepdims=True))
    return jnp.concatenate(parts, axis=1)


PACKED_ROWS = 5 * TILE + 8


def pack(matrix, out):
    def block(i, j):
        return matrix[i * TILE : (i + 1) * TILE, j * TILE : (j + 1) * TILE]

    rows = lax.broadcasted_iota(jnp.int32, (TILE, TILE), 0)
    columns = lax.broadcasted_iota(jnp.int32, (TILE, TILE), 1)
    for place, (i, j) in enumerate(((0, 1), (0, 2), (1, 2))):
        out[place * TILE : (place + 1) * TILE, :] = block(i, j) + block(j, i).T
    one, two = (block(0, 0), block(1, 1))
    merged = jnp.where(rows < columns, one + one.T, jnp.where(rows > columns, two + two.T, one))
    out[3 * TILE : 4 * TILE, :] = merged
    out[4 * TILE : 5 * TILE, :] = block(2, 2)
    row = jnp.sum(jnp.where(rows == columns, two, 0.0), axis=0, keepdims=True)
    out[5 * TILE :, :] = jnp.broadcast_to(row, (8, TILE))


def unpack(packed, out):
    rows = lax.broadcasted_iota(jnp.int32, (TILE, TILE), 0)
    columns = lax.broadcasted_iota(jnp.int32, (TILE, TILE), 1)
    out[...] = jnp.zeros_like(out)
    for place, (i, j) in enumerate(((0, 1), (0, 2), (1, 2))):
        value = packed[place * TILE : (place + 1) * TILE, :]
        out[i * TILE : (i + 1) * TILE, j * TILE : (j + 1) * TILE] = value
    merged = packed[3 * TILE : 4 * TILE, :]
    row = packed[5 * TILE : 5 * TILE + 1, :]
    out[:TILE, :TILE] = jnp.where(rows <= columns, merged, 0.0)
    out[TILE : 2 * TILE, TILE : 2 * TILE] = jnp.where(
        rows > columns, merged, jnp.where(rows == columns, row, 0.0)
    )
    out[2 * TILE :, 2 * TILE :] = packed[4 * TILE : 5 * TILE, :]


def pair_kernel(index_ref, iso, coupling, lead, cells, own, near, first, sent, c_buf, g_buf, lead_buf, row, sems):
    place = index_ref[0]
    core = lax.rem(place, 2)
    n = lead_buf.shape[1]
    sources = []
    for slab in range(2):
        sources.append((coupling.at[slab], c_buf.at[slab]))
        for turn, energy in enumerate((core, 1 - core)):
            sources.append((iso.at[energy, slab], g_buf.at[turn, slab]))
    for turn, energy in enumerate((core, 1 - core)):
        sources.append((lead.at[energy], lead_buf.at[turn]))
    copies = [pltpu.make_async_copy(src, dst, sems.at[i]) for i, (src, dst) in enumerate(sources)]
    for copy in copies:
        copy.start()
    atoms = cells.shape[1]
    row[...] = jnp.zeros_like(row)
    row[0:1, 0:atoms] = cells[0:1, :].astype(F32)
    row[0:1, HALF : HALF + atoms] = cells[1:2, :].astype(F32)
    rows = lax.broadcasted_iota(jnp.int32, (8, TILE), 0)
    for ref in (own, sent):
        ref[2 * n + 8 :, 0:TILE] = jnp.where(rows == place, row[0:1, :], 0.0)
        ref[2 * n + 8 :, TILE:] = jnp.zeros((8, n - TILE), F32)
    steps = []
    for slab in range(2):
        for copy in copies[3 * slab : 3 * slab + 3]:
            copy.wait()
        parts = split(c_buf[slab])
        steps.append([product(split(g_buf[turn, slab]), parts) for turn in range(2)])
    for copy in copies[6:]:
        copy.wait()
    outputs = (own, sent)

    @pl.when(place == 0)
    def _():
        parts = [[split(steps[slab][turn]) for turn in range(2)] for slab in range(2)]
        states = [lead_buf[turn] for turn in range(2)]
        for slab in range(2):
            states = [product(parts[slab][turn], split(states[turn])) for turn in range(2)]
            states = [
                product(split(states[turn]), parts[slab][turn], True) + g_buf[turn, slab]
                for turn in range(2)
            ]
            for turn in range(2):
                outputs[turn][2 * n + slab : 2 * n + slab + 1, :] = diagonal_row(states[turn])
        for turn in range(2):
            outputs[turn][n : 2 * n, :] = states[turn]

    @pl.when(place != 0)
    def _():
        early = [split(steps[0][turn]) for turn in range(2)]
        later = [split(steps[1][turn]) for turn in range(2)]
        terms = [product(later[turn], split(g_buf[turn, 0])) for turn in range(2)]
        maps = [product(later[turn], early[turn]) for turn in range(2)]
        terms = [product(split(terms[turn]), later[turn], True) + g_buf[turn, 1] for turn in range(2)]
        for turn in range(2):
            outputs[turn][0:n, :] = maps[turn]
            outputs[turn][n : 2 * n, :] = terms[turn]
            outputs[turn][2 * n : 2 * n + 1, :] = diagonal_row(g_buf[turn, 0])
            outputs[turn][2 * n + 1 : 2 * n + 2, :] = diagonal_row(terms[turn])
        near[...] = steps[0][0]
        first[...] = steps[0][1]


def advance(map_ref, state):
    n = map_ref.shape[1]
    composed = split(map_ref[0:n, :])
    term = product(composed, split(state))
    return product(split(term), composed, True) + map_ref[n : 2 * n, :]


def relay_kernel(index_ref, own, got, field, left, right, out, first, second):
    place = index_ref[0]
    n = own.shape[1]
    length, rows, depth = field.shape
    even = lax.rem(place, 2) == 0
    for part, block in enumerate((left, field, right)):
        low = block[:REACH].reshape(REACH * rows, depth)
        high = block[length - REACH :].reshape(REACH * rows, depth)
        first[:, part * depth : (part + 1) * depth] = jnp.where(even, high, low)
        second[: REACH * rows, part * depth : (part + 1) * depth] = jnp.where(even, low, high)
    second[REACH * rows :, :] = jnp.zeros((8, n), F32)
    second[REACH * rows :, :TILE] = own[2 * n + 8 :, :TILE] + got[2 * n + 8 :, :TILE]

    @pl.when(place == 0)
    def _():
        pack(advance(got, own[n : 2 * n, :]), out)

    @pl.when(place == 1)
    def _():
        pack(advance(own, got[n : 2 * n, :]), out)


def pass_kernel(turn, index_ref, packed, own, got, out, state):
    place = index_ref[0]
    for core, (near, far) in enumerate(((own, got), (got, own))):

        @pl.when(place == 2 * turn + core)
        def _():
            unpack(packed, state)
            state[...] = advance(near, state[...])
            pack(advance(far, state[...]), out)


def density_kernel(
    pairs,
    index_ref,
    weight_ref,
    group_ref,
    orbital_atom,
    member,
    packed,
    own,
    got,
    own_step,
    got_step,
    extra,
    out,
    state,
    fold,
):
    place = index_ref[0]
    core = lax.rem(place, 2)
    n = state.shape[0]
    atoms = lax.broadcasted_iota(jnp.int32, (TILE, n), 0)
    spots = (atoms == orbital_atom[...]).astype(BF16)

    def folded(matrix, parts):
        both = matrix * product(split(matrix), parts)
        return jnp.sum(jnp.sum(both, axis=1, keepdims=True) * member[...], axis=0, keepdims=True)

    for number, (near, near_step, far, far_step) in enumerate(
        ((own, own_step, got, got_step), (got, got_step, own, own_step))
    ):

        @pl.when(core == number)
        def _():
            rest = jnp.concatenate(
                [near[2 * n : 2 * n + 2, :], far[2 * n : 2 * n + 2, :], jnp.zeros((4, n), F32)],
                axis=0,
            )
            total = jnp.zeros((8, TILE), F32)
            for _ in range(3):
                piece = rest.astype(BF16)
                total = total + dot(piece, spots, True)
                rest = rest - piece.astype(F32)
            fold[...] = total

            @pl.when(place < 2)
            def _():
                state[...] = near[n : 2 * n, :]

            @pl.when(place >= 2)
            def _():
                unpack(packed, state)
                parts = split(state[...])
                fold[0:1, :] += folded(near_step[...], parts)
                matrix = near[0:n, :]
                composed = split(matrix)
                term = product(composed, parts)
                value = jnp.sum(matrix * term, axis=1, keepdims=True) * member[...]
                fold[1:2, :] += jnp.sum(value, axis=0, keepdims=True)
                state[...] = product(split(term), composed, True) + near[n : 2 * n, :]

            parts = split(state[...])
            fold[2:3, :] += folded(far_step[...], parts)
            fold[3:4, :] += folded(far[0:n, :], parts)

    plain = fold[...]
    turned = pltpu.roll(plain, HALF, 1)
    pair_rows = lax.broadcasted_iota(jnp.int32, (pairs, TILE), 0)
    groups = (out.shape[0] - extra.shape[0]) // pairs
    for group in range(groups):
        weight = jnp.where(group_ref[core] == group, weight_ref[core], 0.0)
        block = jnp.zeros((pairs, TILE), F32)
        for half in range(2):
            value = plain[2 * half : 2 * half + 1, :] + turned[2 * half + 1 : 2 * half + 2, :]
            block = block + jnp.where(pair_rows == place - core + half, weight, 0.0) * value
        out[group * pairs : (group + 1) * pairs, :] = block
    out[groups * pairs :, :] = extra[...]


def local_call(kernel, shapes, scratch, specs, name, limit, flops, *operands):
    spaces = {"v": pltpu.VMEM, "s": pltpu.SMEM, "h": pltpu.HBM}
    single = not isinstance(shapes, tuple)
    vmem = pl.BlockSpec(memory_space=pltpu.VMEM)
    return pl.pallas_call(
        kernel,
        out_shape=shapes,
        in_specs=[pl.BlockSpec(memory_space=spaces[spec]) for spec in specs],
        out_specs=vmem if single else (vmem,) * len(shapes),
        scratch_shapes=scratch,
        compiler_params=pltpu.CompilerParams(vmem_limit_bytes=limit * 2**20),
        cost_estimate=pl.CostEstimate(flops=flops, bytes_accessed=2**20, transcendentals=0),
        name=name,
    )(*operands)


def shifted_pair(x, axis):
    size = x.shape[axis]
    before, after = (pltpu.roll(x, 1, axis), pltpu.roll(x, size - 1, axis))
    if axis == x.ndim - 1:
        lanes = lax.broadcasted_iota(jnp.int32, x.shape, axis)
        before = jnp.where(lanes == 0, 0.0, before)
        after = jnp.where(lanes == size - 1, 0.0, after)
    return before, after


def neighbours(x):
    centre = x[1:-1]
    up, down = shifted_pair(centre, 1)
    left, right = shifted_pair(centre, 2)
    return (x[2:] + x[:-2]) + (up + down) + (left + right)


def differences(x):
    centre = x[1:-1]
    up, down = shifted_pair(centre, 1)
    left, right = shifted_pair(centre, 2)
    along = (x[2:] - centre) + (x[:-2] - centre)
    across = (up - centre) + (down - centre)
    deep = (left - centre) + (right - centre)
    return along + (across + deep)


def grid_mask(shape, margin, length, rows, place, devices, wire, wires):
    planes = lax.broadcasted_iota(jnp.int32, shape, 0)
    row = lax.broadcasted_iota(jnp.int32, shape, 1)
    low_x = jnp.where(place == 0, margin, 0)
    high_x = jnp.where(place == devices - 1, margin + length, shape[0])
    low_y = jnp.where(wire == 0, rows, 0)
    high_y = jnp.where(wire == wires - 1, 2 * rows, shape[1])
    inside = (planes >= low_x) & (planes < high_x) & (row >= low_y) & (row < high_y)
    return inside.astype(F32)


def three_parts(x):
    parts = []
    for _ in range(3):
        parts.append(x.astype(BF16))
        x = x - parts[-1].astype(F32)
    return parts


def coordinates(cell, rows_y, depth):
    z_part = cell - depth * jnp.floor(cell * (1.0 / depth))
    plane = jnp.floor(cell * (1.0 / depth))
    x_part = jnp.floor(plane * (1.0 / rows_y))
    return x_part, plane - rows_y * x_part, z_part


WALKS = ((0, 1),), ((1, 1),), ((0, 2), (2, 1)), ((1, 3), (3, 1)), ((0, 6), (2, 4), (4, 1)), ((1, 10), (3, 5), (5, 1))
FACTORIAL = (1.0, 1.0, 2.0, 6.0, 24.0, 120.0)


def walk_counts(here, there, length):
    apart = jnp.abs(here - there)
    low = here + there + 2.0
    high = 2.0 * length - here - there
    at = []
    for steps in range(6):
        value = (apart == steps).astype(F32)
        if steps >= 2:
            value = value - (low == steps).astype(F32) - (high == steps).astype(F32)
        at.append(value)
    counts = []
    for steps, terms in enumerate(WALKS):
        total = None
        for distance, count in terms:
            term = at[distance] * (count / FACTORIAL[steps])
            total = term if total is None else total + term
        counts.append(total)
    return counts


def convolved(left, right):
    result = []
    for steps in range(6):
        total = left[0] * right[steps]
        for part in range(1, steps + 1):
            total = total + left[part] * right[steps - part]
        result.append(total)
    return result


def prepare_kernel(
    devices,
    wires,
    index_ref,
    orbital_atom,
    own,
    field,
    left,
    right,
    first,
    second,
    all_cells,
    out,
    walks,
    row_hot,
    deep_hot,
    member,
    wide_field,
):
    place, wire = (index_ref[0], index_ref[1])
    length, rows, depth = field.shape
    planes = length + 2 * REACH
    width_x = length // 2
    atoms = walks.shape[1] // (2 * devices)
    grid_y = rows * wires
    pairs = devices
    n = orbital_atom.shape[1]
    even = lax.rem(place, 2) == 0
    edges = REACH * rows
    before = jnp.where(even, second[:edges, :], first[...])
    after = jnp.where(even, first[...], second[:edges, :])

    def block_of(x, part):
        return x[:, part * depth : (part + 1) * depth].reshape(REACH, rows, depth)

    columns = [
        jnp.concatenate([block_of(before, part), block[...], block_of(after, part)], axis=0)
        for part, block in enumerate((left, field, right))
    ]
    whole = (planes, 3 * rows, depth)
    mask = grid_mask(whole, REACH, length, rows, place, devices, wire, wires)
    source = jnp.concatenate(columns, axis=1) * mask
    margin = ITERS - 1
    wide_field[...] = source[REACH - margin : REACH + length + margin]
    spots = lax.broadcasted_iota(jnp.int32, (TILE, n), 0) == orbital_atom[...]
    spots = spots.astype(F32)
    for start in range(0, n, TILE):
        member[start : start + TILE, :] = spots[:, start : start + TILE].T
    if devices > 4:
        cells = all_cells[...]
    else:
        cells = second[edges:, :depth] + all_cells[...]

    def inner(x):
        extra = (x.shape[0] - length) // 2
        return x[extra : extra + length, rows : 2 * rows]

    chain = [source]
    for step in range(1, 6):
        chain.append(neighbours(chain[-1]) * mask[step : planes - step])
    blocks = [inner(x) for x in chain]
    near = source[2:-2]
    other = [near]
    for step in range(1, 4):
        other.append(differences(other[-1]) * mask[2 + step : planes - 2 - step])
    other = [inner(x) for x in other]
    lanes = lax.broadcasted_iota(jnp.int32, (8, depth), 1)
    sums = jnp.zeros((8, depth), F32)
    for base, fields in enumerate((blocks, other)):
        for steps in range(6):
            part = jnp.sum(fields[steps // 2] * fields[(steps + 1) // 2], axis=0)
            part = jnp.sum(jnp.sum(part, axis=1, keepdims=True), axis=0, keepdims=True)
            sums = jnp.where(lanes == 8 * base + steps, part, sums)
    out[...] = jnp.zeros_like(out)
    out[6 * pairs : 6 * pairs + 8, :] = sums
    mine = own[2 * n + 8 :, :depth]
    mine = jnp.sum(mine, axis=0, keepdims=True)
    lane = lax.broadcasted_iota(jnp.int32, (1, depth), 1)
    odd = (lane >= HALF).astype(F32)
    used = lax.rem(lane, HALF) < atoms
    x_part, y_part, z_part = coordinates(mine, grid_y, depth)
    start = (wire * rows).astype(F32)
    ours = used & (y_part >= start) & (y_part < start + rows)
    at_row = jnp.where(ours, (x_part + width_x * odd) * rows + y_part - start, -1.0)
    cell_rows = length * rows
    row_iota = lax.broadcasted_iota(jnp.int32, (cell_rows, depth), 0).astype(F32)
    deep_iota = lax.broadcasted_iota(jnp.int32, (depth, depth), 0).astype(F32)
    at_rows = (row_iota == at_row).astype(F32)
    at_deep = (deep_iota == z_part).astype(BF16)
    for steps, block in enumerate(blocks):
        value = jnp.zeros((cell_rows, depth), F32)
        for part in three_parts(block.reshape(cell_rows, depth)):
            value = value + dot(part, at_deep, False)
        value = jnp.sum(value * at_rows, axis=0, keepdims=True)
        out[pl.ds(steps * pairs + place, 1), :] = value
    row_cells = cells
    row_x, row_y, row_z = coordinates(row_cells, grid_y, depth)
    padded = jnp.concatenate([row_cells, jnp.zeros((depth - 8, depth), F32)], axis=0)
    column_x, column_y, column_z = coordinates(padded.T, grid_y, depth)
    row_lane = lax.broadcasted_iota(jnp.int32, (8, depth), 1)
    next_x, next_y, next_z = [jnp.concatenate([v[1:], v[:1]], axis=0) for v in (row_x, row_y, row_z)]

    def turned(now, later, step_now, step_later):
        value = jnp.where(row_lane >= HALF, now + step_now, later + step_later)
        return pltpu.roll(value, HALF, 1)

    even_x = row_x + width_x * (row_lane >= HALF).astype(F32)
    odd_x, odd_y, odd_z = (
        turned(row_x, next_x, 0.0, float(width_x)),
        turned(row_y, next_y, 0.0, 0.0),
        turned(row_z, next_z, 0.0, 0.0),
    )
    for slab in range(2 * pairs):
        pair, side = (slab // 2, slab % 2)
        base = float(slab * width_x)
        if side:
            there = (odd_x, odd_y, odd_z)
        else:
            there = (even_x, row_y, row_z)
        there = [v[pair : pair + 1, :] for v in there]
        here = [
            v[side * HALF : side * HALF + atoms, pair : pair + 1]
            for v in (column_x, column_y, column_z)
        ]
        shape = (atoms, depth)
        sizes = (2 * pairs * width_x, grid_y, depth)
        axes = []
        for axis in range(3):
            shift = base if axis == 0 else 0.0
            axes.append(
                walk_counts(
                    jnp.broadcast_to(here[axis] + shift, shape),
                    jnp.broadcast_to(there[axis] + shift, shape),
                    float(sizes[axis]),
                )
            )
        total = convolved(convolved(axes[0], axes[1]), axes[2])
        for steps in range(6):
            walks[steps, slab * atoms : (slab + 1) * atoms, :] = total[steps] * FACTORIAL[steps]
    wide = length + 4
    first_x = (place * length - 2).astype(F32)
    first_y = start - rows
    count = wide * 3 * rows
    rows_iota = lax.broadcasted_iota(jnp.int32, (count, depth), 0).astype(F32)
    used_row = lax.rem(row_lane, HALF) < atoms
    for pair in range(pairs):
        x_at = even_x[pair : pair + 1, :] + float(2 * pair * width_x) - first_x
        y_at = row_y[pair : pair + 1, :] - first_y
        good = (x_at >= 0) & (x_at < wide) & (y_at >= 0) & (y_at < 3 * rows) & used_row[0:1, :]
        target = jnp.where(good, x_at * (3 * rows) + y_at, -1.0)
        row_hot[:, pair * depth : (pair + 1) * depth] = (rows_iota == target).astype(BF16)
        z_at = column_z[:, pair : pair + 1]
        lanes_z = lax.broadcasted_iota(jnp.int32, (depth, depth), 1).astype(F32)
        deep_hot[pair * depth : (pair + 1) * depth, :] = (lanes_z == z_at).astype(F32)


def total_of(x):
    return jnp.sum(jnp.sum(x, axis=1, keepdims=True), axis=0, keepdims=True)


def quadratic_form(poly, moments, shift):
    total = None
    for i, one in enumerate(poly):
        for j, two in enumerate(poly):
            if j < i:
                continue
            term = one * two * moments[i + j + shift] * (1.0 if i == j else 2.0)
            total = term if total is None else total + term
    return total


def finish_kernel(
    devices,
    wires,
    atoms,
    index_ref,
    charge_ref,
    payload,
    walks,
    row_hot,
    deep_hot,
    field,
    density,
    potential,
):
    place, wire = (index_ref[0], index_ref[1])
    length, rows, depth = potential.shape
    pairs = devices
    groups = density.shape[0]
    charge = charge_ref[0] * payload[0:pairs, :]
    for group in range(1, groups):
        charge = charge + charge_ref[group] * payload[group * pairs : (group + 1) * pairs, :]
    for group in range(groups):
        value = payload[pl.ds(group * pairs + place, 1), :]
        density[group, 0:1, :] = value[:, :atoms]
        density[group, 1:2, :] = pltpu.roll(value, HALF, 1)[:, :atoms]
    square = jnp.concatenate([charge, jnp.zeros((depth - pairs, depth), F32)], axis=0)
    columns = square.T
    later = jnp.concatenate([charge[1:], jnp.zeros((1, depth), F32)], axis=0)
    lanes = lax.broadcasted_iota(jnp.int32, (pairs, depth), 1)
    even_row = jnp.where(lanes >= HALF, 2.0 * charge, charge)
    odd_row = pltpu.roll(jnp.where(lanes >= HALF, charge, 2.0 * later), HALF, 1)
    totals = [None] * 6
    for slab in range(2 * pairs):
        pair, side = (slab // 2, slab % 2)
        row = (odd_row if side else even_row)[pair : pair + 1, :]
        column = columns[side * HALF : side * HALF + atoms, pair : pair + 1]
        outer = column * row
        for steps in range(6):
            term = walks[steps, slab * atoms : (slab + 1) * atoms, :] * outer
            totals[steps] = term if totals[steps] is None else totals[steps] + term
    base = groups * pairs
    crossed = []
    for steps in range(6):
        cross = 2.0 * charge * payload[base + steps * pairs : base + (steps + 1) * pairs, :]
        crossed.append(total_of(totals[steps]) + total_of(cross))
    sums = payload[base + 6 * pairs : base + 6 * pairs + 1, :]
    plain = [sums[:, steps : steps + 1] + crossed[steps] for steps in range(6)]
    moved = []
    for steps in range(6):
        value = sums[:, 8 + steps : 9 + steps]
        binomial = 1
        for part in range(steps, -1, -1):
            value = value + (binomial * (-6.0) ** (steps - part)) * crossed[part]
            binomial = binomial * part // (steps - part + 1)
        moved.append(value)
    smooth = plain[1] > 3.5 * plain[0]
    level = jnp.where(smooth, 0.5, 6.5)
    moments = [jnp.where(smooth, two, one) for one, two in zip(plain, moved)]
    residual, direction = ([jnp.ones_like(level)], [jnp.ones_like(level)])
    norm = moments[0]
    alphas, betas = ([], [])
    for turn in range(ITERS):
        energy = level * quadratic_form(direction, moments, 0) - quadratic_form(direction, moments, 1)
        alpha = norm / energy
        alphas.append(alpha)
        if turn + 1 == ITERS:
            break
        longer = residual + [jnp.zeros_like(level)]
        for i, value in enumerate(direction):
            longer[i] = longer[i] - alpha * level * value
            longer[i + 1] = longer[i + 1] + alpha * value
        residual = longer
        following = quadratic_form(residual, moments, 0)
        beta = following / norm
        betas.append(beta)
        norm = following
        direction = [
            value + beta * direction[i] if i < len(direction) else value
            for i, value in enumerate(residual)
        ]
    pieces = [[], [], []]
    for pair in range(pairs):
        hot = deep_hot[pair * depth : (pair + 1) * depth, :]
        for place_in, piece in enumerate(three_parts(columns[:, pair : pair + 1] * hot)):
            pieces[place_in].append(piece)
    spread = jnp.concatenate([jnp.concatenate(piece, axis=0) for piece in pieces], axis=1)
    placed = dot(row_hot[...], spread, False)
    placed = placed[:, :depth] + (placed[:, depth : 2 * depth] + placed[:, 2 * depth :])
    margin = ITERS - 1
    wide = (length + 2 * margin, 3 * rows, depth)
    mask = grid_mask(wide, margin, length, rows, place, devices, wire, wires)
    source = field[...] + placed.reshape(wide)
    residual, direction = (source, source)
    total = alphas[0] * source[margin:-margin, rows : 2 * rows]
    for turn in range(ITERS - 1):
        image = 6.5 * direction[1:-1] - neighbours(direction)
        inner_mask = mask[turn + 1 : wide[0] - turn - 1]
        residual = (residual[1:-1] - alphas[turn] * image) * inner_mask
        direction = residual + betas[turn] * direction[1:-1]
        extra = margin - turn - 1
        block = direction[extra : extra + length, rows : 2 * rows]
        total = total + alphas[turn + 1] * block
    potential[...] = total


def hop(count, turn):
    moves = {i: i for i in range(count)}
    for core in range(2):
        here, there = (2 * turn - 2 + core, 2 * turn + core)
        moves[here], moves[there] = (there, here)
    return sorted(moves.items())


def pairs_of(count):
    return [(i, i ^ 1) for i in range(count)]


def total_over(value, axis, strides):
    size = 1
    for name in axis if isinstance(axis, tuple) else (axis,):
        size *= lax.axis_size(name)
    got = [lax.ppermute(value, axis, [(i, i ^ k) for i in range(size)]) for k in strides]
    if len(got) == 1:
        return value + got[0]
    return (value + got[0]) + (got[1] + got[2])


def total_over_all(value):
    wires, slabs = (lax.axis_size("energy"), lax.axis_size("slab"))
    value = total_over(value, "slab", (1,))
    stride = 2
    while stride * 2 < slabs:
        value = total_over(value, "slab", (stride,))
        stride *= 2
    value = total_over(value, BOTH, (stride, slabs, stride + slabs))
    stride = 2
    while stride * 4 <= wires:
        value = total_over(value, "energy", (stride, 2 * stride, 3 * stride))
        stride *= 4
    if stride < wires:
        value = total_over(value, "energy", (stride,))
    return value


def neighbour_turn(count):
    return [(i, (i + 1) % count if i % 2 else (i - 1) % count) for i in range(count)]


def on_device(
    green_iso,
    coupling,
    lead_green,
    energy_weight,
    energy_group,
    group_charge,
    orbital_atom,
    atom_cell,
    doping,
):
    devices, wires = (lax.axis_size("slab"), lax.axis_size("energy"))
    groups = group_charge.shape[0]
    atoms = atom_cell.shape[1]
    n = lead_green.shape[-1]
    length, rows, depth = doping.shape
    shape = jax.ShapeDtypeStruct
    index = jnp.stack([lax.axis_index("slab"), lax.axis_index("energy")]).astype(jnp.int32)
    orbital_row = orbital_atom.reshape(1, n)
    maps = shape((2 * n + 16, n), F32)
    own, own_step, sent_step, sent = local_call(
        pair_kernel,
        (maps, shape((n, n), F32), shape((n, n), F32), maps),
        [
            pltpu.VMEM((2, n, n), F32),
            pltpu.VMEM((2, 2, n, n), F32),
            pltpu.VMEM((2, n, n), F32),
            pltpu.VMEM((8, TILE), F32),
            pltpu.SemaphoreType.DMA((8,)),
        ],
        "shhhv",
        "pair",
        28,
        72 * n**3,
        index,
        green_iso,
        coupling,
        lead_green,
        atom_cell,
    )
    got = lax.ppermute(sent, "slab", pairs_of(devices))
    left = lax.ppermute(doping, "energy", [(i, (i + 1) % wires) for i in range(wires)])
    right = lax.ppermute(doping, "energy", [((i + 1) % wires, i) for i in range(wires)])
    planes = REACH * rows
    passed, first, second = local_call(
        relay_kernel,
        (shape((PACKED_ROWS, TILE), F32), shape((planes, n), F32), shape((planes + 8, n), F32)),
        [],
        "svvvvv",
        "relay",
        20,
        12 * n**3,
        index,
        own,
        got,
        doping,
        left,
        right,
    )
    second_in = lax.ppermute(second, "slab", neighbour_turn(devices))
    packed = lax.ppermute(passed, "slab", hop(devices, 1))
    first_in = lax.ppermute(first, "slab", pairs_of(devices))
    got_step = lax.ppermute(sent_step, "slab", pairs_of(devices))
    cells = second[planes:, :depth]
    if devices > 4:
        cells = lax.psum(own[2 * n + 8 :, :depth], "slab")
    wide = (length + 2 * ITERS - 2, 3 * rows, depth)
    extra, walks, row_hot, deep_hot, member, wide_field = local_call(
        functools.partial(prepare_kernel, devices, wires),
        (
            shape((6 * devices + 8, depth), F32),
            shape((6, 2 * devices * atoms, depth), F32),
            shape((wide[0] * wide[1], devices * depth), BF16),
            shape((devices * depth, depth), F32),
            shape((n, TILE), F32),
            shape(wide, F32),
        ),
        [],
        "svvvvvvvv",
        "prepare",
        28,
        2**30,
        index,
        orbital_row,
        own,
        doping,
        left,
        right,
        first_in,
        second_in,
        cells,
    )
    for turn in range(1, devices // 2 - 1):
        passed = local_call(
            functools.partial(pass_kernel, turn),
            shape((PACKED_ROWS, TILE), F32),
            [pltpu.VMEM((n, n), F32)],
            "svvv",
            "pass_on",
            20,
            24 * n**3,
            index,
            packed,
            own,
            got,
        )
        arrived = lax.ppermute(passed, "slab", hop(devices, turn + 1))
        packed = jnp.where(index[0] // 2 == turn + 1, arrived, packed)
    payload = local_call(
        functools.partial(density_kernel, devices),
        shape(((groups + 6) * devices + 8, TILE), F32),
        [pltpu.VMEM((n, n), F32), pltpu.VMEM((8, TILE), F32)],
        "sssvvvvvvvv",
        "density",
        20,
        30 * n**3,
        index,
        energy_weight,
        energy_group,
        orbital_row,
        member,
        packed,
        own,
        got,
        own_step,
        got_step,
        extra,
    )
    payload = total_over_all(payload)
    return local_call(
        functools.partial(finish_kernel, devices, wires, atoms),
        (shape((groups, 2, atoms), F32), shape(doping.shape, F32)),
        [],
        "ssvvvvv",
        "finish",
        28,
        2**29,
        index,
        group_charge,
        payload,
        walks,
        row_hot,
        deep_hot,
        wide_field,
    )


def solution(mesh):
    in_specs = (
        P("energy", "slab", None, None),
        P("slab", None, None),
        P("energy", None, None),
        P("energy"),
        P("energy"),
        P(),
        P(),
        P("slab", None),
        P("slab", "energy", None),
    )
    out_specs = (P(None, "slab", None), P("slab", "energy", None))
    return jax.shard_map(
        on_device, mesh=mesh, in_specs=in_specs, out_specs=out_specs, check_vma=False
    )
```

```python
import functools

import jax
import jax.numpy as jnp
from jax import lax
from jax.experimental import pallas as pl
from jax.experimental.pallas import tpu as pltpu
from jax.sharding import PartitionSpec as P

ITERS = 3
F32 = jnp.float32
BF16 = jnp.bfloat16
TILE = 128
BOTH = ("energy", "slab")
REACH = 5
HALF = 64


def split(a):
    high = a.astype(BF16)
    return high, (a - high.astype(F32)).astype(BF16)


def dot(a, b, transposed):
    dims = (((1,), (1 if transposed else 0,)), ((), ()))
    return lax.dot_general(a, b, dims, preferred_element_type=F32)


def product(left, right, transposed=False):
    n = right[0].shape[0 if transposed else 1]
    wide = dot(left[0], jnp.concatenate(right, 0 if transposed else 1), transposed)
    return wide[:, :n] + (wide[:, n:] + dot(left[1], right[0], transposed))


def diagonal_row(matrix):
    rows = lax.broadcasted_iota(jnp.int32, (TILE, TILE), 0)
    columns = lax.broadcasted_iota(jnp.int32, (TILE, TILE), 1)
    parts = []
    for start in range(0, matrix.shape[0], TILE):
        block = matrix[start : start + TILE, start : start + TILE]
        parts.append(jnp.sum(jnp.where(rows == columns, block, 0.0), axis=0, keepdims=True))
    return jnp.concatenate(parts, axis=1)


PACKED_ROWS = 5 * TILE + 8


def pack(matrix, out):
    def block(i, j):
        return matrix[i * TILE : (i + 1) * TILE, j * TILE : (j + 1) * TILE]

    rows = lax.broadcasted_iota(jnp.int32, (TILE, TILE), 0)
    columns = lax.broadcasted_iota(jnp.int32, (TILE, TILE), 1)
    for place, (i, j) in enumerate(((0, 1), (0, 2), (1, 2))):
        out[place * TILE : (place + 1) * TILE, :] = block(i, j) + block(j, i).T
    one, two = (block(0, 0), block(1, 1))
    merged = jnp.where(rows < columns, one + one.T, jnp.where(rows > columns, two + two.T, one))
    out[3 * TILE : 4 * TILE, :] = merged
    out[4 * TILE : 5 * TILE, :] = block(2, 2)
    row = jnp.sum(jnp.where(rows == columns, two, 0.0), axis=0, keepdims=True)
    out[5 * TILE :, :] = jnp.broadcast_to(row, (8, TILE))


def unpack(packed, out):
    rows = lax.broadcasted_iota(jnp.int32, (TILE, TILE), 0)
    columns = lax.broadcasted_iota(jnp.int32, (TILE, TILE), 1)
    out[...] = jnp.zeros_like(out)
    for place, (i, j) in enumerate(((0, 1), (0, 2), (1, 2))):
        value = packed[place * TILE : (place + 1) * TILE, :]
        out[i * TILE : (i + 1) * TILE, j * TILE : (j + 1) * TILE] = value
    merged = packed[3 * TILE : 4 * TILE, :]
    row = packed[5 * TILE : 5 * TILE + 1, :]
    out[:TILE, :TILE] = jnp.where(rows <= columns, merged, 0.0)
    out[TILE : 2 * TILE, TILE : 2 * TILE] = jnp.where(
        rows > columns, merged, jnp.where(rows == columns, row, 0.0)
    )
    out[2 * TILE :, 2 * TILE :] = packed[4 * TILE : 5 * TILE, :]


def plane_rows(n, plane):
    start = 2 * n + 16 + 8 * (plane // 3)
    return slice(start, start + 8)


def plane_lanes(plane):
    return slice((plane % 3) * TILE, (plane % 3 + 1) * TILE)


def pair_kernel(
    iso,
    coupling,
    lead,
    cells_in,
    field_in,
    own,
    near,
    first,
    sent,
    planes,
    c_buf,
    g_buf,
    lead_buf,
    row,
    cells,
    field,
    sems,
):
    place = lax.axis_index("slab")
    core = lax.rem(place, 2)
    n = lead_buf.shape[1]
    sources = []
    for slab in range(2):
        sources.append((coupling.at[slab], c_buf.at[slab]))
        for turn, energy in enumerate((core, 1 - core)):
            sources.append((iso.at[energy, slab], g_buf.at[turn, slab]))
    for turn, energy in enumerate((core, 1 - core)):
        sources.append((lead.at[energy], lead_buf.at[turn]))
    sources += [(cells_in, cells), (field_in, field)]
    copies = [pltpu.make_async_copy(src, dst, sems.at[i]) for i, (src, dst) in enumerate(sources)]
    for copy in copies:
        copy.start()
    steps = []
    for slab in range(2):
        for copy in copies[3 * slab : 3 * slab + 3]:
            copy.wait()
        parts = split(c_buf[slab])
        steps.append([product(split(g_buf[turn, slab]), parts) for turn in range(2)])
    for copy in copies[6:8]:
        copy.wait()
    for copy in copies[8:]:
        copy.wait()
    atoms = cells.shape[1]
    row[...] = jnp.zeros_like(row)
    row[0:1, 0:atoms] = cells[0:1, :].astype(F32)
    row[0:1, HALF : HALF + atoms] = cells[1:2, :].astype(F32)
    rows = lax.broadcasted_iota(jnp.int32, (8, TILE), 0)
    mine = jnp.where(rows == place, row[0:1, :], 0.0)
    own[2 * n + 8 : 2 * n + 16, 0:TILE] = mine
    sent[2 * n + 8 : 2 * n + 16, 0:TILE] = mine
    planes[REACH * 8 :, :] = mine
    length = field.shape[0]
    even = core == 0
    for plane in range(REACH):
        low, high = (field[plane], field[length - REACH + plane])
        planes[plane * 8 : plane * 8 + 8, :] = jnp.where(even, low, high)
        sent[plane_rows(n, plane), plane_lanes(plane)] = jnp.where(even, high, low)
    outputs = (own, sent)

    @pl.when(place == 0)
    def _():
        parts = [[split(steps[slab][turn]) for turn in range(2)] for slab in range(2)]
        states = [lead_buf[turn] for turn in range(2)]
        for slab in range(2):
            states = [product(parts[slab][turn], split(states[turn])) for turn in range(2)]
            states = [
                product(split(states[turn]), parts[slab][turn], True) + g_buf[turn, slab]
                for turn in range(2)
            ]
            for turn in range(2):
                outputs[turn][2 * n + slab : 2 * n + slab + 1, :] = diagonal_row(states[turn])
        for turn in range(2):
            outputs[turn][n : 2 * n, :] = states[turn]

    @pl.when(place != 0)
    def _():
        early = [split(steps[0][turn]) for turn in range(2)]
        later = [split(steps[1][turn]) for turn in range(2)]
        terms = [product(later[turn], split(g_buf[turn, 0])) for turn in range(2)]
        maps = [product(later[turn], early[turn]) for turn in range(2)]
        terms = [product(split(terms[turn]), later[turn], True) + g_buf[turn, 1] for turn in range(2)]
        for turn in range(2):
            outputs[turn][0:n, :] = maps[turn]
            outputs[turn][n : 2 * n, :] = terms[turn]
            outputs[turn][2 * n : 2 * n + 1, :] = diagonal_row(g_buf[turn, 0])
            outputs[turn][2 * n + 1 : 2 * n + 2, :] = diagonal_row(terms[turn])
        near[...] = steps[0][0]
        first[...] = steps[0][1]


def advance(map_ref, state):
    n = map_ref.shape[1]
    composed = split(map_ref[0:n, :])
    term = product(composed, split(state))
    return product(split(term), composed, True) + map_ref[n : 2 * n, :]


def relay_kernel(own, got, field, second, out, wide, cells):
    place = lax.axis_index("slab")
    n = own.shape[1]
    length = field.shape[0]
    even = lax.rem(place, 2) == 0
    wide[REACH : REACH + length] = field[...]
    for plane in range(REACH):
        one = got[plane_rows(n, plane), plane_lanes(plane)]
        two = second[plane * 8 : plane * 8 + 8, :]
        wide[plane] = jnp.where(even, two, one)
        wide[REACH + length + plane] = jnp.where(even, one, two)
    spot = slice(2 * n + 8, 2 * n + 16)
    cells[...] = own[spot, :TILE] + got[spot, :TILE] + second[REACH * 8 :, :]

    @pl.when(place == 0)
    def _():
        pack(advance(got, own[n : 2 * n, :]), out)

    @pl.when(place == 1)
    def _():
        pack(advance(own, got[n : 2 * n, :]), out)


def pass_kernel(turn, packed, own, got, out, state):
    place = lax.axis_index("slab")
    for core, (near, far) in enumerate(((own, got), (got, own))):

        @pl.when(place == 2 * turn + core)
        def _():
            unpack(packed, state)
            state[...] = advance(near, state[...])
            pack(advance(far, state[...]), out)


def density_kernel(
    pairs,
    weight_ref,
    group_ref,
    orbital_atom,
    member,
    packed,
    own,
    got,
    own_step,
    got_step,
    extra,
    out,
    state,
    fold,
):
    place = lax.axis_index("slab")
    core = lax.rem(place, 2)
    n = state.shape[0]
    atoms = lax.broadcasted_iota(jnp.int32, (TILE, n), 0)
    spots = (atoms == orbital_atom[...]).astype(BF16)

    def folded(matrix, parts):
        both = matrix * product(split(matrix), parts)
        return jnp.sum(jnp.sum(both, axis=1, keepdims=True) * member[...], axis=0, keepdims=True)

    for number, (near, near_step, far, far_step) in enumerate(
        ((own, own_step, got, got_step), (got, got_step, own, own_step))
    ):

        @pl.when(core == number)
        def _():
            rest = jnp.concatenate(
                [near[2 * n : 2 * n + 2, :], far[2 * n : 2 * n + 2, :], jnp.zeros((4, n), F32)],
                axis=0,
            )
            total = jnp.zeros((8, TILE), F32)
            for _ in range(3):
                piece = rest.astype(BF16)
                total = total + dot(piece, spots, True)
                rest = rest - piece.astype(F32)
            fold[...] = total

            @pl.when(place < 2)
            def _():
                state[...] = near[n : 2 * n, :]

            @pl.when(place >= 2)
            def _():
                unpack(packed, state)
                parts = split(state[...])
                fold[0:1, :] += folded(near_step[...], parts)
                matrix = near[0:n, :]
                composed = split(matrix)
                term = product(composed, parts)
                value = jnp.sum(matrix * term, axis=1, keepdims=True) * member[...]
                fold[1:2, :] += jnp.sum(value, axis=0, keepdims=True)
                state[...] = product(split(term), composed, True) + near[n : 2 * n, :]

            parts = split(state[...])
            fold[2:3, :] += folded(far_step[...], parts)
            fold[3:4, :] += folded(far[0:n, :], parts)

    plain = fold[...]
    turned = pltpu.roll(plain, HALF, 1)
    pair_rows = lax.broadcasted_iota(jnp.int32, (pairs, TILE), 0)
    groups = (out.shape[0] - extra.shape[0]) // pairs
    for group in range(groups):
        weight = jnp.where(group_ref[core] == group, weight_ref[core], 0.0)
        block = jnp.zeros((pairs, TILE), F32)
        for half in range(2):
            value = plain[2 * half : 2 * half + 1, :] + turned[2 * half + 1 : 2 * half + 2, :]
            block = block + jnp.where(pair_rows == place - core + half, weight, 0.0) * value
        out[group * pairs : (group + 1) * pairs, :] = block
    out[groups * pairs :, :] = extra[...]


def local_call(kernel, shapes, scratch, specs, name, limit, flops, *operands):
    spaces = {"v": pltpu.VMEM, "s": pltpu.SMEM, "h": pltpu.HBM}
    single = not isinstance(shapes, tuple)
    vmem = pl.BlockSpec(memory_space=pltpu.VMEM)
    return pl.pallas_call(
        kernel,
        out_shape=shapes,
        in_specs=[pl.BlockSpec(memory_space=spaces[spec]) for spec in specs],
        out_specs=vmem if single else (vmem,) * len(shapes),
        scratch_shapes=scratch,
        compiler_params=pltpu.CompilerParams(vmem_limit_bytes=limit * 2**20),
        cost_estimate=pl.CostEstimate(flops=flops, bytes_accessed=2**20, transcendentals=0),
        name=name,
    )(*operands)


def shifted_pair(x, axis):
    size = x.shape[axis]
    before, after = (pltpu.roll(x, 1, axis), pltpu.roll(x, size - 1, axis))
    if axis == x.ndim - 1:
        lanes = lax.broadcasted_iota(jnp.int32, x.shape, axis)
        before = jnp.where(lanes == 0, 0.0, before)
        after = jnp.where(lanes == size - 1, 0.0, after)
    return before, after


def neighbours(x):
    centre = x[1:-1]
    up, down = shifted_pair(centre, 1)
    left, right = shifted_pair(centre, 2)
    return (x[2:] + x[:-2]) + (up + down) + (left + right)


def differences(x):
    centre = x[1:-1]
    up, down = shifted_pair(centre, 1)
    left, right = shifted_pair(centre, 2)
    along = (x[2:] - centre) + (x[:-2] - centre)
    across = (up - centre) + (down - centre)
    deep = (left - centre) + (right - centre)
    return along + (across + deep)


def grid_mask(shape, margin, length, rows, place, devices, wire, wires):
    planes = lax.broadcasted_iota(jnp.int32, shape, 0)
    row = lax.broadcasted_iota(jnp.int32, shape, 1)
    low_x = jnp.where(place == 0, margin, 0)
    high_x = jnp.where(place == devices - 1, margin + length, shape[0])
    low_y = jnp.where(wire == 0, rows, 0)
    high_y = jnp.where(wire == wires - 1, 2 * rows, shape[1])
    inside = (planes >= low_x) & (planes < high_x) & (row >= low_y) & (row < high_y)
    return inside.astype(F32)


def three_parts(x):
    parts = []
    for _ in range(3):
        parts.append(x.astype(BF16))
        x = x - parts[-1].astype(F32)
    return parts


def coordinates(cell, rows_y, depth):
    z_part = cell - depth * jnp.floor(cell * (1.0 / depth))
    plane = jnp.floor(cell * (1.0 / depth))
    x_part = jnp.floor(plane * (1.0 / rows_y))
    return x_part, plane - rows_y * x_part, z_part


WALKS = ((0, 1),), ((1, 1),), ((0, 2), (2, 1)), ((1, 3), (3, 1)), ((0, 6), (2, 4), (4, 1)), ((1, 10), (3, 5), (5, 1))
FACTORIAL = (1.0, 1.0, 2.0, 6.0, 24.0, 120.0)


def walk_counts(here, there, length):
    apart = jnp.abs(here - there)
    low = here + there + 2.0
    high = 2.0 * length - here - there
    at = []
    for steps in range(6):
        value = (apart == steps).astype(F32)
        if steps >= 2:
            value = value - (low == steps).astype(F32) - (high == steps).astype(F32)
        at.append(value)
    counts = []
    for steps, terms in enumerate(WALKS):
        total = None
        for distance, count in terms:
            term = at[distance] * (count / FACTORIAL[steps])
            total = term if total is None else total + term
        counts.append(total)
    return counts


def convolved(left, right):
    result = []
    for steps in range(6):
        total = left[0] * right[steps]
        for part in range(1, steps + 1):
            total = total + left[part] * right[steps - part]
        result.append(total)
    return result


def moments_kernel(devices, wires, own, field, one_beside, two_beside, cells, out, wide_field):
    place, wire = (lax.axis_index("slab"), lax.axis_index("energy"))
    planes, rows, depth = field.shape
    length = planes - 2 * REACH
    width_x = length // 2
    atoms = cells.shape[1]
    grid_y = rows * wires
    pairs = devices
    n = own.shape[1]
    even = lax.rem(wire, 2) == 0
    left = jnp.where(even, two_beside[...], one_beside[...])
    right = jnp.where(even, one_beside[...], two_beside[...])
    whole = (planes, 3 * rows, depth)
    mask = grid_mask(whole, REACH, length, rows, place, devices, wire, wires)
    source = jnp.concatenate([left, field[...], right], axis=1)
    source = jnp.where(mask > 0, source, 0.0)
    margin = ITERS - 1
    wide_field[...] = source[REACH - margin : REACH + length + margin]

    def inner(x):
        extra = (x.shape[0] - length) // 2
        return x[extra : extra + length, rows : 2 * rows]

    chain = [source]
    for step in range(1, 6):
        chain.append(neighbours(chain[-1]) * mask[step : planes - step])
    blocks = [inner(x) for x in chain]
    near = source[2:-2]
    other = [near]
    for step in range(1, 4):
        other.append(differences(other[-1]) * mask[2 + step : planes - 2 - step])
    other = [inner(x) for x in other]
    lanes = lax.broadcasted_iota(jnp.int32, (8, depth), 1)
    sums = jnp.zeros((8, depth), F32)
    for base, fields in enumerate((blocks, other)):
        for steps in range(6):
            part = jnp.sum(fields[steps // 2] * fields[(steps + 1) // 2], axis=0)
            part = jnp.sum(jnp.sum(part, axis=1, keepdims=True), axis=0, keepdims=True)
            sums = jnp.where(lanes == 8 * base + steps, part, sums)
    out[...] = jnp.zeros_like(out)
    out[6 * pairs : 6 * pairs + 8, :] = sums
    mine = own[2 * n + 8 : 2 * n + 16, :depth]
    mine = jnp.sum(mine, axis=0, keepdims=True)
    lane = lax.broadcasted_iota(jnp.int32, (1, depth), 1)
    odd = (lane >= HALF).astype(F32)
    used = lax.rem(lane, HALF) < atoms
    x_part, y_part, z_part = coordinates(mine, grid_y, depth)
    start = (wire * rows).astype(F32)
    ours = used & (y_part >= start) & (y_part < start + rows)
    at_row = jnp.where(ours, (x_part + width_x * odd) * rows + y_part - start, -1.0)
    cell_rows = length * rows
    row_iota = lax.broadcasted_iota(jnp.int32, (cell_rows, depth), 0).astype(F32)
    deep_iota = lax.broadcasted_iota(jnp.int32, (depth, depth), 0).astype(F32)
    at_rows = (row_iota == at_row).astype(F32)
    at_deep = (deep_iota == z_part).astype(BF16)
    for steps, block in enumerate(blocks):
        value = jnp.zeros((cell_rows, depth), F32)
        for part in three_parts(block.reshape(cell_rows, depth)):
            value = value + dot(part, at_deep, False)
        value = jnp.sum(value * at_rows, axis=0, keepdims=True)
        out[pl.ds(steps * pairs + place, 1), :] = value


def atoms_kernel(
    devices,
    wires,
    length,
    orbital_atom,
    some_cells,
    other_cells,
    walks,
    row_hot,
    deep_hot,
    member,
):
    place, wire = (lax.axis_index("slab"), lax.axis_index("energy"))
    rows, depth = some_cells.shape
    width_x = length // 2
    atoms = walks.shape[1] // (2 * devices)
    grid_y = rows * wires
    pairs = devices
    n = orbital_atom.shape[1]
    start = (wire * rows).astype(F32)
    cells = jnp.maximum(some_cells[...], other_cells[...])
    spots = lax.broadcasted_iota(jnp.int32, (TILE, n), 0) == orbital_atom[...]
    spots = spots.astype(F32)
    for first in range(0, n, TILE):
        member[first : first + TILE, :] = spots[:, first : first + TILE].T
    row_cells = cells
    row_x, row_y, row_z = coordinates(row_cells, grid_y, depth)
    padded = jnp.concatenate([row_cells, jnp.zeros((depth - 8, depth), F32)], axis=0)
    column_x, column_y, column_z = coordinates(padded.T, grid_y, depth)
    row_lane = lax.broadcasted_iota(jnp.int32, (8, depth), 1)
    next_x, next_y, next_z = [jnp.concatenate([v[1:], v[:1]], axis=0) for v in (row_x, row_y, row_z)]

    def turned(now, later, step_now, step_later):
        value = jnp.where(row_lane >= HALF, now + step_now, later + step_later)
        return pltpu.roll(value, HALF, 1)

    even_x = row_x + width_x * (row_lane >= HALF).astype(F32)
    odd_x, odd_y, odd_z = (
        turned(row_x, next_x, 0.0, float(width_x)),
        turned(row_y, next_y, 0.0, 0.0),
        turned(row_z, next_z, 0.0, 0.0),
    )
    for slab in range(2 * pairs):
        pair, side = (slab // 2, slab % 2)
        base = float(slab * width_x)
        if side:
            there = (odd_x, odd_y, odd_z)
        else:
            there = (even_x, row_y, row_z)
        there = [v[pair : pair + 1, :] for v in there]
        here = [
            v[side * HALF : side * HALF + atoms, pair : pair + 1]
            for v in (column_x, column_y, column_z)
        ]
        shape = (atoms, depth)
        sizes = (2 * pairs * width_x, grid_y, depth)
        axes = []
        for axis in range(3):
            shift = base if axis == 0 else 0.0
            axes.append(
                walk_counts(
                    jnp.broadcast_to(here[axis] + shift, shape),
                    jnp.broadcast_to(there[axis] + shift, shape),
                    float(sizes[axis]),
                )
            )
        total = convolved(convolved(axes[0], axes[1]), axes[2])
        for steps in range(6):
            walks[steps, slab * atoms : (slab + 1) * atoms, :] = total[steps] * FACTORIAL[steps]
    wide = length + 4
    first_x = (place * length - 2).astype(F32)
    first_y = start - rows
    count = wide * 3 * rows
    rows_iota = lax.broadcasted_iota(jnp.int32, (count, depth), 0).astype(F32)
    used_row = lax.rem(row_lane, HALF) < atoms
    for pair in range(pairs):
        x_at = even_x[pair : pair + 1, :] + float(2 * pair * width_x) - first_x
        y_at = row_y[pair : pair + 1, :] - first_y
        good = (x_at >= 0) & (x_at < wide) & (y_at >= 0) & (y_at < 3 * rows) & used_row[0:1, :]
        target = jnp.where(good, x_at * (3 * rows) + y_at, -1.0)
        row_hot[:, pair * depth : (pair + 1) * depth] = (rows_iota == target).astype(BF16)
        z_at = column_z[:, pair : pair + 1]
        lanes_z = lax.broadcasted_iota(jnp.int32, (depth, depth), 1).astype(F32)
        deep_hot[pair * depth : (pair + 1) * depth, :] = (lanes_z == z_at).astype(F32)


def total_of(x):
    return jnp.sum(jnp.sum(x, axis=1, keepdims=True), axis=0, keepdims=True)


def quadratic_form(poly, moments, shift):
    total = None
    for i, one in enumerate(poly):
        for j, two in enumerate(poly):
            if j < i:
                continue
            term = one * two * moments[i + j + shift] * (1.0 if i == j else 2.0)
            total = term if total is None else total + term
    return total


def finish_kernel(
    devices,
    wires,
    atoms,
    charge_ref,
    payload,
    walks,
    row_hot,
    deep_hot,
    field,
    density,
    potential,
):
    place, wire = (lax.axis_index("slab"), lax.axis_index("energy"))
    length, rows, depth = potential.shape
    pairs = devices
    groups = density.shape[0]
    charge = charge_ref[0] * payload[0:pairs, :]
    for group in range(1, groups):
        charge = charge + charge_ref[group] * payload[group * pairs : (group + 1) * pairs, :]
    for group in range(groups):
        value = payload[pl.ds(group * pairs + place, 1), :]
        density[group, 0:1, :] = value[:, :atoms]
        density[group, 1:2, :] = pltpu.roll(value, HALF, 1)[:, :atoms]
    square = jnp.concatenate([charge, jnp.zeros((depth - pairs, depth), F32)], axis=0)
    columns = square.T
    later = jnp.concatenate([charge[1:], jnp.zeros((1, depth), F32)], axis=0)
    lanes = lax.broadcasted_iota(jnp.int32, (pairs, depth), 1)
    even_row = jnp.where(lanes >= HALF, 2.0 * charge, charge)
    odd_row = pltpu.roll(jnp.where(lanes >= HALF, charge, 2.0 * later), HALF, 1)
    totals = [None] * 6
    for slab in range(2 * pairs):
        pair, side = (slab // 2, slab % 2)
        row = (odd_row if side else even_row)[pair : pair + 1, :]
        column = columns[side * HALF : side * HALF + atoms, pair : pair + 1]
        outer = column * row
        for steps in range(6):
            term = walks[steps, slab * atoms : (slab + 1) * atoms, :] * outer
            totals[steps] = term if totals[steps] is None else totals[steps] + term
    base = groups * pairs
    crossed = []
    for steps in range(6):
        cross = 2.0 * charge * payload[base + steps * pairs : base + (steps + 1) * pairs, :]
        crossed.append(total_of(totals[steps]) + total_of(cross))
    sums = payload[base + 6 * pairs : base + 6 * pairs + 1, :]
    plain = [sums[:, steps : steps + 1] + crossed[steps] for steps in range(6)]
    moved = []
    for steps in range(6):
        value = sums[:, 8 + steps : 9 + steps]
        binomial = 1
        for part in range(steps, -1, -1):
            value = value + (binomial * (-6.0) ** (steps - part)) * crossed[part]
            binomial = binomial * part // (steps - part + 1)
        moved.append(value)
    smooth = plain[1] > 3.5 * plain[0]
    level = jnp.where(smooth, 0.5, 6.5)
    moments = [jnp.where(smooth, two, one) for one, two in zip(plain, moved)]
    residual, direction = ([jnp.ones_like(level)], [jnp.ones_like(level)])
    norm = moments[0]
    alphas, betas = ([], [])
    for turn in range(ITERS):
        energy = level * quadratic_form(direction, moments, 0) - quadratic_form(direction, moments, 1)
        alpha = norm / energy
        alphas.append(alpha)
        if turn + 1 == ITERS:
            break
        longer = residual + [jnp.zeros_like(level)]
        for i, value in enumerate(direction):
            longer[i] = longer[i] - alpha * level * value
            longer[i + 1] = longer[i + 1] + alpha * value
        residual = longer
        following = quadratic_form(residual, moments, 0)
        beta = following / norm
        betas.append(beta)
        norm = following
        direction = [
            value + beta * direction[i] if i < len(direction) else value
            for i, value in enumerate(residual)
        ]
    pieces = [[], [], []]
    for pair in range(pairs):
        hot = deep_hot[pair * depth : (pair + 1) * depth, :]
        for place_in, piece in enumerate(three_parts(columns[:, pair : pair + 1] * hot)):
            pieces[place_in].append(piece)
    spread = jnp.concatenate([jnp.concatenate(piece, axis=0) for piece in pieces], axis=1)
    placed = dot(row_hot[...], spread, False)
    placed = placed[:, :depth] + (placed[:, depth : 2 * depth] + placed[:, 2 * depth :])
    margin = ITERS - 1
    wide = (length + 2 * margin, 3 * rows, depth)
    mask = grid_mask(wide, margin, length, rows, place, devices, wire, wires)
    source = field[...] + placed.reshape(wide)
    residual, direction = (source, source)
    total = alphas[0] * source[margin:-margin, rows : 2 * rows]
    for turn in range(ITERS - 1):
        image = 6.5 * direction[1:-1] - neighbours(direction)
        inner_mask = mask[turn + 1 : wide[0] - turn - 1]
        residual = (residual[1:-1] - alphas[turn] * image) * inner_mask
        direction = residual + betas[turn] * direction[1:-1]
        extra = margin - turn - 1
        block = direction[extra : extra + length, rows : 2 * rows]
        total = total + alphas[turn + 1] * block
    potential[...] = total


def hop(count, turn):
    moves = {i: i for i in range(count)}
    for core in range(2):
        here, there = (2 * turn - 2 + core, 2 * turn + core)
        moves[here], moves[there] = (there, here)
    return sorted(moves.items())


def pairs_of(count):
    return [(i, i ^ 1) for i in range(count)]


def total_over(value, axis, strides):
    size = 1
    for name in axis if isinstance(axis, tuple) else (axis,):
        size *= lax.axis_size(name)
    got = [lax.ppermute(value, axis, [(i, i ^ k) for i in range(size)]) for k in strides]
    if len(got) == 1:
        return value + got[0]
    return (value + got[0]) + (got[1] + got[2])


def total_over_all(value):
    wires, slabs = (lax.axis_size("energy"), lax.axis_size("slab"))
    value = total_over(value, "slab", (1,))
    stride = 2
    while stride * 2 < slabs:
        value = total_over(value, "slab", (stride,))
        stride *= 2
    value = total_over(value, BOTH, (stride, slabs, stride + slabs))
    stride = 2
    while stride * 4 <= wires:
        value = total_over(value, "energy", (stride, 2 * stride, 3 * stride))
        stride *= 4
    if stride < wires:
        value = total_over(value, "energy", (stride,))
    return value


def inner_pairs(count):
    return [(i, i + 1 if i % 2 else i - 1) for i in range(1, count - 1)]


def neighbour_turn(count):
    return [(i, (i + 1) % count if i % 2 else (i - 1) % count) for i in range(count)]


def on_device(
    green_iso,
    coupling,
    lead_green,
    energy_weight,
    energy_group,
    group_charge,
    orbital_atom,
    atom_cell,
    doping,
):
    devices, wires = (lax.axis_size("slab"), lax.axis_size("energy"))
    groups = group_charge.shape[0]
    atoms = atom_cell.shape[1]
    n = lead_green.shape[-1]
    length, rows, depth = doping.shape
    shape = jax.ShapeDtypeStruct
    orbital_row = orbital_atom.reshape(1, n)
    maps = shape((2 * n + 32, n), F32)
    edge_rows = REACH * rows + 8
    own, own_step, sent_step, sent, edge = local_call(
        pair_kernel,
        (maps, shape((n, n), F32), shape((n, n), F32), maps, shape((edge_rows, depth), F32)),
        [
            pltpu.VMEM((2, n, n), F32),
            pltpu.VMEM((2, 2, n, n), F32),
            pltpu.VMEM((2, n, n), F32),
            pltpu.VMEM((8, TILE), F32),
            pltpu.VMEM(atom_cell.shape, jnp.int32),
            pltpu.VMEM(doping.shape, F32),
            pltpu.SemaphoreType.DMA((10,)),
        ],
        "hhhhh",
        "pair",
        30,
        72 * n**3,
        *[
            pltpu.with_memory_space_constraint(x, pltpu.HBM)
            for x in (green_iso, coupling, lead_green, atom_cell, doping)
        ],
    )
    got = lax.ppermute(sent, "slab", pairs_of(devices))
    second = lax.ppermute(edge, "slab", neighbour_turn(devices))
    passed, wide_block, cells = local_call(
        relay_kernel,
        (
            shape((PACKED_ROWS, TILE), F32),
            shape((length + 2 * REACH, rows, depth), F32),
            shape((8, depth), F32),
        ),
        [],
        "vvvv",
        "relay",
        20,
        12 * n**3,
        own,
        got,
        doping,
        second,
    )
    packed = lax.ppermute(passed, "slab", hop(devices, 1))
    one_beside = lax.ppermute(wide_block, "energy", pairs_of(wires))
    two_beside = lax.ppermute(wide_block, "energy", inner_pairs(wires))
    other_cells = lax.ppermute(cells, "slab", pairs_of(devices))
    if devices > 4:
        other_cells = lax.psum(own[2 * n + 8 : 2 * n + 16, :depth], "slab")
    got_step = lax.ppermute(sent_step, "slab", pairs_of(devices))
    wide = (length + 2 * ITERS - 2, 3 * rows, depth)
    walks, row_hot, deep_hot, member = local_call(
        functools.partial(atoms_kernel, devices, wires, length),
        (
            shape((6, 2 * devices * atoms, depth), F32),
            shape((wide[0] * wide[1], devices * depth), BF16),
            shape((devices * depth, depth), F32),
            shape((n, TILE), F32),
        ),
        [],
        "vvv",
        "atoms",
        28,
        2 * 2**30,
        orbital_row,
        cells,
        other_cells,
    )
    extra, wide_field = local_call(
        functools.partial(moments_kernel, devices, wires),
        (shape((6 * devices + 8, depth), F32), shape(wide, F32)),
        [],
        "vvvvv",
        "moments",
        20,
        2**30,
        own,
        wide_block,
        one_beside,
        two_beside,
        atom_cell,
    )
    for turn in range(1, devices // 2 - 1):
        passed = local_call(
            functools.partial(pass_kernel, turn),
            shape((PACKED_ROWS, TILE), F32),
            [pltpu.VMEM((n, n), F32)],
            "vvv",
            "pass_on",
            20,
            24 * n**3,
                packed,
            own,
            got,
        )
        arrived = lax.ppermute(passed, "slab", hop(devices, turn + 1))
        packed = jnp.where(lax.axis_index("slab") // 2 == turn + 1, arrived, packed)
    payload = local_call(
        functools.partial(density_kernel, devices),
        shape(((groups + 6) * devices + 8, TILE), F32),
        [pltpu.VMEM((n, n), F32), pltpu.VMEM((8, TILE), F32)],
        "ssvvvvvvvv",
        "density",
        20,
        30 * n**3,
        energy_weight,
        energy_group,
        orbital_row,
        member,
        packed,
        own,
        got,
        own_step,
        got_step,
        extra,
    )
    payload = total_over_all(payload)
    return local_call(
        functools.partial(finish_kernel, devices, wires, atoms),
        (shape((groups, 2, atoms), F32), shape(doping.shape, F32)),
        [],
        "svvvvv",
        "finish",
        28,
        2**29,
        group_charge,
        payload,
        walks,
        row_hot,
        deep_hot,
        wide_field,
    )


def solution(mesh):
    in_specs = (
        P("energy", "slab", None, None),
        P("slab", None, None),
        P("energy", None, None),
        P("energy"),
        P("energy"),
        P(),
        P(),
        P("slab", None),
        P("slab", "energy", None),
    )
    out_specs = (P(None, "slab", None), P("slab", "energy", None))
    return jax.shard_map(
        on_device, mesh=mesh, in_specs=in_specs, out_specs=out_specs, check_vma=False
    )
```

```python
import functools

import jax
import jax.numpy as jnp
from jax import lax
from jax.experimental import pallas as pl
from jax.experimental.pallas import tpu as pltpu
from jax.sharding import PartitionSpec as P

ITERS = 3
F32 = jnp.float32
BF16 = jnp.bfloat16
TILE = 128
BOTH = ("energy", "slab")
REACH = 5
HALF = 64


def split(a):
    high = a.astype(BF16)
    return high, (a - high.astype(F32)).astype(BF16)


def dot(a, b, transposed):
    dims = (((1,), (1 if transposed else 0,)), ((), ()))
    return lax.dot_general(a, b, dims, preferred_element_type=F32)


def product(left, right, transposed=False):
    n = right[0].shape[0 if transposed else 1]
    wide = dot(left[0], jnp.concatenate(right, 0 if transposed else 1), transposed)
    return wide[:, :n] + (wide[:, n:] + dot(left[1], right[0], transposed))


def joined(left):
    return jnp.concatenate([left[0], left[1], left[0]], axis=1)


def product_joined(wide, right, transposed=False):
    high, low = right
    axis = 0 if transposed else 1
    n = high.shape[axis]
    cut = n - TILE

    def part(x, start, stop):
        return lax.slice_in_dim(x, start, stop, axis=axis)

    first = [part(x, 0, cut) for x in (high, high, low)]
    last_high, last_low = (part(high, cut, n), part(low, cut, n))
    last = [
        jnp.concatenate([last_high, last_low], axis),
        jnp.concatenate([last_high, jnp.zeros_like(last_high)], axis),
    ]
    one = dot(wide, jnp.concatenate(first, 1 - axis), transposed)
    two = dot(wide[:, : 2 * high.shape[1 - axis]], jnp.concatenate(last, 1 - axis), transposed)
    return jnp.concatenate([one, two[:, :TILE] + two[:, TILE:]], axis=1)


def diagonal_row(matrix):
    rows = lax.broadcasted_iota(jnp.int32, (TILE, TILE), 0)
    columns = lax.broadcasted_iota(jnp.int32, (TILE, TILE), 1)
    parts = []
    for start in range(0, matrix.shape[0], TILE):
        block = matrix[start : start + TILE, start : start + TILE]
        parts.append(jnp.sum(jnp.where(rows == columns, block, 0.0), axis=0, keepdims=True))
    return jnp.concatenate(parts, axis=1)


PACKED_ROWS = 5 * TILE + 8


def pack(matrix, out):
    def block(i, j):
        return matrix[i * TILE : (i + 1) * TILE, j * TILE : (j + 1) * TILE]

    rows = lax.broadcasted_iota(jnp.int32, (TILE, TILE), 0)
    columns = lax.broadcasted_iota(jnp.int32, (TILE, TILE), 1)
    for place, (i, j) in enumerate(((0, 1), (0, 2), (1, 2))):
        out[place * TILE : (place + 1) * TILE, :] = block(i, j) + block(j, i).T
    one, two = (block(0, 0), block(1, 1))
    merged = jnp.where(rows < columns, one + one.T, jnp.where(rows > columns, two + two.T, one))
    out[3 * TILE : 4 * TILE, :] = merged
    out[4 * TILE : 5 * TILE, :] = block(2, 2)
    row = jnp.sum(jnp.where(rows == columns, two, 0.0), axis=0, keepdims=True)
    out[5 * TILE :, :] = jnp.broadcast_to(row, (8, TILE))


def unpack(packed, out):
    rows = lax.broadcasted_iota(jnp.int32, (TILE, TILE), 0)
    columns = lax.broadcasted_iota(jnp.int32, (TILE, TILE), 1)
    out[...] = jnp.zeros_like(out)
    for place, (i, j) in enumerate(((0, 1), (0, 2), (1, 2))):
        value = packed[place * TILE : (place + 1) * TILE, :]
        out[i * TILE : (i + 1) * TILE, j * TILE : (j + 1) * TILE] = value
    merged = packed[3 * TILE : 4 * TILE, :]
    row = packed[5 * TILE : 5 * TILE + 1, :]
    out[:TILE, :TILE] = jnp.where(rows <= columns, merged, 0.0)
    out[TILE : 2 * TILE, TILE : 2 * TILE] = jnp.where(
        rows > columns, merged, jnp.where(rows == columns, row, 0.0)
    )
    out[2 * TILE :, 2 * TILE :] = packed[4 * TILE : 5 * TILE, :]


def plane_rows(n, plane):
    start = 2 * n + 16 + 8 * (plane // 3)
    return slice(start, start + 8)


def plane_lanes(plane):
    return slice((plane % 3) * TILE, (plane % 3 + 1) * TILE)


def pair_kernel(
    iso,
    coupling,
    lead,
    cells_in,
    field_in,
    own,
    near,
    first,
    sent,
    planes,
    c_buf,
    g_buf,
    lead_buf,
    row,
    cells,
    field,
    sems,
):
    place = lax.axis_index("slab")
    core = lax.rem(place, 2)
    n = lead_buf.shape[1]
    sources = []
    for slab in range(2):
        sources.append((coupling.at[slab], c_buf.at[slab]))
        for turn, energy in enumerate((core, 1 - core)):
            sources.append((iso.at[energy, slab], g_buf.at[turn, slab]))
    for turn, energy in enumerate((core, 1 - core)):
        sources.append((lead.at[energy], lead_buf.at[turn]))
    sources += [(cells_in, cells), (field_in, field)]
    copies = [pltpu.make_async_copy(src, dst, sems.at[i]) for i, (src, dst) in enumerate(sources)]
    for copy in copies:
        copy.start()
    steps = []
    for slab in range(2):
        for copy in copies[3 * slab : 3 * slab + 3]:
            copy.wait()
        parts = split(c_buf[slab])
        steps.append([product_joined(joined(split(g_buf[turn, slab])), parts) for turn in range(2)])
    for copy in copies[6:8]:
        copy.wait()
    for copy in copies[8:]:
        copy.wait()
    atoms = cells.shape[1]
    row[...] = jnp.zeros_like(row)
    row[0:1, 0:atoms] = cells[0:1, :].astype(F32)
    row[0:1, HALF : HALF + atoms] = cells[1:2, :].astype(F32)
    rows = lax.broadcasted_iota(jnp.int32, (8, TILE), 0)
    mine = jnp.where(rows == place, row[0:1, :], 0.0)
    own[2 * n + 8 : 2 * n + 16, 0:TILE] = mine
    sent[2 * n + 8 : 2 * n + 16, 0:TILE] = mine
    planes[REACH * 8 :, :] = mine
    length = field.shape[0]
    even = core == 0
    for plane in range(REACH):
        low, high = (field[plane], field[length - REACH + plane])
        planes[plane * 8 : plane * 8 + 8, :] = jnp.where(even, low, high)
        sent[plane_rows(n, plane), plane_lanes(plane)] = jnp.where(even, high, low)
    outputs = (own, sent)

    @pl.when(place == 0)
    def _():
        parts = [[split(steps[slab][turn]) for turn in range(2)] for slab in range(2)]
        states = [lead_buf[turn] for turn in range(2)]
        for slab in range(2):
            states = [
                product_joined(joined(parts[slab][turn]), split(states[turn])) for turn in range(2)
            ]
            states = [
                product_joined(joined(split(states[turn])), parts[slab][turn], True)
                + g_buf[turn, slab]
                for turn in range(2)
            ]
            for turn in range(2):
                outputs[turn][2 * n + slab : 2 * n + slab + 1, :] = diagonal_row(states[turn])
        for turn in range(2):
            outputs[turn][n : 2 * n, :] = states[turn]

    @pl.when(place != 0)
    def _():
        early = [split(steps[0][turn]) for turn in range(2)]
        later = [split(steps[1][turn]) for turn in range(2)]
        wide = [joined(later[turn]) for turn in range(2)]
        terms = [product_joined(wide[turn], split(g_buf[turn, 0])) for turn in range(2)]
        maps = [product_joined(wide[turn], early[turn]) for turn in range(2)]
        terms = [
            product_joined(joined(split(terms[turn])), later[turn], True) + g_buf[turn, 1]
            for turn in range(2)
        ]
        for turn in range(2):
            outputs[turn][0:n, :] = maps[turn]
            outputs[turn][n : 2 * n, :] = terms[turn]
            outputs[turn][2 * n : 2 * n + 1, :] = diagonal_row(g_buf[turn, 0])
            outputs[turn][2 * n + 1 : 2 * n + 2, :] = diagonal_row(terms[turn])
        near[...] = steps[0][0]
        first[...] = steps[0][1]


def advance(map_ref, state):
    n = map_ref.shape[1]
    composed = split(map_ref[0:n, :])
    term = product(composed, split(state))
    return product(split(term), composed, True) + map_ref[n : 2 * n, :]


def relay_kernel(own, got, field, second, out, wide, cells, one_side, two_side):
    place, wire = (lax.axis_index("slab"), lax.axis_index("energy"))
    n = own.shape[1]
    length, rows, _ = field.shape
    even = lax.rem(place, 2) == 0
    wide[REACH : REACH + length] = field[...]
    for plane in range(REACH):
        one = got[plane_rows(n, plane), plane_lanes(plane)]
        two = second[plane * 8 : plane * 8 + 8, :]
        wide[plane] = jnp.where(even, two, one)
        wide[REACH + length + plane] = jnp.where(even, one, two)
    spot = slice(2 * n + 8, 2 * n + 16)
    cells[...] = own[spot, :TILE] + got[spot, :TILE] + second[REACH * 8 :, :]
    even = lax.rem(wire, 2) == 0
    for plane in range(length + 2 * REACH):
        low, high = (wide[plane, :REACH, :], wide[plane, rows - REACH :, :])
        spot = slice(plane * REACH, (plane + 1) * REACH)
        one_side[spot, :] = jnp.where(even, high, low)
        two_side[spot, :] = jnp.where(even, low, high)

    @pl.when(place == 0)
    def _():
        pack(advance(got, own[n : 2 * n, :]), out)

    @pl.when(place == 1)
    def _():
        pack(advance(own, got[n : 2 * n, :]), out)


def pass_kernel(turn, packed, own, got, out, state):
    place = lax.axis_index("slab")
    for core, (near, far) in enumerate(((own, got), (got, own))):

        @pl.when(place == 2 * turn + core)
        def _():
            unpack(packed, state)
            state[...] = advance(near, state[...])
            pack(advance(far, state[...]), out)


def compose_kernel(orbital_atom, member, own, got, own_step, got_step, stack, wide, fold):
    core = lax.rem(lax.axis_index("slab"), 2)
    n = own.shape[1]
    atoms = lax.broadcasted_iota(jnp.int32, (TILE, n), 0)
    spots = (atoms == orbital_atom[...]).astype(BF16)

    def near_far(mine, other):
        return jnp.where(core == 0, mine, other), jnp.where(core == 0, other, mine)

    near_step, far_step = near_far(own_step[...], got_step[...])
    near_map, far_map = near_far(own[0:n, :], got[0:n, :])
    near_source = jnp.where(core == 0, own[n : 2 * n, :], got[n : 2 * n, :])
    far = jnp.concatenate([far_step, far_map], axis=0)
    high, low = split(jnp.concatenate([near_map, near_source], axis=1))
    both = dot(joined(split(far)), jnp.concatenate([high, high, low], axis=0), False)
    maps = (near_step, near_map, both[:n, :n], both[n:, :n])
    for number, value in enumerate(maps):
        stack[number * n : (number + 1) * n, :] = value
        wide[number * n : (number + 1) * n, :] = joined(split(value))
    near_rows, far_rows = near_far(own[2 * n : 2 * n + 2, :], got[2 * n : 2 * n + 2, :])
    rest = jnp.concatenate([near_rows, far_rows, jnp.zeros((4, n), F32)], axis=0)
    total = jnp.zeros((8, TILE), F32)
    for _ in range(3):
        piece = rest.astype(BF16)
        total = total + dot(piece, spots, True)
        rest = rest - piece.astype(F32)
    fold[...] = total
    for number in range(2):
        rows = slice(number * n, (number + 1) * n)
        value = jnp.sum(far[rows] * both[rows, n:], axis=1, keepdims=True) * member[...]
        fold[2 + number : 3 + number, :] += jnp.sum(value, axis=0, keepdims=True)


def density_kernel(
    pairs,
    weight_ref,
    group_ref,
    member,
    packed,
    stack,
    wide,
    known,
    extra,
    out,
    state,
    fold,
):
    place = lax.axis_index("slab")
    core = lax.rem(place, 2)
    n = state.shape[0]
    fold[...] = known[...]

    @pl.when(place >= 2)
    def _():
        unpack(packed, state)
        both = product_joined(wide[...], split(state[...]))
        for number in range(4):
            rows = slice(number * n, (number + 1) * n)
            value = jnp.sum(stack[rows, :] * both[rows], axis=1, keepdims=True) * member[...]
            fold[number : number + 1, :] += jnp.sum(value, axis=0, keepdims=True)

    plain = fold[...]
    turned = pltpu.roll(plain, HALF, 1)
    pair_rows = lax.broadcasted_iota(jnp.int32, (pairs, TILE), 0)
    groups = (out.shape[0] - extra.shape[0]) // pairs
    for group in range(groups):
        weight = jnp.where(group_ref[core] == group, weight_ref[core], 0.0)
        block = jnp.zeros((pairs, TILE), F32)
        for half in range(2):
            value = plain[2 * half : 2 * half + 1, :] + turned[2 * half + 1 : 2 * half + 2, :]
            block = block + jnp.where(pair_rows == place - core + half, weight, 0.0) * value
        out[group * pairs : (group + 1) * pairs, :] = block
    out[groups * pairs :, :] = extra[...]


def local_call(kernel, shapes, scratch, specs, name, limit, flops, *operands):
    spaces = {"v": pltpu.VMEM, "s": pltpu.SMEM, "h": pltpu.HBM}
    single = not isinstance(shapes, tuple)
    vmem = pl.BlockSpec(memory_space=pltpu.VMEM)
    return pl.pallas_call(
        kernel,
        out_shape=shapes,
        in_specs=[pl.BlockSpec(memory_space=spaces[spec]) for spec in specs],
        out_specs=vmem if single else (vmem,) * len(shapes),
        scratch_shapes=scratch,
        compiler_params=pltpu.CompilerParams(vmem_limit_bytes=limit * 2**20),
        cost_estimate=pl.CostEstimate(flops=flops, bytes_accessed=2**20, transcendentals=0),
        name=name,
    )(*operands)


def shifted_pair(x, axis):
    size = x.shape[axis]
    before, after = (pltpu.roll(x, 1, axis), pltpu.roll(x, size - 1, axis))
    if axis == x.ndim - 1:
        lanes = lax.broadcasted_iota(jnp.int32, x.shape, axis)
        before = jnp.where(lanes == 0, 0.0, before)
        after = jnp.where(lanes == size - 1, 0.0, after)
    return before, after


def neighbours(x):
    centre = x[1:-1]
    up, down = shifted_pair(centre, 1)
    left, right = shifted_pair(centre, 2)
    return (x[2:] + x[:-2]) + (up + down) + (left + right)


def differences(x):
    centre = x[1:-1]
    up, down = shifted_pair(centre, 1)
    left, right = shifted_pair(centre, 2)
    along = (x[2:] - centre) + (x[:-2] - centre)
    across = (up - centre) + (down - centre)
    deep = (left - centre) + (right - centre)
    return along + (across + deep)


def grid_mask(shape, margin, length, rows, place, devices, wire, wires):
    planes = lax.broadcasted_iota(jnp.int32, shape, 0)
    row = lax.broadcasted_iota(jnp.int32, shape, 1)
    low_x = jnp.where(place == 0, margin, 0)
    high_x = jnp.where(place == devices - 1, margin + length, shape[0])
    low_y = jnp.where(wire == 0, rows, 0)
    high_y = jnp.where(wire == wires - 1, 2 * rows, shape[1])
    inside = (planes >= low_x) & (planes < high_x) & (row >= low_y) & (row < high_y)
    return inside.astype(F32)


def three_parts(x):
    parts = []
    for _ in range(3):
        parts.append(x.astype(BF16))
        x = x - parts[-1].astype(F32)
    return parts


def coordinates(cell, rows_y, depth):
    z_part = cell - depth * jnp.floor(cell * (1.0 / depth))
    plane = jnp.floor(cell * (1.0 / depth))
    x_part = jnp.floor(plane * (1.0 / rows_y))
    return x_part, plane - rows_y * x_part, z_part


WALKS = ((0, 1),), ((1, 1),), ((0, 2), (2, 1)), ((1, 3), (3, 1)), ((0, 6), (2, 4), (4, 1)), ((1, 10), (3, 5), (5, 1))
FACTORIAL = (1.0, 1.0, 2.0, 6.0, 24.0, 120.0)


def walk_counts(here, there, length):
    apart = jnp.abs(here - there)
    low = here + there + 2.0
    high = 2.0 * length - here - there
    at = []
    for steps in range(6):
        value = (apart == steps).astype(F32)
        if steps >= 2:
            value = value - (low == steps).astype(F32) - (high == steps).astype(F32)
        at.append(value)
    counts = []
    for steps, terms in enumerate(WALKS):
        total = None
        for distance, count in terms:
            term = at[distance] * (count / FACTORIAL[steps])
            total = term if total is None else total + term
        counts.append(total)
    return counts


def convolved(left, right):
    result = []
    for steps in range(6):
        total = left[0] * right[steps]
        for part in range(1, steps + 1):
            total = total + left[part] * right[steps - part]
        result.append(total)
    return result


def moments_kernel(devices, wires, own, field, one_beside, two_beside, cells, out, wide_field, whole_field):
    place, wire = (lax.axis_index("slab"), lax.axis_index("energy"))
    planes, rows, depth = field.shape
    length = planes - 2 * REACH
    width_x = length // 2
    atoms = cells.shape[1]
    grid_y = rows * wires
    pairs = devices
    n = own.shape[1]
    even = lax.rem(wire, 2) == 0
    whole_field[...] = jnp.zeros_like(whole_field)
    whole_field[:, rows : 2 * rows, :] = field[...]
    for plane in range(planes):
        spot = slice(plane * REACH, (plane + 1) * REACH)
        one, two = (one_beside[spot, :], two_beside[spot, :])
        whole_field[plane, rows - REACH : rows, :] = jnp.where(even, two, one)
        whole_field[plane, 2 * rows : 2 * rows + REACH, :] = jnp.where(even, one, two)
    whole = (planes, 3 * rows, depth)
    mask = grid_mask(whole, REACH, length, rows, place, devices, wire, wires)
    source = jnp.where(mask > 0, whole_field[...], 0.0)
    margin = ITERS - 1
    wide_field[...] = source[REACH - margin : REACH + length + margin]

    def inner(x):
        extra = (x.shape[0] - length) // 2
        return x[extra : extra + length, rows : 2 * rows]

    chain = [source]
    for step in range(1, 6):
        chain.append(neighbours(chain[-1]) * mask[step : planes - step])
    blocks = [inner(x) for x in chain]
    near = source[2:-2]
    other = [near]
    for step in range(1, 4):
        other.append(differences(other[-1]) * mask[2 + step : planes - 2 - step])
    other = [inner(x) for x in other]
    lanes = lax.broadcasted_iota(jnp.int32, (8, depth), 1)
    sums = jnp.zeros((8, depth), F32)
    for base, fields in enumerate((blocks, other)):
        for steps in range(6):
            part = jnp.sum(fields[steps // 2] * fields[(steps + 1) // 2], axis=0)
            part = jnp.sum(jnp.sum(part, axis=1, keepdims=True), axis=0, keepdims=True)
            sums = jnp.where(lanes == 8 * base + steps, part, sums)
    out[...] = jnp.zeros_like(out)
    out[6 * pairs : 6 * pairs + 8, :] = sums
    mine = own[2 * n + 8 : 2 * n + 16, :depth]
    mine = jnp.sum(mine, axis=0, keepdims=True)
    lane = lax.broadcasted_iota(jnp.int32, (1, depth), 1)
    odd = (lane >= HALF).astype(F32)
    used = lax.rem(lane, HALF) < atoms
    x_part, y_part, z_part = coordinates(mine, grid_y, depth)
    start = (wire * rows).astype(F32)
    ours = used & (y_part >= start) & (y_part < start + rows)
    at_row = jnp.where(ours, (x_part + width_x * odd) * rows + y_part - start, -1.0)
    cell_rows = length * rows
    row_iota = lax.broadcasted_iota(jnp.int32, (cell_rows, depth), 0).astype(F32)
    deep_iota = lax.broadcasted_iota(jnp.int32, (depth, depth), 0).astype(F32)
    at_rows = (row_iota == at_row).astype(F32)
    at_deep = (deep_iota == z_part).astype(BF16)
    for steps, block in enumerate(blocks):
        value = jnp.zeros((cell_rows, depth), F32)
        for part in three_parts(block.reshape(cell_rows, depth)):
            value = value + dot(part, at_deep, False)
        value = jnp.sum(value * at_rows, axis=0, keepdims=True)
        out[pl.ds(steps * pairs + place, 1), :] = value


def atoms_kernel(
    devices,
    wires,
    length,
    orbital_atom,
    some_cells,
    other_cells,
    walks,
    row_hot,
    deep_hot,
    member,
):
    place, wire = (lax.axis_index("slab"), lax.axis_index("energy"))
    rows, depth = some_cells.shape
    width_x = length // 2
    atoms = walks.shape[1] // (2 * devices)
    grid_y = rows * wires
    pairs = devices
    n = orbital_atom.shape[1]
    start = (wire * rows).astype(F32)
    cells = jnp.maximum(some_cells[...], other_cells[...])
    spots = lax.broadcasted_iota(jnp.int32, (TILE, n), 0) == orbital_atom[...]
    spots = spots.astype(F32)
    for first in range(0, n, TILE):
        member[first : first + TILE, :] = spots[:, first : first + TILE].T
    row_cells = cells
    row_x, row_y, row_z = coordinates(row_cells, grid_y, depth)
    padded = jnp.concatenate([row_cells, jnp.zeros((depth - 8, depth), F32)], axis=0)
    column_x, column_y, column_z = coordinates(padded.T, grid_y, depth)
    row_lane = lax.broadcasted_iota(jnp.int32, (8, depth), 1)
    next_x, next_y, next_z = [jnp.concatenate([v[1:], v[:1]], axis=0) for v in (row_x, row_y, row_z)]

    def turned(now, later, step_now, step_later):
        value = jnp.where(row_lane >= HALF, now + step_now, later + step_later)
        return pltpu.roll(value, HALF, 1)

    even_x = row_x + width_x * (row_lane >= HALF).astype(F32)
    odd_x, odd_y, odd_z = (
        turned(row_x, next_x, 0.0, float(width_x)),
        turned(row_y, next_y, 0.0, 0.0),
        turned(row_z, next_z, 0.0, 0.0),
    )
    for slab in range(2 * pairs):
        pair, side = (slab // 2, slab % 2)
        base = float(slab * width_x)
        if side:
            there = (odd_x, odd_y, odd_z)
        else:
            there = (even_x, row_y, row_z)
        there = [v[pair : pair + 1, :] for v in there]
        here = [
            v[side * HALF : side * HALF + atoms, pair : pair + 1]
            for v in (column_x, column_y, column_z)
        ]
        shape = (atoms, depth)
        sizes = (2 * pairs * width_x, grid_y, depth)
        axes = []
        for axis in range(3):
            shift = base if axis == 0 else 0.0
            axes.append(
                walk_counts(
                    jnp.broadcast_to(here[axis] + shift, shape),
                    jnp.broadcast_to(there[axis] + shift, shape),
                    float(sizes[axis]),
                )
            )
        total = convolved(convolved(axes[0], axes[1]), axes[2])
        for steps in range(6):
            walks[steps, slab * atoms : (slab + 1) * atoms, :] = total[steps] * FACTORIAL[steps]
    wide = length + 4
    first_x = (place * length - 2).astype(F32)
    first_y = start - rows
    count = wide * 3 * rows
    rows_iota = lax.broadcasted_iota(jnp.int32, (count, depth), 0).astype(F32)
    used_row = lax.rem(row_lane, HALF) < atoms
    for pair in range(pairs):
        x_at = even_x[pair : pair + 1, :] + float(2 * pair * width_x) - first_x
        y_at = row_y[pair : pair + 1, :] - first_y
        good = (x_at >= 0) & (x_at < wide) & (y_at >= 0) & (y_at < 3 * rows) & used_row[0:1, :]
        target = jnp.where(good, x_at * (3 * rows) + y_at, -1.0)
        row_hot[:, pair * depth : (pair + 1) * depth] = (rows_iota == target).astype(BF16)
        z_at = column_z[:, pair : pair + 1]
        lanes_z = lax.broadcasted_iota(jnp.int32, (depth, depth), 1).astype(F32)
        deep_hot[pair * depth : (pair + 1) * depth, :] = (lanes_z == z_at).astype(F32)


def total_of(x):
    return jnp.sum(jnp.sum(x, axis=1, keepdims=True), axis=0, keepdims=True)


def quadratic_form(poly, moments, shift):
    total = None
    for i, one in enumerate(poly):
        for j, two in enumerate(poly):
            if j < i:
                continue
            term = one * two * moments[i + j + shift] * (1.0 if i == j else 2.0)
            total = term if total is None else total + term
    return total


def finish_kernel(
    devices,
    wires,
    atoms,
    charge_ref,
    payload,
    walks,
    row_hot,
    deep_hot,
    field,
    density,
    potential,
):
    place, wire = (lax.axis_index("slab"), lax.axis_index("energy"))
    length, rows, depth = potential.shape
    pairs = devices
    groups = density.shape[0]
    charge = charge_ref[0] * payload[0:pairs, :]
    for group in range(1, groups):
        charge = charge + charge_ref[group] * payload[group * pairs : (group + 1) * pairs, :]
    for group in range(groups):
        value = payload[pl.ds(group * pairs + place, 1), :]
        density[group, 0:1, :] = value[:, :atoms]
        density[group, 1:2, :] = pltpu.roll(value, HALF, 1)[:, :atoms]
    square = jnp.concatenate([charge, jnp.zeros((depth - pairs, depth), F32)], axis=0)
    columns = square.T
    later = jnp.concatenate([charge[1:], jnp.zeros((1, depth), F32)], axis=0)
    lanes = lax.broadcasted_iota(jnp.int32, (pairs, depth), 1)
    even_row = jnp.where(lanes >= HALF, 2.0 * charge, charge)
    odd_row = pltpu.roll(jnp.where(lanes >= HALF, charge, 2.0 * later), HALF, 1)
    totals = [None] * 6
    for slab in range(2 * pairs):
        pair, side = (slab // 2, slab % 2)
        row = (odd_row if side else even_row)[pair : pair + 1, :]
        column = columns[side * HALF : side * HALF + atoms, pair : pair + 1]
        outer = column * row
        for steps in range(6):
            term = walks[steps, slab * atoms : (slab + 1) * atoms, :] * outer
            totals[steps] = term if totals[steps] is None else totals[steps] + term
    base = groups * pairs
    crossed = []
    for steps in range(6):
        cross = 2.0 * charge * payload[base + steps * pairs : base + (steps + 1) * pairs, :]
        crossed.append(total_of(totals[steps]) + total_of(cross))
    sums = payload[base + 6 * pairs : base + 6 * pairs + 1, :]
    plain = [sums[:, steps : steps + 1] + crossed[steps] for steps in range(6)]
    moved = []
    for steps in range(6):
        value = sums[:, 8 + steps : 9 + steps]
        binomial = 1
        for part in range(steps, -1, -1):
            value = value + (binomial * (-6.0) ** (steps - part)) * crossed[part]
            binomial = binomial * part // (steps - part + 1)
        moved.append(value)
    smooth = plain[1] > 3.5 * plain[0]
    level = jnp.where(smooth, 0.5, 6.5)
    moments = [jnp.where(smooth, two, one) for one, two in zip(plain, moved)]
    residual, direction = ([jnp.ones_like(level)], [jnp.ones_like(level)])
    norm = moments[0]
    alphas, betas = ([], [])
    for turn in range(ITERS):
        energy = level * quadratic_form(direction, moments, 0) - quadratic_form(direction, moments, 1)
        alpha = norm / energy
        alphas.append(alpha)
        if turn + 1 == ITERS:
            break
        longer = residual + [jnp.zeros_like(level)]
        for i, value in enumerate(direction):
            longer[i] = longer[i] - alpha * level * value
            longer[i + 1] = longer[i + 1] + alpha * value
        residual = longer
        following = quadratic_form(residual, moments, 0)
        beta = following / norm
        betas.append(beta)
        norm = following
        direction = [
            value + beta * direction[i] if i < len(direction) else value
            for i, value in enumerate(residual)
        ]
    pieces = [[], [], []]
    for pair in range(pairs):
        hot = deep_hot[pair * depth : (pair + 1) * depth, :]
        for place_in, piece in enumerate(three_parts(columns[:, pair : pair + 1] * hot)):
            pieces[place_in].append(piece)
    spread = jnp.concatenate([jnp.concatenate(piece, axis=0) for piece in pieces], axis=1)
    placed = dot(row_hot[...], spread, False)
    placed = placed[:, :depth] + (placed[:, depth : 2 * depth] + placed[:, 2 * depth :])
    margin = ITERS - 1
    wide = (length + 2 * margin, 3 * rows, depth)
    mask = grid_mask(wide, margin, length, rows, place, devices, wire, wires)
    source = field[...] + placed.reshape(wide)
    residual, direction = (source, source)
    total = alphas[0] * source[margin:-margin, rows : 2 * rows]
    for turn in range(ITERS - 1):
        image = 6.5 * direction[1:-1] - neighbours(direction)
        inner_mask = mask[turn + 1 : wide[0] - turn - 1]
        residual = (residual[1:-1] - alphas[turn] * image) * inner_mask
        direction = residual + betas[turn] * direction[1:-1]
        extra = margin - turn - 1
        block = direction[extra : extra + length, rows : 2 * rows]
        total = total + alphas[turn + 1] * block
    potential[...] = total


def hop(count, turn):
    moves = {i: i for i in range(count)}
    for core in range(2):
        here, there = (2 * turn - 2 + core, 2 * turn + core)
        moves[here], moves[there] = (there, here)
    return sorted(moves.items())


def pairs_of(count):
    return [(i, i ^ 1) for i in range(count)]


def total_over(value, axis, strides):
    size = 1
    for name in axis if isinstance(axis, tuple) else (axis,):
        size *= lax.axis_size(name)
    got = [lax.ppermute(value, axis, [(i, i ^ k) for i in range(size)]) for k in strides]
    if len(got) == 1:
        return value + got[0]
    return (value + got[0]) + (got[1] + got[2])


def total_over_all(value):
    wires, slabs = (lax.axis_size("energy"), lax.axis_size("slab"))
    value = total_over(value, "slab", (1,))
    stride = 2
    while stride * 2 < slabs:
        value = total_over(value, "slab", (stride,))
        stride *= 2
    value = total_over(value, BOTH, (stride, slabs, stride + slabs))
    stride = 2
    while stride * 4 <= wires:
        value = total_over(value, "energy", (stride, 2 * stride, 3 * stride))
        stride *= 4
    if stride < wires:
        value = total_over(value, "energy", (stride,))
    return value


def inner_pairs(count):
    return [(i, (i + 1) % count if i % 2 else (i - 1) % count) for i in range(count)]


def neighbour_turn(count):
    return [(i, (i + 1) % count if i % 2 else (i - 1) % count) for i in range(count)]


def on_device(
    green_iso,
    coupling,
    lead_green,
    energy_weight,
    energy_group,
    group_charge,
    orbital_atom,
    atom_cell,
    doping,
):
    devices, wires = (lax.axis_size("slab"), lax.axis_size("energy"))
    groups = group_charge.shape[0]
    atoms = atom_cell.shape[1]
    n = lead_green.shape[-1]
    length, rows, depth = doping.shape
    shape = jax.ShapeDtypeStruct
    orbital_row = orbital_atom.reshape(1, n)
    maps = shape((2 * n + 32, n), F32)
    edge_rows = REACH * rows + 8
    own, own_step, sent_step, sent, edge = local_call(
        pair_kernel,
        (maps, shape((n, n), F32), shape((n, n), F32), maps, shape((edge_rows, depth), F32)),
        [
            pltpu.VMEM((2, n, n), F32),
            pltpu.VMEM((2, 2, n, n), F32),
            pltpu.VMEM((2, n, n), F32),
            pltpu.VMEM((8, TILE), F32),
            pltpu.VMEM(atom_cell.shape, jnp.int32),
            pltpu.VMEM(doping.shape, F32),
            pltpu.SemaphoreType.DMA((10,)),
        ],
        "hhhhh",
        "pair",
        30,
        72 * n**3,
        *[
            pltpu.with_memory_space_constraint(x, pltpu.HBM)
            for x in (green_iso, coupling, lead_green, atom_cell, doping)
        ],
    )
    got = lax.ppermute(sent, "slab", pairs_of(devices))
    second = lax.ppermute(edge, "slab", neighbour_turn(devices))
    side = shape((-(-REACH * (length + 2 * REACH) // 8) * 8, depth), F32)
    passed, wide_block, cells, one_side, two_side = local_call(
        relay_kernel,
        (
            shape((PACKED_ROWS, TILE), F32),
            shape((length + 2 * REACH, rows, depth), F32),
            shape((8, depth), F32),
            side,
            side,
        ),
        [],
        "vvvv",
        "relay",
        20,
        12 * n**3,
        own,
        got,
        doping,
        second,
    )
    packed = lax.ppermute(passed, "slab", hop(devices, 1))
    one_beside = lax.ppermute(one_side, "energy", pairs_of(wires))
    two_beside = lax.ppermute(two_side, "energy", inner_pairs(wires))
    other_cells = lax.ppermute(cells, "slab", pairs_of(devices))
    if devices > 4:
        other_cells = lax.psum(own[2 * n + 8 : 2 * n + 16, :depth], "slab")
    got_step = lax.ppermute(sent_step, "slab", pairs_of(devices))
    wide = (length + 2 * ITERS - 2, 3 * rows, depth)
    walks, row_hot, deep_hot, member = local_call(
        functools.partial(atoms_kernel, devices, wires, length),
        (
            shape((6, 2 * devices * atoms, depth), F32),
            shape((wide[0] * wide[1], devices * depth), BF16),
            shape((devices * depth, depth), F32),
            shape((n, TILE), F32),
        ),
        [],
        "vvv",
        "atoms",
        28,
        2**29,
        orbital_row,
        cells,
        other_cells,
    )
    extra, wide_field = local_call(
        functools.partial(moments_kernel, devices, wires),
        (shape((6 * devices + 8, depth), F32), shape(wide, F32)),
        [pltpu.VMEM((length + 2 * REACH, 3 * rows, depth), F32)],
        "vvvvv",
        "moments",
        20,
        2**26,
        own,
        wide_block,
        one_beside,
        two_beside,
        atom_cell,
    )
    stack, stack_parts, known = local_call(
        compose_kernel,
        (shape((4 * n, n), F32), shape((4 * n, 3 * n), BF16), shape((8, TILE), F32)),
        [],
        "vvvvvv",
        "compose",
        28,
        2**28,
        orbital_row,
        member,
        own,
        got,
        own_step,
        got_step,
    )
    for turn in range(1, devices // 2 - 1):
        passed = local_call(
            functools.partial(pass_kernel, turn),
            shape((PACKED_ROWS, TILE), F32),
            [pltpu.VMEM((n, n), F32)],
            "vvv",
            "pass_on",
            20,
            24 * n**3,
                packed,
            own,
            got,
        )
        arrived = lax.ppermute(passed, "slab", hop(devices, turn + 1))
        packed = jnp.where(lax.axis_index("slab") // 2 == turn + 1, arrived, packed)
    payload = local_call(
        functools.partial(density_kernel, devices),
        shape(((groups + 6) * devices + 8, TILE), F32),
        [pltpu.VMEM((n, n), F32), pltpu.VMEM((8, TILE), F32)],
        "ssvvvvvv",
        "density",
        20,
        24 * n**3,
        energy_weight,
        energy_group,
        member,
        packed,
        stack,
        stack_parts,
        known,
        extra,
    )
    payload = total_over_all(payload)
    return local_call(
        functools.partial(finish_kernel, devices, wires, atoms),
        (shape((groups, 2, atoms), F32), shape(doping.shape, F32)),
        [],
        "svvvvv",
        "finish",
        28,
        2**29,
        group_charge,
        payload,
        walks,
        row_hot,
        deep_hot,
        wide_field,
    )


def solution(mesh):
    in_specs = (
        P("energy", "slab", None, None),
        P("slab", None, None),
        P("energy", None, None),
        P("energy"),
        P("energy"),
        P(),
        P(),
        P("slab", None),
        P("slab", "energy", None),
    )
    out_specs = (P(None, "slab", None), P("slab", "energy", None))
    return jax.shard_map(
        on_device, mesh=mesh, in_specs=in_specs, out_specs=out_specs, check_vma=False
    )
```

```python
import functools

import jax
import jax.numpy as jnp
from jax import lax
from jax.experimental import pallas as pl
from jax.experimental.pallas import tpu as pltpu
from jax.sharding import PartitionSpec as P

ITERS = 3
F32 = jnp.float32
BF16 = jnp.bfloat16
TILE = 128
BOTH = ("energy", "slab")
REACH = 5
HALF = 64


def split(a):
    high = a.astype(BF16)
    return high, (a - high.astype(F32)).astype(BF16)


def dot(a, b, transposed):
    dims = (((1,), (1 if transposed else 0,)), ((), ()))
    return lax.dot_general(a, b, dims, preferred_element_type=F32)


def product(left, right, transposed=False):
    n = right[0].shape[0 if transposed else 1]
    wide = dot(left[0], jnp.concatenate(right, 0 if transposed else 1), transposed)
    return wide[:, :n] + (wide[:, n:] + dot(left[1], right[0], transposed))


def joined(left):
    return jnp.concatenate([left[0], left[1], left[0]], axis=1)


def product_joined(wide, right, transposed=False):
    high, low = right
    axis = 0 if transposed else 1
    n = high.shape[axis]
    cut = n - TILE

    def part(x, start, stop):
        return lax.slice_in_dim(x, start, stop, axis=axis)

    first = [part(x, 0, cut) for x in (high, high, low)]
    last_high, last_low = (part(high, cut, n), part(low, cut, n))
    last = [
        jnp.concatenate([last_high, last_low], axis),
        jnp.concatenate([last_high, jnp.zeros_like(last_high)], axis),
    ]
    one = dot(wide, jnp.concatenate(first, 1 - axis), transposed)
    two = dot(wide[:, : 2 * high.shape[1 - axis]], jnp.concatenate(last, 1 - axis), transposed)
    return jnp.concatenate([one, two[:, :TILE] + two[:, TILE:]], axis=1)


def diagonal_row(matrix):
    rows = lax.broadcasted_iota(jnp.int32, (TILE, TILE), 0)
    columns = lax.broadcasted_iota(jnp.int32, (TILE, TILE), 1)
    parts = []
    for start in range(0, matrix.shape[0], TILE):
        block = matrix[start : start + TILE, start : start + TILE]
        parts.append(jnp.sum(jnp.where(rows == columns, block, 0.0), axis=0, keepdims=True))
    return jnp.concatenate(parts, axis=1)


PACKED_ROWS = 5 * TILE + 8


def pack(matrix, out):
    def block(i, j):
        return matrix[i * TILE : (i + 1) * TILE, j * TILE : (j + 1) * TILE]

    rows = lax.broadcasted_iota(jnp.int32, (TILE, TILE), 0)
    columns = lax.broadcasted_iota(jnp.int32, (TILE, TILE), 1)
    for place, (i, j) in enumerate(((0, 1), (0, 2), (1, 2))):
        out[place * TILE : (place + 1) * TILE, :] = block(i, j) + block(j, i).T
    one, two = (block(0, 0), block(1, 1))
    merged = jnp.where(rows < columns, one + one.T, jnp.where(rows > columns, two + two.T, one))
    out[3 * TILE : 4 * TILE, :] = merged
    out[4 * TILE : 5 * TILE, :] = block(2, 2)
    row = jnp.sum(jnp.where(rows == columns, two, 0.0), axis=0, keepdims=True)
    out[5 * TILE :, :] = jnp.broadcast_to(row, (8, TILE))


def unpack(packed, out):
    rows = lax.broadcasted_iota(jnp.int32, (TILE, TILE), 0)
    columns = lax.broadcasted_iota(jnp.int32, (TILE, TILE), 1)
    out[...] = jnp.zeros_like(out)
    for place, (i, j) in enumerate(((0, 1), (0, 2), (1, 2))):
        value = packed[place * TILE : (place + 1) * TILE, :]
        out[i * TILE : (i + 1) * TILE, j * TILE : (j + 1) * TILE] = value
    merged = packed[3 * TILE : 4 * TILE, :]
    row = packed[5 * TILE : 5 * TILE + 1, :]
    out[:TILE, :TILE] = jnp.where(rows <= columns, merged, 0.0)
    out[TILE : 2 * TILE, TILE : 2 * TILE] = jnp.where(
        rows > columns, merged, jnp.where(rows == columns, row, 0.0)
    )
    out[2 * TILE :, 2 * TILE :] = packed[4 * TILE : 5 * TILE, :]


def plane_rows(n, plane):
    start = 2 * n + 16 + 8 * (plane // 3)
    return slice(start, start + 8)


def plane_lanes(plane):
    return slice((plane % 3) * TILE, (plane % 3 + 1) * TILE)


def copy_all(pairs, sems):
    copies = [pltpu.make_async_copy(src, dst, sems.at[i]) for i, (src, dst) in enumerate(pairs)]
    for copy in copies:
        copy.start()
    return copies


def slabs(early, late, isos, lead, maps, step):
    place = lax.axis_index("slab")
    n = early.shape[0]

    @pl.when(place == 0)
    def _():
        state = lead[...]
        for slab, value in enumerate((early, late)):
            parts = split(value)
            state = product(parts, split(state))
            state = product(split(state), parts, True) + isos[slab]
            maps[2 * n + slab : 2 * n + slab + 1, :] = diagonal_row(state)
        maps[n : 2 * n, :] = state

    @pl.when(place != 0)
    def _():
        later = split(late)
        wide = joined(later)
        term = product_joined(wide, split(isos[0]))
        maps[0:n, :] = product_joined(wide, split(early))
        term = product(split(term), later, True) + isos[1]
        maps[n : 2 * n, :] = term
        maps[2 * n : 2 * n + 1, :] = diagonal_row(isos[0])
        maps[2 * n + 1 : 2 * n + 2, :] = diagonal_row(term)
        if step is not None:
            step[...] = early


def other_kernel(
    iso,
    coupling,
    lead,
    cells_in,
    field_in,
    step,
    sent,
    planes,
    own_early,
    own_late,
    own_iso,
    own_lead,
    c_buf,
    g_buf,
    lead_buf,
    sems,
    row,
    cells,
    field,
    more_sems,
):
    place = lax.axis_index("slab")
    core = lax.rem(place, 2)
    n = lead_buf.shape[1]
    sources = []
    for slab in range(2):
        sources.append((coupling.at[slab], c_buf.at[slab]))
        sources.append((iso.at[1 - core, slab], g_buf.at[slab]))
        sources.append((iso.at[core, slab], own_iso.at[slab]))
    sources.append((lead.at[1 - core], lead_buf))
    sources.append((lead.at[core], own_lead))
    waits = copy_all(sources, sems)
    copies = copy_all([(cells_in, cells), (field_in, field)], more_sems)
    steps = []
    for slab in range(2):
        for copy in waits[3 * slab : 3 * slab + 3]:
            copy.wait()
        parts = split(c_buf[slab])
        for buf in (g_buf, own_iso):
            steps.append(product_joined(joined(split(buf[slab])), parts))
    waits[6].wait()
    own_early[...] = steps[1]
    own_late[...] = steps[3]
    slabs(steps[0], steps[2], g_buf, lead_buf, sent, step)
    waits[7].wait()
    for copy in copies:
        copy.wait()
    atoms = cells.shape[1]
    row[...] = jnp.zeros_like(row)
    row[0:1, 0:atoms] = cells[0:1, :].astype(F32)
    row[0:1, HALF : HALF + atoms] = cells[1:2, :].astype(F32)
    rows = lax.broadcasted_iota(jnp.int32, (8, TILE), 0)
    mine = jnp.where(rows == place, row[0:1, :], 0.0)
    sent[2 * n + 8 : 2 * n + 16, 0:TILE] = mine
    planes[REACH * 8 :, :] = mine
    length = field.shape[0]
    even = core == 0
    for plane in range(REACH):
        low, high = (field[plane], field[length - REACH + plane])
        planes[plane * 8 : plane * 8 + 8, :] = jnp.where(even, low, high)
        sent[plane_rows(n, plane), plane_lanes(plane)] = jnp.where(even, high, low)


def own_kernel(planes, early, late, isos, lead, own):
    n = lead.shape[0]
    own[2 * n + 8 : 2 * n + 16, 0:TILE] = planes[REACH * 8 :, :]
    slabs(early[...], late[...], isos, lead, own, None)


def advance(map_ref, state):
    n = map_ref.shape[1]
    composed = split(map_ref[0:n, :])
    term = product(composed, split(state))
    return product(split(term), composed, True) + map_ref[n : 2 * n, :]


def near_far(mine, other):
    core = lax.rem(lax.axis_index("slab"), 2)
    return jnp.where(core == 0, mine, other), jnp.where(core == 0, other, mine)


def relay_kernel(
    own, got, own_step, got_step, field, second, out, stack, parts, wide, cells, one_side, two_side
):
    place, wire = (lax.axis_index("slab"), lax.axis_index("energy"))
    n = own.shape[1]
    length, height, _ = field.shape
    even = lax.rem(place, 2) == 0
    wide[REACH : REACH + length] = field[...]
    for plane in range(REACH):
        one = got[plane_rows(n, plane), plane_lanes(plane)]
        two = second[plane * 8 : plane * 8 + 8, :]
        wide[plane] = jnp.where(even, two, one)
        wide[REACH + length + plane] = jnp.where(even, one, two)
    spot = slice(2 * n + 8, 2 * n + 16)
    cells[...] = own[spot, :TILE] + got[spot, :TILE] + second[REACH * 8 :, :]
    even = lax.rem(wire, 2) == 0
    for plane in range(length + 2 * REACH):
        low, high = (wide[plane, :REACH, :], wide[plane, height - REACH :, :])
        spot = slice(plane * REACH, (plane + 1) * REACH)
        one_side[spot, :] = jnp.where(even, high, low)
        two_side[spot, :] = jnp.where(even, low, high)

    @pl.when(place == 0)
    def _():
        pack(advance(got, own[n : 2 * n, :]), out)

    @pl.when(place == 1)
    def _():
        pack(advance(own, got[n : 2 * n, :]), out)

    @pl.when(place >= 2)
    def _():
        near_step, far_step = near_far(own_step[...], got_step[...])
        near_map, far_map = near_far(own[0:n, :], got[0:n, :])
        far = jnp.concatenate([far_step, far_map], axis=0)
        both = product_joined(joined(split(far)), split(near_map))
        for number, value in enumerate((near_step, near_map, both[:n], both[n:])):
            rows = slice(number * n, (number + 1) * n)
            stack[rows, :] = value
            high, low = split(value)
            parts[rows, :] = jnp.concatenate(
                [high, low, high[:, : n - TILE], low[:, : n - TILE], high[:, : n - TILE]], axis=1
            )


def pass_kernel(turn, packed, own, got, out, state):
    place = lax.axis_index("slab")
    for core, (near, far) in enumerate(((own, got), (got, own))):

        @pl.when(place == 2 * turn + core)
        def _():
            unpack(packed, state)
            state[...] = advance(near, state[...])
            pack(advance(far, state[...]), out)


def known_kernel(orbital_atom, member, own, got, own_step, got_step, fold):
    n = own.shape[1]
    atoms = lax.broadcasted_iota(jnp.int32, (TILE, n), 0)
    spots = (atoms == orbital_atom[...]).astype(BF16)
    _, far_step = near_far(own_step[...], got_step[...])
    _, far_map = near_far(own[0:n, :], got[0:n, :])
    near_source, _ = near_far(own[n : 2 * n, :], got[n : 2 * n, :])
    far = jnp.concatenate([far_step, far_map], axis=0)
    both = product_joined(joined(split(far)), split(near_source))
    near_rows, far_rows = near_far(own[2 * n : 2 * n + 2, :], got[2 * n : 2 * n + 2, :])
    rest = jnp.concatenate([near_rows, far_rows, jnp.zeros((4, n), F32)], axis=0)
    total = jnp.zeros((8, TILE), F32)
    for _ in range(3):
        piece = rest.astype(BF16)
        total = total + dot(piece, spots, True)
        rest = rest - piece.astype(F32)
    fold[...] = total
    for number in range(2):
        rows = slice(number * n, (number + 1) * n)
        value = jnp.sum(far[rows] * both[rows], axis=1, keepdims=True) * member[...]
        fold[2 + number : 3 + number, :] += jnp.sum(value, axis=0, keepdims=True)


def density_kernel(
    pairs,
    weight_ref,
    group_ref,
    member,
    packed,
    stack,
    wide,
    known,
    extra,
    out,
    state,
    fold,
):
    place = lax.axis_index("slab")
    core = lax.rem(place, 2)
    n = state.shape[0]
    fold[...] = known[...]

    @pl.when(place >= 2)
    def _():
        unpack(packed, state)
        high, low = split(state[...])
        cut = n - TILE
        corner = [x[:cut, :cut] for x in (high, high, low)]
        one = dot(wide[:, 2 * n :], jnp.concatenate(corner, axis=0), False)
        last_high, last_low = (high[:, cut:], low[:, cut:])
        last = [
            jnp.concatenate([last_high, last_low], axis=1),
            jnp.concatenate([last_high, jnp.zeros_like(last_high)], axis=1),
        ]
        two = dot(wide[:, : 2 * n], jnp.concatenate(last, axis=0), False)
        both = jnp.concatenate([one, two[:, :TILE] + two[:, TILE:]], axis=1)
        for number in range(4):
            rows = slice(number * n, (number + 1) * n)
            value = jnp.sum(stack[rows, :] * both[rows], axis=1, keepdims=True) * member[...]
            fold[number : number + 1, :] += jnp.sum(value, axis=0, keepdims=True)

    plain = fold[...]
    turned = pltpu.roll(plain, HALF, 1)
    pair_rows = lax.broadcasted_iota(jnp.int32, (pairs, TILE), 0)
    groups = (out.shape[0] - extra.shape[0]) // pairs
    for group in range(groups):
        weight = jnp.where(group_ref[core] == group, weight_ref[core], 0.0)
        block = jnp.zeros((pairs, TILE), F32)
        for half in range(2):
            value = plain[2 * half : 2 * half + 1, :] + turned[2 * half + 1 : 2 * half + 2, :]
            block = block + jnp.where(pair_rows == place - core + half, weight, 0.0) * value
        out[group * pairs : (group + 1) * pairs, :] = block
    out[groups * pairs :, :] = extra[...]


def local_call(kernel, shapes, scratch, specs, name, limit, flops, *operands):
    spaces = {"v": pltpu.VMEM, "s": pltpu.SMEM, "h": pltpu.HBM}
    single = not isinstance(shapes, tuple)
    vmem = pl.BlockSpec(memory_space=pltpu.VMEM)
    return pl.pallas_call(
        kernel,
        out_shape=shapes,
        in_specs=[pl.BlockSpec(memory_space=spaces[spec]) for spec in specs],
        out_specs=vmem if single else (vmem,) * len(shapes),
        scratch_shapes=scratch,
        compiler_params=pltpu.CompilerParams(vmem_limit_bytes=limit * 2**20),
        cost_estimate=pl.CostEstimate(flops=flops, bytes_accessed=2**20, transcendentals=0),
        name=name,
    )(*operands)


def shifted_pair(x, axis):
    size = x.shape[axis]
    before, after = (pltpu.roll(x, 1, axis), pltpu.roll(x, size - 1, axis))
    if axis == x.ndim - 1:
        lanes = lax.broadcasted_iota(jnp.int32, x.shape, axis)
        before = jnp.where(lanes == 0, 0.0, before)
        after = jnp.where(lanes == size - 1, 0.0, after)
    return before, after


def neighbours(x):
    centre = x[1:-1]
    up, down = shifted_pair(centre, 1)
    left, right = shifted_pair(centre, 2)
    return (x[2:] + x[:-2]) + (up + down) + (left + right)


def differences(x):
    centre = x[1:-1]
    up, down = shifted_pair(centre, 1)
    left, right = shifted_pair(centre, 2)
    along = (x[2:] - centre) + (x[:-2] - centre)
    across = (up - centre) + (down - centre)
    deep = (left - centre) + (right - centre)
    return along + (across + deep)


def grid_mask(shape, margin, length, rows, place, devices, wire, wires):
    planes = lax.broadcasted_iota(jnp.int32, shape, 0)
    row = lax.broadcasted_iota(jnp.int32, shape, 1)
    low_x = jnp.where(place == 0, margin, 0)
    high_x = jnp.where(place == devices - 1, margin + length, shape[0])
    low_y = jnp.where(wire == 0, rows, 0)
    high_y = jnp.where(wire == wires - 1, 2 * rows, shape[1])
    inside = (planes >= low_x) & (planes < high_x) & (row >= low_y) & (row < high_y)
    return inside.astype(F32)


def three_parts(x):
    parts = []
    for _ in range(3):
        parts.append(x.astype(BF16))
        x = x - parts[-1].astype(F32)
    return parts


def coordinates(cell, rows_y, depth):
    z_part = cell - depth * jnp.floor(cell * (1.0 / depth))
    plane = jnp.floor(cell * (1.0 / depth))
    x_part = jnp.floor(plane * (1.0 / rows_y))
    return x_part, plane - rows_y * x_part, z_part


WALKS = ((0, 1),), ((1, 1),), ((0, 2), (2, 1)), ((1, 3), (3, 1)), ((0, 6), (2, 4), (4, 1)), ((1, 10), (3, 5), (5, 1))
FACTORIAL = (1.0, 1.0, 2.0, 6.0, 24.0, 120.0)


def walk_counts(here, there, length):
    apart = jnp.abs(here - there)
    low = here + there + 2.0
    high = 2.0 * length - here - there
    at = []
    for steps in range(6):
        value = (apart == steps).astype(F32)
        if steps >= 2:
            value = value - (low == steps).astype(F32) - (high == steps).astype(F32)
        at.append(value)
    counts = []
    for steps, terms in enumerate(WALKS):
        total = None
        for distance, count in terms:
            term = at[distance] * (count / FACTORIAL[steps])
            total = term if total is None else total + term
        counts.append(total)
    return counts


def convolved(left, right):
    result = []
    for steps in range(6):
        total = left[0] * right[steps]
        for part in range(1, steps + 1):
            total = total + left[part] * right[steps - part]
        result.append(total)
    return result


def moments_kernel(devices, wires, own, field, one_beside, two_beside, cells, out, wide_field, whole_field):
    place, wire = (lax.axis_index("slab"), lax.axis_index("energy"))
    planes, rows, depth = field.shape
    length = planes - 2 * REACH
    width_x = length // 2
    atoms = cells.shape[1]
    grid_y = rows * wires
    pairs = devices
    n = own.shape[1]
    even = lax.rem(wire, 2) == 0
    whole_field[...] = jnp.zeros_like(whole_field)
    whole_field[:, rows : 2 * rows, :] = field[...]
    for plane in range(planes):
        spot = slice(plane * REACH, (plane + 1) * REACH)
        one, two = (one_beside[spot, :], two_beside[spot, :])
        whole_field[plane, rows - REACH : rows, :] = jnp.where(even, two, one)
        whole_field[plane, 2 * rows : 2 * rows + REACH, :] = jnp.where(even, one, two)
    whole = (planes, 3 * rows, depth)
    mask = grid_mask(whole, REACH, length, rows, place, devices, wire, wires)
    source = jnp.where(mask > 0, whole_field[...], 0.0)
    margin = ITERS - 1
    wide_field[...] = source[REACH - margin : REACH + length + margin]

    def inner(x):
        extra = (x.shape[0] - length) // 2
        return x[extra : extra + length, rows : 2 * rows]

    chain = [source]
    for step in range(1, 6):
        chain.append(neighbours(chain[-1]) * mask[step : planes - step])
    blocks = [inner(x) for x in chain]
    near = source[2:-2]
    other = [near]
    for step in range(1, 4):
        other.append(differences(other[-1]) * mask[2 + step : planes - 2 - step])
    other = [inner(x) for x in other]
    lanes = lax.broadcasted_iota(jnp.int32, (8, depth), 1)
    sums = jnp.zeros((8, depth), F32)
    for base, fields in enumerate((blocks, other)):
        for steps in range(6):
            part = jnp.sum(fields[steps // 2] * fields[(steps + 1) // 2], axis=0)
            part = jnp.sum(jnp.sum(part, axis=1, keepdims=True), axis=0, keepdims=True)
            sums = jnp.where(lanes == 8 * base + steps, part, sums)
    out[...] = jnp.zeros_like(out)
    out[6 * pairs : 6 * pairs + 8, :] = sums
    mine = own[2 * n + 8 : 2 * n + 16, :depth]
    mine = jnp.sum(mine, axis=0, keepdims=True)
    lane = lax.broadcasted_iota(jnp.int32, (1, depth), 1)
    odd = (lane >= HALF).astype(F32)
    used = lax.rem(lane, HALF) < atoms
    x_part, y_part, z_part = coordinates(mine, grid_y, depth)
    start = (wire * rows).astype(F32)
    ours = used & (y_part >= start) & (y_part < start + rows)
    at_row = jnp.where(ours, (x_part + width_x * odd) * rows + y_part - start, -1.0)
    cell_rows = length * rows
    row_iota = lax.broadcasted_iota(jnp.int32, (cell_rows, depth), 0).astype(F32)
    deep_iota = lax.broadcasted_iota(jnp.int32, (depth, depth), 0).astype(F32)
    at_rows = (row_iota == at_row).astype(F32)
    at_deep = (deep_iota == z_part).astype(BF16)
    for steps, block in enumerate(blocks):
        value = jnp.zeros((cell_rows, depth), F32)
        for part in three_parts(block.reshape(cell_rows, depth)):
            value = value + dot(part, at_deep, False)
        value = jnp.sum(value * at_rows, axis=0, keepdims=True)
        out[pl.ds(steps * pairs + place, 1), :] = value


def atoms_kernel(
    devices,
    wires,
    length,
    orbital_atom,
    some_cells,
    other_cells,
    walks,
    row_hot,
    deep_hot,
    member,
):
    place, wire = (lax.axis_index("slab"), lax.axis_index("energy"))
    rows, depth = some_cells.shape
    width_x = length // 2
    atoms = walks.shape[1] // (2 * devices)
    grid_y = rows * wires
    pairs = devices
    n = orbital_atom.shape[1]
    start = (wire * rows).astype(F32)
    cells = jnp.maximum(some_cells[...], other_cells[...])
    spots = lax.broadcasted_iota(jnp.int32, (TILE, n), 0) == orbital_atom[...]
    spots = spots.astype(F32)
    for first in range(0, n, TILE):
        member[first : first + TILE, :] = spots[:, first : first + TILE].T
    row_cells = cells
    row_x, row_y, row_z = coordinates(row_cells, grid_y, depth)
    padded = jnp.concatenate([row_cells, jnp.zeros((depth - 8, depth), F32)], axis=0)
    column_x, column_y, column_z = coordinates(padded.T, grid_y, depth)
    row_lane = lax.broadcasted_iota(jnp.int32, (8, depth), 1)
    next_x, next_y, next_z = [jnp.concatenate([v[1:], v[:1]], axis=0) for v in (row_x, row_y, row_z)]

    def turned(now, later, step_now, step_later):
        value = jnp.where(row_lane >= HALF, now + step_now, later + step_later)
        return pltpu.roll(value, HALF, 1)

    even_x = row_x + width_x * (row_lane >= HALF).astype(F32)
    odd_x, odd_y, odd_z = (
        turned(row_x, next_x, 0.0, float(width_x)),
        turned(row_y, next_y, 0.0, 0.0),
        turned(row_z, next_z, 0.0, 0.0),
    )
    for slab in range(2 * pairs):
        pair, side = (slab // 2, slab % 2)
        base = float(slab * width_x)
        if side:
            there = (odd_x, odd_y, odd_z)
        else:
            there = (even_x, row_y, row_z)
        there = [v[pair : pair + 1, :] for v in there]
        here = [
            v[side * HALF : side * HALF + atoms, pair : pair + 1]
            for v in (column_x, column_y, column_z)
        ]
        shape = (atoms, depth)
        sizes = (2 * pairs * width_x, grid_y, depth)
        axes = []
        for axis in range(3):
            shift = base if axis == 0 else 0.0
            axes.append(
                walk_counts(
                    jnp.broadcast_to(here[axis] + shift, shape),
                    jnp.broadcast_to(there[axis] + shift, shape),
                    float(sizes[axis]),
                )
            )
        total = convolved(convolved(axes[0], axes[1]), axes[2])
        for steps in range(6):
            walks[steps, slab * atoms : (slab + 1) * atoms, :] = total[steps] * FACTORIAL[steps]
    wide = length + 4
    first_x = (place * length - 2).astype(F32)
    first_y = start - rows
    count = wide * 3 * rows
    rows_iota = lax.broadcasted_iota(jnp.int32, (count, depth), 0).astype(F32)
    used_row = lax.rem(row_lane, HALF) < atoms
    for pair in range(pairs):
        x_at = even_x[pair : pair + 1, :] + float(2 * pair * width_x) - first_x
        y_at = row_y[pair : pair + 1, :] - first_y
        good = (x_at >= 0) & (x_at < wide) & (y_at >= 0) & (y_at < 3 * rows) & used_row[0:1, :]
        target = jnp.where(good, x_at * (3 * rows) + y_at, -1.0)
        row_hot[:, pair * depth : (pair + 1) * depth] = (rows_iota == target).astype(BF16)
        z_at = column_z[:, pair : pair + 1]
        lanes_z = lax.broadcasted_iota(jnp.int32, (depth, depth), 1).astype(F32)
        deep_hot[pair * depth : (pair + 1) * depth, :] = (lanes_z == z_at).astype(F32)


def total_of(x):
    return jnp.sum(jnp.sum(x, axis=1, keepdims=True), axis=0, keepdims=True)


def quadratic_form(poly, moments, shift):
    total = None
    for i, one in enumerate(poly):
        for j, two in enumerate(poly):
            if j < i:
                continue
            term = one * two * moments[i + j + shift] * (1.0 if i == j else 2.0)
            total = term if total is None else total + term
    return total


def finish_kernel(
    devices,
    wires,
    atoms,
    charge_ref,
    payload,
    walks,
    row_hot,
    deep_hot,
    field,
    density,
    potential,
):
    place, wire = (lax.axis_index("slab"), lax.axis_index("energy"))
    length, rows, depth = potential.shape
    pairs = devices
    groups = density.shape[0]
    charge = charge_ref[0] * payload[0:pairs, :]
    for group in range(1, groups):
        charge = charge + charge_ref[group] * payload[group * pairs : (group + 1) * pairs, :]
    for group in range(groups):
        value = payload[pl.ds(group * pairs + place, 1), :]
        density[group, 0:1, :] = value[:, :atoms]
        density[group, 1:2, :] = pltpu.roll(value, HALF, 1)[:, :atoms]
    square = jnp.concatenate([charge, jnp.zeros((depth - pairs, depth), F32)], axis=0)
    columns = square.T
    later = jnp.concatenate([charge[1:], jnp.zeros((1, depth), F32)], axis=0)
    lanes = lax.broadcasted_iota(jnp.int32, (pairs, depth), 1)
    even_row = jnp.where(lanes >= HALF, 2.0 * charge, charge)
    odd_row = pltpu.roll(jnp.where(lanes >= HALF, charge, 2.0 * later), HALF, 1)
    totals = [None] * 6
    for slab in range(2 * pairs):
        pair, side = (slab // 2, slab % 2)
        row = (odd_row if side else even_row)[pair : pair + 1, :]
        column = columns[side * HALF : side * HALF + atoms, pair : pair + 1]
        outer = column * row
        for steps in range(6):
            term = walks[steps, slab * atoms : (slab + 1) * atoms, :] * outer
            totals[steps] = term if totals[steps] is None else totals[steps] + term
    base = groups * pairs
    crossed = []
    for steps in range(6):
        cross = 2.0 * charge * payload[base + steps * pairs : base + (steps + 1) * pairs, :]
        crossed.append(total_of(totals[steps]) + total_of(cross))
    sums = payload[base + 6 * pairs : base + 6 * pairs + 1, :]
    plain = [sums[:, steps : steps + 1] + crossed[steps] for steps in range(6)]
    moved = []
    for steps in range(6):
        value = sums[:, 8 + steps : 9 + steps]
        binomial = 1
        for part in range(steps, -1, -1):
            value = value + (binomial * (-6.0) ** (steps - part)) * crossed[part]
            binomial = binomial * part // (steps - part + 1)
        moved.append(value)
    smooth = plain[1] > 3.5 * plain[0]
    level = jnp.where(smooth, 0.5, 6.5)
    moments = [jnp.where(smooth, two, one) for one, two in zip(plain, moved)]
    residual, direction = ([jnp.ones_like(level)], [jnp.ones_like(level)])
    norm = moments[0]
    alphas, betas = ([], [])
    for turn in range(ITERS):
        energy = level * quadratic_form(direction, moments, 0) - quadratic_form(direction, moments, 1)
        alpha = norm / energy
        alphas.append(alpha)
        if turn + 1 == ITERS:
            break
        longer = residual + [jnp.zeros_like(level)]
        for i, value in enumerate(direction):
            longer[i] = longer[i] - alpha * level * value
            longer[i + 1] = longer[i + 1] + alpha * value
        residual = longer
        following = quadratic_form(residual, moments, 0)
        beta = following / norm
        betas.append(beta)
        norm = following
        direction = [
            value + beta * direction[i] if i < len(direction) else value
            for i, value in enumerate(residual)
        ]
    pieces = [[], [], []]
    for pair in range(pairs):
        hot = deep_hot[pair * depth : (pair + 1) * depth, :]
        for place_in, piece in enumerate(three_parts(columns[:, pair : pair + 1] * hot)):
            pieces[place_in].append(piece)
    spread = jnp.concatenate([jnp.concatenate(piece, axis=0) for piece in pieces], axis=1)
    placed = dot(row_hot[...], spread, False)
    placed = placed[:, :depth] + (placed[:, depth : 2 * depth] + placed[:, 2 * depth :])
    margin = ITERS - 1
    wide = (length + 2 * margin, 3 * rows, depth)
    mask = grid_mask(wide, margin, length, rows, place, devices, wire, wires)
    source = field[...] + placed.reshape(wide)
    residual, direction = (source, source)
    total = alphas[0] * source[margin:-margin, rows : 2 * rows]
    for turn in range(ITERS - 1):
        image = 6.5 * direction[1:-1] - neighbours(direction)
        inner_mask = mask[turn + 1 : wide[0] - turn - 1]
        residual = (residual[1:-1] - alphas[turn] * image) * inner_mask
        direction = residual + betas[turn] * direction[1:-1]
        extra = margin - turn - 1
        block = direction[extra : extra + length, rows : 2 * rows]
        total = total + alphas[turn + 1] * block
    potential[...] = total


def hop(count, turn):
    moves = {i: i for i in range(count)}
    for core in range(2):
        here, there = (2 * turn - 2 + core, 2 * turn + core)
        moves[here], moves[there] = (there, here)
    return sorted(moves.items())


def pairs_of(count):
    return [(i, i ^ 1) for i in range(count)]


def total_over(value, axis, strides):
    size = 1
    for name in axis if isinstance(axis, tuple) else (axis,):
        size *= lax.axis_size(name)
    got = [lax.ppermute(value, axis, [(i, i ^ k) for i in range(size)]) for k in strides]
    if len(got) == 1:
        return value + got[0]
    return (value + got[0]) + (got[1] + got[2])


def total_over_all(value):
    wires, slabs = (lax.axis_size("energy"), lax.axis_size("slab"))
    value = total_over(value, "slab", (1,))
    stride = 2
    while stride * 2 < slabs:
        value = total_over(value, "slab", (stride,))
        stride *= 2
    value = total_over(value, BOTH, (stride, slabs, stride + slabs))
    stride = 2
    while stride * 4 <= wires:
        value = total_over(value, "energy", (stride, 2 * stride, 3 * stride))
        stride *= 4
    if stride < wires:
        value = total_over(value, "energy", (stride,))
    return value


def inner_pairs(count):
    return [(i, (i + 1) % count if i % 2 else (i - 1) % count) for i in range(count)]


def neighbour_turn(count):
    return [(i, (i + 1) % count if i % 2 else (i - 1) % count) for i in range(count)]


def on_device(
    green_iso,
    coupling,
    lead_green,
    energy_weight,
    energy_group,
    group_charge,
    orbital_atom,
    atom_cell,
    doping,
):
    devices, wires = (lax.axis_size("slab"), lax.axis_size("energy"))
    groups = group_charge.shape[0]
    atoms = atom_cell.shape[1]
    n = lead_green.shape[-1]
    length, rows, depth = doping.shape
    shape = jax.ShapeDtypeStruct
    orbital_row = orbital_atom.reshape(1, n)
    maps = shape((2 * n + 32, n), F32)
    edge_rows = REACH * rows + 8
    held = [
        pltpu.with_memory_space_constraint(x, pltpu.HBM)
        for x in (green_iso, coupling, lead_green, atom_cell, doping)
    ]
    matrix = shape((n, n), F32)
    two = shape((2, n, n), F32)
    sent_step, sent, edge, own_step, own_late, own_iso, own_lead = local_call(
        other_kernel,
        (matrix, maps, shape((edge_rows, depth), F32), matrix, matrix, two, matrix),
        [
            pltpu.VMEM((2, n, n), F32),
            pltpu.VMEM((2, n, n), F32),
            pltpu.VMEM((n, n), F32),
            pltpu.SemaphoreType.DMA((8,)),
            pltpu.VMEM((8, TILE), F32),
            pltpu.VMEM(atom_cell.shape, jnp.int32),
            pltpu.VMEM(doping.shape, F32),
            pltpu.SemaphoreType.DMA((2,)),
        ],
        "hhhhh",
        "other",
        28,
        48 * n**3,
        *held,
    )
    got = lax.ppermute(sent, "slab", pairs_of(devices))
    second = lax.ppermute(edge, "slab", neighbour_turn(devices))
    own = local_call(
        own_kernel,
        maps,
        [],
        "vvvvv",
        "own",
        24,
        2**31,
        edge,
        own_step,
        own_late,
        own_iso,
        own_lead,
    )
    side = shape((-(-REACH * (length + 2 * REACH) // 8) * 8, depth), F32)
    got_step = lax.ppermute(sent_step, "slab", pairs_of(devices))
    passed, stack, stack_parts, wide_block, cells, one_side, two_side = local_call(
        relay_kernel,
        (
            shape((PACKED_ROWS, TILE), F32),
            shape((4 * n, n), F32),
            shape((4 * n, 5 * n - 3 * TILE), BF16),
            shape((length + 2 * REACH, rows, depth), F32),
            shape((8, depth), F32),
            side,
            side,
        ),
        [],
        "vvvvvv",
        "relay",
        28,
        12 * n**3,
        own,
        got,
        own_step,
        got_step,
        doping,
        second,
    )
    packed = lax.ppermute(passed, "slab", hop(devices, 1))
    one_beside = lax.ppermute(one_side, "energy", pairs_of(wires))
    two_beside = lax.ppermute(two_side, "energy", inner_pairs(wires))
    other_cells = lax.ppermute(cells, "slab", pairs_of(devices))
    if devices > 4:
        other_cells = lax.psum(own[2 * n + 8 : 2 * n + 16, :depth], "slab")
    wide = (length + 2 * ITERS - 2, 3 * rows, depth)
    walks, row_hot, deep_hot, member = local_call(
        functools.partial(atoms_kernel, devices, wires, length),
        (
            shape((6, 2 * devices * atoms, depth), F32),
            shape((wide[0] * wide[1], devices * depth), BF16),
            shape((devices * depth, depth), F32),
            shape((n, TILE), F32),
        ),
        [],
        "vvv",
        "atoms",
        28,
        2**29,
        orbital_row,
        cells,
        other_cells,
    )
    extra, wide_field = local_call(
        functools.partial(moments_kernel, devices, wires),
        (shape((6 * devices + 8, depth), F32), shape(wide, F32)),
        [pltpu.VMEM((length + 2 * REACH, 3 * rows, depth), F32)],
        "vvvvv",
        "moments",
        20,
        2**26,
        own,
        wide_block,
        one_beside,
        two_beside,
        atom_cell,
    )
    known = local_call(
        known_kernel,
        shape((8, TILE), F32),
        [],
        "vvvvvv",
        "known",
        24,
        2**28,
        orbital_row,
        member,
        own,
        got,
        own_step,
        got_step,
    )
    for turn in range(1, devices // 2 - 1):
        passed = local_call(
            functools.partial(pass_kernel, turn),
            shape((PACKED_ROWS, TILE), F32),
            [pltpu.VMEM((n, n), F32)],
            "vvv",
            "pass_on",
            20,
            24 * n**3,
                packed,
            own,
            got,
        )
        arrived = lax.ppermute(passed, "slab", hop(devices, turn + 1))
        packed = jnp.where(lax.axis_index("slab") // 2 == turn + 1, arrived, packed)
    payload = local_call(
        functools.partial(density_kernel, devices),
        shape(((groups + 6) * devices + 8, TILE), F32),
        [pltpu.VMEM((n, n), F32), pltpu.VMEM((8, TILE), F32)],
        "ssvvvvvv",
        "density",
        20,
        24 * n**3,
        energy_weight,
        energy_group,
        member,
        packed,
        stack,
        stack_parts,
        known,
        extra,
    )
    payload = total_over_all(payload)
    return local_call(
        functools.partial(finish_kernel, devices, wires, atoms),
        (shape((groups, 2, atoms), F32), shape(doping.shape, F32)),
        [],
        "svvvvv",
        "finish",
        28,
        2**29,
        group_charge,
        payload,
        walks,
        row_hot,
        deep_hot,
        wide_field,
    )


def solution(mesh):
    in_specs = (
        P("energy", "slab", None, None),
        P("slab", None, None),
        P("energy", None, None),
        P("energy"),
        P("energy"),
        P(),
        P(),
        P("slab", None),
        P("slab", "energy", None),
    )
    out_specs = (P(None, "slab", None), P("slab", "energy", None))
    return jax.shard_map(
        on_device, mesh=mesh, in_specs=in_specs, out_specs=out_specs, check_vma=False
    )
```

```python
import functools

import jax
import jax.numpy as jnp
from jax import lax
from jax.experimental import pallas as pl
from jax.experimental.pallas import tpu as pltpu
from jax.sharding import PartitionSpec as P

ITERS = 3
F32 = jnp.float32
BF16 = jnp.bfloat16
TILE = 128
BOTH = ("energy", "slab")
REACH = 5
HALF = 64


def split(a):
    high = a.astype(BF16)
    return high, (a - high.astype(F32)).astype(BF16)


def dot(a, b, transposed):
    dims = (((1,), (1 if transposed else 0,)), ((), ()))
    return lax.dot_general(a, b, dims, preferred_element_type=F32)


def product(left, right, transposed=False):
    n = right[0].shape[0 if transposed else 1]
    wide = dot(left[0], jnp.concatenate(right, 0 if transposed else 1), transposed)
    return wide[:, :n] + (wide[:, n:] + dot(left[1], right[0], transposed))


def joined(left):
    return jnp.concatenate([left[0], left[1], left[0]], axis=1)


def product_joined(wide, right, transposed=False):
    high, low = right
    axis = 0 if transposed else 1
    n = high.shape[axis]
    cut = n - TILE

    def part(x, start, stop):
        return lax.slice_in_dim(x, start, stop, axis=axis)

    first = [part(x, 0, cut) for x in (high, high, low)]
    last_high, last_low = (part(high, cut, n), part(low, cut, n))
    last = [
        jnp.concatenate([last_high, last_low], axis),
        jnp.concatenate([last_high, jnp.zeros_like(last_high)], axis),
    ]
    one = dot(wide, jnp.concatenate(first, 1 - axis), transposed)
    two = dot(wide[:, : 2 * high.shape[1 - axis]], jnp.concatenate(last, 1 - axis), transposed)
    return jnp.concatenate([one, two[:, :TILE] + two[:, TILE:]], axis=1)


def diagonal_row(matrix):
    rows = lax.broadcasted_iota(jnp.int32, (TILE, TILE), 0)
    columns = lax.broadcasted_iota(jnp.int32, (TILE, TILE), 1)
    parts = []
    for start in range(0, matrix.shape[0], TILE):
        block = matrix[start : start + TILE, start : start + TILE]
        parts.append(jnp.sum(jnp.where(rows == columns, block, 0.0), axis=0, keepdims=True))
    return jnp.concatenate(parts, axis=1)


PACKED_ROWS = 5 * TILE + 8


def pack(matrix, out):
    def block(i, j):
        return matrix[i * TILE : (i + 1) * TILE, j * TILE : (j + 1) * TILE]

    rows = lax.broadcasted_iota(jnp.int32, (TILE, TILE), 0)
    columns = lax.broadcasted_iota(jnp.int32, (TILE, TILE), 1)
    for place, (i, j) in enumerate(((0, 1), (0, 2), (1, 2))):
        out[place * TILE : (place + 1) * TILE, :] = block(i, j) + block(j, i).T
    one, two = (block(0, 0), block(1, 1))
    merged = jnp.where(rows < columns, one + one.T, jnp.where(rows > columns, two + two.T, one))
    out[3 * TILE : 4 * TILE, :] = merged
    out[4 * TILE : 5 * TILE, :] = block(2, 2)
    row = jnp.sum(jnp.where(rows == columns, two, 0.0), axis=0, keepdims=True)
    out[5 * TILE :, :] = jnp.broadcast_to(row, (8, TILE))


def unpack(packed, out):
    rows = lax.broadcasted_iota(jnp.int32, (TILE, TILE), 0)
    columns = lax.broadcasted_iota(jnp.int32, (TILE, TILE), 1)
    out[...] = jnp.zeros_like(out)
    for place, (i, j) in enumerate(((0, 1), (0, 2), (1, 2))):
        value = packed[place * TILE : (place + 1) * TILE, :]
        out[i * TILE : (i + 1) * TILE, j * TILE : (j + 1) * TILE] = value
    merged = packed[3 * TILE : 4 * TILE, :]
    row = packed[5 * TILE : 5 * TILE + 1, :]
    out[:TILE, :TILE] = jnp.where(rows <= columns, merged, 0.0)
    out[TILE : 2 * TILE, TILE : 2 * TILE] = jnp.where(
        rows > columns, merged, jnp.where(rows == columns, row, 0.0)
    )
    out[2 * TILE :, 2 * TILE :] = packed[4 * TILE : 5 * TILE, :]


def plane_rows(n, plane):
    start = 2 * n + 16 + 8 * (plane // 3)
    return slice(start, start + 8)


def plane_lanes(plane):
    return slice((plane % 3) * TILE, (plane % 3 + 1) * TILE)


def copy_all(pairs, sems):
    copies = [pltpu.make_async_copy(src, dst, sems.at[i]) for i, (src, dst) in enumerate(pairs)]
    for copy in copies:
        copy.start()
    return copies


def slabs(early, late, isos, lead, maps, step):
    place = lax.axis_index("slab")
    n = early.shape[0]

    @pl.when(place == 0)
    def _():
        state = lead[...]
        for slab, value in enumerate((early, late)):
            parts = split(value)
            state = product(parts, split(state))
            state = product(split(state), parts, True) + isos[slab]
            maps[2 * n + slab : 2 * n + slab + 1, :] = diagonal_row(state)
        maps[n : 2 * n, :] = state

    @pl.when(place != 0)
    def _():
        later = split(late)
        wide = joined(later)
        term = product_joined(wide, split(isos[0]))
        maps[0:n, :] = product_joined(wide, split(early))
        term = product(split(term), later, True) + isos[1]
        maps[n : 2 * n, :] = term
        maps[2 * n : 2 * n + 1, :] = diagonal_row(isos[0])
        maps[2 * n + 1 : 2 * n + 2, :] = diagonal_row(term)
        if step is not None:
            step[...] = early


def other_kernel(
    iso,
    coupling,
    lead,
    cells_in,
    field_in,
    step,
    sent,
    planes,
    own_early,
    own_late,
    own_iso,
    own_lead,
    c_buf,
    g_buf,
    lead_buf,
    sems,
    row,
    cells,
    field,
    more_sems,
):
    place = lax.axis_index("slab")
    core = lax.rem(place, 2)
    n = lead_buf.shape[1]
    sources = []
    for slab in range(2):
        sources.append((coupling.at[slab], c_buf.at[slab]))
        sources.append((iso.at[1 - core, slab], g_buf.at[slab]))
        sources.append((iso.at[core, slab], own_iso.at[slab]))
    sources.append((lead.at[1 - core], lead_buf))
    sources.append((lead.at[core], own_lead))
    waits = copy_all(sources, sems)
    copies = copy_all([(cells_in, cells), (field_in, field)], more_sems)
    steps = []
    for slab in range(2):
        for copy in waits[3 * slab : 3 * slab + 3]:
            copy.wait()
        parts = split(c_buf[slab])
        for buf in (g_buf, own_iso):
            steps.append(product_joined(joined(split(buf[slab])), parts))
    waits[6].wait()
    own_early[...] = steps[1]
    own_late[...] = steps[3]
    slabs(steps[0], steps[2], g_buf, lead_buf, sent, step)
    waits[7].wait()
    for copy in copies:
        copy.wait()
    atoms = cells.shape[1]
    row[...] = jnp.zeros_like(row)
    row[0:1, 0:atoms] = cells[0:1, :].astype(F32)
    row[0:1, HALF : HALF + atoms] = cells[1:2, :].astype(F32)
    rows = lax.broadcasted_iota(jnp.int32, (8, TILE), 0)
    mine = jnp.where(rows == place, row[0:1, :], 0.0)
    sent[2 * n + 8 : 2 * n + 16, 0:TILE] = mine
    planes[REACH * 8 :, :] = mine
    length = field.shape[0]
    even = core == 0
    for plane in range(REACH):
        low, high = (field[plane], field[length - REACH + plane])
        planes[plane * 8 : plane * 8 + 8, :] = jnp.where(even, low, high)
        sent[plane_rows(n, plane), plane_lanes(plane)] = jnp.where(even, high, low)


def own_kernel(planes, early, late, isos, lead, own):
    n = lead.shape[0]
    own[2 * n + 8 : 2 * n + 16, 0:TILE] = planes[REACH * 8 :, :]
    slabs(early[...], late[...], isos, lead, own, None)


def advance(map_ref, state):
    n = map_ref.shape[1]
    composed = split(map_ref[0:n, :])
    term = product(composed, split(state))
    return product(split(term), composed, True) + map_ref[n : 2 * n, :]


def near_far(mine, other):
    core = lax.rem(lax.axis_index("slab"), 2)
    return jnp.where(core == 0, mine, other), jnp.where(core == 0, other, mine)


def relay_kernel(
    own, got, own_step, got_step, field, second, out, stack, parts, wide, cells, one_side, two_side
):
    place, wire = (lax.axis_index("slab"), lax.axis_index("energy"))
    n = own.shape[1]
    length, height, _ = field.shape
    even = lax.rem(place, 2) == 0
    wide[REACH : REACH + length] = field[...]
    for plane in range(REACH):
        one = got[plane_rows(n, plane), plane_lanes(plane)]
        two = second[plane * 8 : plane * 8 + 8, :]
        wide[plane] = jnp.where(even, two, one)
        wide[REACH + length + plane] = jnp.where(even, one, two)
    spot = slice(2 * n + 8, 2 * n + 16)
    cells[...] = own[spot, :TILE] + got[spot, :TILE] + second[REACH * 8 :, :]
    even = lax.rem(wire, 2) == 0
    for plane in range(length + 2 * REACH):
        low, high = (wide[plane, :REACH, :], wide[plane, height - REACH :, :])
        spot = slice(plane * REACH, (plane + 1) * REACH)
        one_side[spot, :] = jnp.where(even, high, low)
        two_side[spot, :] = jnp.where(even, low, high)

    @pl.when(place == 0)
    def _():
        pack(advance(got, own[n : 2 * n, :]), out)

    @pl.when(place == 1)
    def _():
        pack(advance(own, got[n : 2 * n, :]), out)

    @pl.when(place >= 2)
    def _():
        near_step, far_step = near_far(own_step[...], got_step[...])
        near_map, far_map = near_far(own[0:n, :], got[0:n, :])
        far = jnp.concatenate([far_step, far_map], axis=0)
        both = product_joined(joined(split(far)), split(near_map))
        for number, value in enumerate((near_step, near_map, both[:n], both[n:])):
            rows = slice(number * n, (number + 1) * n)
            stack[rows, :] = value
            high, low = split(value)
            parts[rows, :] = jnp.concatenate(
                [high, low, high[:, : n - TILE], low[:, : n - TILE], high[:, : n - TILE]], axis=1
            )


def pass_kernel(turn, packed, own, got, out, state):
    place = lax.axis_index("slab")
    for core, (near, far) in enumerate(((own, got), (got, own))):

        @pl.when(place == 2 * turn + core)
        def _():
            unpack(packed, state)
            state[...] = advance(near, state[...])
            pack(advance(far, state[...]), out)


def known_kernel(
    pairs, weight_ref, group_ref, orbital_atom, member, own, got, own_step, got_step, fold, weights
):
    place = lax.axis_index("slab")
    core = lax.rem(place, 2)
    pair_rows = lax.broadcasted_iota(jnp.int32, (pairs, TILE), 0)
    mine_weight = jnp.where(core == 0, weight_ref[:, 0:1], weight_ref[:, 1:2])
    mine_group = jnp.where(core == 0, group_ref[:, 0:1], group_ref[:, 1:2])
    groups = weights.shape[0] // (2 * pairs)
    for half in range(2):
        for group in range(groups):
            weight = jnp.where(mine_group == group, mine_weight, 0.0)
            start = (half * groups + group) * pairs
            weights[start : start + pairs, :] = jnp.where(
                pair_rows == place - core + half, jnp.broadcast_to(weight, (pairs, TILE)), 0.0
            )
    n = own.shape[1]
    atoms = lax.broadcasted_iota(jnp.int32, (TILE, n), 0)
    spots = (atoms == orbital_atom[...]).astype(BF16)
    _, far_step = near_far(own_step[...], got_step[...])
    _, far_map = near_far(own[0:n, :], got[0:n, :])
    near_source, _ = near_far(own[n : 2 * n, :], got[n : 2 * n, :])
    far = jnp.concatenate([far_step, far_map], axis=0)
    both = product_joined(joined(split(far)), split(near_source))
    near_rows, far_rows = near_far(own[2 * n : 2 * n + 2, :], got[2 * n : 2 * n + 2, :])
    rest = jnp.concatenate([near_rows, far_rows, jnp.zeros((4, n), F32)], axis=0)
    total = jnp.zeros((8, TILE), F32)
    for _ in range(3):
        piece = rest.astype(BF16)
        total = total + dot(piece, spots, True)
        rest = rest - piece.astype(F32)
    fold[...] = total
    for number in range(2):
        rows = slice(number * n, (number + 1) * n)
        value = jnp.sum(far[rows] * both[rows], axis=1, keepdims=True) * member[...]
        fold[2 + number : 3 + number, :] += jnp.sum(value, axis=0, keepdims=True)


def density_kernel(
    pairs,
    member,
    packed,
    stack,
    wide,
    known,
    weights,
    extra,
    out,
    state,
    fold,
):
    place = lax.axis_index("slab")
    n = state.shape[0]
    fold[...] = known[...]

    @pl.when(place >= 2)
    def _():
        unpack(packed, state)
        high, low = split(state[...])
        cut = n - TILE
        corner = [x[:cut, :cut] for x in (high, high, low)]
        one = dot(wide[:, 2 * n :], jnp.concatenate(corner, axis=0), False)
        last_high, last_low = (high[:, cut:], low[:, cut:])
        last = [
            jnp.concatenate([last_high, last_low], axis=1),
            jnp.concatenate([last_high, jnp.zeros_like(last_high)], axis=1),
        ]
        two = dot(wide[:, : 2 * n], jnp.concatenate(last, axis=0), False)
        both = jnp.concatenate([one, two[:, :TILE] + two[:, TILE:]], axis=1)
        for number in range(4):
            rows = slice(number * n, (number + 1) * n)
            value = jnp.sum(stack[rows, :] * both[rows], axis=1, keepdims=True) * member[...]
            fold[number : number + 1, :] += jnp.sum(value, axis=0, keepdims=True)

    plain = fold[...]
    turned = pltpu.roll(plain, HALF, 1)
    rows = out.shape[0] - extra.shape[0]
    values = [plain[2 * i : 2 * i + 1, :] + turned[2 * i + 1 : 2 * i + 2, :] for i in range(2)]
    out[:rows, :] = weights[:rows, :] * values[0] + weights[rows:, :] * values[1]
    out[rows:, :] = extra[...]


def local_call(kernel, shapes, scratch, specs, name, limit, flops, *operands):
    spaces = {"v": pltpu.VMEM, "s": pltpu.SMEM, "h": pltpu.HBM}
    single = not isinstance(shapes, tuple)
    vmem = pl.BlockSpec(memory_space=pltpu.VMEM)
    return pl.pallas_call(
        kernel,
        out_shape=shapes,
        in_specs=[pl.BlockSpec(memory_space=spaces[spec]) for spec in specs],
        out_specs=vmem if single else (vmem,) * len(shapes),
        scratch_shapes=scratch,
        compiler_params=pltpu.CompilerParams(vmem_limit_bytes=limit * 2**20),
        cost_estimate=pl.CostEstimate(flops=flops, bytes_accessed=2**20, transcendentals=0),
        name=name,
    )(*operands)


def shifted_pair(x, axis):
    size = x.shape[axis]
    before, after = (pltpu.roll(x, 1, axis), pltpu.roll(x, size - 1, axis))
    if axis == x.ndim - 1:
        lanes = lax.broadcasted_iota(jnp.int32, x.shape, axis)
        before = jnp.where(lanes == 0, 0.0, before)
        after = jnp.where(lanes == size - 1, 0.0, after)
    return before, after


def neighbours(x):
    centre = x[1:-1]
    up, down = shifted_pair(centre, 1)
    left, right = shifted_pair(centre, 2)
    return (x[2:] + x[:-2]) + (up + down) + (left + right)


def differences(x):
    centre = x[1:-1]
    up, down = shifted_pair(centre, 1)
    left, right = shifted_pair(centre, 2)
    along = (x[2:] - centre) + (x[:-2] - centre)
    across = (up - centre) + (down - centre)
    deep = (left - centre) + (right - centre)
    return along + (across + deep)


def grid_mask(shape, margin, length, rows, place, devices, wire, wires):
    planes = lax.broadcasted_iota(jnp.int32, shape, 0)
    row = lax.broadcasted_iota(jnp.int32, shape, 1)
    low_x = jnp.where(place == 0, margin, 0)
    high_x = jnp.where(place == devices - 1, margin + length, shape[0])
    low_y = jnp.where(wire == 0, rows, 0)
    high_y = jnp.where(wire == wires - 1, 2 * rows, shape[1])
    inside = (planes >= low_x) & (planes < high_x) & (row >= low_y) & (row < high_y)
    return inside.astype(F32)


def three_parts(x):
    parts = []
    for _ in range(3):
        parts.append(x.astype(BF16))
        x = x - parts[-1].astype(F32)
    return parts


def coordinates(cell, rows_y, depth):
    z_part = cell - depth * jnp.floor(cell * (1.0 / depth))
    plane = jnp.floor(cell * (1.0 / depth))
    x_part = jnp.floor(plane * (1.0 / rows_y))
    return x_part, plane - rows_y * x_part, z_part


WALKS = ((0, 1),), ((1, 1),), ((0, 2), (2, 1)), ((1, 3), (3, 1)), ((0, 6), (2, 4), (4, 1)), ((1, 10), (3, 5), (5, 1))
FACTORIAL = (1.0, 1.0, 2.0, 6.0, 24.0, 120.0)


def walk_counts(here, there, length):
    apart = jnp.abs(here - there)
    low = here + there + 2.0
    high = 2.0 * length - here - there
    at = []
    for steps in range(6):
        value = (apart == steps).astype(F32)
        if steps >= 2:
            value = value - (low == steps).astype(F32) - (high == steps).astype(F32)
        at.append(value)
    counts = []
    for steps, terms in enumerate(WALKS):
        total = None
        for distance, count in terms:
            term = at[distance] * (count / FACTORIAL[steps])
            total = term if total is None else total + term
        counts.append(total)
    return counts


def convolved(left, right):
    result = []
    for steps in range(6):
        total = left[0] * right[steps]
        for part in range(1, steps + 1):
            total = total + left[part] * right[steps - part]
        result.append(total)
    return result


def moments_kernel(devices, wires, own, field, one_beside, two_beside, cells, out, wide_field, whole_field):
    place, wire = (lax.axis_index("slab"), lax.axis_index("energy"))
    planes, rows, depth = field.shape
    length = planes - 2 * REACH
    width_x = length // 2
    atoms = cells.shape[1]
    grid_y = rows * wires
    pairs = devices
    n = own.shape[1]
    even = lax.rem(wire, 2) == 0
    whole_field[...] = jnp.zeros_like(whole_field)
    whole_field[:, rows : 2 * rows, :] = field[...]
    for plane in range(planes):
        spot = slice(plane * REACH, (plane + 1) * REACH)
        one, two = (one_beside[spot, :], two_beside[spot, :])
        whole_field[plane, rows - REACH : rows, :] = jnp.where(even, two, one)
        whole_field[plane, 2 * rows : 2 * rows + REACH, :] = jnp.where(even, one, two)
    whole = (planes, 3 * rows, depth)
    mask = grid_mask(whole, REACH, length, rows, place, devices, wire, wires)
    source = jnp.where(mask > 0, whole_field[...], 0.0)
    margin = ITERS - 1
    wide_field[...] = source[REACH - margin : REACH + length + margin]

    def inner(x):
        extra = (x.shape[0] - length) // 2
        return x[extra : extra + length, rows : 2 * rows]

    chain = [source]
    for step in range(1, 6):
        chain.append(neighbours(chain[-1]) * mask[step : planes - step])
    blocks = [inner(x) for x in chain]
    near = source[2:-2]
    other = [near]
    for step in range(1, 4):
        other.append(differences(other[-1]) * mask[2 + step : planes - 2 - step])
    other = [inner(x) for x in other]
    lanes = lax.broadcasted_iota(jnp.int32, (1, depth), 1)
    sums = jnp.zeros((1, depth), F32)
    for base, fields in enumerate((blocks, other)):
        for steps in range(6):
            part = jnp.sum(fields[steps // 2] * fields[(steps + 1) // 2], axis=0)
            part = jnp.sum(jnp.sum(part, axis=1, keepdims=True), axis=0, keepdims=True)
            sums = jnp.where(lanes == atoms + 6 * base + steps, part, sums)
    out[...] = jnp.zeros_like(out)
    mine = own[2 * n + 8 : 2 * n + 16, :depth]
    mine = jnp.sum(mine, axis=0, keepdims=True)
    lane = lax.broadcasted_iota(jnp.int32, (1, depth), 1)
    odd = (lane >= HALF).astype(F32)
    used = lax.rem(lane, HALF) < atoms
    x_part, y_part, z_part = coordinates(mine, grid_y, depth)
    start = (wire * rows).astype(F32)
    ours = used & (y_part >= start) & (y_part < start + rows)
    at_row = jnp.where(ours, (x_part + width_x * odd) * rows + y_part - start, -1.0)
    cell_rows = length * rows
    row_iota = lax.broadcasted_iota(jnp.int32, (cell_rows, depth), 0).astype(F32)
    deep_iota = lax.broadcasted_iota(jnp.int32, (depth, depth), 0).astype(F32)
    at_rows = (row_iota == at_row).astype(F32)
    at_deep = (deep_iota == z_part).astype(BF16)
    for steps, block in enumerate(blocks):
        value = jnp.zeros((cell_rows, depth), F32)
        for part in three_parts(block.reshape(cell_rows, depth)):
            value = value + dot(part, at_deep, False)
        value = jnp.sum(value * at_rows, axis=0, keepdims=True)
        out[pl.ds(steps * pairs + place, 1), :] = value
    out[0:1, :] += sums


def atoms_kernel(
    devices,
    wires,
    length,
    charge_ref,
    orbital_atom,
    some_cells,
    other_cells,
    walks,
    row_hot,
    deep_hot,
    member,
    charges,
):
    place, wire = (lax.axis_index("slab"), lax.axis_index("energy"))
    rows, depth = some_cells.shape
    width_x = length // 2
    atoms = walks.shape[1] // (2 * devices)
    grid_y = rows * wires
    pairs = devices
    n = orbital_atom.shape[1]
    start = (wire * rows).astype(F32)
    for group in range(charges.shape[0] // pairs):
        charges[group * pairs : (group + 1) * pairs, :] = jnp.broadcast_to(
            charge_ref[:, group : group + 1], (pairs, depth)
        )
    cells = jnp.maximum(some_cells[...], other_cells[...])
    spots = lax.broadcasted_iota(jnp.int32, (TILE, n), 0) == orbital_atom[...]
    spots = spots.astype(F32)
    for first in range(0, n, TILE):
        member[first : first + TILE, :] = spots[:, first : first + TILE].T
    row_cells = cells
    row_x, row_y, row_z = coordinates(row_cells, grid_y, depth)
    padded = jnp.concatenate([row_cells, jnp.zeros((depth - 8, depth), F32)], axis=0)
    column_x, column_y, column_z = coordinates(padded.T, grid_y, depth)
    row_lane = lax.broadcasted_iota(jnp.int32, (8, depth), 1)
    next_x, next_y, next_z = [jnp.concatenate([v[1:], v[:1]], axis=0) for v in (row_x, row_y, row_z)]

    def turned(now, later, step_now, step_later):
        value = jnp.where(row_lane >= HALF, now + step_now, later + step_later)
        return pltpu.roll(value, HALF, 1)

    even_x = row_x + width_x * (row_lane >= HALF).astype(F32)
    odd_x, odd_y, odd_z = (
        turned(row_x, next_x, 0.0, float(width_x)),
        turned(row_y, next_y, 0.0, 0.0),
        turned(row_z, next_z, 0.0, 0.0),
    )
    for slab in range(2 * pairs):
        pair, side = (slab // 2, slab % 2)
        base = float(slab * width_x)
        if side:
            there = (odd_x, odd_y, odd_z)
        else:
            there = (even_x, row_y, row_z)
        there = [v[pair : pair + 1, :] for v in there]
        here = [
            v[side * HALF : side * HALF + atoms, pair : pair + 1]
            for v in (column_x, column_y, column_z)
        ]
        shape = (atoms, depth)
        sizes = (2 * pairs * width_x, grid_y, depth)
        axes = []
        for axis in range(3):
            shift = base if axis == 0 else 0.0
            axes.append(
                walk_counts(
                    jnp.broadcast_to(here[axis] + shift, shape),
                    jnp.broadcast_to(there[axis] + shift, shape),
                    float(sizes[axis]),
                )
            )
        total = convolved(convolved(axes[0], axes[1]), axes[2])
        for steps in range(6):
            walks[steps, slab * atoms : (slab + 1) * atoms, :] = total[steps] * FACTORIAL[steps]
    wide = length + 4
    first_x = (place * length - 2).astype(F32)
    first_y = start - rows
    count = wide * 3 * rows
    rows_iota = lax.broadcasted_iota(jnp.int32, (count, depth), 0).astype(F32)
    used_row = lax.rem(row_lane, HALF) < atoms
    for pair in range(pairs):
        x_at = even_x[pair : pair + 1, :] + float(2 * pair * width_x) - first_x
        y_at = row_y[pair : pair + 1, :] - first_y
        good = (x_at >= 0) & (x_at < wide) & (y_at >= 0) & (y_at < 3 * rows) & used_row[0:1, :]
        target = jnp.where(good, x_at * (3 * rows) + y_at, -1.0)
        row_hot[:, pair * depth : (pair + 1) * depth] = (rows_iota == target).astype(BF16)
        z_at = column_z[:, pair : pair + 1]
        lanes_z = lax.broadcasted_iota(jnp.int32, (depth, depth), 1).astype(F32)
        deep_hot[pair * depth : (pair + 1) * depth, :] = (lanes_z == z_at).astype(F32)


def total_of(x):
    return jnp.sum(jnp.sum(x, axis=1, keepdims=True), axis=0, keepdims=True)


def quadratic_form(poly, moments, shift):
    total = None
    for i, one in enumerate(poly):
        for j, two in enumerate(poly):
            if j < i:
                continue
            term = one * two * moments[i + j + shift] * (1.0 if i == j else 2.0)
            total = term if total is None else total + term
    return total


def finish_kernel(
    devices,
    wires,
    atoms,
    payload,
    walks,
    row_hot,
    deep_hot,
    charges,
    field,
    density,
    potential,
):
    place, wire = (lax.axis_index("slab"), lax.axis_index("energy"))
    length, rows, depth = potential.shape
    pairs = devices
    groups = density.shape[0]
    held = charges[...] * payload[: groups * pairs, :]
    charge = held[:pairs]
    for group in range(1, groups):
        charge = charge + held[group * pairs : (group + 1) * pairs]
    for group in range(groups):
        value = payload[pl.ds(group * pairs + place, 1), :]
        density[group, 0:1, :] = value[:, :atoms]
        density[group, 1:2, :] = pltpu.roll(value, HALF, 1)[:, :atoms]
    square = jnp.concatenate([charge, jnp.zeros((depth - pairs, depth), F32)], axis=0)
    columns = square.T
    later = jnp.concatenate([charge[1:], jnp.zeros((1, depth), F32)], axis=0)
    lanes = lax.broadcasted_iota(jnp.int32, (pairs, depth), 1)
    even_row = jnp.where(lanes >= HALF, 2.0 * charge, charge)
    odd_row = pltpu.roll(jnp.where(lanes >= HALF, charge, 2.0 * later), HALF, 1)
    totals = [None] * 6
    for slab in range(2 * pairs):
        pair, side = (slab // 2, slab % 2)
        row = (odd_row if side else even_row)[pair : pair + 1, :]
        column = columns[side * HALF : side * HALF + atoms, pair : pair + 1]
        outer = column * row
        for steps in range(6):
            term = walks[steps, slab * atoms : (slab + 1) * atoms, :] * outer
            totals[steps] = term if totals[steps] is None else totals[steps] + term
    base = groups * pairs
    crossed = []
    for steps in range(6):
        cross = 2.0 * charge * payload[base + steps * pairs : base + (steps + 1) * pairs, :]
        parts = [totals[steps][i : i + 8] for i in range(0, atoms, 8)]
        if pairs < 8:
            cross = jnp.concatenate([cross, jnp.zeros((8 - pairs, depth), F32)], axis=0)
        parts.append(cross)
        while len(parts) > 1:
            parts = [sum(parts[i : i + 2][1:], parts[i]) for i in range(0, len(parts), 2)]
        crossed.append(total_of(parts[0]))
    lane = lax.broadcasted_iota(jnp.int32, (1, depth), 1)
    row = payload[base : base + 1, :]
    sums = [
        jnp.sum(jnp.where(lane == atoms + i, row, 0.0), axis=1, keepdims=True) for i in range(12)
    ]
    plain = [sums[steps] + crossed[steps] for steps in range(6)]
    moved = []
    for steps in range(6):
        value = sums[6 + steps]
        binomial = 1
        for part in range(steps, -1, -1):
            value = value + (binomial * (-6.0) ** (steps - part)) * crossed[part]
            binomial = binomial * part // (steps - part + 1)
        moved.append(value)
    smooth = plain[1] > 3.5 * plain[0]
    level = jnp.where(smooth, 0.5, 6.5)
    moments = [jnp.where(smooth, two, one) for one, two in zip(plain, moved)]
    residual, direction = ([jnp.ones_like(level)], [jnp.ones_like(level)])
    norm = moments[0]
    alphas, betas = ([], [])
    for turn in range(ITERS):
        energy = level * quadratic_form(direction, moments, 0) - quadratic_form(direction, moments, 1)
        alpha = norm / energy
        alphas.append(alpha)
        if turn + 1 == ITERS:
            break
        longer = residual + [jnp.zeros_like(level)]
        for i, value in enumerate(direction):
            longer[i] = longer[i] - alpha * level * value
            longer[i + 1] = longer[i + 1] + alpha * value
        residual = longer
        following = quadratic_form(residual, moments, 0)
        beta = following / norm
        betas.append(beta)
        norm = following
        direction = [
            value + beta * direction[i] if i < len(direction) else value
            for i, value in enumerate(residual)
        ]
    pieces = [[], [], []]
    for pair in range(pairs):
        hot = deep_hot[pair * depth : (pair + 1) * depth, :]
        for place_in, piece in enumerate(three_parts(columns[:, pair : pair + 1] * hot)):
            pieces[place_in].append(piece)
    spread = jnp.concatenate([jnp.concatenate(piece, axis=0) for piece in pieces], axis=1)
    placed = dot(row_hot[...], spread, False)
    placed = placed[:, :depth] + (placed[:, depth : 2 * depth] + placed[:, 2 * depth :])
    margin = ITERS - 1
    wide = (length + 2 * margin, 3 * rows, depth)
    mask = grid_mask(wide, margin, length, rows, place, devices, wire, wires)
    source = field[...] + placed.reshape(wide)
    residual, direction = (source, source)
    total = alphas[0] * source[margin:-margin, rows : 2 * rows]
    for turn in range(ITERS - 1):
        image = 6.5 * direction[1:-1] - neighbours(direction)
        inner_mask = mask[turn + 1 : wide[0] - turn - 1]
        residual = (residual[1:-1] - alphas[turn] * image) * inner_mask
        direction = residual + betas[turn] * direction[1:-1]
        extra = margin - turn - 1
        block = direction[extra : extra + length, rows : 2 * rows]
        total = total + alphas[turn + 1] * block
    potential[...] = total


def hop(count, turn):
    moves = {i: i for i in range(count)}
    for core in range(2):
        here, there = (2 * turn - 2 + core, 2 * turn + core)
        moves[here], moves[there] = (there, here)
    return sorted(moves.items())


def pairs_of(count):
    return [(i, i ^ 1) for i in range(count)]


def total_over(value, axis, strides):
    size = 1
    for name in axis if isinstance(axis, tuple) else (axis,):
        size *= lax.axis_size(name)
    got = [lax.ppermute(value, axis, [(i, i ^ k) for i in range(size)]) for k in strides]
    if len(got) == 1:
        return value + got[0]
    return (value + got[0]) + (got[1] + got[2])


def total_over_all(value):
    wires, slabs = (lax.axis_size("energy"), lax.axis_size("slab"))
    value = total_over(value, "slab", (1,))
    stride = 2
    while stride * 2 < slabs:
        value = total_over(value, "slab", (stride,))
        stride *= 2
    value = total_over(value, BOTH, (stride, slabs, stride + slabs))
    stride = 2
    while stride * 4 <= wires:
        value = total_over(value, "energy", (stride, 2 * stride, 3 * stride))
        stride *= 4
    if stride < wires:
        value = total_over(value, "energy", (stride,))
    return value


def inner_pairs(count):
    return [(i, (i + 1) % count if i % 2 else (i - 1) % count) for i in range(count)]


def neighbour_turn(count):
    return [(i, (i + 1) % count if i % 2 else (i - 1) % count) for i in range(count)]


def on_device(
    green_iso,
    coupling,
    lead_green,
    energy_weight,
    energy_group,
    group_charge,
    orbital_atom,
    atom_cell,
    doping,
):
    devices, wires = (lax.axis_size("slab"), lax.axis_size("energy"))
    groups = group_charge.shape[0]
    atoms = atom_cell.shape[1]
    n = lead_green.shape[-1]
    length, rows, depth = doping.shape
    shape = jax.ShapeDtypeStruct
    orbital_row = orbital_atom.reshape(1, n)
    maps = shape((2 * n + 32, n), F32)
    edge_rows = REACH * rows + 8
    held = [
        pltpu.with_memory_space_constraint(x, pltpu.HBM)
        for x in (green_iso, coupling, lead_green, atom_cell, doping)
    ]
    matrix = shape((n, n), F32)
    two = shape((2, n, n), F32)
    sent_step, sent, edge, own_step, own_late, own_iso, own_lead = local_call(
        other_kernel,
        (matrix, maps, shape((edge_rows, depth), F32), matrix, matrix, two, matrix),
        [
            pltpu.VMEM((2, n, n), F32),
            pltpu.VMEM((2, n, n), F32),
            pltpu.VMEM((n, n), F32),
            pltpu.SemaphoreType.DMA((8,)),
            pltpu.VMEM((8, TILE), F32),
            pltpu.VMEM(atom_cell.shape, jnp.int32),
            pltpu.VMEM(doping.shape, F32),
            pltpu.SemaphoreType.DMA((2,)),
        ],
        "hhhhh",
        "other",
        28,
        48 * n**3,
        *held,
    )
    got = lax.ppermute(sent, "slab", pairs_of(devices))
    second = lax.ppermute(edge, "slab", neighbour_turn(devices))
    own = local_call(
        own_kernel,
        maps,
        [],
        "vvvvv",
        "own",
        24,
        2**31,
        edge,
        own_step,
        own_late,
        own_iso,
        own_lead,
    )
    side = shape((-(-REACH * (length + 2 * REACH) // 8) * 8, depth), F32)
    got_step = lax.ppermute(sent_step, "slab", pairs_of(devices))
    passed, stack, stack_parts, wide_block, cells, one_side, two_side = local_call(
        relay_kernel,
        (
            shape((PACKED_ROWS, TILE), F32),
            shape((4 * n, n), F32),
            shape((4 * n, 5 * n - 3 * TILE), BF16),
            shape((length + 2 * REACH, rows, depth), F32),
            shape((8, depth), F32),
            side,
            side,
        ),
        [],
        "vvvvvv",
        "relay",
        28,
        12 * n**3,
        own,
        got,
        own_step,
        got_step,
        doping,
        second,
    )
    packed = lax.ppermute(passed, "slab", hop(devices, 1))
    one_beside = lax.ppermute(one_side, "energy", pairs_of(wires))
    two_beside = lax.ppermute(two_side, "energy", inner_pairs(wires))
    other_cells = lax.ppermute(cells, "slab", pairs_of(devices))
    if devices > 4:
        other_cells = lax.psum(own[2 * n + 8 : 2 * n + 16, :depth], "slab")
    wide = (length + 2 * ITERS - 2, 3 * rows, depth)
    walks, row_hot, deep_hot, member, charges = local_call(
        functools.partial(atoms_kernel, devices, wires, length),
        (
            shape((6, 2 * devices * atoms, depth), F32),
            shape((wide[0] * wide[1], devices * depth), BF16),
            shape((devices * depth, depth), F32),
            shape((n, TILE), F32),
            shape((groups * devices, depth), F32),
        ),
        [],
        "vvvv",
        "atoms",
        28,
        2**29,
        group_charge.reshape(1, groups),
        orbital_row,
        cells,
        other_cells,
    )
    extra, wide_field = local_call(
        functools.partial(moments_kernel, devices, wires),
        (shape((6 * devices, depth), F32), shape(wide, F32)),
        [pltpu.VMEM((length + 2 * REACH, 3 * rows, depth), F32)],
        "vvvvv",
        "moments",
        20,
        2**26,
        own,
        wide_block,
        one_beside,
        two_beside,
        atom_cell,
    )
    known, weights = local_call(
        functools.partial(known_kernel, devices),
        (shape((8, TILE), F32), shape((2 * groups * devices, TILE), F32)),
        [],
        "vvvvvvvv",
        "known",
        24,
        2**28,
        energy_weight.reshape(1, -1),
        energy_group.reshape(1, -1),
        orbital_row,
        member,
        own,
        got,
        own_step,
        got_step,
    )
    for turn in range(1, devices // 2 - 1):
        passed = local_call(
            functools.partial(pass_kernel, turn),
            shape((PACKED_ROWS, TILE), F32),
            [pltpu.VMEM((n, n), F32)],
            "vvv",
            "pass_on",
            20,
            24 * n**3,
                packed,
            own,
            got,
        )
        arrived = lax.ppermute(passed, "slab", hop(devices, turn + 1))
        packed = jnp.where(lax.axis_index("slab") // 2 == turn + 1, arrived, packed)
    payload = local_call(
        functools.partial(density_kernel, devices),
        shape(((groups + 6) * devices, TILE), F32),
        [pltpu.VMEM((n, n), F32), pltpu.VMEM((8, TILE), F32)],
        "vvvvvvv",
        "density",
        20,
        24 * n**3,
        member,
        packed,
        stack,
        stack_parts,
        known,
        weights,
        extra,
    )
    payload = total_over_all(payload)
    return local_call(
        functools.partial(finish_kernel, devices, wires, atoms),
        (shape((groups, 2, atoms), F32), shape(doping.shape, F32)),
        [],
        "vvvvvv",
        "finish",
        28,
        2**29,
        payload,
        walks,
        row_hot,
        deep_hot,
        charges,
        wide_field,
    )


def solution(mesh):
    in_specs = (
        P("energy", "slab", None, None),
        P("slab", None, None),
        P("energy", None, None),
        P("energy"),
        P("energy"),
        P(),
        P(),
        P("slab", None),
        P("slab", "energy", None),
    )
    out_specs = (P(None, "slab", None), P("slab", "energy", None))
    return jax.shard_map(
        on_device, mesh=mesh, in_specs=in_specs, out_specs=out_specs, check_vma=False
    )
```

```python
import functools

import jax
import jax.numpy as jnp
from jax import lax
from jax.experimental import pallas as pl
from jax.experimental.pallas import tpu as pltpu
from jax.sharding import PartitionSpec as P

ITERS = 3
F32 = jnp.float32
BF16 = jnp.bfloat16
TILE = 128
BOTH = ("energy", "slab")
REACH = 5
HALF = 64


def split(a):
    high = a.astype(BF16)
    return high, (a - high.astype(F32)).astype(BF16)


def dot(a, b, transposed):
    dims = (((1,), (1 if transposed else 0,)), ((), ()))
    return lax.dot_general(a, b, dims, preferred_element_type=F32)


def product(left, right, transposed=False):
    n = right[0].shape[0 if transposed else 1]
    wide = dot(left[0], jnp.concatenate(right, 0 if transposed else 1), transposed)
    return wide[:, :n] + (wide[:, n:] + dot(left[1], right[0], transposed))


def joined(left):
    return jnp.concatenate([left[0], left[1], left[0]], axis=1)


def product_joined(wide, right, transposed=False):
    high, low = right
    axis = 0 if transposed else 1
    n = high.shape[axis]
    cut = n - TILE

    def part(x, start, stop):
        return lax.slice_in_dim(x, start, stop, axis=axis)

    first = [part(x, 0, cut) for x in (high, high, low)]
    last_high, last_low = (part(high, cut, n), part(low, cut, n))
    last = [
        jnp.concatenate([last_high, last_low], axis),
        jnp.concatenate([last_high, jnp.zeros_like(last_high)], axis),
    ]
    one = dot(wide, jnp.concatenate(first, 1 - axis), transposed)
    two = dot(wide[:, : 2 * high.shape[1 - axis]], jnp.concatenate(last, 1 - axis), transposed)
    return jnp.concatenate([one, two[:, :TILE] + two[:, TILE:]], axis=1)


def diagonal_row(matrix):
    rows = lax.broadcasted_iota(jnp.int32, (TILE, TILE), 0)
    columns = lax.broadcasted_iota(jnp.int32, (TILE, TILE), 1)
    parts = []
    for start in range(0, matrix.shape[0], TILE):
        block = matrix[start : start + TILE, start : start + TILE]
        parts.append(jnp.sum(jnp.where(rows == columns, block, 0.0), axis=0, keepdims=True))
    return jnp.concatenate(parts, axis=1)


SMALL = TILE // 2
PACKED_ROWS = 4 * TILE + SMALL + 8


def pack(matrix, out):
    def block(i, j):
        return matrix[i * TILE : (i + 1) * TILE, j * TILE : (j + 1) * TILE]

    rows = lax.broadcasted_iota(jnp.int32, (TILE, TILE), 0)
    columns = lax.broadcasted_iota(jnp.int32, (TILE, TILE), 1)
    for place, (i, j) in enumerate(((0, 1), (0, 2), (1, 2))):
        out[place * TILE : (place + 1) * TILE, :] = block(i, j) + block(j, i).T
    one, two, three = (block(i, i) for i in range(3))
    merged = jnp.where(rows < columns, one + one.T, jnp.where(rows > columns, two + two.T, one))
    out[3 * TILE : 4 * TILE, :] = merged
    whole = jnp.where(rows == columns, three, three + three.T)
    turned = pltpu.roll(whole[SMALL:], SMALL, 1)
    low = (rows > columns)[:SMALL]
    out[4 * TILE : 4 * TILE + SMALL, :] = jnp.where(low, turned, whole[:SMALL])
    row = jnp.sum(jnp.where(rows == columns, two, 0.0), axis=0, keepdims=True)
    last = jnp.sum(jnp.where(rows == columns, three, 0.0), axis=0, keepdims=True)
    first = lax.broadcasted_iota(jnp.int32, (8, TILE), 0) == 0
    out[4 * TILE + SMALL :, :] = jnp.where(first, row, last)


def unpack(packed, out):
    rows = lax.broadcasted_iota(jnp.int32, (TILE, TILE), 0)
    columns = lax.broadcasted_iota(jnp.int32, (TILE, TILE), 1)
    out[...] = jnp.zeros_like(out)
    for place, (i, j) in enumerate(((0, 1), (0, 2), (1, 2))):
        value = packed[place * TILE : (place + 1) * TILE, :]
        out[i * TILE : (i + 1) * TILE, j * TILE : (j + 1) * TILE] = value
    merged = packed[3 * TILE : 4 * TILE, :]
    start = 4 * TILE + SMALL
    row, last = (packed[start : start + 1, :], packed[start + 1 : start + 2, :])
    out[:TILE, :TILE] = jnp.where(rows <= columns, merged, 0.0)
    out[TILE : 2 * TILE, TILE : 2 * TILE] = jnp.where(
        rows > columns, merged, jnp.where(rows == columns, row, 0.0)
    )
    half = packed[4 * TILE : start, :]
    out[2 * TILE : 2 * TILE + SMALL, 2 * TILE :] = jnp.where((rows <= columns)[:SMALL], half, 0.0)
    turned = pltpu.roll(half, SMALL, 1)
    inside = (columns >= SMALL) & (rows > columns)
    value = jnp.where(rows[SMALL:] == columns[SMALL:], last, 0.0)
    out[2 * TILE + SMALL :, 2 * TILE :] = jnp.where(inside[SMALL:], turned, value)


def plane_rows(n, plane):
    start = 2 * n + 16 + 8 * (plane // 3)
    return slice(start, start + 8)


def plane_lanes(plane):
    return slice((plane % 3) * TILE, (plane % 3 + 1) * TILE)


def copy_all(pairs, sems):
    copies = [pltpu.make_async_copy(src, dst, sems.at[i]) for i, (src, dst) in enumerate(pairs)]
    for copy in copies:
        copy.start()
    return copies


def slabs(early, late, isos, lead, maps, step):
    place = lax.axis_index("slab")
    n = early.shape[0]

    @pl.when(place == 0)
    def _():
        state = lead[...]
        for slab, value in enumerate((early, late)):
            parts = split(value)
            state = product(parts, split(state))
            state = product(split(state), parts, True) + isos[slab]
            maps[2 * n + slab : 2 * n + slab + 1, :] = diagonal_row(state)
        maps[n : 2 * n, :] = state

    @pl.when(place != 0)
    def _():
        later = split(late)
        wide = joined(later)
        term = product_joined(wide, split(isos[0]))
        maps[0:n, :] = product_joined(wide, split(early))
        term = product(split(term), later, True) + isos[1]
        maps[n : 2 * n, :] = term
        maps[2 * n : 2 * n + 1, :] = diagonal_row(isos[0])
        maps[2 * n + 1 : 2 * n + 2, :] = diagonal_row(term)
        if step is not None:
            step[...] = early


def other_kernel(
    iso,
    coupling,
    lead,
    cells_in,
    field_in,
    step,
    sent,
    planes,
    own_early,
    own_late,
    own_iso,
    own_lead,
    c_buf,
    g_buf,
    lead_buf,
    sems,
    row,
    cells,
    field,
    more_sems,
):
    place = lax.axis_index("slab")
    core = lax.rem(place, 2)
    n = lead_buf.shape[1]
    sources = []
    for slab in range(2):
        sources.append((coupling.at[slab], c_buf.at[slab]))
        sources.append((iso.at[1 - core, slab], g_buf.at[slab]))
        sources.append((iso.at[core, slab], own_iso.at[slab]))
    sources.append((lead.at[1 - core], lead_buf))
    sources.append((lead.at[core], own_lead))
    waits = copy_all(sources, sems)
    copies = copy_all([(cells_in, cells), (field_in, field)], more_sems)
    steps = []
    for slab in range(2):
        for copy in waits[3 * slab : 3 * slab + 3]:
            copy.wait()
        parts = split(c_buf[slab])
        for buf in (g_buf, own_iso):
            steps.append(product_joined(joined(split(buf[slab])), parts))
    waits[6].wait()
    own_early[...] = steps[1]
    own_late[...] = steps[3]
    slabs(steps[0], steps[2], g_buf, lead_buf, sent, step)
    waits[7].wait()
    for copy in copies:
        copy.wait()
    atoms = cells.shape[1]
    row[...] = jnp.zeros_like(row)
    row[0:1, 0:atoms] = cells[0:1, :].astype(F32)
    row[0:1, HALF : HALF + atoms] = cells[1:2, :].astype(F32)
    rows = lax.broadcasted_iota(jnp.int32, (8, TILE), 0)
    mine = jnp.where(rows == place, row[0:1, :], 0.0)
    sent[2 * n + 8 : 2 * n + 16, 0:TILE] = mine
    planes[REACH * 8 :, :] = mine
    length = field.shape[0]
    even = core == 0
    for plane in range(REACH):
        low, high = (field[plane], field[length - REACH + plane])
        planes[plane * 8 : plane * 8 + 8, :] = jnp.where(even, low, high)
        sent[plane_rows(n, plane), plane_lanes(plane)] = jnp.where(even, high, low)


def own_kernel(planes, early, late, isos, lead, own):
    n = lead.shape[0]
    own[2 * n + 8 : 2 * n + 16, 0:TILE] = planes[REACH * 8 :, :]
    slabs(early[...], late[...], isos, lead, own, None)


def advance(map_ref, state):
    n = map_ref.shape[1]
    composed = split(map_ref[0:n, :])
    term = product(composed, split(state))
    return product(split(term), composed, True) + map_ref[n : 2 * n, :]


def near_far(mine, other):
    core = lax.rem(lax.axis_index("slab"), 2)
    return jnp.where(core == 0, mine, other), jnp.where(core == 0, other, mine)


def relay_kernel(
    own, got, own_step, got_step, field, second, out, stack, parts, wide, cells, one_side, two_side
):
    place, wire = (lax.axis_index("slab"), lax.axis_index("energy"))
    n = own.shape[1]
    length, height, _ = field.shape
    even = lax.rem(place, 2) == 0
    wide[REACH : REACH + length] = field[...]
    for plane in range(REACH):
        one = got[plane_rows(n, plane), plane_lanes(plane)]
        two = second[plane * 8 : plane * 8 + 8, :]
        wide[plane] = jnp.where(even, two, one)
        wide[REACH + length + plane] = jnp.where(even, one, two)
    spot = slice(2 * n + 8, 2 * n + 16)
    cells[...] = own[spot, :TILE] + got[spot, :TILE] + second[REACH * 8 :, :]
    even = lax.rem(wire, 2) == 0
    for plane in range(length + 2 * REACH):
        low, high = (wide[plane, :REACH, :], wide[plane, height - REACH :, :])
        spot = slice(plane * REACH, (plane + 1) * REACH)
        one_side[spot, :] = jnp.where(even, high, low)
        two_side[spot, :] = jnp.where(even, low, high)

    @pl.when(place == 0)
    def _():
        pack(advance(got, own[n : 2 * n, :]), out)

    @pl.when(place == 1)
    def _():
        pack(advance(own, got[n : 2 * n, :]), out)

    @pl.when(place >= 2)
    def _():
        near_step, far_step = near_far(own_step[...], got_step[...])
        near_map, far_map = near_far(own[0:n, :], got[0:n, :])
        far = jnp.concatenate([far_step, far_map], axis=0)
        both = product_joined(joined(split(far)), split(near_map))
        for number, value in enumerate((near_step, near_map, both[:n], both[n:])):
            rows = slice(number * n, (number + 1) * n)
            stack[rows, :] = value
            high, low = split(value)
            parts[rows, :] = jnp.concatenate(
                [high, low, high[:, : n - TILE], low[:, : n - TILE], high[:, : n - TILE]], axis=1
            )


def pass_kernel(turn, packed, own, got, out, state):
    place = lax.axis_index("slab")
    for core, (near, far) in enumerate(((own, got), (got, own))):

        @pl.when(place == 2 * turn + core)
        def _():
            unpack(packed, state)
            state[...] = advance(near, state[...])
            pack(advance(far, state[...]), out)


def known_kernel(
    pairs, weight_ref, group_ref, orbital_atom, member, own, got, own_step, got_step, fold, weights
):
    place = lax.axis_index("slab")
    core = lax.rem(place, 2)
    pair_rows = lax.broadcasted_iota(jnp.int32, (pairs, TILE), 0)
    mine_weight = jnp.where(core == 0, weight_ref[:, 0:1], weight_ref[:, 1:2])
    mine_group = jnp.where(core == 0, group_ref[:, 0:1], group_ref[:, 1:2])
    groups = weights.shape[0] // (2 * pairs)
    for half in range(2):
        for group in range(groups):
            weight = jnp.where(mine_group == group, mine_weight, 0.0)
            start = (half * groups + group) * pairs
            weights[start : start + pairs, :] = jnp.where(
                pair_rows == place - core + half, jnp.broadcast_to(weight, (pairs, TILE)), 0.0
            )
    n = own.shape[1]
    atoms = lax.broadcasted_iota(jnp.int32, (TILE, n), 0)
    spots = (atoms == orbital_atom[...]).astype(BF16)
    _, far_step = near_far(own_step[...], got_step[...])
    _, far_map = near_far(own[0:n, :], got[0:n, :])
    near_source, _ = near_far(own[n : 2 * n, :], got[n : 2 * n, :])
    far = jnp.concatenate([far_step, far_map], axis=0)
    both = product_joined(joined(split(far)), split(near_source))
    near_rows, far_rows = near_far(own[2 * n : 2 * n + 2, :], got[2 * n : 2 * n + 2, :])
    rest = jnp.concatenate([near_rows, far_rows, jnp.zeros((4, n), F32)], axis=0)
    total = jnp.zeros((8, TILE), F32)
    for _ in range(3):
        piece = rest.astype(BF16)
        total = total + dot(piece, spots, True)
        rest = rest - piece.astype(F32)
    fold[...] = total
    for number in range(2):
        rows = slice(number * n, (number + 1) * n)
        value = jnp.sum(far[rows] * both[rows], axis=1, keepdims=True) * member[...]
        fold[2 + number : 3 + number, :] += jnp.sum(value, axis=0, keepdims=True)


def density_kernel(
    pairs,
    member,
    packed,
    stack,
    wide,
    known,
    weights,
    extra,
    out,
    state,
    fold,
):
    place = lax.axis_index("slab")
    n = state.shape[0]
    fold[...] = known[...]

    @pl.when(place >= 2)
    def _():
        unpack(packed, state)
        high, low = split(state[...])
        cut = n - TILE
        corner = [x[:cut, :cut] for x in (high, high, low)]
        one = dot(wide[:, 2 * n :], jnp.concatenate(corner, axis=0), False)
        last_high, last_low = (high[:, cut:], low[:, cut:])
        last = [
            jnp.concatenate([last_high, last_low], axis=1),
            jnp.concatenate([last_high, jnp.zeros_like(last_high)], axis=1),
        ]
        two = dot(wide[:, : 2 * n], jnp.concatenate(last, axis=0), False)
        both = jnp.concatenate([one, two[:, :TILE] + two[:, TILE:]], axis=1)
        for number in range(4):
            rows = slice(number * n, (number + 1) * n)
            value = jnp.sum(stack[rows, :] * both[rows], axis=1, keepdims=True) * member[...]
            fold[number : number + 1, :] += jnp.sum(value, axis=0, keepdims=True)

    plain = fold[...]
    turned = pltpu.roll(plain, HALF, 1)
    rows = out.shape[0] - extra.shape[0]
    values = [plain[2 * i : 2 * i + 1, :] + turned[2 * i + 1 : 2 * i + 2, :] for i in range(2)]
    out[:rows, :] = weights[:rows, :] * values[0] + weights[rows:, :] * values[1]
    out[rows:, :] = extra[...]


def local_call(kernel, shapes, scratch, specs, name, limit, flops, *operands):
    spaces = {"v": pltpu.VMEM, "s": pltpu.SMEM, "h": pltpu.HBM}
    single = not isinstance(shapes, tuple)
    vmem = pl.BlockSpec(memory_space=pltpu.VMEM)
    return pl.pallas_call(
        kernel,
        out_shape=shapes,
        in_specs=[pl.BlockSpec(memory_space=spaces[spec]) for spec in specs],
        out_specs=vmem if single else (vmem,) * len(shapes),
        scratch_shapes=scratch,
        compiler_params=pltpu.CompilerParams(vmem_limit_bytes=limit * 2**20),
        cost_estimate=pl.CostEstimate(flops=flops, bytes_accessed=2**20, transcendentals=0),
        name=name,
    )(*operands)


def shifted_pair(x, axis):
    size = x.shape[axis]
    before, after = (pltpu.roll(x, 1, axis), pltpu.roll(x, size - 1, axis))
    if axis == x.ndim - 1:
        lanes = lax.broadcasted_iota(jnp.int32, x.shape, axis)
        before = jnp.where(lanes == 0, 0.0, before)
        after = jnp.where(lanes == size - 1, 0.0, after)
    return before, after


def neighbours(x):
    centre = x[1:-1]
    up, down = shifted_pair(centre, 1)
    left, right = shifted_pair(centre, 2)
    return (x[2:] + x[:-2]) + (up + down) + (left + right)


def differences(x):
    centre = x[1:-1]
    up, down = shifted_pair(centre, 1)
    left, right = shifted_pair(centre, 2)
    along = (x[2:] - centre) + (x[:-2] - centre)
    across = (up - centre) + (down - centre)
    deep = (left - centre) + (right - centre)
    return along + (across + deep)


def grid_mask(shape, margin, length, rows, place, devices, wire, wires):
    planes = lax.broadcasted_iota(jnp.int32, shape, 0)
    row = lax.broadcasted_iota(jnp.int32, shape, 1)
    low_x = jnp.where(place == 0, margin, 0)
    high_x = jnp.where(place == devices - 1, margin + length, shape[0])
    low_y = jnp.where(wire == 0, rows, 0)
    high_y = jnp.where(wire == wires - 1, 2 * rows, shape[1])
    inside = (planes >= low_x) & (planes < high_x) & (row >= low_y) & (row < high_y)
    return inside.astype(F32)


def three_parts(x):
    parts = []
    for _ in range(3):
        parts.append(x.astype(BF16))
        x = x - parts[-1].astype(F32)
    return parts


def coordinates(cell, rows_y, depth):
    z_part = cell - depth * jnp.floor(cell * (1.0 / depth))
    plane = jnp.floor(cell * (1.0 / depth))
    x_part = jnp.floor(plane * (1.0 / rows_y))
    return x_part, plane - rows_y * x_part, z_part


WALKS = ((0, 1),), ((1, 1),), ((0, 2), (2, 1)), ((1, 3), (3, 1)), ((0, 6), (2, 4), (4, 1)), ((1, 10), (3, 5), (5, 1))
FACTORIAL = (1.0, 1.0, 2.0, 6.0, 24.0, 120.0)


def walk_counts(here, there, length):
    apart = jnp.abs(here - there)
    low = here + there + 2.0
    high = 2.0 * length - here - there
    at = []
    for steps in range(6):
        value = (apart == steps).astype(F32)
        if steps >= 2:
            value = value - (low == steps).astype(F32) - (high == steps).astype(F32)
        at.append(value)
    counts = []
    for steps, terms in enumerate(WALKS):
        total = None
        for distance, count in terms:
            term = at[distance] * (count / FACTORIAL[steps])
            total = term if total is None else total + term
        counts.append(total)
    return counts


def convolved(left, right):
    result = []
    for steps in range(6):
        total = left[0] * right[steps]
        for part in range(1, steps + 1):
            total = total + left[part] * right[steps - part]
        result.append(total)
    return result


def moments_kernel(devices, wires, own, field, one_beside, two_beside, cells, out, wide_field, whole_field):
    place, wire = (lax.axis_index("slab"), lax.axis_index("energy"))
    planes, rows, depth = field.shape
    length = planes - 2 * REACH
    width_x = length // 2
    atoms = cells.shape[1]
    grid_y = rows * wires
    pairs = devices
    n = own.shape[1]
    even = lax.rem(wire, 2) == 0
    whole_field[...] = jnp.zeros_like(whole_field)
    whole_field[:, rows : 2 * rows, :] = field[...]
    for plane in range(planes):
        spot = slice(plane * REACH, (plane + 1) * REACH)
        one, two = (one_beside[spot, :], two_beside[spot, :])
        whole_field[plane, rows - REACH : rows, :] = jnp.where(even, two, one)
        whole_field[plane, 2 * rows : 2 * rows + REACH, :] = jnp.where(even, one, two)
    whole = (planes, 3 * rows, depth)
    mask = grid_mask(whole, REACH, length, rows, place, devices, wire, wires)
    source = jnp.where(mask > 0, whole_field[...], 0.0)
    margin = ITERS - 1
    wide_field[...] = source[REACH - margin : REACH + length + margin]

    def inner(x):
        extra = (x.shape[0] - length) // 2
        return x[extra : extra + length, rows : 2 * rows]

    chain = [source]
    for step in range(1, 6):
        chain.append(neighbours(chain[-1]) * mask[step : planes - step])
    blocks = [inner(x) for x in chain]
    near = source[2:-2]
    other = [near]
    for step in range(1, 4):
        other.append(differences(other[-1]) * mask[2 + step : planes - 2 - step])
    other = [inner(x) for x in other]
    lanes = lax.broadcasted_iota(jnp.int32, (1, depth), 1)
    sums = jnp.zeros((1, depth), F32)
    for base, fields in enumerate((blocks, other)):
        for steps in range(6):
            part = jnp.sum(fields[steps // 2] * fields[(steps + 1) // 2], axis=0)
            part = jnp.sum(jnp.sum(part, axis=1, keepdims=True), axis=0, keepdims=True)
            sums = jnp.where(lanes == atoms + 6 * base + steps, part, sums)
    out[...] = jnp.zeros_like(out)
    mine = own[2 * n + 8 : 2 * n + 16, :depth]
    mine = jnp.sum(mine, axis=0, keepdims=True)
    lane = lax.broadcasted_iota(jnp.int32, (1, depth), 1)
    odd = (lane >= HALF).astype(F32)
    used = lax.rem(lane, HALF) < atoms
    x_part, y_part, z_part = coordinates(mine, grid_y, depth)
    start = (wire * rows).astype(F32)
    ours = used & (y_part >= start) & (y_part < start + rows)
    at_row = jnp.where(ours, (x_part + width_x * odd) * rows + y_part - start, -1.0)
    cell_rows = length * rows
    row_iota = lax.broadcasted_iota(jnp.int32, (cell_rows, depth), 0).astype(F32)
    deep_iota = lax.broadcasted_iota(jnp.int32, (depth, depth), 0).astype(F32)
    at_rows = (row_iota == at_row).astype(F32)
    at_deep = (deep_iota == z_part).astype(BF16)
    for steps, block in enumerate(blocks):
        value = jnp.zeros((cell_rows, depth), F32)
        for part in three_parts(block.reshape(cell_rows, depth)):
            value = value + dot(part, at_deep, False)
        value = jnp.sum(value * at_rows, axis=0, keepdims=True)
        out[pl.ds(steps * pairs + place, 1), :] = value
    out[0:1, :] += sums


def atoms_kernel(
    devices,
    wires,
    length,
    charge_ref,
    orbital_atom,
    some_cells,
    other_cells,
    walks,
    row_hot,
    deep_hot,
    member,
    charges,
):
    place, wire = (lax.axis_index("slab"), lax.axis_index("energy"))
    rows, depth = some_cells.shape
    width_x = length // 2
    atoms = walks.shape[1] // (2 * devices)
    grid_y = rows * wires
    pairs = devices
    n = orbital_atom.shape[1]
    start = (wire * rows).astype(F32)
    for group in range(charges.shape[0] // pairs):
        charges[group * pairs : (group + 1) * pairs, :] = jnp.broadcast_to(
            charge_ref[:, group : group + 1], (pairs, depth)
        )
    cells = jnp.maximum(some_cells[...], other_cells[...])
    spots = lax.broadcasted_iota(jnp.int32, (TILE, n), 0) == orbital_atom[...]
    spots = spots.astype(F32)
    for first in range(0, n, TILE):
        member[first : first + TILE, :] = spots[:, first : first + TILE].T
    row_cells = cells
    row_x, row_y, row_z = coordinates(row_cells, grid_y, depth)
    padded = jnp.concatenate([row_cells, jnp.zeros((depth - 8, depth), F32)], axis=0)
    column_x, column_y, column_z = coordinates(padded.T, grid_y, depth)
    row_lane = lax.broadcasted_iota(jnp.int32, (8, depth), 1)
    next_x, next_y, next_z = [jnp.concatenate([v[1:], v[:1]], axis=0) for v in (row_x, row_y, row_z)]

    def turned(now, later, step_now, step_later):
        value = jnp.where(row_lane >= HALF, now + step_now, later + step_later)
        return pltpu.roll(value, HALF, 1)

    even_x = row_x + width_x * (row_lane >= HALF).astype(F32)
    odd_x, odd_y, odd_z = (
        turned(row_x, next_x, 0.0, float(width_x)),
        turned(row_y, next_y, 0.0, 0.0),
        turned(row_z, next_z, 0.0, 0.0),
    )
    for slab in range(2 * pairs):
        pair, side = (slab // 2, slab % 2)
        base = float(slab * width_x)
        if side:
            there = (odd_x, odd_y, odd_z)
        else:
            there = (even_x, row_y, row_z)
        there = [v[pair : pair + 1, :] for v in there]
        here = [
            v[side * HALF : side * HALF + atoms, pair : pair + 1]
            for v in (column_x, column_y, column_z)
        ]
        shape = (atoms, depth)
        sizes = (2 * pairs * width_x, grid_y, depth)
        axes = []
        for axis in range(3):
            shift = base if axis == 0 else 0.0
            axes.append(
                walk_counts(
                    jnp.broadcast_to(here[axis] + shift, shape),
                    jnp.broadcast_to(there[axis] + shift, shape),
                    float(sizes[axis]),
                )
            )
        total = convolved(convolved(axes[0], axes[1]), axes[2])
        for steps in range(6):
            walks[steps, slab * atoms : (slab + 1) * atoms, :] = total[steps] * FACTORIAL[steps]
    wide = length + 4
    first_x = (place * length - 2).astype(F32)
    first_y = start - rows
    count = wide * 3 * rows
    rows_iota = lax.broadcasted_iota(jnp.int32, (count, depth), 0).astype(F32)
    used_row = lax.rem(row_lane, HALF) < atoms
    for pair in range(pairs):
        x_at = even_x[pair : pair + 1, :] + float(2 * pair * width_x) - first_x
        y_at = row_y[pair : pair + 1, :] - first_y
        good = (x_at >= 0) & (x_at < wide) & (y_at >= 0) & (y_at < 3 * rows) & used_row[0:1, :]
        target = jnp.where(good, x_at * (3 * rows) + y_at, -1.0)
        row_hot[:, pair * depth : (pair + 1) * depth] = (rows_iota == target).astype(BF16)
        z_at = column_z[:, pair : pair + 1]
        lanes_z = lax.broadcasted_iota(jnp.int32, (depth, depth), 1).astype(F32)
        deep_hot[pair * depth : (pair + 1) * depth, :] = (lanes_z == z_at).astype(F32)


def total_of(x):
    return jnp.sum(jnp.sum(x, axis=1, keepdims=True), axis=0, keepdims=True)


def quadratic_form(poly, moments, shift):
    total = None
    for i, one in enumerate(poly):
        for j, two in enumerate(poly):
            if j < i:
                continue
            term = one * two * moments[i + j + shift] * (1.0 if i == j else 2.0)
            total = term if total is None else total + term
    return total


def finish_kernel(
    devices,
    wires,
    atoms,
    payload,
    walks,
    row_hot,
    deep_hot,
    charges,
    field,
    density,
    potential,
):
    place, wire = (lax.axis_index("slab"), lax.axis_index("energy"))
    length, rows, depth = potential.shape
    pairs = devices
    groups = density.shape[0]
    held = charges[...] * payload[: groups * pairs, :]
    charge = held[:pairs]
    for group in range(1, groups):
        charge = charge + held[group * pairs : (group + 1) * pairs]
    for group in range(groups):
        value = payload[pl.ds(group * pairs + place, 1), :]
        density[group, 0:1, :] = value[:, :atoms]
        density[group, 1:2, :] = pltpu.roll(value, HALF, 1)[:, :atoms]
    square = jnp.concatenate([charge, jnp.zeros((depth - pairs, depth), F32)], axis=0)
    columns = square.T
    later = jnp.concatenate([charge[1:], jnp.zeros((1, depth), F32)], axis=0)
    lanes = lax.broadcasted_iota(jnp.int32, (pairs, depth), 1)
    even_row = jnp.where(lanes >= HALF, 2.0 * charge, charge)
    odd_row = pltpu.roll(jnp.where(lanes >= HALF, charge, 2.0 * later), HALF, 1)
    totals = [None] * 6
    for slab in range(2 * pairs):
        pair, side = (slab // 2, slab % 2)
        row = (odd_row if side else even_row)[pair : pair + 1, :]
        column = columns[side * HALF : side * HALF + atoms, pair : pair + 1]
        outer = column * row
        for steps in range(6):
            term = walks[steps, slab * atoms : (slab + 1) * atoms, :] * outer
            totals[steps] = term if totals[steps] is None else totals[steps] + term
    base = groups * pairs
    crossed = []
    for steps in range(6):
        cross = 2.0 * charge * payload[base + steps * pairs : base + (steps + 1) * pairs, :]
        parts = [totals[steps][i : i + 8] for i in range(0, atoms, 8)]
        if pairs < 8:
            cross = jnp.concatenate([cross, jnp.zeros((8 - pairs, depth), F32)], axis=0)
        parts.append(cross)
        while len(parts) > 1:
            parts = [sum(parts[i : i + 2][1:], parts[i]) for i in range(0, len(parts), 2)]
        crossed.append(total_of(parts[0]))
    lane = lax.broadcasted_iota(jnp.int32, (1, depth), 1)
    row = payload[base : base + 1, :]
    sums = [
        jnp.sum(jnp.where(lane == atoms + i, row, 0.0), axis=1, keepdims=True) for i in range(12)
    ]
    plain = [sums[steps] + crossed[steps] for steps in range(6)]
    moved = []
    for steps in range(6):
        value = sums[6 + steps]
        binomial = 1
        for part in range(steps, -1, -1):
            value = value + (binomial * (-6.0) ** (steps - part)) * crossed[part]
            binomial = binomial * part // (steps - part + 1)
        moved.append(value)
    smooth = plain[1] > 3.5 * plain[0]
    level = jnp.where(smooth, 0.5, 6.5)
    moments = [jnp.where(smooth, two, one) for one, two in zip(plain, moved)]
    residual, direction = ([jnp.ones_like(level)], [jnp.ones_like(level)])
    norm = moments[0]
    alphas, betas = ([], [])
    for turn in range(ITERS):
        energy = level * quadratic_form(direction, moments, 0) - quadratic_form(direction, moments, 1)
        alpha = norm / energy
        alphas.append(alpha)
        if turn + 1 == ITERS:
            break
        longer = residual + [jnp.zeros_like(level)]
        for i, value in enumerate(direction):
            longer[i] = longer[i] - alpha * level * value
            longer[i + 1] = longer[i + 1] + alpha * value
        residual = longer
        following = quadratic_form(residual, moments, 0)
        beta = following / norm
        betas.append(beta)
        norm = following
        direction = [
            value + beta * direction[i] if i < len(direction) else value
            for i, value in enumerate(residual)
        ]
    pieces = [[], [], []]
    for pair in range(pairs):
        hot = deep_hot[pair * depth : (pair + 1) * depth, :]
        for place_in, piece in enumerate(three_parts(columns[:, pair : pair + 1] * hot)):
            pieces[place_in].append(piece)
    spread = jnp.concatenate([jnp.concatenate(piece, axis=0) for piece in pieces], axis=1)
    placed = dot(row_hot[...], spread, False)
    placed = placed[:, :depth] + (placed[:, depth : 2 * depth] + placed[:, 2 * depth :])
    margin = ITERS - 1
    wide = (length + 2 * margin, 3 * rows, depth)
    mask = grid_mask(wide, margin, length, rows, place, devices, wire, wires)
    source = field[...] + placed.reshape(wide)
    residual, direction = (source, source)
    total = alphas[0] * source[margin:-margin, rows : 2 * rows]
    for turn in range(ITERS - 1):
        image = 6.5 * direction[1:-1] - neighbours(direction)
        inner_mask = mask[turn + 1 : wide[0] - turn - 1]
        residual = (residual[1:-1] - alphas[turn] * image) * inner_mask
        direction = residual + betas[turn] * direction[1:-1]
        extra = margin - turn - 1
        block = direction[extra : extra + length, rows : 2 * rows]
        total = total + alphas[turn + 1] * block
    potential[...] = total


def hop(count, turn):
    moves = {i: i for i in range(count)}
    for core in range(2):
        here, there = (2 * turn - 2 + core, 2 * turn + core)
        moves[here], moves[there] = (there, here)
    return sorted(moves.items())


def pairs_of(count):
    return [(i, i ^ 1) for i in range(count)]


def total_over(value, axis, strides):
    size = 1
    for name in axis if isinstance(axis, tuple) else (axis,):
        size *= lax.axis_size(name)
    got = [lax.ppermute(value, axis, [(i, i ^ k) for i in range(size)]) for k in strides]
    if len(got) == 1:
        return value + got[0]
    return (value + got[0]) + (got[1] + got[2])


def total_over_all(value):
    wires, slabs = (lax.axis_size("energy"), lax.axis_size("slab"))
    value = total_over(value, "slab", (1,))
    stride = 2
    while stride * 2 < slabs:
        value = total_over(value, "slab", (stride,))
        stride *= 2
    value = total_over(value, BOTH, (stride, slabs, stride + slabs))
    stride = 2
    while stride * 4 <= wires:
        value = total_over(value, "energy", (stride, 2 * stride, 3 * stride))
        stride *= 4
    if stride < wires:
        value = total_over(value, "energy", (stride,))
    return value


def inner_pairs(count, slabs):
    moves = []
    for i in range(count * slabs):
        wire, place = divmod(i, slabs)
        if wire in (0, count - 1):
            moves.append((i, i ^ 1))
        else:
            moves.append((i, (wire + 1 if wire % 2 else wire - 1) * slabs + place))
    return moves


def neighbour_turn(count):
    return [(i, (i + 1) % count if i % 2 else (i - 1) % count) for i in range(count)]


def on_device(
    green_iso,
    coupling,
    lead_green,
    energy_weight,
    energy_group,
    group_charge,
    orbital_atom,
    atom_cell,
    doping,
):
    devices, wires = (lax.axis_size("slab"), lax.axis_size("energy"))
    groups = group_charge.shape[0]
    atoms = atom_cell.shape[1]
    n = lead_green.shape[-1]
    length, rows, depth = doping.shape
    shape = jax.ShapeDtypeStruct
    orbital_row = orbital_atom.reshape(1, n)
    maps = shape((2 * n + 32, n), F32)
    edge_rows = REACH * rows + 8
    held = [
        pltpu.with_memory_space_constraint(x, pltpu.HBM)
        for x in (green_iso, coupling, lead_green, atom_cell, doping)
    ]
    matrix = shape((n, n), F32)
    two = shape((2, n, n), F32)
    sent_step, sent, edge, own_step, own_late, own_iso, own_lead = local_call(
        other_kernel,
        (matrix, maps, shape((edge_rows, depth), F32), matrix, matrix, two, matrix),
        [
            pltpu.VMEM((2, n, n), F32),
            pltpu.VMEM((2, n, n), F32),
            pltpu.VMEM((n, n), F32),
            pltpu.SemaphoreType.DMA((8,)),
            pltpu.VMEM((8, TILE), F32),
            pltpu.VMEM(atom_cell.shape, jnp.int32),
            pltpu.VMEM(doping.shape, F32),
            pltpu.SemaphoreType.DMA((2,)),
        ],
        "hhhhh",
        "other",
        28,
        48 * n**3,
        *held,
    )
    got = lax.ppermute(sent, "slab", pairs_of(devices))
    second = lax.ppermute(edge, "slab", neighbour_turn(devices))
    own = local_call(
        own_kernel,
        maps,
        [],
        "vvvvv",
        "own",
        24,
        2**31,
        edge,
        own_step,
        own_late,
        own_iso,
        own_lead,
    )
    side = shape((-(-REACH * (length + 2 * REACH) // 8) * 8, depth), F32)
    got_step = lax.ppermute(sent_step, "slab", pairs_of(devices))
    passed, stack, stack_parts, wide_block, cells, one_side, two_side = local_call(
        relay_kernel,
        (
            shape((PACKED_ROWS, TILE), F32),
            shape((4 * n, n), F32),
            shape((4 * n, 5 * n - 3 * TILE), BF16),
            shape((length + 2 * REACH, rows, depth), F32),
            shape((8, depth), F32),
            side,
            side,
        ),
        [],
        "vvvvvv",
        "relay",
        28,
        12 * n**3,
        own,
        got,
        own_step,
        got_step,
        doping,
        second,
    )
    packed = lax.ppermute(passed, "slab", hop(devices, 1))
    one_beside = lax.ppermute(one_side, "energy", pairs_of(wires))
    two_beside = lax.ppermute(two_side, BOTH, inner_pairs(wires, devices))
    other_cells = lax.ppermute(cells, "slab", pairs_of(devices))
    if devices > 4:
        other_cells = lax.psum(own[2 * n + 8 : 2 * n + 16, :depth], "slab")
    wide = (length + 2 * ITERS - 2, 3 * rows, depth)
    walks, row_hot, deep_hot, member, charges = local_call(
        functools.partial(atoms_kernel, devices, wires, length),
        (
            shape((6, 2 * devices * atoms, depth), F32),
            shape((wide[0] * wide[1], devices * depth), BF16),
            shape((devices * depth, depth), F32),
            shape((n, TILE), F32),
            shape((groups * devices, depth), F32),
        ),
        [],
        "vvvv",
        "atoms",
        28,
        2**29,
        group_charge.reshape(1, groups),
        orbital_row,
        cells,
        other_cells,
    )
    extra, wide_field = local_call(
        functools.partial(moments_kernel, devices, wires),
        (shape((6 * devices, depth), F32), shape(wide, F32)),
        [pltpu.VMEM((length + 2 * REACH, 3 * rows, depth), F32)],
        "vvvvv",
        "moments",
        20,
        2**26,
        own,
        wide_block,
        one_beside,
        two_beside,
        atom_cell,
    )
    known, weights = local_call(
        functools.partial(known_kernel, devices),
        (shape((8, TILE), F32), shape((2 * groups * devices, TILE), F32)),
        [],
        "vvvvvvvv",
        "known",
        24,
        2**28,
        energy_weight.reshape(1, -1),
        energy_group.reshape(1, -1),
        orbital_row,
        member,
        own,
        got,
        own_step,
        got_step,
    )
    for turn in range(1, devices // 2 - 1):
        passed = local_call(
            functools.partial(pass_kernel, turn),
            shape((PACKED_ROWS, TILE), F32),
            [pltpu.VMEM((n, n), F32)],
            "vvv",
            "pass_on",
            20,
            24 * n**3,
                packed,
            own,
            got,
        )
        arrived = lax.ppermute(passed, "slab", hop(devices, turn + 1))
        packed = jnp.where(lax.axis_index("slab") // 2 == turn + 1, arrived, packed)
    payload = local_call(
        functools.partial(density_kernel, devices),
        shape(((groups + 6) * devices, TILE), F32),
        [pltpu.VMEM((n, n), F32), pltpu.VMEM((8, TILE), F32)],
        "vvvvvvv",
        "density",
        20,
        24 * n**3,
        member,
        packed,
        stack,
        stack_parts,
        known,
        weights,
        extra,
    )
    payload = total_over_all(payload)
    return local_call(
        functools.partial(finish_kernel, devices, wires, atoms),
        (shape((groups, 2, atoms), F32), shape(doping.shape, F32)),
        [],
        "vvvvvv",
        "finish",
        28,
        2**29,
        payload,
        walks,
        row_hot,
        deep_hot,
        charges,
        wide_field,
    )


def solution(mesh):
    in_specs = (
        P("energy", "slab", None, None),
        P("slab", None, None),
        P("energy", None, None),
        P("energy"),
        P("energy"),
        P(),
        P(),
        P("slab", None),
        P("slab", "energy", None),
    )
    out_specs = (P(None, "slab", None), P("slab", "energy", None))
    return jax.shard_map(
        on_device, mesh=mesh, in_specs=in_specs, out_specs=out_specs, check_vma=False
    )
```

```python
import functools

import jax
import jax.numpy as jnp
from jax import lax
from jax.experimental import pallas as pl
from jax.experimental.pallas import tpu as pltpu
from jax.sharding import PartitionSpec as P

ITERS = 3
F32 = jnp.float32
BF16 = jnp.bfloat16
TILE = 128
BOTH = ("energy", "slab")
REACH = 5
HALF = 64


def split(a):
    high = a.astype(BF16)
    return high, (a - high.astype(F32)).astype(BF16)


def dot(a, b, transposed):
    dims = (((1,), (1 if transposed else 0,)), ((), ()))
    return lax.dot_general(a, b, dims, preferred_element_type=F32)


def product(left, right, transposed=False):
    n = right[0].shape[0 if transposed else 1]
    wide = dot(left[0], jnp.concatenate(right, 0 if transposed else 1), transposed)
    return wide[:, :n] + (wide[:, n:] + dot(left[1], right[0], transposed))


def joined(left):
    return jnp.concatenate([left[0], left[1], left[0]], axis=1)


def product_joined(wide, right, transposed=False):
    high, low = right
    axis = 0 if transposed else 1
    n = high.shape[axis]
    cut = n - TILE

    def part(x, start, stop):
        return lax.slice_in_dim(x, start, stop, axis=axis)

    first = [part(x, 0, cut) for x in (high, high, low)]
    last_high, last_low = (part(high, cut, n), part(low, cut, n))
    last = [
        jnp.concatenate([last_high, last_low], axis),
        jnp.concatenate([last_high, jnp.zeros_like(last_high)], axis),
    ]
    one = dot(wide, jnp.concatenate(first, 1 - axis), transposed)
    two = dot(wide[:, : 2 * high.shape[1 - axis]], jnp.concatenate(last, 1 - axis), transposed)
    return jnp.concatenate([one, two[:, :TILE] + two[:, TILE:]], axis=1)


def diagonal_row(matrix):
    rows = lax.broadcasted_iota(jnp.int32, (TILE, TILE), 0)
    columns = lax.broadcasted_iota(jnp.int32, (TILE, TILE), 1)
    parts = []
    for start in range(0, matrix.shape[0], TILE):
        block = matrix[start : start + TILE, start : start + TILE]
        parts.append(jnp.sum(jnp.where(rows == columns, block, 0.0), axis=0, keepdims=True))
    return jnp.concatenate(parts, axis=1)


SMALL = TILE // 2
PACKED_ROWS = 4 * TILE + SMALL + 8


def pack(matrix, out):
    def block(i, j):
        return matrix[i * TILE : (i + 1) * TILE, j * TILE : (j + 1) * TILE]

    rows = lax.broadcasted_iota(jnp.int32, (TILE, TILE), 0)
    columns = lax.broadcasted_iota(jnp.int32, (TILE, TILE), 1)
    for place, (i, j) in enumerate(((0, 1), (0, 2), (1, 2))):
        out[place * TILE : (place + 1) * TILE, :] = block(i, j) + block(j, i).T
    one, two, three = (block(i, i) for i in range(3))
    merged = jnp.where(rows < columns, one + one.T, jnp.where(rows > columns, two + two.T, one))
    out[3 * TILE : 4 * TILE, :] = merged
    whole = jnp.where(rows == columns, three, three + three.T)
    turned = pltpu.roll(whole[SMALL:], SMALL, 1)
    low = (rows > columns)[:SMALL]
    out[4 * TILE : 4 * TILE + SMALL, :] = jnp.where(low, turned, whole[:SMALL])
    row = jnp.sum(jnp.where(rows == columns, two, 0.0), axis=0, keepdims=True)
    last = jnp.sum(jnp.where(rows == columns, three, 0.0), axis=0, keepdims=True)
    first = lax.broadcasted_iota(jnp.int32, (8, TILE), 0) == 0
    out[4 * TILE + SMALL :, :] = jnp.where(first, row, last)


def unpack(packed, out):
    rows = lax.broadcasted_iota(jnp.int32, (TILE, TILE), 0)
    columns = lax.broadcasted_iota(jnp.int32, (TILE, TILE), 1)
    out[...] = jnp.zeros_like(out)
    for place, (i, j) in enumerate(((0, 1), (0, 2), (1, 2))):
        value = packed[place * TILE : (place + 1) * TILE, :]
        out[i * TILE : (i + 1) * TILE, j * TILE : (j + 1) * TILE] = value
    merged = packed[3 * TILE : 4 * TILE, :]
    start = 4 * TILE + SMALL
    row, last = (packed[start : start + 1, :], packed[start + 1 : start + 2, :])
    out[:TILE, :TILE] = jnp.where(rows <= columns, merged, 0.0)
    out[TILE : 2 * TILE, TILE : 2 * TILE] = jnp.where(
        rows > columns, merged, jnp.where(rows == columns, row, 0.0)
    )
    half = packed[4 * TILE : start, :]
    out[2 * TILE : 2 * TILE + SMALL, 2 * TILE :] = jnp.where((rows <= columns)[:SMALL], half, 0.0)
    turned = pltpu.roll(half, SMALL, 1)
    inside = (columns >= SMALL) & (rows > columns)
    value = jnp.where(rows[SMALL:] == columns[SMALL:], last, 0.0)
    out[2 * TILE + SMALL :, 2 * TILE :] = jnp.where(inside[SMALL:], turned, value)


def plane_rows(n, plane):
    start = 2 * n + 16 + 8 * (plane // 3)
    return slice(start, start + 8)


def plane_lanes(plane):
    return slice((plane % 3) * TILE, (plane % 3 + 1) * TILE)


def copy_all(pairs, sems):
    copies = [pltpu.make_async_copy(src, dst, sems.at[i]) for i, (src, dst) in enumerate(pairs)]
    for copy in copies:
        copy.start()
    return copies


def slabs(early, late, isos, lead, maps, step):
    place = lax.axis_index("slab")
    n = early.shape[0]

    @pl.when(place == 0)
    def _():
        state = lead[...]
        for slab, value in enumerate((early, late)):
            parts = split(value)
            state = product(parts, split(state))
            state = product(split(state), parts, True) + isos[slab]
            maps[2 * n + slab : 2 * n + slab + 1, :] = diagonal_row(state)
        maps[n : 2 * n, :] = state

    @pl.when(place != 0)
    def _():
        later = split(late)
        wide = joined(later)
        term = product_joined(wide, split(isos[0]))
        maps[0:n, :] = product_joined(wide, split(early))
        term = product(split(term), later, True) + isos[1]
        maps[n : 2 * n, :] = term
        maps[2 * n : 2 * n + 1, :] = diagonal_row(isos[0])
        maps[2 * n + 1 : 2 * n + 2, :] = diagonal_row(term)
        if step is not None:
            step[...] = early


def other_kernel(
    iso,
    coupling,
    lead,
    cells_in,
    field_in,
    step,
    sent,
    planes,
    own_early,
    own_late,
    own_iso,
    own_lead,
    c_buf,
    g_buf,
    lead_buf,
    sems,
    row,
    cells,
    field,
    more_sems,
):
    place = lax.axis_index("slab")
    core = lax.rem(place, 2)
    n = lead_buf.shape[1]
    sources = []
    for slab in range(2):
        sources.append((coupling.at[slab], c_buf.at[slab]))
        sources.append((iso.at[1 - core, slab], g_buf.at[slab]))
        sources.append((iso.at[core, slab], own_iso.at[slab]))
    sources.append((lead.at[1 - core], lead_buf))
    sources.append((lead.at[core], own_lead))
    waits = copy_all(sources, sems)
    copies = copy_all([(cells_in, cells), (field_in, field)], more_sems)
    steps = []
    for slab in range(2):
        for copy in waits[3 * slab : 3 * slab + 3]:
            copy.wait()
        parts = split(c_buf[slab])
        for buf in (g_buf, own_iso):
            steps.append(product_joined(joined(split(buf[slab])), parts))
    waits[6].wait()
    own_early[...] = steps[1]
    own_late[...] = steps[3]
    slabs(steps[0], steps[2], g_buf, lead_buf, sent, step)
    waits[7].wait()
    for copy in copies:
        copy.wait()
    atoms = cells.shape[1]
    row[...] = jnp.zeros_like(row)
    row[0:1, 0:atoms] = cells[0:1, :].astype(F32)
    row[0:1, HALF : HALF + atoms] = cells[1:2, :].astype(F32)
    rows = lax.broadcasted_iota(jnp.int32, (8, TILE), 0)
    mine = jnp.where(rows == place, row[0:1, :], 0.0)
    sent[2 * n + 8 : 2 * n + 16, 0:TILE] = mine
    planes[REACH * 8 :, :] = mine
    length = field.shape[0]
    even = core == 0
    for plane in range(REACH):
        low, high = (field[plane], field[length - REACH + plane])
        planes[plane * 8 : plane * 8 + 8, :] = jnp.where(even, low, high)
        sent[plane_rows(n, plane), plane_lanes(plane)] = jnp.where(even, high, low)


def own_kernel(planes, early, late, isos, lead, own):
    n = lead.shape[0]
    own[2 * n + 8 : 2 * n + 16, 0:TILE] = planes[REACH * 8 :, :]
    slabs(early[...], late[...], isos, lead, own, None)


def advance(map_ref, state):
    n = map_ref.shape[1]
    composed = split(map_ref[0:n, :])
    term = product(composed, split(state))
    return product(split(term), composed, True) + map_ref[n : 2 * n, :]


def near_far(mine, other):
    core = lax.rem(lax.axis_index("slab"), 2)
    return jnp.where(core == 0, mine, other), jnp.where(core == 0, other, mine)


def relay_kernel(
    own, got, own_step, got_step, field, second, out, stack, parts, wide, cells, one_side, two_side
):
    place, wire = (lax.axis_index("slab"), lax.axis_index("energy"))
    n = own.shape[1]
    length, height, _ = field.shape
    even = lax.rem(place, 2) == 0
    wide[REACH : REACH + length] = field[...]
    for plane in range(REACH):
        one = got[plane_rows(n, plane), plane_lanes(plane)]
        two = second[plane * 8 : plane * 8 + 8, :]
        wide[plane] = jnp.where(even, two, one)
        wide[REACH + length + plane] = jnp.where(even, one, two)
    spot = slice(2 * n + 8, 2 * n + 16)
    cells[...] = own[spot, :TILE] + got[spot, :TILE] + second[REACH * 8 :, :]
    even = lax.rem(wire, 2) == 0
    for plane in range(length + 2 * REACH):
        low, high = (wide[plane, :REACH, :], wide[plane, height - REACH :, :])
        spot = slice(plane * REACH, (plane + 1) * REACH)
        one_side[spot, :] = jnp.where(even, high, low)
        two_side[spot, :] = jnp.where(even, low, high)

    @pl.when(place == 0)
    def _():
        pack(advance(got, own[n : 2 * n, :]), out)

    @pl.when(place == 1)
    def _():
        pack(advance(own, got[n : 2 * n, :]), out)

    @pl.when(place >= 2)
    def _():
        near_step, far_step = near_far(own_step[...], got_step[...])
        near_map, far_map = near_far(own[0:n, :], got[0:n, :])
        far = jnp.concatenate([far_step, far_map], axis=0)
        both = product_joined(joined(split(far)), split(near_map))
        for number, value in enumerate((near_step, near_map, both[:n], both[n:])):
            rows = slice(number * n, (number + 1) * n)
            stack[rows, :] = value
            high, low = split(value)
            parts[rows, :] = jnp.concatenate(
                [high, low, high[:, : n - TILE], low[:, : n - TILE], high[:, : n - TILE]], axis=1
            )


def pass_kernel(turn, packed, own, got, out, state):
    place = lax.axis_index("slab")
    for core, (near, far) in enumerate(((own, got), (got, own))):

        @pl.when(place == 2 * turn + core)
        def _():
            unpack(packed, state)
            state[...] = advance(near, state[...])
            pack(advance(far, state[...]), out)


def known_kernel(
    pairs, weight_ref, group_ref, orbital_atom, member, own, got, own_step, got_step, fold, weights
):
    place = lax.axis_index("slab")
    core = lax.rem(place, 2)
    pair_rows = lax.broadcasted_iota(jnp.int32, (pairs, TILE), 0)
    mine_weight = jnp.where(core == 0, weight_ref[:, 0:1], weight_ref[:, 1:2])
    mine_group = jnp.where(core == 0, group_ref[:, 0:1], group_ref[:, 1:2])
    groups = weights.shape[0] // (2 * pairs)
    for half in range(2):
        for group in range(groups):
            weight = jnp.where(mine_group == group, mine_weight, 0.0)
            start = (half * groups + group) * pairs
            weights[start : start + pairs, :] = jnp.where(
                pair_rows == place - core + half, jnp.broadcast_to(weight, (pairs, TILE)), 0.0
            )
    n = own.shape[1]
    atoms = lax.broadcasted_iota(jnp.int32, (TILE, n), 0)
    spots = (atoms == orbital_atom[...]).astype(BF16)
    _, far_step = near_far(own_step[...], got_step[...])
    _, far_map = near_far(own[0:n, :], got[0:n, :])
    near_source, _ = near_far(own[n : 2 * n, :], got[n : 2 * n, :])
    far = jnp.concatenate([far_step, far_map], axis=0)
    both = product_joined(joined(split(far)), split(near_source))
    near_rows, far_rows = near_far(own[2 * n : 2 * n + 2, :], got[2 * n : 2 * n + 2, :])
    rest = jnp.concatenate([near_rows, far_rows, jnp.zeros((4, n), F32)], axis=0)
    total = jnp.zeros((8, TILE), F32)
    for _ in range(3):
        piece = rest.astype(BF16)
        total = total + dot(piece, spots, True)
        rest = rest - piece.astype(F32)
    fold[...] = total
    for number in range(2):
        rows = slice(number * n, (number + 1) * n)
        value = jnp.sum(far[rows] * both[rows], axis=1, keepdims=True) * member[...]
        fold[2 + number : 3 + number, :] += jnp.sum(value, axis=0, keepdims=True)


def density_kernel(
    pairs,
    member,
    packed,
    stack,
    wide,
    known,
    weights,
    extra,
    out,
    state,
    fold,
):
    place = lax.axis_index("slab")
    n = state.shape[0]
    fold[...] = known[...]

    @pl.when(place >= 2)
    def _():
        unpack(packed, state)
        high, low = split(state[...])
        cut = n - TILE
        corner = [x[:cut, :cut] for x in (high, high, low)]
        one = dot(wide[:, 2 * n :], jnp.concatenate(corner, axis=0), False)
        last_high, last_low = (high[:, cut:], low[:, cut:])
        last = [
            jnp.concatenate([last_high, last_low], axis=1),
            jnp.concatenate([last_high, jnp.zeros_like(last_high)], axis=1),
        ]
        two = dot(wide[:, : 2 * n], jnp.concatenate(last, axis=0), False)
        both = jnp.concatenate([one, two[:, :TILE] + two[:, TILE:]], axis=1)
        for number in range(4):
            rows = slice(number * n, (number + 1) * n)
            value = jnp.sum(stack[rows, :] * both[rows], axis=1, keepdims=True) * member[...]
            fold[number : number + 1, :] += jnp.sum(value, axis=0, keepdims=True)

    plain = fold[...]
    turned = pltpu.roll(plain, HALF, 1)
    rows = out.shape[0] - extra.shape[0]
    values = [plain[2 * i : 2 * i + 1, :] + turned[2 * i + 1 : 2 * i + 2, :] for i in range(2)]
    out[:rows, :] = weights[:rows, :] * values[0] + weights[rows:, :] * values[1]
    out[rows:, :] = extra[...]


def local_call(kernel, shapes, scratch, specs, name, limit, flops, *operands):
    spaces = {"v": pltpu.VMEM, "s": pltpu.SMEM, "h": pltpu.HBM}
    single = not isinstance(shapes, tuple)
    vmem = pl.BlockSpec(memory_space=pltpu.VMEM)
    return pl.pallas_call(
        kernel,
        out_shape=shapes,
        in_specs=[pl.BlockSpec(memory_space=spaces[spec]) for spec in specs],
        out_specs=vmem if single else (vmem,) * len(shapes),
        scratch_shapes=scratch,
        compiler_params=pltpu.CompilerParams(vmem_limit_bytes=limit * 2**20),
        cost_estimate=pl.CostEstimate(flops=flops, bytes_accessed=2**20, transcendentals=0),
        name=name,
    )(*operands)


def shifted_pair(x, axis):
    size = x.shape[axis]
    before, after = (pltpu.roll(x, 1, axis), pltpu.roll(x, size - 1, axis))
    if axis == x.ndim - 1:
        lanes = lax.broadcasted_iota(jnp.int32, x.shape, axis)
        before = jnp.where(lanes == 0, 0.0, before)
        after = jnp.where(lanes == size - 1, 0.0, after)
    return before, after


def neighbours(x):
    centre = x[1:-1]
    up, down = shifted_pair(centre, 1)
    left, right = shifted_pair(centre, 2)
    return (x[2:] + x[:-2]) + (up + down) + (left + right)


def differences(x):
    centre = x[1:-1]
    up, down = shifted_pair(centre, 1)
    left, right = shifted_pair(centre, 2)
    along = (x[2:] - centre) + (x[:-2] - centre)
    across = (up - centre) + (down - centre)
    deep = (left - centre) + (right - centre)
    return along + (across + deep)


def grid_mask(shape, margin, length, rows, place, devices, wire, wires):
    planes = lax.broadcasted_iota(jnp.int32, shape, 0)
    row = lax.broadcasted_iota(jnp.int32, shape, 1)
    low_x = jnp.where(place == 0, margin, 0)
    high_x = jnp.where(place == devices - 1, margin + length, shape[0])
    low_y = jnp.where(wire == 0, rows, 0)
    high_y = jnp.where(wire == wires - 1, 2 * rows, shape[1])
    inside = (planes >= low_x) & (planes < high_x) & (row >= low_y) & (row < high_y)
    return inside.astype(F32)


def three_parts(x):
    parts = []
    for _ in range(3):
        parts.append(x.astype(BF16))
        x = x - parts[-1].astype(F32)
    return parts


def coordinates(cell, rows_y, depth):
    z_part = cell - depth * jnp.floor(cell * (1.0 / depth))
    plane = jnp.floor(cell * (1.0 / depth))
    x_part = jnp.floor(plane * (1.0 / rows_y))
    return x_part, plane - rows_y * x_part, z_part


WALKS = ((0, 1),), ((1, 1),), ((0, 2), (2, 1)), ((1, 3), (3, 1)), ((0, 6), (2, 4), (4, 1)), ((1, 10), (3, 5), (5, 1))
FACTORIAL = (1.0, 1.0, 2.0, 6.0, 24.0, 120.0)


def walk_counts(here, there, length):
    apart = jnp.abs(here - there)
    low = here + there + 2.0
    high = 2.0 * length - here - there
    at = []
    for steps in range(6):
        value = (apart == steps).astype(F32)
        if steps >= 2:
            value = value - (low == steps).astype(F32) - (high == steps).astype(F32)
        at.append(value)
    counts = []
    for steps, terms in enumerate(WALKS):
        total = None
        for distance, count in terms:
            term = at[distance] * (count / FACTORIAL[steps])
            total = term if total is None else total + term
        counts.append(total)
    return counts


def convolved(left, right):
    result = []
    for steps in range(6):
        total = left[0] * right[steps]
        for part in range(1, steps + 1):
            total = total + left[part] * right[steps - part]
        result.append(total)
    return result


def moments_kernel(devices, wires, own, field, one_beside, two_beside, cells, out, wide_field, whole_field):
    place, wire = (lax.axis_index("slab"), lax.axis_index("energy"))
    planes, rows, depth = field.shape
    length = planes - 2 * REACH
    width_x = length // 2
    atoms = cells.shape[1]
    grid_y = rows * wires
    pairs = devices
    n = own.shape[1]
    even = lax.rem(wire, 2) == 0
    whole_field[...] = jnp.zeros_like(whole_field)
    whole_field[:, rows : 2 * rows, :] = field[...]
    for plane in range(planes):
        spot = slice(plane * REACH, (plane + 1) * REACH)
        one, two = (one_beside[spot, :], two_beside[spot, :])
        whole_field[plane, rows - REACH : rows, :] = jnp.where(even, two, one)
        whole_field[plane, 2 * rows : 2 * rows + REACH, :] = jnp.where(even, one, two)
    whole = (planes, 3 * rows, depth)
    mask = grid_mask(whole, REACH, length, rows, place, devices, wire, wires)
    source = jnp.where(mask > 0, whole_field[...], 0.0)
    margin = ITERS - 1
    wide_field[...] = source[REACH - margin : REACH + length + margin]

    def inner(x):
        extra = (x.shape[0] - length) // 2
        return x[extra : extra + length, rows : 2 * rows]

    chain = [source]
    for step in range(1, 6):
        chain.append(neighbours(chain[-1]) * mask[step : planes - step])
    blocks = [inner(x) for x in chain]
    near = source[2:-2]
    other = [near]
    for step in range(1, 4):
        other.append(differences(other[-1]) * mask[2 + step : planes - 2 - step])
    other = [inner(x) for x in other]
    lanes = lax.broadcasted_iota(jnp.int32, (1, depth), 1)
    sums = jnp.zeros((1, depth), F32)
    for base, fields in enumerate((blocks, other)):
        for steps in range(6):
            part = jnp.sum(fields[steps // 2] * fields[(steps + 1) // 2], axis=0)
            part = jnp.sum(jnp.sum(part, axis=1, keepdims=True), axis=0, keepdims=True)
            sums = jnp.where(lanes == atoms + 6 * base + steps, part, sums)
    out[...] = jnp.zeros_like(out)
    mine = own[2 * n + 8 : 2 * n + 16, :depth]
    mine = jnp.sum(mine, axis=0, keepdims=True)
    lane = lax.broadcasted_iota(jnp.int32, (1, depth), 1)
    odd = (lane >= HALF).astype(F32)
    used = lax.rem(lane, HALF) < atoms
    x_part, y_part, z_part = coordinates(mine, grid_y, depth)
    start = (wire * rows).astype(F32)
    ours = used & (y_part >= start) & (y_part < start + rows)
    at_row = jnp.where(ours, (x_part + width_x * odd) * rows + y_part - start, -1.0)
    cell_rows = length * rows
    row_iota = lax.broadcasted_iota(jnp.int32, (cell_rows, depth), 0).astype(F32)
    deep_iota = lax.broadcasted_iota(jnp.int32, (depth, depth), 0).astype(F32)
    at_rows = (row_iota == at_row).astype(F32)
    at_deep = (deep_iota == z_part).astype(BF16)
    for steps, block in enumerate(blocks):
        value = jnp.zeros((cell_rows, depth), F32)
        for part in three_parts(block.reshape(cell_rows, depth)):
            value = value + dot(part, at_deep, False)
        value = jnp.sum(value * at_rows, axis=0, keepdims=True)
        out[pl.ds(steps * pairs + place, 1), :] = value
    out[0:1, :] += sums


def atoms_kernel(
    devices,
    wires,
    length,
    charge_ref,
    orbital_atom,
    some_cells,
    other_cells,
    walks,
    row_hot,
    deep_hot,
    member,
    charges,
):
    place, wire = (lax.axis_index("slab"), lax.axis_index("energy"))
    rows, depth = some_cells.shape
    width_x = length // 2
    atoms = walks.shape[1] // (2 * devices)
    grid_y = rows * wires
    pairs = devices
    n = orbital_atom.shape[1]
    start = (wire * rows).astype(F32)
    for group in range(charges.shape[0] // pairs):
        charges[group * pairs : (group + 1) * pairs, :] = jnp.broadcast_to(
            charge_ref[:, group : group + 1], (pairs, depth)
        )
    cells = jnp.maximum(some_cells[...], other_cells[...])
    spots = lax.broadcasted_iota(jnp.int32, (TILE, n), 0) == orbital_atom[...]
    spots = spots.astype(F32)
    for first in range(0, n, TILE):
        member[first : first + TILE, :] = spots[:, first : first + TILE].T
    row_cells = cells
    row_x, row_y, row_z = coordinates(row_cells, grid_y, depth)
    padded = jnp.concatenate([row_cells, jnp.zeros((depth - 8, depth), F32)], axis=0)
    column_x, column_y, column_z = coordinates(padded.T, grid_y, depth)
    row_lane = lax.broadcasted_iota(jnp.int32, (8, depth), 1)
    next_x, next_y, next_z = [jnp.concatenate([v[1:], v[:1]], axis=0) for v in (row_x, row_y, row_z)]

    def turned(now, later, step_now, step_later):
        value = jnp.where(row_lane >= HALF, now + step_now, later + step_later)
        return pltpu.roll(value, HALF, 1)

    even_x = row_x + width_x * (row_lane >= HALF).astype(F32)
    odd_x, odd_y, odd_z = (
        turned(row_x, next_x, 0.0, float(width_x)),
        turned(row_y, next_y, 0.0, 0.0),
        turned(row_z, next_z, 0.0, 0.0),
    )
    for slab in range(2 * pairs):
        pair, side = (slab // 2, slab % 2)
        base = float(slab * width_x)
        if side:
            there = (odd_x, odd_y, odd_z)
        else:
            there = (even_x, row_y, row_z)
        there = [v[pair : pair + 1, :] for v in there]
        here = [
            v[side * HALF : side * HALF + atoms, pair : pair + 1]
            for v in (column_x, column_y, column_z)
        ]
        shape = (atoms, depth)
        sizes = (2 * pairs * width_x, grid_y, depth)
        axes = []
        for axis in range(3):
            shift = base if axis == 0 else 0.0
            axes.append(
                walk_counts(
                    jnp.broadcast_to(here[axis] + shift, shape),
                    jnp.broadcast_to(there[axis] + shift, shape),
                    float(sizes[axis]),
                )
            )
        total = convolved(convolved(axes[0], axes[1]), axes[2])
        for steps in range(6):
            walks[steps, slab * atoms : (slab + 1) * atoms, :] = total[steps] * FACTORIAL[steps]
    wide = length + 4
    first_x = (place * length - 2).astype(F32)
    first_y = start - rows
    count = wide * 3 * rows
    rows_iota = lax.broadcasted_iota(jnp.int32, (count, depth), 0).astype(F32)
    used_row = lax.rem(row_lane, HALF) < atoms
    for pair in range(pairs):
        x_at = even_x[pair : pair + 1, :] + float(2 * pair * width_x) - first_x
        y_at = row_y[pair : pair + 1, :] - first_y
        good = (x_at >= 0) & (x_at < wide) & (y_at >= 0) & (y_at < 3 * rows) & used_row[0:1, :]
        target = jnp.where(good, x_at * (3 * rows) + y_at, -1.0)
        row_hot[:, pair * depth : (pair + 1) * depth] = (rows_iota == target).astype(BF16)
        z_at = column_z[:, pair : pair + 1]
        lanes_z = lax.broadcasted_iota(jnp.int32, (depth, depth), 1).astype(F32)
        deep_hot[pair * depth : (pair + 1) * depth, :] = (lanes_z == z_at).astype(F32)


def total_of(x):
    return jnp.sum(jnp.sum(x, axis=1, keepdims=True), axis=0, keepdims=True)


def quadratic_form(poly, moments, shift):
    total = None
    for i, one in enumerate(poly):
        for j, two in enumerate(poly):
            if j < i:
                continue
            term = one * two * moments[i + j + shift] * (1.0 if i == j else 2.0)
            total = term if total is None else total + term
    return total


def finish_kernel(
    devices,
    wires,
    atoms,
    payload,
    walks,
    row_hot,
    deep_hot,
    charges,
    field,
    density,
    potential,
):
    place, wire = (lax.axis_index("slab"), lax.axis_index("energy"))
    length, rows, depth = potential.shape
    pairs = devices
    groups = density.shape[0]
    held = charges[...] * payload[: groups * pairs, :]
    charge = held[:pairs]
    for group in range(1, groups):
        charge = charge + held[group * pairs : (group + 1) * pairs]
    for group in range(groups):
        value = payload[pl.ds(group * pairs + place, 1), :]
        density[group, 0:1, :] = value[:, :atoms]
        density[group, 1:2, :] = pltpu.roll(value, HALF, 1)[:, :atoms]
    square = jnp.concatenate([charge, jnp.zeros((depth - pairs, depth), F32)], axis=0)
    columns = square.T
    later = jnp.concatenate([charge[1:], jnp.zeros((1, depth), F32)], axis=0)
    lanes = lax.broadcasted_iota(jnp.int32, (pairs, depth), 1)
    even_row = jnp.where(lanes >= HALF, 2.0 * charge, charge)
    odd_row = pltpu.roll(jnp.where(lanes >= HALF, charge, 2.0 * later), HALF, 1)
    totals = [None] * 6
    for slab in range(2 * pairs):
        pair, side = (slab // 2, slab % 2)
        row = (odd_row if side else even_row)[pair : pair + 1, :]
        column = columns[side * HALF : side * HALF + atoms, pair : pair + 1]
        outer = column * row
        for steps in range(6):
            term = walks[steps, slab * atoms : (slab + 1) * atoms, :] * outer
            totals[steps] = term if totals[steps] is None else totals[steps] + term
    base = groups * pairs
    crossed = []
    for steps in range(6):
        cross = 2.0 * charge * payload[base + steps * pairs : base + (steps + 1) * pairs, :]
        parts = [totals[steps][i : i + 8] for i in range(0, atoms, 8)]
        if pairs < 8:
            cross = jnp.concatenate([cross, jnp.zeros((8 - pairs, depth), F32)], axis=0)
        parts.append(cross)
        while len(parts) > 1:
            parts = [sum(parts[i : i + 2][1:], parts[i]) for i in range(0, len(parts), 2)]
        crossed.append(total_of(parts[0]))
    lane = lax.broadcasted_iota(jnp.int32, (1, depth), 1)
    row = payload[base : base + 1, :]
    sums = [
        jnp.sum(jnp.where(lane == atoms + i, row, 0.0), axis=1, keepdims=True) for i in range(12)
    ]
    plain = [sums[steps] + crossed[steps] for steps in range(6)]
    moved = []
    for steps in range(6):
        value = sums[6 + steps]
        binomial = 1
        for part in range(steps, -1, -1):
            value = value + (binomial * (-6.0) ** (steps - part)) * crossed[part]
            binomial = binomial * part // (steps - part + 1)
        moved.append(value)
    smooth = plain[1] > 3.5 * plain[0]
    level = jnp.where(smooth, 0.5, 6.5)
    moments = [jnp.where(smooth, two, one) for one, two in zip(plain, moved)]
    residual, direction = ([jnp.ones_like(level)], [jnp.ones_like(level)])
    norm = moments[0]
    alphas, betas = ([], [])
    for turn in range(ITERS):
        energy = level * quadratic_form(direction, moments, 0) - quadratic_form(direction, moments, 1)
        alpha = jnp.clip(norm / energy, 1.0 / 12.5, 2.0)
        alphas.append(alpha)
        if turn + 1 == ITERS:
            break
        longer = residual + [jnp.zeros_like(level)]
        for i, value in enumerate(direction):
            longer[i] = longer[i] - alpha * level * value
            longer[i + 1] = longer[i + 1] + alpha * value
        residual = longer
        following = quadratic_form(residual, moments, 0)
        beta = jnp.clip(following / norm, 0.0, 25.0)
        betas.append(beta)
        norm = following
        direction = [
            value + beta * direction[i] if i < len(direction) else value
            for i, value in enumerate(residual)
        ]
    pieces = [[], [], []]
    for pair in range(pairs):
        hot = deep_hot[pair * depth : (pair + 1) * depth, :]
        for place_in, piece in enumerate(three_parts(columns[:, pair : pair + 1] * hot)):
            pieces[place_in].append(piece)
    spread = jnp.concatenate([jnp.concatenate(piece, axis=0) for piece in pieces], axis=1)
    placed = dot(row_hot[...], spread, False)
    placed = placed[:, :depth] + (placed[:, depth : 2 * depth] + placed[:, 2 * depth :])
    margin = ITERS - 1
    wide = (length + 2 * margin, 3 * rows, depth)
    mask = grid_mask(wide, margin, length, rows, place, devices, wire, wires)
    source = field[...] + placed.reshape(wide)
    residual, direction = (source, source)
    total = alphas[0] * source[margin:-margin, rows : 2 * rows]
    for turn in range(ITERS - 1):
        image = 6.5 * direction[1:-1] - neighbours(direction)
        inner_mask = mask[turn + 1 : wide[0] - turn - 1]
        residual = (residual[1:-1] - alphas[turn] * image) * inner_mask
        direction = residual + betas[turn] * direction[1:-1]
        extra = margin - turn - 1
        block = direction[extra : extra + length, rows : 2 * rows]
        total = total + alphas[turn + 1] * block
    potential[...] = total


def hop(count, turn):
    moves = {i: i for i in range(count)}
    for core in range(2):
        here, there = (2 * turn - 2 + core, 2 * turn + core)
        moves[here], moves[there] = (there, here)
    return sorted(moves.items())


def pairs_of(count):
    return [(i, i ^ 1) for i in range(count)]


def total_over(value, axis, strides):
    size = 1
    for name in axis if isinstance(axis, tuple) else (axis,):
        size *= lax.axis_size(name)
    got = [lax.ppermute(value, axis, [(i, i ^ k) for i in range(size)]) for k in strides]
    if len(got) == 1:
        return value + got[0]
    return (value + got[0]) + (got[1] + got[2])


def total_over_all(value):
    wires, slabs = (lax.axis_size("energy"), lax.axis_size("slab"))
    value = total_over(value, "slab", (1,))
    stride = 2
    while stride * 2 < slabs:
        value = total_over(value, "slab", (stride,))
        stride *= 2
    value = total_over(value, BOTH, (stride, slabs, stride + slabs))
    stride = 2
    while stride * 4 <= wires:
        value = total_over(value, "energy", (stride, 2 * stride, 3 * stride))
        stride *= 4
    if stride < wires:
        value = total_over(value, "energy", (stride,))
    return value


def inner_pairs(count, slabs):
    moves = []
    for i in range(count * slabs):
        wire, place = divmod(i, slabs)
        if wire in (0, count - 1):
            moves.append((i, i ^ 1))
        else:
            moves.append((i, (wire + 1 if wire % 2 else wire - 1) * slabs + place))
    return moves


def neighbour_turn(count):
    return [(i, (i + 1) % count if i % 2 else (i - 1) % count) for i in range(count)]


def on_device(
    green_iso,
    coupling,
    lead_green,
    energy_weight,
    energy_group,
    group_charge,
    orbital_atom,
    atom_cell,
    doping,
):
    devices, wires = (lax.axis_size("slab"), lax.axis_size("energy"))
    groups = group_charge.shape[0]
    atoms = atom_cell.shape[1]
    n = lead_green.shape[-1]
    length, rows, depth = doping.shape
    shape = jax.ShapeDtypeStruct
    orbital_row = orbital_atom.reshape(1, n)
    maps = shape((2 * n + 32, n), F32)
    edge_rows = REACH * rows + 8
    held = [
        pltpu.with_memory_space_constraint(x, pltpu.HBM)
        for x in (green_iso, coupling, lead_green, atom_cell, doping)
    ]
    matrix = shape((n, n), F32)
    two = shape((2, n, n), F32)
    sent_step, sent, edge, own_step, own_late, own_iso, own_lead = local_call(
        other_kernel,
        (matrix, maps, shape((edge_rows, depth), F32), matrix, matrix, two, matrix),
        [
            pltpu.VMEM((2, n, n), F32),
            pltpu.VMEM((2, n, n), F32),
            pltpu.VMEM((n, n), F32),
            pltpu.SemaphoreType.DMA((8,)),
            pltpu.VMEM((8, TILE), F32),
            pltpu.VMEM(atom_cell.shape, jnp.int32),
            pltpu.VMEM(doping.shape, F32),
            pltpu.SemaphoreType.DMA((2,)),
        ],
        "hhhhh",
        "other",
        28,
        48 * n**3,
        *held,
    )
    got = lax.ppermute(sent, "slab", pairs_of(devices))
    second = lax.ppermute(edge, "slab", neighbour_turn(devices))
    own = local_call(
        own_kernel,
        maps,
        [],
        "vvvvv",
        "own",
        24,
        2**31,
        edge,
        own_step,
        own_late,
        own_iso,
        own_lead,
    )
    side = shape((-(-REACH * (length + 2 * REACH) // 8) * 8, depth), F32)
    got_step = lax.ppermute(sent_step, "slab", pairs_of(devices))
    passed, stack, stack_parts, wide_block, cells, one_side, two_side = local_call(
        relay_kernel,
        (
            shape((PACKED_ROWS, TILE), F32),
            shape((4 * n, n), F32),
            shape((4 * n, 5 * n - 3 * TILE), BF16),
            shape((length + 2 * REACH, rows, depth), F32),
            shape((8, depth), F32),
            side,
            side,
        ),
        [],
        "vvvvvv",
        "relay",
        28,
        12 * n**3,
        own,
        got,
        own_step,
        got_step,
        doping,
        second,
    )
    packed = lax.ppermute(passed, "slab", hop(devices, 1))
    one_beside = lax.ppermute(one_side, "energy", pairs_of(wires))
    two_beside = lax.ppermute(two_side, BOTH, inner_pairs(wires, devices))
    other_cells = lax.ppermute(cells, "slab", pairs_of(devices))
    if devices > 4:
        other_cells = lax.psum(own[2 * n + 8 : 2 * n + 16, :depth], "slab")
    wide = (length + 2 * ITERS - 2, 3 * rows, depth)
    walks, row_hot, deep_hot, member, charges = local_call(
        functools.partial(atoms_kernel, devices, wires, length),
        (
            shape((6, 2 * devices * atoms, depth), F32),
            shape((wide[0] * wide[1], devices * depth), BF16),
            shape((devices * depth, depth), F32),
            shape((n, TILE), F32),
            shape((groups * devices, depth), F32),
        ),
        [],
        "vvvv",
        "atoms",
        28,
        2**29,
        group_charge.reshape(1, groups),
        orbital_row,
        cells,
        other_cells,
    )
    extra, wide_field = local_call(
        functools.partial(moments_kernel, devices, wires),
        (shape((6 * devices, depth), F32), shape(wide, F32)),
        [pltpu.VMEM((length + 2 * REACH, 3 * rows, depth), F32)],
        "vvvvv",
        "moments",
        20,
        2**26,
        own,
        wide_block,
        one_beside,
        two_beside,
        atom_cell,
    )
    known, weights = local_call(
        functools.partial(known_kernel, devices),
        (shape((8, TILE), F32), shape((2 * groups * devices, TILE), F32)),
        [],
        "vvvvvvvv",
        "known",
        24,
        2**28,
        energy_weight.reshape(1, -1),
        energy_group.reshape(1, -1),
        orbital_row,
        member,
        own,
        got,
        own_step,
        got_step,
    )
    for turn in range(1, devices // 2 - 1):
        passed = local_call(
            functools.partial(pass_kernel, turn),
            shape((PACKED_ROWS, TILE), F32),
            [pltpu.VMEM((n, n), F32)],
            "vvv",
            "pass_on",
            20,
            24 * n**3,
                packed,
            own,
            got,
        )
        arrived = lax.ppermute(passed, "slab", hop(devices, turn + 1))
        packed = jnp.where(lax.axis_index("slab") // 2 == turn + 1, arrived, packed)
    payload = local_call(
        functools.partial(density_kernel, devices),
        shape(((groups + 6) * devices, TILE), F32),
        [pltpu.VMEM((n, n), F32), pltpu.VMEM((8, TILE), F32)],
        "vvvvvvv",
        "density",
        20,
        24 * n**3,
        member,
        packed,
        stack,
        stack_parts,
        known,
        weights,
        extra,
    )
    payload = total_over_all(payload)
    return local_call(
        functools.partial(finish_kernel, devices, wires, atoms),
        (shape((groups, 2, atoms), F32), shape(doping.shape, F32)),
        [],
        "vvvvvv",
        "finish",
        28,
        2**29,
        payload,
        walks,
        row_hot,
        deep_hot,
        charges,
        wide_field,
    )


def solution(mesh):
    in_specs = (
        P("energy", "slab", None, None),
        P("slab", None, None),
        P("energy", None, None),
        P("energy"),
        P("energy"),
        P(),
        P(),
        P("slab", None),
        P("slab", "energy", None),
    )
    out_specs = (P(None, "slab", None), P("slab", "energy", None))
    return jax.shard_map(
        on_device, mesh=mesh, in_specs=in_specs, out_specs=out_specs, check_vma=False
    )
```

```python
import functools

import jax
import jax.numpy as jnp
from jax import lax
from jax.experimental import pallas as pl
from jax.experimental.pallas import tpu as pltpu
from jax.sharding import PartitionSpec as P

ITERS = 3
F32 = jnp.float32
BF16 = jnp.bfloat16
TILE = 128
BOTH = ("energy", "slab")
REACH = 5
HALF = 64


def split(a):
    high = a.astype(BF16)
    return high, (a - high.astype(F32)).astype(BF16)


def dot(a, b, transposed):
    dims = (((1,), (1 if transposed else 0,)), ((), ()))
    return lax.dot_general(a, b, dims, preferred_element_type=F32)


def product(left, right, transposed=False):
    n = right[0].shape[0 if transposed else 1]
    wide = dot(left[0], jnp.concatenate(right, 0 if transposed else 1), transposed)
    return wide[:, :n] + (wide[:, n:] + dot(left[1], right[0], transposed))


def joined(left):
    return jnp.concatenate([left[0], left[1], left[0]], axis=1)


def product_joined(wide, right, transposed=False):
    high, low = right
    axis = 0 if transposed else 1
    n = high.shape[axis]
    cut = n - TILE

    def part(x, start, stop):
        return lax.slice_in_dim(x, start, stop, axis=axis)

    first = [part(x, 0, cut) for x in (high, high, low)]
    last_high, last_low = (part(high, cut, n), part(low, cut, n))
    last = [
        jnp.concatenate([last_high, last_low], axis),
        jnp.concatenate([last_high, jnp.zeros_like(last_high)], axis),
    ]
    one = dot(wide, jnp.concatenate(first, 1 - axis), transposed)
    two = dot(wide[:, : 2 * high.shape[1 - axis]], jnp.concatenate(last, 1 - axis), transposed)
    return jnp.concatenate([one, two[:, :TILE] + two[:, TILE:]], axis=1)


def diagonal_row(matrix):
    rows = lax.broadcasted_iota(jnp.int32, (TILE, TILE), 0)
    columns = lax.broadcasted_iota(jnp.int32, (TILE, TILE), 1)
    parts = []
    for start in range(0, matrix.shape[0], TILE):
        block = matrix[start : start + TILE, start : start + TILE]
        parts.append(jnp.sum(jnp.where(rows == columns, block, 0.0), axis=0, keepdims=True))
    return jnp.concatenate(parts, axis=1)


SMALL = TILE // 2
PACKED_ROWS = 4 * TILE + SMALL + 8


def pack(matrix, out):
    def block(i, j):
        return matrix[i * TILE : (i + 1) * TILE, j * TILE : (j + 1) * TILE]

    rows = lax.broadcasted_iota(jnp.int32, (TILE, TILE), 0)
    columns = lax.broadcasted_iota(jnp.int32, (TILE, TILE), 1)
    for place, (i, j) in enumerate(((0, 1), (0, 2), (1, 2))):
        out[place * TILE : (place + 1) * TILE, :] = block(i, j) + block(j, i).T
    one, two, three = (block(i, i) for i in range(3))
    merged = jnp.where(rows < columns, one + one.T, jnp.where(rows > columns, two + two.T, one))
    out[3 * TILE : 4 * TILE, :] = merged
    whole = jnp.where(rows == columns, three, three + three.T)
    turned = pltpu.roll(whole[SMALL:], SMALL, 1)
    low = (rows > columns)[:SMALL]
    out[4 * TILE : 4 * TILE + SMALL, :] = jnp.where(low, turned, whole[:SMALL])
    row = jnp.sum(jnp.where(rows == columns, two, 0.0), axis=0, keepdims=True)
    last = jnp.sum(jnp.where(rows == columns, three, 0.0), axis=0, keepdims=True)
    first = lax.broadcasted_iota(jnp.int32, (8, TILE), 0) == 0
    out[4 * TILE + SMALL :, :] = jnp.where(first, row, last)


def unpack(packed, out):
    rows = lax.broadcasted_iota(jnp.int32, (TILE, TILE), 0)
    columns = lax.broadcasted_iota(jnp.int32, (TILE, TILE), 1)
    out[...] = jnp.zeros_like(out)
    for place, (i, j) in enumerate(((0, 1), (0, 2), (1, 2))):
        value = packed[place * TILE : (place + 1) * TILE, :]
        out[i * TILE : (i + 1) * TILE, j * TILE : (j + 1) * TILE] = value
    merged = packed[3 * TILE : 4 * TILE, :]
    start = 4 * TILE + SMALL
    row, last = (packed[start : start + 1, :], packed[start + 1 : start + 2, :])
    out[:TILE, :TILE] = jnp.where(rows <= columns, merged, 0.0)
    out[TILE : 2 * TILE, TILE : 2 * TILE] = jnp.where(
        rows > columns, merged, jnp.where(rows == columns, row, 0.0)
    )
    half = packed[4 * TILE : start, :]
    out[2 * TILE : 2 * TILE + SMALL, 2 * TILE :] = jnp.where((rows <= columns)[:SMALL], half, 0.0)
    turned = pltpu.roll(half, SMALL, 1)
    inside = (columns >= SMALL) & (rows > columns)
    value = jnp.where(rows[SMALL:] == columns[SMALL:], last, 0.0)
    out[2 * TILE + SMALL :, 2 * TILE :] = jnp.where(inside[SMALL:], turned, value)


def plane_rows(n, plane):
    start = 2 * n + 16 + 8 * (plane // 3)
    return slice(start, start + 8)


def plane_lanes(plane):
    return slice((plane % 3) * TILE, (plane % 3 + 1) * TILE)


def copy_all(pairs, sems):
    copies = [pltpu.make_async_copy(src, dst, sems.at[i]) for i, (src, dst) in enumerate(pairs)]
    for copy in copies:
        copy.start()
    return copies


def slabs(early, late, isos, lead, maps, step):
    place = lax.axis_index("slab")
    n = early.shape[0]

    @pl.when(place == 0)
    def _():
        state = lead[...]
        for slab, value in enumerate((early, late)):
            parts = split(value)
            state = product(parts, split(state))
            state = product(split(state), parts, True) + isos[slab]
            maps[2 * n + slab : 2 * n + slab + 1, :] = diagonal_row(state)
        maps[n : 2 * n, :] = state

    @pl.when(place != 0)
    def _():
        later = split(late)
        wide = joined(later)
        term = product_joined(wide, split(isos[0]))
        maps[0:n, :] = product_joined(wide, split(early))
        term = product(split(term), later, True) + isos[1]
        maps[n : 2 * n, :] = term
        maps[2 * n : 2 * n + 1, :] = diagonal_row(isos[0])
        maps[2 * n + 1 : 2 * n + 2, :] = diagonal_row(term)
        if step is not None:
            step[...] = early


def other_kernel(
    iso,
    coupling,
    lead,
    cells_in,
    field_in,
    step,
    sent,
    planes,
    own_early,
    own_late,
    own_iso,
    own_lead,
    c_buf,
    g_buf,
    lead_buf,
    sems,
    row,
    cells,
    field,
    more_sems,
):
    place = lax.axis_index("slab")
    core = lax.rem(place, 2)
    n = lead_buf.shape[1]
    sources = []
    for slab in range(2):
        sources.append((coupling.at[slab], c_buf.at[slab]))
        sources.append((iso.at[1 - core, slab], g_buf.at[slab]))
        sources.append((iso.at[core, slab], own_iso.at[slab]))
    sources.append((lead.at[1 - core], lead_buf))
    sources.append((lead.at[core], own_lead))
    waits = copy_all(sources, sems)
    copies = copy_all([(cells_in, cells), (field_in, field)], more_sems)
    steps = []
    for slab in range(2):
        for copy in waits[3 * slab : 3 * slab + 3]:
            copy.wait()
        parts = split(c_buf[slab])
        for buf in (g_buf, own_iso):
            steps.append(product_joined(joined(split(buf[slab])), parts))
    waits[6].wait()
    own_early[...] = steps[1]
    own_late[...] = steps[3]
    slabs(steps[0], steps[2], g_buf, lead_buf, sent, step)
    waits[7].wait()
    for copy in copies:
        copy.wait()
    atoms = cells.shape[1]
    row[...] = jnp.zeros_like(row)
    row[0:1, 0:atoms] = cells[0:1, :].astype(F32)
    row[0:1, HALF : HALF + atoms] = cells[1:2, :].astype(F32)
    rows = lax.broadcasted_iota(jnp.int32, (8, TILE), 0)
    mine = jnp.where(rows == place, row[0:1, :], 0.0)
    sent[2 * n + 8 : 2 * n + 16, 0:TILE] = mine
    planes[REACH * 8 :, :] = mine
    length = field.shape[0]
    even = core == 0
    for plane in range(REACH):
        low, high = (field[plane], field[length - REACH + plane])
        planes[plane * 8 : plane * 8 + 8, :] = jnp.where(even, low, high)
        sent[plane_rows(n, plane), plane_lanes(plane)] = jnp.where(even, high, low)


def own_kernel(planes, early, late, isos, lead, own):
    n = lead.shape[0]
    own[2 * n + 8 : 2 * n + 16, 0:TILE] = planes[REACH * 8 :, :]
    slabs(early[...], late[...], isos, lead, own, None)


def advance(map_ref, state):
    n = map_ref.shape[1]
    composed = split(map_ref[0:n, :])
    term = product(composed, split(state))
    return product(split(term), composed, True) + map_ref[n : 2 * n, :]


def near_far(mine, other):
    core = lax.rem(lax.axis_index("slab"), 2)
    return jnp.where(core == 0, mine, other), jnp.where(core == 0, other, mine)


def relay_kernel(
    own, got, own_step, got_step, field, second, out, stack, parts, wide, cells, one_side, two_side
):
    place, wire = (lax.axis_index("slab"), lax.axis_index("energy"))
    n = own.shape[1]
    length, height, _ = field.shape
    even = lax.rem(place, 2) == 0
    wide[REACH : REACH + length] = field[...]
    for plane in range(REACH):
        one = got[plane_rows(n, plane), plane_lanes(plane)]
        two = second[plane * 8 : plane * 8 + 8, :]
        wide[plane] = jnp.where(even, two, one)
        wide[REACH + length + plane] = jnp.where(even, one, two)
    spot = slice(2 * n + 8, 2 * n + 16)
    cells[...] = own[spot, :TILE] + got[spot, :TILE] + second[REACH * 8 :, :]
    even = lax.rem(wire, 2) == 0
    for plane in range(length + 2 * REACH):
        low, high = (wide[plane, :REACH, :], wide[plane, height - REACH :, :])
        spot = slice(plane * REACH, (plane + 1) * REACH)
        one_side[spot, :] = jnp.where(even, high, low)
        two_side[spot, :] = jnp.where(even, low, high)

    @pl.when(place == 0)
    def _():
        pack(advance(got, own[n : 2 * n, :]), out)

    @pl.when(place == 1)
    def _():
        pack(advance(own, got[n : 2 * n, :]), out)

    @pl.when(place >= 2)
    def _():
        near_step, far_step = near_far(own_step[...], got_step[...])
        near_map, far_map = near_far(own[0:n, :], got[0:n, :])
        far = jnp.concatenate([far_step, far_map], axis=0)
        both = product_joined(joined(split(far)), split(near_map))
        for number, value in enumerate((near_step, near_map, both[:n], both[n:])):
            rows = slice(number * n, (number + 1) * n)
            stack[rows, :] = value
            high, low = split(value)
            parts[rows, :] = jnp.concatenate(
                [high, low, high[:, : n - TILE], low[:, : n - TILE], high[:, : n - TILE]], axis=1
            )


def pass_kernel(turn, packed, own, got, out, state):
    place = lax.axis_index("slab")
    for core, (near, far) in enumerate(((own, got), (got, own))):

        @pl.when(place == 2 * turn + core)
        def _():
            unpack(packed, state)
            state[...] = advance(near, state[...])
            pack(advance(far, state[...]), out)


def known_kernel(
    pairs, weight_ref, group_ref, orbital_atom, member, own, got, own_step, got_step, fold, weights
):
    place = lax.axis_index("slab")
    core = lax.rem(place, 2)
    pair_rows = lax.broadcasted_iota(jnp.int32, (pairs, TILE), 0)
    mine_weight = jnp.where(core == 0, weight_ref[:, 0:1], weight_ref[:, 1:2])
    mine_group = jnp.where(core == 0, group_ref[:, 0:1], group_ref[:, 1:2])
    groups = weights.shape[0] // (2 * pairs)
    for half in range(2):
        for group in range(groups):
            weight = jnp.where(mine_group == group, mine_weight, 0.0)
            start = (half * groups + group) * pairs
            weights[start : start + pairs, :] = jnp.where(
                pair_rows == place - core + half, jnp.broadcast_to(weight, (pairs, TILE)), 0.0
            )
    n = own.shape[1]
    atoms = lax.broadcasted_iota(jnp.int32, (TILE, n), 0)
    spots = (atoms == orbital_atom[...]).astype(BF16)
    _, far_step = near_far(own_step[...], got_step[...])
    _, far_map = near_far(own[0:n, :], got[0:n, :])
    near_source, _ = near_far(own[n : 2 * n, :], got[n : 2 * n, :])
    far = jnp.concatenate([far_step, far_map], axis=0)
    both = product_joined(joined(split(far)), split(near_source))
    near_rows, far_rows = near_far(own[2 * n : 2 * n + 2, :], got[2 * n : 2 * n + 2, :])
    rest = jnp.concatenate([near_rows, far_rows, jnp.zeros((4, n), F32)], axis=0)
    total = jnp.zeros((8, TILE), F32)
    for _ in range(3):
        piece = rest.astype(BF16)
        total = total + dot(piece, spots, True)
        rest = rest - piece.astype(F32)
    fold[...] = total
    for number in range(2):
        rows = slice(number * n, (number + 1) * n)
        value = jnp.sum(far[rows] * both[rows], axis=1, keepdims=True) * member[...]
        fold[2 + number : 3 + number, :] += jnp.sum(value, axis=0, keepdims=True)


def density_kernel(
    pairs,
    member,
    packed,
    stack,
    wide,
    known,
    weights,
    extra,
    out,
    state,
    fold,
):
    place = lax.axis_index("slab")
    n = state.shape[0]
    fold[...] = known[...]

    @pl.when(place >= 2)
    def _():
        unpack(packed, state)
        high, low = split(state[...])
        cut = n - TILE
        corner = [x[:cut, :cut] for x in (high, high, low)]
        one = dot(wide[:, 2 * n :], jnp.concatenate(corner, axis=0), False)
        last_high, last_low = (high[:, cut:], low[:, cut:])
        last = [
            jnp.concatenate([last_high, last_low], axis=1),
            jnp.concatenate([last_high, jnp.zeros_like(last_high)], axis=1),
        ]
        two = dot(wide[:, : 2 * n], jnp.concatenate(last, axis=0), False)
        both = jnp.concatenate([one, two[:, :TILE] + two[:, TILE:]], axis=1)
        for number in range(4):
            rows = slice(number * n, (number + 1) * n)
            value = jnp.sum(stack[rows, :] * both[rows], axis=1, keepdims=True) * member[...]
            fold[number : number + 1, :] += jnp.sum(value, axis=0, keepdims=True)

    plain = fold[...]
    turned = pltpu.roll(plain, HALF, 1)
    rows = out.shape[0] - extra.shape[0]
    values = [plain[2 * i : 2 * i + 1, :] + turned[2 * i + 1 : 2 * i + 2, :] for i in range(2)]
    out[:rows, :] = weights[:rows, :] * values[0] + weights[rows:, :] * values[1]
    out[rows:, :] = extra[...]


def local_call(kernel, shapes, scratch, specs, name, limit, flops, *operands):
    spaces = {"v": pltpu.VMEM, "s": pltpu.SMEM, "h": pltpu.HBM}
    single = not isinstance(shapes, tuple)
    vmem = pl.BlockSpec(memory_space=pltpu.VMEM)
    return pl.pallas_call(
        kernel,
        out_shape=shapes,
        in_specs=[pl.BlockSpec(memory_space=spaces[spec]) for spec in specs],
        out_specs=vmem if single else (vmem,) * len(shapes),
        scratch_shapes=scratch,
        compiler_params=pltpu.CompilerParams(vmem_limit_bytes=limit * 2**20),
        cost_estimate=pl.CostEstimate(flops=flops, bytes_accessed=2**20, transcendentals=0),
        name=name,
    )(*operands)


def shifted_pair(x, axis):
    size = x.shape[axis]
    before, after = (pltpu.roll(x, 1, axis), pltpu.roll(x, size - 1, axis))
    if axis == x.ndim - 1:
        lanes = lax.broadcasted_iota(jnp.int32, x.shape, axis)
        before = jnp.where(lanes == 0, 0.0, before)
        after = jnp.where(lanes == size - 1, 0.0, after)
    return before, after


def neighbours(x):
    centre = x[1:-1]
    up, down = shifted_pair(centre, 1)
    left, right = shifted_pair(centre, 2)
    return (x[2:] + x[:-2]) + (up + down) + (left + right)


def differences(x):
    centre = x[1:-1]
    up, down = shifted_pair(centre, 1)
    left, right = shifted_pair(centre, 2)
    along = (x[2:] - centre) + (x[:-2] - centre)
    across = (up - centre) + (down - centre)
    deep = (left - centre) + (right - centre)
    return along + (across + deep)


def grid_mask(shape, margin, length, rows, place, devices, wire, wires):
    planes = lax.broadcasted_iota(jnp.int32, shape, 0)
    row = lax.broadcasted_iota(jnp.int32, shape, 1)
    low_x = jnp.where(place == 0, margin, 0)
    high_x = jnp.where(place == devices - 1, margin + length, shape[0])
    low_y = jnp.where(wire == 0, rows, 0)
    high_y = jnp.where(wire == wires - 1, 2 * rows, shape[1])
    inside = (planes >= low_x) & (planes < high_x) & (row >= low_y) & (row < high_y)
    return inside.astype(F32)


def three_parts(x):
    parts = []
    for _ in range(3):
        parts.append(x.astype(BF16))
        x = x - parts[-1].astype(F32)
    return parts


def coordinates(cell, rows_y, depth):
    z_part = cell - depth * jnp.floor(cell * (1.0 / depth))
    plane = jnp.floor(cell * (1.0 / depth))
    x_part = jnp.floor(plane * (1.0 / rows_y))
    return x_part, plane - rows_y * x_part, z_part


WALKS = ((0, 1),), ((1, 1),), ((0, 2), (2, 1)), ((1, 3), (3, 1)), ((0, 6), (2, 4), (4, 1)), ((1, 10), (3, 5), (5, 1))
FACTORIAL = (1.0, 1.0, 2.0, 6.0, 24.0, 120.0)


def walk_counts(here, there, length):
    apart = jnp.abs(here - there)
    low = here + there + 2.0
    high = 2.0 * length - here - there
    at = []
    for steps in range(6):
        value = (apart == steps).astype(F32)
        if steps >= 2:
            value = value - (low == steps).astype(F32) - (high == steps).astype(F32)
        at.append(value)
    counts = []
    for steps, terms in enumerate(WALKS):
        total = None
        for distance, count in terms:
            term = at[distance] * (count / FACTORIAL[steps])
            total = term if total is None else total + term
        counts.append(total)
    return counts


def convolved(left, right):
    result = []
    for steps in range(6):
        total = left[0] * right[steps]
        for part in range(1, steps + 1):
            total = total + left[part] * right[steps - part]
        result.append(total)
    return result


def moments_kernel(devices, wires, own, field, one_beside, two_beside, cells, out, wide_field, whole_field):
    place, wire = (lax.axis_index("slab"), lax.axis_index("energy"))
    planes, rows, depth = field.shape
    length = planes - 2 * REACH
    width_x = length // 2
    atoms = cells.shape[1]
    grid_y = rows * wires
    pairs = devices
    n = own.shape[1]
    even = lax.rem(wire, 2) == 0
    whole_field[...] = jnp.zeros_like(whole_field)
    whole_field[:, rows : 2 * rows, :] = field[...]
    for plane in range(planes):
        spot = slice(plane * REACH, (plane + 1) * REACH)
        one, two = (one_beside[spot, :], two_beside[spot, :])
        whole_field[plane, rows - REACH : rows, :] = jnp.where(even, two, one)
        whole_field[plane, 2 * rows : 2 * rows + REACH, :] = jnp.where(even, one, two)
    whole = (planes, 3 * rows, depth)
    mask = grid_mask(whole, REACH, length, rows, place, devices, wire, wires)
    source = jnp.where(mask > 0, whole_field[...], 0.0)
    margin = ITERS - 1
    wide_field[...] = source[REACH - margin : REACH + length + margin]

    def inner(x):
        extra = (x.shape[0] - length) // 2
        return x[extra : extra + length, rows : 2 * rows]

    chain = [source]
    for step in range(1, 6):
        chain.append(neighbours(chain[-1]) * mask[step : planes - step])
    blocks = [inner(x) for x in chain]
    near = source[2:-2]
    other = [near]
    for step in range(1, 4):
        other.append(differences(other[-1]) * mask[2 + step : planes - 2 - step])
    other = [inner(x) for x in other]
    lanes = lax.broadcasted_iota(jnp.int32, (1, depth), 1)
    sums = jnp.zeros((1, depth), F32)
    for base, fields in enumerate((blocks, other)):
        for steps in range(6):
            part = jnp.sum(fields[steps // 2] * fields[(steps + 1) // 2], axis=0)
            part = jnp.sum(jnp.sum(part, axis=1, keepdims=True), axis=0, keepdims=True)
            sums = jnp.where(lanes == atoms + 6 * base + steps, part, sums)
    out[...] = jnp.zeros_like(out)
    mine = own[2 * n + 8 : 2 * n + 16, :depth]
    mine = jnp.sum(mine, axis=0, keepdims=True)
    lane = lax.broadcasted_iota(jnp.int32, (1, depth), 1)
    odd = (lane >= HALF).astype(F32)
    used = lax.rem(lane, HALF) < atoms
    x_part, y_part, z_part = coordinates(mine, grid_y, depth)
    start = (wire * rows).astype(F32)
    ours = used & (y_part >= start) & (y_part < start + rows)
    at_row = jnp.where(ours, (x_part + width_x * odd) * rows + y_part - start, -1.0)
    cell_rows = length * rows
    row_iota = lax.broadcasted_iota(jnp.int32, (cell_rows, depth), 0).astype(F32)
    deep_iota = lax.broadcasted_iota(jnp.int32, (depth, depth), 0).astype(F32)
    at_rows = (row_iota == at_row).astype(F32)
    at_deep = (deep_iota == z_part).astype(BF16)
    for steps, block in enumerate(blocks):
        value = jnp.zeros((cell_rows, depth), F32)
        for part in three_parts(block.reshape(cell_rows, depth)):
            value = value + dot(part, at_deep, False)
        value = jnp.sum(value * at_rows, axis=0, keepdims=True)
        out[pl.ds(steps * pairs + place, 1), :] = value
    out[0:1, :] += sums


def atoms_kernel(
    devices,
    wires,
    length,
    charge_ref,
    orbital_atom,
    some_cells,
    other_cells,
    walks,
    row_hot,
    deep_hot,
    member,
    charges,
):
    place, wire = (lax.axis_index("slab"), lax.axis_index("energy"))
    rows, depth = some_cells.shape
    width_x = length // 2
    atoms = walks.shape[1] // (2 * devices)
    grid_y = rows * wires
    pairs = devices
    n = orbital_atom.shape[1]
    start = (wire * rows).astype(F32)
    for group in range(charges.shape[0] // pairs):
        charges[group * pairs : (group + 1) * pairs, :] = jnp.broadcast_to(
            charge_ref[:, group : group + 1], (pairs, depth)
        )
    cells = jnp.maximum(some_cells[...], other_cells[...])
    spots = lax.broadcasted_iota(jnp.int32, (TILE, n), 0) == orbital_atom[...]
    spots = spots.astype(F32)
    for first in range(0, n, TILE):
        member[first : first + TILE, :] = spots[:, first : first + TILE].T
    row_cells = cells
    row_x, row_y, row_z = coordinates(row_cells, grid_y, depth)
    padded = jnp.concatenate([row_cells, jnp.zeros((depth - 8, depth), F32)], axis=0)
    column_x, column_y, column_z = coordinates(padded.T, grid_y, depth)
    row_lane = lax.broadcasted_iota(jnp.int32, (8, depth), 1)
    next_x, next_y, next_z = [jnp.concatenate([v[1:], v[:1]], axis=0) for v in (row_x, row_y, row_z)]

    def turned(now, later, step_now, step_later):
        value = jnp.where(row_lane >= HALF, now + step_now, later + step_later)
        return pltpu.roll(value, HALF, 1)

    even_x = row_x + width_x * (row_lane >= HALF).astype(F32)
    odd_x, odd_y, odd_z = (
        turned(row_x, next_x, 0.0, float(width_x)),
        turned(row_y, next_y, 0.0, 0.0),
        turned(row_z, next_z, 0.0, 0.0),
    )
    for slab in range(2 * pairs):
        pair, side = (slab // 2, slab % 2)
        base = float(slab * width_x)
        if side:
            there = (odd_x, odd_y, odd_z)
        else:
            there = (even_x, row_y, row_z)
        there = [v[pair : pair + 1, :] for v in there]
        here = [
            v[side * HALF : side * HALF + atoms, pair : pair + 1]
            for v in (column_x, column_y, column_z)
        ]
        shape = (atoms, depth)
        sizes = (2 * pairs * width_x, grid_y, depth)
        axes = []
        for axis in range(3):
            shift = base if axis == 0 else 0.0
            axes.append(
                walk_counts(
                    jnp.broadcast_to(here[axis] + shift, shape),
                    jnp.broadcast_to(there[axis] + shift, shape),
                    float(sizes[axis]),
                )
            )
        total = convolved(convolved(axes[0], axes[1]), axes[2])
        for steps in range(6):
            walks[steps, slab * atoms : (slab + 1) * atoms, :] = total[steps] * FACTORIAL[steps]
    wide = length + 4
    first_x = (place * length - 2).astype(F32)
    first_y = start - rows
    count = wide * 3 * rows
    rows_iota = lax.broadcasted_iota(jnp.int32, (count, depth), 0).astype(F32)
    used_row = lax.rem(row_lane, HALF) < atoms
    for pair in range(pairs):
        x_at = even_x[pair : pair + 1, :] + float(2 * pair * width_x) - first_x
        y_at = row_y[pair : pair + 1, :] - first_y
        good = (x_at >= 0) & (x_at < wide) & (y_at >= 0) & (y_at < 3 * rows) & used_row[0:1, :]
        target = jnp.where(good, x_at * (3 * rows) + y_at, -1.0)
        row_hot[:, pair * depth : (pair + 1) * depth] = (rows_iota == target).astype(BF16)
        z_at = column_z[:, pair : pair + 1]
        lanes_z = lax.broadcasted_iota(jnp.int32, (depth, depth), 1).astype(F32)
        deep_hot[pair * depth : (pair + 1) * depth, :] = (lanes_z == z_at).astype(F32)


def total_of(x):
    return jnp.sum(jnp.sum(x, axis=1, keepdims=True), axis=0, keepdims=True)


def quadratic_form(poly, moments, shift):
    total = None
    for i, one in enumerate(poly):
        for j, two in enumerate(poly):
            if j < i:
                continue
            term = one * two * moments[i + j + shift] * (1.0 if i == j else 2.0)
            total = term if total is None else total + term
    return total


def finish_kernel(
    devices,
    wires,
    atoms,
    payload,
    walks,
    row_hot,
    deep_hot,
    charges,
    field,
    density,
    potential,
):
    place, wire = (lax.axis_index("slab"), lax.axis_index("energy"))
    length, rows, depth = potential.shape
    pairs = devices
    groups = density.shape[0]
    held = charges[...] * payload[: groups * pairs, :]
    charge = held[:pairs]
    for group in range(1, groups):
        charge = charge + held[group * pairs : (group + 1) * pairs]
    for group in range(groups):
        value = payload[pl.ds(group * pairs + place, 1), :]
        density[group, 0:1, :] = value[:, :atoms]
        density[group, 1:2, :] = pltpu.roll(value, HALF, 1)[:, :atoms]
    square = jnp.concatenate([charge, jnp.zeros((depth - pairs, depth), F32)], axis=0)
    columns = square.T
    later = jnp.concatenate([charge[1:], jnp.zeros((1, depth), F32)], axis=0)
    lanes = lax.broadcasted_iota(jnp.int32, (pairs, depth), 1)
    even_row = jnp.where(lanes >= HALF, 2.0 * charge, charge)
    odd_row = pltpu.roll(jnp.where(lanes >= HALF, charge, 2.0 * later), HALF, 1)
    totals = [None] * 6
    for slab in range(2 * pairs):
        pair, side = (slab // 2, slab % 2)
        row = (odd_row if side else even_row)[pair : pair + 1, :]
        column = columns[side * HALF : side * HALF + atoms, pair : pair + 1]
        outer = column * row
        for steps in range(6):
            term = walks[steps, slab * atoms : (slab + 1) * atoms, :] * outer
            totals[steps] = term if totals[steps] is None else totals[steps] + term
    base = groups * pairs
    crossed = []
    for steps in range(6):
        cross = 2.0 * charge * payload[base + steps * pairs : base + (steps + 1) * pairs, :]
        parts = [totals[steps][i : i + 8] for i in range(0, atoms, 8)]
        if pairs < 8:
            cross = jnp.concatenate([cross, jnp.zeros((8 - pairs, depth), F32)], axis=0)
        parts.append(cross)
        while len(parts) > 1:
            parts = [sum(parts[i : i + 2][1:], parts[i]) for i in range(0, len(parts), 2)]
        crossed.append(total_of(parts[0]))
    lane = lax.broadcasted_iota(jnp.int32, (1, depth), 1)
    row = payload[base : base + 1, :]
    sums = [
        jnp.sum(jnp.where(lane == atoms + i, row, 0.0), axis=1, keepdims=True) for i in range(12)
    ]
    plain = [sums[steps] + crossed[steps] for steps in range(6)]
    moved = []
    for steps in range(6):
        value = sums[6 + steps]
        binomial = 1
        for part in range(steps, -1, -1):
            value = value + (binomial * (-6.0) ** (steps - part)) * crossed[part]
            binomial = binomial * part // (steps - part + 1)
        moved.append(value)
    smooth = plain[1] > 3.5 * plain[0]
    level = jnp.where(smooth, 0.5, 6.5)
    moments = [jnp.where(smooth, two, one) for one, two in zip(plain, moved)]
    residual, direction = ([jnp.ones_like(level)], [jnp.ones_like(level)])
    norm = moments[0]
    alphas, betas = ([], [])
    for turn in range(ITERS):
        energy = level * quadratic_form(direction, moments, 0) - quadratic_form(direction, moments, 1)
        alpha = jnp.clip(norm / energy, 1.0 / 12.5, 2.0)
        alphas.append(alpha)
        if turn + 1 == ITERS:
            break
        longer = residual + [jnp.zeros_like(level)]
        for i, value in enumerate(direction):
            longer[i] = longer[i] - alpha * level * value
            longer[i + 1] = longer[i + 1] + alpha * value
        residual = longer
        following = quadratic_form(residual, moments, 0)
        beta = jnp.clip(following / norm, 0.0, 25.0)
        betas.append(beta)
        norm = following
        direction = [
            value + beta * direction[i] if i < len(direction) else value
            for i, value in enumerate(residual)
        ]
    pieces = [[], [], []]
    for pair in range(pairs):
        hot = deep_hot[pair * depth : (pair + 1) * depth, :]
        for place_in, piece in enumerate(three_parts(columns[:, pair : pair + 1] * hot)):
            pieces[place_in].append(piece)
    spread = jnp.concatenate([jnp.concatenate(piece, axis=0) for piece in pieces], axis=1)
    placed = dot(row_hot[...], spread, False)
    placed = placed[:, :depth] + (placed[:, depth : 2 * depth] + placed[:, 2 * depth :])
    margin = ITERS - 1
    wide = (length + 2 * margin, 3 * rows, depth)
    mask = grid_mask(wide, margin, length, rows, place, devices, wire, wires)
    source = field[...] + placed.reshape(wide)
    residual, direction = (source, source)
    total = alphas[0] * source[margin:-margin, rows : 2 * rows]
    for turn in range(ITERS - 1):
        image = 6.5 * direction[1:-1] - neighbours(direction)
        inner_mask = mask[turn + 1 : wide[0] - turn - 1]
        residual = (residual[1:-1] - alphas[turn] * image) * inner_mask
        direction = residual + betas[turn] * direction[1:-1]
        extra = margin - turn - 1
        block = direction[extra : extra + length, rows : 2 * rows]
        total = total + alphas[turn + 1] * block
    potential[...] = total


def hop(count, turn):
    moves = {i: i for i in range(count)}
    for core in range(2):
        here, there = (2 * turn - 2 + core, 2 * turn + core)
        moves[here], moves[there] = (there, here)
    return sorted(moves.items())


def pairs_of(count):
    return [(i, i ^ 1) for i in range(count)]


def total_over(value, axis, strides):
    size = 1
    for name in axis if isinstance(axis, tuple) else (axis,):
        size *= lax.axis_size(name)
    got = [lax.ppermute(value, axis, [(i, i ^ k) for i in range(size)]) for k in strides]
    if len(got) == 1:
        return value + got[0]
    return (value + got[0]) + (got[1] + got[2])


def total_over_all(value):
    size, slabs = (lax.axis_size("energy") * lax.axis_size("slab"), lax.axis_size("slab"))
    value = total_over(value, "slab", (1,))
    strides = [1 << i for i in range(1, size.bit_length() - 1)]
    far = [stride for stride in strides if stride > slabs // 2]
    near = [stride for stride in strides if stride <= slabs // 2]
    order = far[:2] + near + far[2:]
    while order:
        one, *rest = order[:2]
        value = total_over(value, BOTH, (one, *rest, *[one + two for two in rest]))
        order = order[2:]
    return value


def inner_pairs(count, slabs):
    moves = []
    for i in range(count * slabs):
        wire, place = divmod(i, slabs)
        if wire in (0, count - 1):
            moves.append((i, i ^ 1))
        else:
            moves.append((i, (wire + 1 if wire % 2 else wire - 1) * slabs + place))
    return moves


def neighbour_turn(count):
    return [(i, (i + 1) % count if i % 2 else (i - 1) % count) for i in range(count)]


def on_device(
    green_iso,
    coupling,
    lead_green,
    energy_weight,
    energy_group,
    group_charge,
    orbital_atom,
    atom_cell,
    doping,
):
    devices, wires = (lax.axis_size("slab"), lax.axis_size("energy"))
    groups = group_charge.shape[0]
    atoms = atom_cell.shape[1]
    n = lead_green.shape[-1]
    length, rows, depth = doping.shape
    shape = jax.ShapeDtypeStruct
    orbital_row = orbital_atom.reshape(1, n)
    maps = shape((2 * n + 32, n), F32)
    edge_rows = REACH * rows + 8
    held = [
        pltpu.with_memory_space_constraint(x, pltpu.HBM)
        for x in (green_iso, coupling, lead_green, atom_cell, doping)
    ]
    matrix = shape((n, n), F32)
    two = shape((2, n, n), F32)
    sent_step, sent, edge, own_step, own_late, own_iso, own_lead = local_call(
        other_kernel,
        (matrix, maps, shape((edge_rows, depth), F32), matrix, matrix, two, matrix),
        [
            pltpu.VMEM((2, n, n), F32),
            pltpu.VMEM((2, n, n), F32),
            pltpu.VMEM((n, n), F32),
            pltpu.SemaphoreType.DMA((8,)),
            pltpu.VMEM((8, TILE), F32),
            pltpu.VMEM(atom_cell.shape, jnp.int32),
            pltpu.VMEM(doping.shape, F32),
            pltpu.SemaphoreType.DMA((2,)),
        ],
        "hhhhh",
        "other",
        28,
        48 * n**3,
        *held,
    )
    got = lax.ppermute(sent, "slab", pairs_of(devices))
    second = lax.ppermute(edge, "slab", neighbour_turn(devices))
    own = local_call(
        own_kernel,
        maps,
        [],
        "vvvvv",
        "own",
        24,
        2**31,
        edge,
        own_step,
        own_late,
        own_iso,
        own_lead,
    )
    side = shape((-(-REACH * (length + 2 * REACH) // 8) * 8, depth), F32)
    got_step = lax.ppermute(sent_step, "slab", pairs_of(devices))
    passed, stack, stack_parts, wide_block, cells, one_side, two_side = local_call(
        relay_kernel,
        (
            shape((PACKED_ROWS, TILE), F32),
            shape((4 * n, n), F32),
            shape((4 * n, 5 * n - 3 * TILE), BF16),
            shape((length + 2 * REACH, rows, depth), F32),
            shape((8, depth), F32),
            side,
            side,
        ),
        [],
        "vvvvvv",
        "relay",
        28,
        12 * n**3,
        own,
        got,
        own_step,
        got_step,
        doping,
        second,
    )
    packed = lax.ppermute(passed, "slab", hop(devices, 1))
    one_beside = lax.ppermute(one_side, "energy", pairs_of(wires))
    two_beside = lax.ppermute(two_side, BOTH, inner_pairs(wires, devices))
    other_cells = lax.ppermute(cells, "slab", pairs_of(devices))
    if devices > 4:
        other_cells = lax.psum(own[2 * n + 8 : 2 * n + 16, :depth], "slab")
    wide = (length + 2 * ITERS - 2, 3 * rows, depth)
    walks, row_hot, deep_hot, member, charges = local_call(
        functools.partial(atoms_kernel, devices, wires, length),
        (
            shape((6, 2 * devices * atoms, depth), F32),
            shape((wide[0] * wide[1], devices * depth), BF16),
            shape((devices * depth, depth), F32),
            shape((n, TILE), F32),
            shape((groups * devices, depth), F32),
        ),
        [],
        "vvvv",
        "atoms",
        28,
        2**29,
        group_charge.reshape(1, groups),
        orbital_row,
        cells,
        other_cells,
    )
    extra, wide_field = local_call(
        functools.partial(moments_kernel, devices, wires),
        (shape((6 * devices, depth), F32), shape(wide, F32)),
        [pltpu.VMEM((length + 2 * REACH, 3 * rows, depth), F32)],
        "vvvvv",
        "moments",
        20,
        2**26,
        own,
        wide_block,
        one_beside,
        two_beside,
        atom_cell,
    )
    known, weights = local_call(
        functools.partial(known_kernel, devices),
        (shape((8, TILE), F32), shape((2 * groups * devices, TILE), F32)),
        [],
        "vvvvvvvv",
        "known",
        24,
        2**28,
        energy_weight.reshape(1, -1),
        energy_group.reshape(1, -1),
        orbital_row,
        member,
        own,
        got,
        own_step,
        got_step,
    )
    for turn in range(1, devices // 2 - 1):
        passed = local_call(
            functools.partial(pass_kernel, turn),
            shape((PACKED_ROWS, TILE), F32),
            [pltpu.VMEM((n, n), F32)],
            "vvv",
            "pass_on",
            20,
            24 * n**3,
                packed,
            own,
            got,
        )
        arrived = lax.ppermute(passed, "slab", hop(devices, turn + 1))
        packed = jnp.where(lax.axis_index("slab") // 2 == turn + 1, arrived, packed)
    payload = local_call(
        functools.partial(density_kernel, devices),
        shape(((groups + 6) * devices, TILE), F32),
        [pltpu.VMEM((n, n), F32), pltpu.VMEM((8, TILE), F32)],
        "vvvvvvv",
        "density",
        20,
        24 * n**3,
        member,
        packed,
        stack,
        stack_parts,
        known,
        weights,
        extra,
    )
    payload = total_over_all(payload)
    return local_call(
        functools.partial(finish_kernel, devices, wires, atoms),
        (shape((groups, 2, atoms), F32), shape(doping.shape, F32)),
        [],
        "vvvvvv",
        "finish",
        28,
        2**29,
        payload,
        walks,
        row_hot,
        deep_hot,
        charges,
        wide_field,
    )


def solution(mesh):
    in_specs = (
        P("energy", "slab", None, None),
        P("slab", None, None),
        P("energy", None, None),
        P("energy"),
        P("energy"),
        P(),
        P(),
        P("slab", None),
        P("slab", "energy", None),
    )
    out_specs = (P(None, "slab", None), P("slab", "energy", None))
    return jax.shard_map(
        on_device, mesh=mesh, in_specs=in_specs, out_specs=out_specs, check_vma=False
    )
```

```python
import functools

import jax
import jax.numpy as jnp
from jax import lax
from jax.experimental import pallas as pl
from jax.experimental.pallas import tpu as pltpu
from jax.sharding import PartitionSpec as P

ITERS = 3
F32 = jnp.float32
BF16 = jnp.bfloat16
TILE = 128
BOTH = ("energy", "slab")
REACH = 5
HALF = 64


def split(a):
    high = a.astype(BF16)
    return high, (a - high.astype(F32)).astype(BF16)


def dot(a, b, transposed):
    dims = (((1,), (1 if transposed else 0,)), ((), ()))
    return lax.dot_general(a, b, dims, preferred_element_type=F32)


def product(left, right, transposed=False):
    n = right[0].shape[0 if transposed else 1]
    wide = dot(left[0], jnp.concatenate(right, 0 if transposed else 1), transposed)
    return wide[:, :n] + (wide[:, n:] + dot(left[1], right[0], transposed))


def joined(left):
    return jnp.concatenate([left[0], left[1], left[0]], axis=1)


def product_joined(wide, right, transposed=False):
    high, low = right
    axis = 0 if transposed else 1
    n = high.shape[axis]
    cut = n - TILE

    def part(x, start, stop):
        return lax.slice_in_dim(x, start, stop, axis=axis)

    first = [part(x, 0, cut) for x in (high, high, low)]
    last_high, last_low = (part(high, cut, n), part(low, cut, n))
    last = [
        jnp.concatenate([last_high, last_low], axis),
        jnp.concatenate([last_high, jnp.zeros_like(last_high)], axis),
    ]
    one = dot(wide, jnp.concatenate(first, 1 - axis), transposed)
    two = dot(wide[:, : 2 * high.shape[1 - axis]], jnp.concatenate(last, 1 - axis), transposed)
    return jnp.concatenate([one, two[:, :TILE] + two[:, TILE:]], axis=1)


def diagonal_row(matrix):
    rows = lax.broadcasted_iota(jnp.int32, (TILE, TILE), 0)
    columns = lax.broadcasted_iota(jnp.int32, (TILE, TILE), 1)
    parts = []
    for start in range(0, matrix.shape[0], TILE):
        block = matrix[start : start + TILE, start : start + TILE]
        parts.append(jnp.sum(jnp.where(rows == columns, block, 0.0), axis=0, keepdims=True))
    return jnp.concatenate(parts, axis=1)


SMALL = TILE // 2
PACKED_ROWS = 4 * TILE + SMALL + 8


def pack(matrix, out):
    def block(i, j):
        return matrix[i * TILE : (i + 1) * TILE, j * TILE : (j + 1) * TILE]

    rows = lax.broadcasted_iota(jnp.int32, (TILE, TILE), 0)
    columns = lax.broadcasted_iota(jnp.int32, (TILE, TILE), 1)
    for place, (i, j) in enumerate(((0, 1), (0, 2), (1, 2))):
        out[place * TILE : (place + 1) * TILE, :] = block(i, j) + block(j, i).T
    one, two, three = (block(i, i) for i in range(3))
    merged = jnp.where(rows < columns, one + one.T, jnp.where(rows > columns, two + two.T, one))
    out[3 * TILE : 4 * TILE, :] = merged
    whole = jnp.where(rows == columns, three, three + three.T)
    turned = pltpu.roll(whole[SMALL:], SMALL, 1)
    low = (rows > columns)[:SMALL]
    out[4 * TILE : 4 * TILE + SMALL, :] = jnp.where(low, turned, whole[:SMALL])
    row = jnp.sum(jnp.where(rows == columns, two, 0.0), axis=0, keepdims=True)
    last = jnp.sum(jnp.where(rows == columns, three, 0.0), axis=0, keepdims=True)
    first = lax.broadcasted_iota(jnp.int32, (8, TILE), 0) == 0
    out[4 * TILE + SMALL :, :] = jnp.where(first, row, last)


def unpack(packed, out):
    rows = lax.broadcasted_iota(jnp.int32, (TILE, TILE), 0)
    columns = lax.broadcasted_iota(jnp.int32, (TILE, TILE), 1)
    out[...] = jnp.zeros_like(out)
    for place, (i, j) in enumerate(((0, 1), (0, 2), (1, 2))):
        value = packed[place * TILE : (place + 1) * TILE, :]
        out[i * TILE : (i + 1) * TILE, j * TILE : (j + 1) * TILE] = value
    merged = packed[3 * TILE : 4 * TILE, :]
    start = 4 * TILE + SMALL
    row, last = (packed[start : start + 1, :], packed[start + 1 : start + 2, :])
    out[:TILE, :TILE] = jnp.where(rows <= columns, merged, 0.0)
    out[TILE : 2 * TILE, TILE : 2 * TILE] = jnp.where(
        rows > columns, merged, jnp.where(rows == columns, row, 0.0)
    )
    half = packed[4 * TILE : start, :]
    out[2 * TILE : 2 * TILE + SMALL, 2 * TILE :] = jnp.where((rows <= columns)[:SMALL], half, 0.0)
    turned = pltpu.roll(half, SMALL, 1)
    inside = (columns >= SMALL) & (rows > columns)
    value = jnp.where(rows[SMALL:] == columns[SMALL:], last, 0.0)
    out[2 * TILE + SMALL :, 2 * TILE :] = jnp.where(inside[SMALL:], turned, value)


def plane_rows(n, plane):
    start = 2 * n + 16 + 8 * (plane // 3)
    return slice(start, start + 8)


def plane_lanes(plane):
    return slice((plane % 3) * TILE, (plane % 3 + 1) * TILE)


def copy_all(pairs, sems):
    copies = [pltpu.make_async_copy(src, dst, sems.at[i]) for i, (src, dst) in enumerate(pairs)]
    for copy in copies:
        copy.start()
    return copies


def slabs(early, late, isos, lead, maps, step):
    place = lax.axis_index("slab")
    n = early.shape[0]

    @pl.when(place == 0)
    def _():
        state = lead[...]
        for slab, value in enumerate((early, late)):
            parts = split(value)
            state = product(parts, split(state))
            state = product(split(state), parts, True) + isos[slab]
            maps[2 * n + slab : 2 * n + slab + 1, :] = diagonal_row(state)
        maps[n : 2 * n, :] = state

    @pl.when(place != 0)
    def _():
        later = split(late)
        wide = joined(later)
        term = product_joined(wide, split(isos[0]))
        maps[0:n, :] = product_joined(wide, split(early))
        term = product(split(term), later, True) + isos[1]
        maps[n : 2 * n, :] = term
        maps[2 * n : 2 * n + 1, :] = diagonal_row(isos[0])
        maps[2 * n + 1 : 2 * n + 2, :] = diagonal_row(term)
        if step is not None:
            step[...] = early


def other_kernel(
    iso,
    coupling,
    lead,
    cells_in,
    field_in,
    step,
    sent,
    planes,
    own_early,
    own_late,
    own_iso,
    own_lead,
    c_buf,
    g_buf,
    lead_buf,
    sems,
    row,
    cells,
    field,
    more_sems,
):
    place = lax.axis_index("slab")
    core = lax.rem(place, 2)
    n = lead_buf.shape[1]
    sources = []
    for slab in range(2):
        sources.append((coupling.at[slab], c_buf.at[slab]))
        sources.append((iso.at[1 - core, slab], g_buf.at[slab]))
        sources.append((iso.at[core, slab], own_iso.at[slab]))
    sources.append((lead.at[1 - core], lead_buf))
    sources.append((lead.at[core], own_lead))
    waits = copy_all(sources, sems)
    copies = copy_all([(cells_in, cells), (field_in, field)], more_sems)
    steps = []
    for slab in range(2):
        for copy in waits[3 * slab : 3 * slab + 3]:
            copy.wait()
        parts = split(c_buf[slab])
        for buf in (g_buf, own_iso):
            steps.append(product_joined(joined(split(buf[slab])), parts))
    waits[6].wait()
    own_early[...] = steps[1]
    own_late[...] = steps[3]
    slabs(steps[0], steps[2], g_buf, lead_buf, sent, step)
    waits[7].wait()
    for copy in copies:
        copy.wait()
    atoms = cells.shape[1]
    row[...] = jnp.zeros_like(row)
    row[0:1, 0:atoms] = cells[0:1, :].astype(F32)
    row[0:1, HALF : HALF + atoms] = cells[1:2, :].astype(F32)
    rows = lax.broadcasted_iota(jnp.int32, (8, TILE), 0)
    mine = jnp.where(rows == place, row[0:1, :], 0.0)
    sent[2 * n + 8 : 2 * n + 16, 0:TILE] = mine
    planes[REACH * 8 :, :] = mine
    length = field.shape[0]
    even = core == 0
    for plane in range(REACH):
        low, high = (field[plane], field[length - REACH + plane])
        planes[plane * 8 : plane * 8 + 8, :] = jnp.where(even, low, high)
        sent[plane_rows(n, plane), plane_lanes(plane)] = jnp.where(even, high, low)


def own_kernel(planes, early, late, isos, lead, own):
    n = lead.shape[0]
    own[2 * n + 8 : 2 * n + 16, 0:TILE] = planes[REACH * 8 :, :]
    slabs(early[...], late[...], isos, lead, own, None)


def advance(map_ref, state):
    n = map_ref.shape[1]
    composed = split(map_ref[0:n, :])
    term = product(composed, split(state))
    return product(split(term), composed, True) + map_ref[n : 2 * n, :]


def near_far(mine, other):
    core = lax.rem(lax.axis_index("slab"), 2)
    return jnp.where(core == 0, mine, other), jnp.where(core == 0, other, mine)


def relay_kernel(
    own, got, own_step, got_step, field, second, out, stack, parts, wide, cells, one_side, two_side
):
    place, wire = (lax.axis_index("slab"), lax.axis_index("energy"))
    n = own.shape[1]
    length, height, _ = field.shape
    even = lax.rem(place, 2) == 0
    wide[REACH : REACH + length] = field[...]
    for plane in range(REACH):
        one = got[plane_rows(n, plane), plane_lanes(plane)]
        two = second[plane * 8 : plane * 8 + 8, :]
        wide[plane] = jnp.where(even, two, one)
        wide[REACH + length + plane] = jnp.where(even, one, two)
    spot = slice(2 * n + 8, 2 * n + 16)
    cells[...] = own[spot, :TILE] + got[spot, :TILE] + second[REACH * 8 :, :]
    even = lax.rem(wire, 2) == 0
    for plane in range(length + 2 * REACH):
        low, high = (wide[plane, :REACH, :], wide[plane, height - REACH :, :])
        spot = slice(plane * REACH, (plane + 1) * REACH)
        one_side[spot, :] = jnp.where(even, high, low)
        two_side[spot, :] = jnp.where(even, low, high)

    @pl.when(place == 0)
    def _():
        pack(advance(got, own[n : 2 * n, :]), out)

    @pl.when(place == 1)
    def _():
        pack(advance(own, got[n : 2 * n, :]), out)

    @pl.when(place >= 2)
    def _():
        near_step, far_step = near_far(own_step[...], got_step[...])
        near_map, far_map = near_far(own[0:n, :], got[0:n, :])
        far = jnp.concatenate([far_step, far_map], axis=0)
        both = product_joined(joined(split(far)), split(near_map))
        for number, value in enumerate((near_step, near_map, both[:n], both[n:])):
            rows = slice(number * n, (number + 1) * n)
            stack[rows, :] = value
            high, low = split(value)
            parts[rows, :] = jnp.concatenate(
                [high, low, high[:, : n - TILE], low[:, : n - TILE], high[:, : n - TILE]], axis=1
            )


def pass_kernel(turn, packed, own, got, out, state):
    place = lax.axis_index("slab")
    for core, (near, far) in enumerate(((own, got), (got, own))):

        @pl.when(place == 2 * turn + core)
        def _():
            unpack(packed, state)
            state[...] = advance(near, state[...])
            pack(advance(far, state[...]), out)


def known_kernel(
    pairs, weight_ref, group_ref, orbital_atom, member, own, got, own_step, got_step, fold, weights
):
    place = lax.axis_index("slab")
    core = lax.rem(place, 2)
    pair_rows = lax.broadcasted_iota(jnp.int32, (pairs, TILE), 0)
    mine_weight = jnp.where(core == 0, weight_ref[:, 0:1], weight_ref[:, 1:2])
    mine_group = jnp.where(core == 0, group_ref[:, 0:1], group_ref[:, 1:2])
    groups = weights.shape[0] // (2 * pairs)
    for half in range(2):
        for group in range(groups):
            weight = jnp.where(mine_group == group, mine_weight, 0.0)
            start = (half * groups + group) * pairs
            weights[start : start + pairs, :] = jnp.where(
                pair_rows == place - core + half, jnp.broadcast_to(weight, (pairs, TILE)), 0.0
            )
    n = own.shape[1]
    atoms = lax.broadcasted_iota(jnp.int32, (TILE, n), 0)
    spots = (atoms == orbital_atom[...]).astype(BF16)
    _, far_step = near_far(own_step[...], got_step[...])
    _, far_map = near_far(own[0:n, :], got[0:n, :])
    near_source, _ = near_far(own[n : 2 * n, :], got[n : 2 * n, :])
    far = jnp.concatenate([far_step, far_map], axis=0)
    both = product_joined(joined(split(far)), split(near_source))
    near_rows, far_rows = near_far(own[2 * n : 2 * n + 2, :], got[2 * n : 2 * n + 2, :])
    rest = jnp.concatenate([near_rows, far_rows, jnp.zeros((4, n), F32)], axis=0)
    total = jnp.zeros((8, TILE), F32)
    for _ in range(3):
        piece = rest.astype(BF16)
        total = total + dot(piece, spots, True)
        rest = rest - piece.astype(F32)
    fold[...] = total
    for number in range(2):
        rows = slice(number * n, (number + 1) * n)
        value = jnp.sum(far[rows] * both[rows], axis=1, keepdims=True) * member[...]
        fold[2 + number : 3 + number, :] += jnp.sum(value, axis=0, keepdims=True)


def density_kernel(
    pairs,
    member,
    packed,
    stack,
    wide,
    known,
    weights,
    extra,
    out,
    state,
    fold,
):
    place = lax.axis_index("slab")
    n = state.shape[0]
    fold[...] = known[...]

    @pl.when(place >= 2)
    def _():
        unpack(packed, state)
        high, low = split(state[...])
        cut = n - TILE
        corner = [x[:cut, :cut] for x in (high, high, low)]
        corner = jnp.concatenate(corner, axis=0)
        last_high, last_low = (high[:, cut:], low[:, cut:])
        last = [
            jnp.concatenate([last_high, last_low], axis=1),
            jnp.concatenate([last_high, jnp.zeros_like(last_high)], axis=1),
        ]
        last = jnp.concatenate(last, axis=0)
        for number in range(4):
            rows = slice(number * n, (number + 1) * n)
            one = dot(wide[rows, 2 * n :], corner, False)
            two = dot(wide[rows, : 2 * n], last, False)
            both = jnp.concatenate([one, two[:, :TILE] + two[:, TILE:]], axis=1)
            value = jnp.sum(stack[rows, :] * both, axis=1, keepdims=True) * member[...]
            fold[number : number + 1, :] += jnp.sum(value, axis=0, keepdims=True)

    plain = fold[...]
    turned = pltpu.roll(plain, HALF, 1)
    rows = out.shape[0] - extra.shape[0]
    values = [plain[2 * i : 2 * i + 1, :] + turned[2 * i + 1 : 2 * i + 2, :] for i in range(2)]
    out[:rows, :] = weights[:rows, :] * values[0] + weights[rows:, :] * values[1]
    out[rows:, :] = extra[...]


def local_call(kernel, shapes, scratch, specs, name, limit, flops, *operands):
    spaces = {"v": pltpu.VMEM, "s": pltpu.SMEM, "h": pltpu.HBM}
    single = not isinstance(shapes, tuple)
    vmem = pl.BlockSpec(memory_space=pltpu.VMEM)
    return pl.pallas_call(
        kernel,
        out_shape=shapes,
        in_specs=[pl.BlockSpec(memory_space=spaces[spec]) for spec in specs],
        out_specs=vmem if single else (vmem,) * len(shapes),
        scratch_shapes=scratch,
        compiler_params=pltpu.CompilerParams(vmem_limit_bytes=limit * 2**20),
        cost_estimate=pl.CostEstimate(flops=flops, bytes_accessed=2**20, transcendentals=0),
        name=name,
    )(*operands)


def shifted_pair(x, axis):
    size = x.shape[axis]
    before, after = (pltpu.roll(x, 1, axis), pltpu.roll(x, size - 1, axis))
    if axis == x.ndim - 1:
        lanes = lax.broadcasted_iota(jnp.int32, x.shape, axis)
        before = jnp.where(lanes == 0, 0.0, before)
        after = jnp.where(lanes == size - 1, 0.0, after)
    return before, after


def neighbours(x):
    centre = x[1:-1]
    up, down = shifted_pair(centre, 1)
    left, right = shifted_pair(centre, 2)
    return (x[2:] + x[:-2]) + (up + down) + (left + right)


def differences(x):
    centre = x[1:-1]
    up, down = shifted_pair(centre, 1)
    left, right = shifted_pair(centre, 2)
    along = (x[2:] - centre) + (x[:-2] - centre)
    across = (up - centre) + (down - centre)
    deep = (left - centre) + (right - centre)
    return along + (across + deep)


def grid_mask(shape, margin, length, rows, place, devices, wire, wires):
    planes = lax.broadcasted_iota(jnp.int32, shape, 0)
    row = lax.broadcasted_iota(jnp.int32, shape, 1)
    low_x = jnp.where(place == 0, margin, 0)
    high_x = jnp.where(place == devices - 1, margin + length, shape[0])
    low_y = jnp.where(wire == 0, rows, 0)
    high_y = jnp.where(wire == wires - 1, 2 * rows, shape[1])
    inside = (planes >= low_x) & (planes < high_x) & (row >= low_y) & (row < high_y)
    return inside.astype(F32)


def three_parts(x):
    parts = []
    for _ in range(3):
        parts.append(x.astype(BF16))
        x = x - parts[-1].astype(F32)
    return parts


def coordinates(cell, rows_y, depth):
    z_part = cell - depth * jnp.floor(cell * (1.0 / depth))
    plane = jnp.floor(cell * (1.0 / depth))
    x_part = jnp.floor(plane * (1.0 / rows_y))
    return x_part, plane - rows_y * x_part, z_part


WALKS = ((0, 1),), ((1, 1),), ((0, 2), (2, 1)), ((1, 3), (3, 1)), ((0, 6), (2, 4), (4, 1)), ((1, 10), (3, 5), (5, 1))
FACTORIAL = (1.0, 1.0, 2.0, 6.0, 24.0, 120.0)


def walk_counts(here, there, length):
    apart = jnp.abs(here - there)
    low = here + there + 2.0
    high = 2.0 * length - here - there
    at = []
    for steps in range(6):
        value = (apart == steps).astype(F32)
        if steps >= 2:
            value = value - (low == steps).astype(F32) - (high == steps).astype(F32)
        at.append(value)
    counts = []
    for steps, terms in enumerate(WALKS):
        total = None
        for distance, count in terms:
            term = at[distance] * (count / FACTORIAL[steps])
            total = term if total is None else total + term
        counts.append(total)
    return counts


def convolved(left, right):
    result = []
    for steps in range(6):
        total = left[0] * right[steps]
        for part in range(1, steps + 1):
            total = total + left[part] * right[steps - part]
        result.append(total)
    return result


def moments_kernel(devices, wires, own, field, one_beside, two_beside, cells, out, wide_field, whole_field):
    place, wire = (lax.axis_index("slab"), lax.axis_index("energy"))
    planes, rows, depth = field.shape
    length = planes - 2 * REACH
    width_x = length // 2
    atoms = cells.shape[1]
    grid_y = rows * wires
    pairs = devices
    n = own.shape[1]
    even = lax.rem(wire, 2) == 0
    whole_field[...] = jnp.zeros_like(whole_field)
    whole_field[:, rows : 2 * rows, :] = field[...]
    for plane in range(planes):
        spot = slice(plane * REACH, (plane + 1) * REACH)
        one, two = (one_beside[spot, :], two_beside[spot, :])
        whole_field[plane, rows - REACH : rows, :] = jnp.where(even, two, one)
        whole_field[plane, 2 * rows : 2 * rows + REACH, :] = jnp.where(even, one, two)
    whole = (planes, 3 * rows, depth)
    mask = grid_mask(whole, REACH, length, rows, place, devices, wire, wires)
    source = jnp.where(mask > 0, whole_field[...], 0.0)
    margin = ITERS - 1
    wide_field[...] = source[REACH - margin : REACH + length + margin]

    def inner(x):
        extra = (x.shape[0] - length) // 2
        return x[extra : extra + length, rows : 2 * rows]

    chain = [source]
    for step in range(1, 6):
        chain.append(neighbours(chain[-1]) * mask[step : planes - step])
    blocks = [inner(x) for x in chain]
    near = source[2:-2]
    other = [near]
    for step in range(1, 4):
        other.append(differences(other[-1]) * mask[2 + step : planes - 2 - step])
    other = [inner(x) for x in other]
    lanes = lax.broadcasted_iota(jnp.int32, (1, depth), 1)
    sums = jnp.zeros((1, depth), F32)
    for base, fields in enumerate((blocks, other)):
        for steps in range(6):
            part = jnp.sum(fields[steps // 2] * fields[(steps + 1) // 2], axis=0)
            part = jnp.sum(jnp.sum(part, axis=1, keepdims=True), axis=0, keepdims=True)
            sums = jnp.where(lanes == atoms + 6 * base + steps, part, sums)
    out[...] = jnp.zeros_like(out)
    mine = own[2 * n + 8 : 2 * n + 16, :depth]
    mine = jnp.sum(mine, axis=0, keepdims=True)
    lane = lax.broadcasted_iota(jnp.int32, (1, depth), 1)
    odd = (lane >= HALF).astype(F32)
    used = lax.rem(lane, HALF) < atoms
    x_part, y_part, z_part = coordinates(mine, grid_y, depth)
    start = (wire * rows).astype(F32)
    ours = used & (y_part >= start) & (y_part < start + rows)
    at_row = jnp.where(ours, (x_part + width_x * odd) * rows + y_part - start, -1.0)
    cell_rows = length * rows
    row_iota = lax.broadcasted_iota(jnp.int32, (cell_rows, depth), 0).astype(F32)
    deep_iota = lax.broadcasted_iota(jnp.int32, (depth, depth), 0).astype(F32)
    at_rows = (row_iota == at_row).astype(F32)
    at_deep = (deep_iota == z_part).astype(BF16)
    for steps, block in enumerate(blocks):
        value = jnp.zeros((cell_rows, depth), F32)
        for part in three_parts(block.reshape(cell_rows, depth)):
            value = value + dot(part, at_deep, False)
        value = jnp.sum(value * at_rows, axis=0, keepdims=True)
        out[pl.ds(steps * pairs + place, 1), :] = value
    out[0:1, :] += sums


def atoms_kernel(
    devices,
    wires,
    length,
    charge_ref,
    orbital_atom,
    some_cells,
    other_cells,
    walks,
    row_hot,
    deep_hot,
    member,
    charges,
):
    place, wire = (lax.axis_index("slab"), lax.axis_index("energy"))
    rows, depth = some_cells.shape
    width_x = length // 2
    atoms = walks.shape[1] // (2 * devices)
    grid_y = rows * wires
    pairs = devices
    n = orbital_atom.shape[1]
    start = (wire * rows).astype(F32)
    for group in range(charges.shape[0] // pairs):
        charges[group * pairs : (group + 1) * pairs, :] = jnp.broadcast_to(
            charge_ref[:, group : group + 1], (pairs, depth)
        )
    cells = jnp.maximum(some_cells[...], other_cells[...])
    spots = lax.broadcasted_iota(jnp.int32, (TILE, n), 0) == orbital_atom[...]
    spots = spots.astype(F32)
    for first in range(0, n, TILE):
        member[first : first + TILE, :] = spots[:, first : first + TILE].T
    row_cells = cells
    row_x, row_y, row_z = coordinates(row_cells, grid_y, depth)
    padded = jnp.concatenate([row_cells, jnp.zeros((depth - 8, depth), F32)], axis=0)
    column_x, column_y, column_z = coordinates(padded.T, grid_y, depth)
    row_lane = lax.broadcasted_iota(jnp.int32, (8, depth), 1)
    next_x, next_y, next_z = [jnp.concatenate([v[1:], v[:1]], axis=0) for v in (row_x, row_y, row_z)]

    def turned(now, later, step_now, step_later):
        value = jnp.where(row_lane >= HALF, now + step_now, later + step_later)
        return pltpu.roll(value, HALF, 1)

    even_x = row_x + width_x * (row_lane >= HALF).astype(F32)
    odd_x, odd_y, odd_z = (
        turned(row_x, next_x, 0.0, float(width_x)),
        turned(row_y, next_y, 0.0, 0.0),
        turned(row_z, next_z, 0.0, 0.0),
    )
    for slab in range(2 * pairs):
        pair, side = (slab // 2, slab % 2)
        base = float(slab * width_x)
        if side:
            there = (odd_x, odd_y, odd_z)
        else:
            there = (even_x, row_y, row_z)
        there = [v[pair : pair + 1, :] for v in there]
        here = [
            v[side * HALF : side * HALF + atoms, pair : pair + 1]
            for v in (column_x, column_y, column_z)
        ]
        shape = (atoms, depth)
        sizes = (2 * pairs * width_x, grid_y, depth)
        axes = []
        for axis in range(3):
            shift = base if axis == 0 else 0.0
            axes.append(
                walk_counts(
                    jnp.broadcast_to(here[axis] + shift, shape),
                    jnp.broadcast_to(there[axis] + shift, shape),
                    float(sizes[axis]),
                )
            )
        total = convolved(convolved(axes[0], axes[1]), axes[2])
        for steps in range(6):
            walks[steps, slab * atoms : (slab + 1) * atoms, :] = total[steps] * FACTORIAL[steps]
    wide = length + 4
    first_x = (place * length - 2).astype(F32)
    first_y = start - rows
    count = wide * 3 * rows
    rows_iota = lax.broadcasted_iota(jnp.int32, (count, depth), 0).astype(F32)
    used_row = lax.rem(row_lane, HALF) < atoms
    for pair in range(pairs):
        x_at = even_x[pair : pair + 1, :] + float(2 * pair * width_x) - first_x
        y_at = row_y[pair : pair + 1, :] - first_y
        good = (x_at >= 0) & (x_at < wide) & (y_at >= 0) & (y_at < 3 * rows) & used_row[0:1, :]
        target = jnp.where(good, x_at * (3 * rows) + y_at, -1.0)
        row_hot[:, pair * depth : (pair + 1) * depth] = (rows_iota == target).astype(BF16)
        z_at = column_z[:, pair : pair + 1]
        lanes_z = lax.broadcasted_iota(jnp.int32, (depth, depth), 1).astype(F32)
        deep_hot[pair * depth : (pair + 1) * depth, :] = (lanes_z == z_at).astype(F32)


def total_of(x):
    return jnp.sum(jnp.sum(x, axis=1, keepdims=True), axis=0, keepdims=True)


def quadratic_form(poly, moments, shift):
    total = None
    for i, one in enumerate(poly):
        for j, two in enumerate(poly):
            if j < i:
                continue
            term = one * two * moments[i + j + shift] * (1.0 if i == j else 2.0)
            total = term if total is None else total + term
    return total


def finish_kernel(
    devices,
    wires,
    atoms,
    payload,
    walks,
    row_hot,
    deep_hot,
    charges,
    field,
    density,
    potential,
):
    place, wire = (lax.axis_index("slab"), lax.axis_index("energy"))
    length, rows, depth = potential.shape
    pairs = devices
    groups = density.shape[0]
    held = charges[...] * payload[: groups * pairs, :]
    charge = held[:pairs]
    for group in range(1, groups):
        charge = charge + held[group * pairs : (group + 1) * pairs]
    for group in range(groups):
        value = payload[pl.ds(group * pairs + place, 1), :]
        density[group, 0:1, :] = value[:, :atoms]
        density[group, 1:2, :] = pltpu.roll(value, HALF, 1)[:, :atoms]
    square = jnp.concatenate([charge, jnp.zeros((depth - pairs, depth), F32)], axis=0)
    columns = square.T
    later = jnp.concatenate([charge[1:], jnp.zeros((1, depth), F32)], axis=0)
    lanes = lax.broadcasted_iota(jnp.int32, (pairs, depth), 1)
    even_row = jnp.where(lanes >= HALF, 2.0 * charge, charge)
    odd_row = pltpu.roll(jnp.where(lanes >= HALF, charge, 2.0 * later), HALF, 1)
    totals = [None] * 6
    for slab in range(2 * pairs):
        pair, side = (slab // 2, slab % 2)
        row = (odd_row if side else even_row)[pair : pair + 1, :]
        column = columns[side * HALF : side * HALF + atoms, pair : pair + 1]
        outer = column * row
        for steps in range(6):
            term = walks[steps, slab * atoms : (slab + 1) * atoms, :] * outer
            totals[steps] = term if totals[steps] is None else totals[steps] + term
    base = groups * pairs
    crossed = []
    for steps in range(6):
        cross = 2.0 * charge * payload[base + steps * pairs : base + (steps + 1) * pairs, :]
        parts = [totals[steps][i : i + 8] for i in range(0, atoms, 8)]
        if pairs < 8:
            cross = jnp.concatenate([cross, jnp.zeros((8 - pairs, depth), F32)], axis=0)
        parts.append(cross)
        while len(parts) > 1:
            parts = [sum(parts[i : i + 2][1:], parts[i]) for i in range(0, len(parts), 2)]
        crossed.append(total_of(parts[0]))
    lane = lax.broadcasted_iota(jnp.int32, (1, depth), 1)
    row = payload[base : base + 1, :]
    sums = [
        jnp.sum(jnp.where(lane == atoms + i, row, 0.0), axis=1, keepdims=True) for i in range(12)
    ]
    plain = [sums[steps] + crossed[steps] for steps in range(6)]
    moved = []
    for steps in range(6):
        value = sums[6 + steps]
        binomial = 1
        for part in range(steps, -1, -1):
            value = value + (binomial * (-6.0) ** (steps - part)) * crossed[part]
            binomial = binomial * part // (steps - part + 1)
        moved.append(value)
    smooth = plain[1] > 3.5 * plain[0]
    level = jnp.where(smooth, 0.5, 6.5)
    moments = [jnp.where(smooth, two, one) for one, two in zip(plain, moved)]
    residual, direction = ([jnp.ones_like(level)], [jnp.ones_like(level)])
    norm = moments[0]
    alphas, betas = ([], [])
    for turn in range(ITERS):
        energy = level * quadratic_form(direction, moments, 0) - quadratic_form(direction, moments, 1)
        alpha = jnp.clip(norm / energy, 1.0 / 12.5, 2.0)
        alphas.append(alpha)
        if turn + 1 == ITERS:
            break
        longer = residual + [jnp.zeros_like(level)]
        for i, value in enumerate(direction):
            longer[i] = longer[i] - alpha * level * value
            longer[i + 1] = longer[i + 1] + alpha * value
        residual = longer
        following = quadratic_form(residual, moments, 0)
        beta = jnp.clip(following / norm, 0.0, 25.0)
        betas.append(beta)
        norm = following
        direction = [
            value + beta * direction[i] if i < len(direction) else value
            for i, value in enumerate(residual)
        ]
    pieces = [[], [], []]
    for pair in range(pairs):
        hot = deep_hot[pair * depth : (pair + 1) * depth, :]
        for place_in, piece in enumerate(three_parts(columns[:, pair : pair + 1] * hot)):
            pieces[place_in].append(piece)
    spread = jnp.concatenate([jnp.concatenate(piece, axis=0) for piece in pieces], axis=1)
    placed = dot(row_hot[...], spread, False)
    placed = placed[:, :depth] + (placed[:, depth : 2 * depth] + placed[:, 2 * depth :])
    margin = ITERS - 1
    wide = (length + 2 * margin, 3 * rows, depth)
    mask = grid_mask(wide, margin, length, rows, place, devices, wire, wires)
    source = field[...] + placed.reshape(wide)
    residual, direction = (source, source)
    total = alphas[0] * source[margin:-margin, rows : 2 * rows]
    for turn in range(ITERS - 1):
        image = 6.5 * direction[1:-1] - neighbours(direction)
        inner_mask = mask[turn + 1 : wide[0] - turn - 1]
        residual = (residual[1:-1] - alphas[turn] * image) * inner_mask
        direction = residual + betas[turn] * direction[1:-1]
        extra = margin - turn - 1
        block = direction[extra : extra + length, rows : 2 * rows]
        total = total + alphas[turn + 1] * block
    potential[...] = total


def hop(count, turn):
    moves = {i: i for i in range(count)}
    for core in range(2):
        here, there = (2 * turn - 2 + core, 2 * turn + core)
        moves[here], moves[there] = (there, here)
    return sorted(moves.items())


def pairs_of(count):
    return [(i, i ^ 1) for i in range(count)]


def total_over(value, axis, strides):
    size = 1
    for name in axis if isinstance(axis, tuple) else (axis,):
        size *= lax.axis_size(name)
    got = [lax.ppermute(value, axis, [(i, i ^ k) for i in range(size)]) for k in strides]
    if len(got) == 1:
        return value + got[0]
    return (value + got[0]) + (got[1] + got[2])


def total_over_all(value):
    size, slabs = (lax.axis_size("energy") * lax.axis_size("slab"), lax.axis_size("slab"))
    value = total_over(value, "slab", (1,))
    strides = [1 << i for i in range(1, size.bit_length() - 1)]
    far = [stride for stride in strides if stride > slabs // 2]
    near = [stride for stride in strides if stride <= slabs // 2]
    order = far[:2] + near + far[2:]
    while order:
        one, *rest = order[:2]
        value = total_over(value, BOTH, (one, *rest, *[one + two for two in rest]))
        order = order[2:]
    return value


def inner_pairs(count, slabs):
    moves = []
    for i in range(count * slabs):
        wire, place = divmod(i, slabs)
        if wire in (0, count - 1):
            moves.append((i, i ^ 1))
        else:
            moves.append((i, (wire + 1 if wire % 2 else wire - 1) * slabs + place))
    return moves


def neighbour_turn(count):
    return [(i, (i + 1) % count if i % 2 else (i - 1) % count) for i in range(count)]


def on_device(
    green_iso,
    coupling,
    lead_green,
    energy_weight,
    energy_group,
    group_charge,
    orbital_atom,
    atom_cell,
    doping,
):
    devices, wires = (lax.axis_size("slab"), lax.axis_size("energy"))
    groups = group_charge.shape[0]
    atoms = atom_cell.shape[1]
    n = lead_green.shape[-1]
    length, rows, depth = doping.shape
    shape = jax.ShapeDtypeStruct
    orbital_row = orbital_atom.reshape(1, n)
    maps = shape((2 * n + 32, n), F32)
    edge_rows = REACH * rows + 8
    held = [
        pltpu.with_memory_space_constraint(x, pltpu.HBM)
        for x in (green_iso, coupling, lead_green, atom_cell, doping)
    ]
    matrix = shape((n, n), F32)
    two = shape((2, n, n), F32)
    sent_step, sent, edge, own_step, own_late, own_iso, own_lead = local_call(
        other_kernel,
        (matrix, maps, shape((edge_rows, depth), F32), matrix, matrix, two, matrix),
        [
            pltpu.VMEM((2, n, n), F32),
            pltpu.VMEM((2, n, n), F32),
            pltpu.VMEM((n, n), F32),
            pltpu.SemaphoreType.DMA((8,)),
            pltpu.VMEM((8, TILE), F32),
            pltpu.VMEM(atom_cell.shape, jnp.int32),
            pltpu.VMEM(doping.shape, F32),
            pltpu.SemaphoreType.DMA((2,)),
        ],
        "hhhhh",
        "other",
        28,
        48 * n**3,
        *held,
    )
    got = lax.ppermute(sent, "slab", pairs_of(devices))
    second = lax.ppermute(edge, "slab", neighbour_turn(devices))
    own = local_call(
        own_kernel,
        maps,
        [],
        "vvvvv",
        "own",
        24,
        2**31,
        edge,
        own_step,
        own_late,
        own_iso,
        own_lead,
    )
    side = shape((-(-REACH * (length + 2 * REACH) // 8) * 8, depth), F32)
    got_step = lax.ppermute(sent_step, "slab", pairs_of(devices))
    passed, stack, stack_parts, wide_block, cells, one_side, two_side = local_call(
        relay_kernel,
        (
            shape((PACKED_ROWS, TILE), F32),
            shape((4 * n, n), F32),
            shape((4 * n, 5 * n - 3 * TILE), BF16),
            shape((length + 2 * REACH, rows, depth), F32),
            shape((8, depth), F32),
            side,
            side,
        ),
        [],
        "vvvvvv",
        "relay",
        28,
        12 * n**3,
        own,
        got,
        own_step,
        got_step,
        doping,
        second,
    )
    packed = lax.ppermute(passed, "slab", hop(devices, 1))
    one_beside = lax.ppermute(one_side, "energy", pairs_of(wires))
    two_beside = lax.ppermute(two_side, BOTH, inner_pairs(wires, devices))
    other_cells = lax.ppermute(cells, "slab", pairs_of(devices))
    if devices > 4:
        other_cells = lax.psum(own[2 * n + 8 : 2 * n + 16, :depth], "slab")
    wide = (length + 2 * ITERS - 2, 3 * rows, depth)
    walks, row_hot, deep_hot, member, charges = local_call(
        functools.partial(atoms_kernel, devices, wires, length),
        (
            shape((6, 2 * devices * atoms, depth), F32),
            shape((wide[0] * wide[1], devices * depth), BF16),
            shape((devices * depth, depth), F32),
            shape((n, TILE), F32),
            shape((groups * devices, depth), F32),
        ),
        [],
        "vvvv",
        "atoms",
        28,
        2**29,
        group_charge.reshape(1, groups),
        orbital_row,
        cells,
        other_cells,
    )
    extra, wide_field = local_call(
        functools.partial(moments_kernel, devices, wires),
        (shape((6 * devices, depth), F32), shape(wide, F32)),
        [pltpu.VMEM((length + 2 * REACH, 3 * rows, depth), F32)],
        "vvvvv",
        "moments",
        20,
        2**26,
        own,
        wide_block,
        one_beside,
        two_beside,
        atom_cell,
    )
    known, weights = local_call(
        functools.partial(known_kernel, devices),
        (shape((8, TILE), F32), shape((2 * groups * devices, TILE), F32)),
        [],
        "vvvvvvvv",
        "known",
        24,
        2**28,
        energy_weight.reshape(1, -1),
        energy_group.reshape(1, -1),
        orbital_row,
        member,
        own,
        got,
        own_step,
        got_step,
    )
    for turn in range(1, devices // 2 - 1):
        passed = local_call(
            functools.partial(pass_kernel, turn),
            shape((PACKED_ROWS, TILE), F32),
            [pltpu.VMEM((n, n), F32)],
            "vvv",
            "pass_on",
            20,
            24 * n**3,
                packed,
            own,
            got,
        )
        arrived = lax.ppermute(passed, "slab", hop(devices, turn + 1))
        packed = jnp.where(lax.axis_index("slab") // 2 == turn + 1, arrived, packed)
    payload = local_call(
        functools.partial(density_kernel, devices),
        shape(((groups + 6) * devices, TILE), F32),
        [pltpu.VMEM((n, n), F32), pltpu.VMEM((8, TILE), F32)],
        "vvvvvvv",
        "density",
        20,
        24 * n**3,
        member,
        packed,
        stack,
        stack_parts,
        known,
        weights,
        extra,
    )
    payload = total_over_all(payload)
    return local_call(
        functools.partial(finish_kernel, devices, wires, atoms),
        (shape((groups, 2, atoms), F32), shape(doping.shape, F32)),
        [],
        "vvvvvv",
        "finish",
        28,
        2**29,
        payload,
        walks,
        row_hot,
        deep_hot,
        charges,
        wide_field,
    )


def solution(mesh):
    in_specs = (
        P("energy", "slab", None, None),
        P("slab", None, None),
        P("energy", None, None),
        P("energy"),
        P("energy"),
        P(),
        P(),
        P("slab", None),
        P("slab", "energy", None),
    )
    out_specs = (P(None, "slab", None), P("slab", "energy", None))
    return jax.shard_map(
        on_device, mesh=mesh, in_specs=in_specs, out_specs=out_specs, check_vma=False
    )
```
